32 devices in a mesh: dp: 4 (over y, x), fsdp: 8 (over z, core).
Axes of the slice: x: 2, y: 2, z: 4, core: 2. Of those that a mesh axis runs over, the one named last changes fastest.
Arguments:
- tokens: bfloat16 [8192, 1536], P(('dp', 'fsdp')), may hold values from -6 to 6
- lengths: int32 [32], P(('dp', 'fsdp')), may hold values from 128 to 256, as said below
- routes: int32 [8192, 4], P(('dp', 'fsdp')), may hold values from 0 to 7, all different within a row; in each aligned block of 256 rows (0 to 255, 256 to 511, ...) at most 160 rows name the same one
- cotangent: bfloat16 [8192, 1536], P(('dp', 'fsdp')), may hold values from -6 to 6
- gain_one: bfloat16 [1536], P(('dp', 'fsdp')), may hold values from 0.5 to 1.5
- w_query: bfloat16 [1536, 1536], P(('dp', 'fsdp')), may hold values from -0.15625 to 0.15625
- key_matrix: bfloat16 [1536, 256], P(('dp', 'fsdp')), may hold values from -0.15625 to 0.15625
- value_matrix: bfloat16 [1536, 256], P(('dp', 'fsdp')), may hold values from -0.15625 to 0.15625
- w_out: bfloat16 [1536, 1536], P(('dp', 'fsdp')), may hold values from -1.25 to 1.25
- gain_two: bfloat16 [1536], P(('dp', 'fsdp')), may hold values from 0.5 to 1.5
- w_router: bfloat16 [1536, 8], P(('dp', 'fsdp')), may hold values from -0.078125 to 0.078125
- w_gate: bfloat16 [8, 1536, 768], P('dp', 'fsdp'), may hold values from -0.15625 to 0.15625
- w_up: bfloat16 [8, 1536, 768], P('dp', 'fsdp'), may hold values from -0.15625 to 0.15625
- w_down: bfloat16 [8, 1536, 768], P('dp', 'fsdp'), may hold values from -1.25 to 1.25
Outputs:
- block_out: bfloat16 [8192, 1536], P(('dp', 'fsdp'))
- grad_tokens: float32 [8192, 1536], P(('dp', 'fsdp'))
- grad_gain_one: float32 [1536], P(('dp', 'fsdp'))
- grad_query: float32 [1536, 1536], P(('dp', 'fsdp'))
- grad_key: float32 [1536, 256], P(('dp', 'fsdp'))
- grad_value: float32 [1536, 256], P(('dp', 'fsdp'))
- grad_out: float32 [1536, 1536], P(('dp', 'fsdp'))
- grad_gain_two: float32 [1536], P(('dp', 'fsdp'))
- grad_router: float32 [1536, 8], P(('dp', 'fsdp'))
- grad_gate: float32 [8, 1536, 768], P('dp', 'fsdp')
- grad_up: float32 [8, 1536, 768], P('dp', 'fsdp')
- grad_down: float32 [8, 1536, 768], P('dp', 'fsdp')
The draws below stay inside these ranges and needn't reach their ends.
Inputs may be any that keep to these rules, and one draw needn't show every extreme that they name: `lengths`: each device's block of 256 slots holds one sequence; some block is full and some holds exactly 128 live tokens. `routes`: each row names 4 different experts. Within the rows of one device no expert is named more than 160 times, and on some device one expert is named exactly 160 times.
All inputs are finite; a program needn't handle non-finite values.
Results may differ from the reference program's by a relative error of at most 0.018.
Values may be sent and summed in bfloat16 or wider, within the bound.
No kernel may reach another device: no remote copies, remote signals or barrier semaphores. Data moves between devices by JAX's collectives and lax.ppermute only.
A program may use at most 192 MiB of HBM per device.

```python
import math
import jax
import jax.numpy as jnp
import numpy as np
from jax import lax

MODEL_WIDTH = 1536
QUERY_HEADS = 12
KEY_VALUE_HEADS = 2
HEAD_SIZE = 128
F = 768
EXPERTS = 8
TOPK = 4
MINLEN = 128
TOK_DEV = 256
CAP = 160
TOKENS = 8192
N_DP = 4
N_FSDP = 8


def draw_lengths(key, part):
    key = jax.random.fold_in(key, 11)
    first_key, second_key = jax.random.split(key)
    blocks = N_DP * N_FSDP
    drawn = jax.random.randint(first_key, (blocks,), MINLEN, TOK_DEV + 1, dtype=jnp.int32)
    order = jax.random.permutation(second_key, blocks)
    drawn = drawn.at[order[0]].set(TOK_DEV)
    drawn = drawn.at[order[1]].set(MINLEN)
    return drawn.astype(jnp.int32)


def levels(own_key, extent, cuts, smallest, largest):
    factor_of = 1.0
    for dim, blocks in cuts:
        heights = jax.random.uniform(jax.random.fold_in(jax.random.fold_in(own_key, 6), dim), (blocks,), jnp.float32, smallest / len(cuts), largest / len(cuts))
        factor_of = factor_of * jnp.repeat(jnp.exp(heights), extent[dim] // blocks).reshape((-1,) + (1,) * (len(extent) - 1 - dim))
    return factor_of


def assign_block(own_key, own, number, rows, count, top, bound, slope):
    ranking = jax.random.permutation(own_key, count)
    heavy_load, common = shares(count, rows * top, bound, slope, True), shares(count, rows * top, bound, slope, False)
    places = jnp.arange(count)

    def named(sizes, rotation):
        used = int((sizes > 0).sum())
        fixed = max(1, used // 4)
        passed = fixed + (places - fixed + rotation * (used - fixed)) % max(1, count - fixed)
        return jnp.zeros((count,), jnp.int32).at[ranking[jnp.where(places < fixed, places, passed)]].set(jnp.asarray(sizes, jnp.int32))

    sizes = jnp.where(number % 4 == 0, named(heavy_load, number // 4), named(common, number - number // 4 - 1))
    mixed = jax.random.permutation(jax.random.fold_in(own, 3), count)
    giver, receiver = mixed[0:count // 2 * 2:2], mixed[1:count // 2 * 2:2]
    slack = jnp.minimum(sizes[giver] - 1, bound - sizes[receiver]) // 2
    slack = jnp.where((giver == ranking[0]) | (receiver == ranking[0]) | (sizes[receiver] == 0), 0, jnp.maximum(slack, 0))
    passed = jax.random.randint(jax.random.fold_in(own, 4), (count // 2,), 0, 1 << 20) % (slack + 1)
    sizes = sizes.at[giver].add(-passed).at[receiver].add(passed)
    items = jnp.searchsorted(jnp.cumsum(sizes), jnp.arange(rows * top), side="right").astype(jnp.int32)
    table = items.reshape(top, rows).T
    table = table[jax.random.permutation(jax.random.fold_in(own, 1), rows)]
    rotation = jax.random.randint(jax.random.fold_in(own, 2), (rows, 1), 0, top)
    return jnp.take_along_axis(table, (jnp.arange(top)[None, :] + rotation) % top, axis=1)


def shares(amount, total, most, skew, full):
    loads = [(1 << 20) // math.isqrt(standing ** skew) + 1 for standing in range(1, amount + 1)]
    largest = most if full else min(most, max(-(-total // amount), total * loads[0] // sum(loads)))
    least = 1 if total - largest >= amount - 1 else 0
    counts, spare = [largest] + [least] * (amount - 1), total - largest - least * (amount - 1)
    while spare > 0:
        free = [i for i in range(1, amount) if counts[i] < largest] or [i for i in range(1, amount) if counts[i] < most]
        mass, budget = sum([loads[i] for i in free]), spare
        for i in free:
            more = min(most - counts[i], max(1, budget * loads[i] // mass), spare)
            counts[i] = counts[i] + more
            spare = spare - more
    return np.array(counts)


def scatter_about(rng, dims, deviation, reach, cuts=(), kind=jnp.bfloat16):
    factor_of = levels(rng, dims, cuts, -0.22, 0.18) if cuts else 1.0
    entries = jax.random.normal(rng, dims, jnp.float32) * deviation * factor_of
    return jnp.minimum(jnp.maximum(entries, -reach), reach).astype(kind)


def setup_inputs(seed: int = 0) -> dict:
    keys = jax.random.split(jax.random.key(seed), 15)
    tokens = scatter_about(keys[0], (TOKENS, MODEL_WIDTH), 1.0, 6.0, ((0, 32),))
    lengths = draw_lengths(jax.random.fold_in(keys[14], 71), 0)
    routes_keys = jax.random.split(jax.random.fold_in(keys[2], 1), TOKENS // TOK_DEV)
    routes_turns = jax.random.permutation(jax.random.fold_in(keys[2], 3), TOKENS // TOK_DEV)
    routes = jax.vmap(lambda own, number: assign_block(jax.random.fold_in(keys[2], 2), own, number, TOK_DEV, EXPERTS, TOPK, CAP, 1))(routes_keys, routes_turns).reshape((TOKENS, TOPK))
    cotangent = scatter_about(keys[3], (TOKENS, MODEL_WIDTH), 1.0, 6.0, ((0, 32),))
    gain_one = jnp.clip(1.0 + 0.1 * jax.random.normal(keys[4], (MODEL_WIDTH,), jnp.float32), 0.5, 1.5).astype(jnp.bfloat16)
    w_query = scatter_about(keys[5], (MODEL_WIDTH, QUERY_HEADS * HEAD_SIZE), MODEL_WIDTH ** -0.5, 0.15625, ((0, 32),))
    key_matrix = scatter_about(keys[6], (MODEL_WIDTH, KEY_VALUE_HEADS * HEAD_SIZE), MODEL_WIDTH ** -0.5, 0.15625, ((0, 32),))
    value_matrix = scatter_about(keys[7], (MODEL_WIDTH, KEY_VALUE_HEADS * HEAD_SIZE), MODEL_WIDTH ** -0.5, 0.15625, ((0, 32),))
    w_out = scatter_about(keys[8], (QUERY_HEADS * HEAD_SIZE, MODEL_WIDTH), (QUERY_HEADS * HEAD_SIZE // 64) ** -0.5, 1.25, ((0, 32),))
    gain_two = jnp.clip(1.0 + 0.1 * jax.random.normal(keys[9], (MODEL_WIDTH,), jnp.float32), 0.5, 1.5).astype(jnp.bfloat16)
    w_router = scatter_about(keys[10], (MODEL_WIDTH, EXPERTS), (4 * MODEL_WIDTH) ** -0.5, 0.078125, ((0, 32),))
    w_gate = scatter_about(keys[11], (EXPERTS, MODEL_WIDTH, F), MODEL_WIDTH ** -0.5, 0.15625, ((0, 4), (1, 8)))
    w_up = scatter_about(keys[12], (EXPERTS, MODEL_WIDTH, F), MODEL_WIDTH ** -0.5, 0.15625, ((0, 4), (1, 8)))
    w_down = scatter_about(keys[13], (EXPERTS, MODEL_WIDTH, F), (F // 32) ** -0.5, 1.25, ((0, 4), (1, 8)))
    return dict(tokens=tokens, lengths=lengths, routes=routes, cotangent=cotangent, gain_one=gain_one, w_query=w_query, key_matrix=key_matrix, value_matrix=value_matrix, w_out=w_out, gain_two=gain_two, w_router=w_router, w_gate=w_gate, w_up=w_up, w_down=w_down)


@jax.custom_vjp
def lower_dtype(v):
    return lax.optimization_barrier(v.astype(jnp.bfloat16)).astype(jnp.float32)

@jax.custom_vjp
def lower_dtype_backward(v):
    return v

def low_keep(v):
    return (lower_dtype(v), None)

def low_pass(kept, grad):
    return (grad,)

def back_keep(v):
    return (v, None)

def back_low(kept, grad):
    return (lower_dtype(grad),)
lower_dtype.defvjp(low_keep, low_pass)
lower_dtype_backward.defvjp(back_keep, back_low)
EPS = 1e-06
ROPE_BASE = 1500000.0
HIGH_PRECISION = lax.Precision.HIGHEST
NEG_FILL = -1e+30

def rms_scale(tok_rows):
    return lax.rsqrt(lax.optimization_barrier(jnp.mean(tok_rows * tok_rows, axis=-1, keepdims=True)) + EPS)

def rope_tables(total_row_count):
    half_width = HEAD_SIZE // 2
    position = jnp.arange(total_row_count).astype(jnp.float32)
    inverse = ROPE_BASE ** (-jnp.arange(half_width).astype(jnp.float32) / half_width)
    angles = position[:, None] * inverse[None, :]
    return (jnp.cos(angles)[:, None, :], jnp.sin(angles)[:, None, :])

def apply_rotation(vals_in, cosine_table, sine_table):
    half_width = vals_in.shape[-1] // 2
    first_half = vals_in[..., :half_width]
    second_half = vals_in[..., half_width:]
    return jnp.concatenate([first_half * cosine_table - second_half * sine_table, second_half * cosine_table + first_half * sine_table], axis=-1)

def slot_index(route_rows):
    flat_routes = route_rows.reshape(-1)
    onehot = (flat_routes[:, None] == jnp.arange(EXPERTS, dtype=jnp.int32)[None, :]).astype(jnp.int32)
    earlier = jnp.cumsum(onehot, axis=0) - onehot
    placed = lax.optimization_barrier(jnp.sum(earlier * onehot, axis=1))
    return (flat_routes * CAP + placed).astype(jnp.int32)

def block_forward(params, tok_rows, length, route_rows):
    gain_one, w_query, key_matrix, value_matrix, w_out, gain_two, w_router, w_gate, w_up, w_down = params
    total_row_count = tok_rows.shape[0]
    query_group_width = QUERY_HEADS // KEY_VALUE_HEADS
    hidden_first = lower_dtype(tok_rows * rms_scale(tok_rows) * gain_one)
    query_unrotated = lower_dtype_backward(jnp.dot(hidden_first, w_query, precision=HIGH_PRECISION))
    key_rows_unrotated = lower_dtype_backward(jnp.dot(hidden_first, key_matrix, precision=HIGH_PRECISION))
    value_rows = lower_dtype(lower_dtype_backward(jnp.dot(hidden_first, value_matrix, precision=HIGH_PRECISION))).reshape(total_row_count, KEY_VALUE_HEADS, HEAD_SIZE)
    cosine_table, sine_table = rope_tables(total_row_count)
    query_rows = lower_dtype(apply_rotation(query_unrotated.reshape(total_row_count, QUERY_HEADS, HEAD_SIZE), cosine_table, sine_table)).reshape(total_row_count, KEY_VALUE_HEADS, query_group_width, HEAD_SIZE)
    key_rows_rotated = lower_dtype(apply_rotation(key_rows_unrotated.reshape(total_row_count, KEY_VALUE_HEADS, HEAD_SIZE), cosine_table, sine_table))
    scores = jnp.einsum('qhgd,shd->hgqs', query_rows, key_rows_rotated, precision=HIGH_PRECISION) * HEAD_SIZE ** (-0.5)
    position = jnp.arange(total_row_count)
    visible = (position[None, :] <= position[:, None]) & (position[None, :] < length)
    scores = lower_dtype_backward(jnp.where(visible, scores, NEG_FILL))
    weights = jax.nn.softmax(scores, axis=-1)
    mixed_rows = jnp.einsum('hgqs,shd->qhgd', lower_dtype(weights), value_rows, precision=HIGH_PRECISION)
    mixed_rows = lower_dtype(lower_dtype_backward(mixed_rows.reshape(total_row_count, QUERY_HEADS * HEAD_SIZE)))
    residual = tok_rows + lower_dtype_backward(jnp.dot(mixed_rows, w_out, precision=HIGH_PRECISION))
    h_two = lower_dtype(residual * rms_scale(residual) * gain_two)
    logits = lower_dtype_backward(jnp.dot(h_two, w_router, precision=HIGH_PRECISION))
    route_probs = jax.nn.softmax(logits, axis=-1)
    gate_vals = jnp.take_along_axis(route_probs, route_rows, axis=1)
    slot_ids = slot_index(route_rows)
    copies = jnp.stack([lower_dtype_backward(h_two) for route_pos in range(TOPK)], axis=1).reshape(total_row_count * TOPK, MODEL_WIDTH)
    buffer = jnp.zeros((EXPERTS * CAP, MODEL_WIDTH), h_two.dtype).at[slot_ids].set(copies).reshape(EXPERTS, CAP, MODEL_WIDTH)
    gate_pre = lower_dtype_backward(jnp.einsum('ecd,edf->ecf', buffer, w_gate, precision=HIGH_PRECISION))
    up_pre = lower_dtype_backward(jnp.einsum('ecd,edf->ecf', buffer, w_up, precision=HIGH_PRECISION))
    inner_act = lower_dtype(jax.nn.silu(gate_pre) * up_pre)
    outcome = lower_dtype(lower_dtype_backward(jnp.einsum('ecf,edf->ecd', inner_act, w_down, precision=HIGH_PRECISION)))
    picked = outcome.reshape(EXPERTS * CAP, MODEL_WIDTH)[slot_ids].reshape(total_row_count, TOPK, MODEL_WIDTH)
    return residual + lax.optimization_barrier(jnp.sum(gate_vals[:, :, None] * picked, axis=1))

def forward(params, tok_all, lengths, routes):
    blocks = N_DP * N_FSDP

    def one_block(pieces):
        return block_forward(params, pieces[0], pieces[1], pieces[2])
    result = lax.map(jax.checkpoint(one_block), (tok_all.reshape(blocks, TOK_DEV, MODEL_WIDTH), lengths, routes.reshape(blocks, TOK_DEV, TOPK)))
    return result.reshape(blocks * TOK_DEV, MODEL_WIDTH)

def reference(tokens, lengths, routes, cotangent, gain_one, w_query, key_matrix, value_matrix, w_out, gain_two, w_router, w_gate, w_up, w_down):
    params = tuple((weight_arg.astype(jnp.float32) for weight_arg in (gain_one, w_query, key_matrix, value_matrix, w_out, gain_two, w_router, w_gate, w_up, w_down)))
    tok_all = tokens.astype(jnp.float32)
    block_out, pullback = jax.vjp(lambda param_set, rows_in: forward(param_set, rows_in, lengths, routes), params, tok_all)
    live_rows = (jnp.arange(TOK_DEV)[None, :] < lengths[:, None]).astype(jnp.float32).reshape(-1, 1)
    grad_params, grad_tokens = pullback(cotangent.astype(jnp.float32) * live_rows)
    return (block_out.astype(jnp.bfloat16), grad_tokens, grad_params[0], grad_params[1], grad_params[2], grad_params[3], grad_params[4], grad_params[5], grad_params[6], grad_params[7], grad_params[8], grad_params[9])
```

```python
import jax
import jax.numpy as jnp
from jax import lax
from jax.sharding import Mesh
from jax.sharding import PartitionSpec as P

MODEL_WIDTH = 1536
QUERY_HEADS = 12
KEY_VALUE_HEADS = 2
HEAD_SIZE = 128
EXPERTS = 8
GROUP = QUERY_HEADS // KEY_VALUE_HEADS
QW = QUERY_HEADS * HEAD_SIZE
KW = KEY_VALUE_HEADS * HEAD_SIZE
PAD = 128
EPS = 1e-06
ROPE_BASE = 1500000.0
NEG_FILL = -1e30
F32 = jnp.float32
BF16 = jnp.bfloat16


def rms_scale(rows):
    return lax.rsqrt(jnp.mean(rows * rows, axis=-1, keepdims=True) + EPS)


def norm_back(normed, row_scale, grad):
    return row_scale * (grad - normed * jnp.mean(grad * normed, axis=-1, keepdims=True))


def rope_tables(rows):
    half = HEAD_SIZE // 2
    position = jnp.arange(rows).astype(F32)
    inverse = ROPE_BASE ** (-jnp.arange(half).astype(F32) / half)
    angles = position[:, None] * inverse[None, :]
    return jnp.cos(angles)[:, None, :], jnp.sin(angles)[:, None, :]


def rotate(vals, cosine, sine):
    half = vals.shape[-1] // 2
    a, b = vals[..., :half], vals[..., half:]
    return jnp.concatenate([a * cosine - b * sine, b * cosine + a * sine], axis=-1)


def exchange(block, axis, size, step):
    return lax.ppermute(block, axis, [(i, i ^ step) for i in range(size)])


def gather_axis(block, axis, size):
    return [block] + [exchange(block, axis, size, k) for k in range(1, size)]


def in_order(parts, axis):
    me = lax.axis_index(axis)
    whole = jnp.zeros((len(parts),) + parts[0].shape, parts[0].dtype)
    for k, part in enumerate(parts):
        whole = lax.dynamic_update_slice_in_dim(whole, part[None], me ^ k, 0)
    return whole


def gather_rows(block, sizes):
    along_z = in_order(gather_axis(block, "z", sizes["z"]), "z")
    along_dp = in_order(gather_axis(along_z, "dp", sizes["dp"]), "dp")
    both = in_order(gather_axis(along_dp, "core", 2), "core")
    whole = jnp.moveaxis(both, 0, 2)
    return whole.reshape(-1, block.shape[-1])


def scatter_rows(grads, sizes):
    ndp, nz = sizes["dp"], sizes["z"]
    blocks = grads.reshape(ndp, nz, 2, -1, grads.shape[-1])
    core, me_dp, me_z = lax.axis_index("core"), lax.axis_index("dp"), lax.axis_index("z")
    mine = lax.dynamic_index_in_dim(blocks, core, 2, keepdims=False)
    other = lax.dynamic_index_in_dim(blocks, 1 - core, 2, keepdims=False)
    half = (mine.astype(F32) + exchange(other, "core", 2, 1).astype(F32)).astype(BF16)
    total = lax.dynamic_index_in_dim(half, me_dp, 0, keepdims=False).astype(F32)
    for k in range(1, ndp):
        sent = lax.dynamic_index_in_dim(half, me_dp ^ k, 0, keepdims=False)
        total = total + exchange(sent, "dp", ndp, k).astype(F32)
    part = total.astype(BF16)
    final = lax.dynamic_index_in_dim(part, me_z, 0, keepdims=False).astype(F32)
    for k in range(1, nz):
        sent = lax.dynamic_index_in_dim(part, me_z ^ k, 0, keepdims=False)
        final = final + exchange(sent, "z", nz, k).astype(F32)
    return final


def dot(a, b):
    return jnp.dot(a, b, preferred_element_type=F32)


def dot_t(a, b):
    return lax.dot_general(a, b, (((1,), (1,)), ((), ())), preferred_element_type=F32)


def t_dot(a, b):
    return lax.dot_general(a, b, (((0,), (0,)), ((), ())), preferred_element_type=F32)


def expert_pass(hidden, grads, gate, w_all, width):
    w_gate, w_up, w_down = w_all[:, :width], w_all[:, width : 2 * width], w_all[:, 2 * width :]
    gate_pre = dot(hidden, w_gate)
    up_pre = dot(hidden, w_up)
    sig = jax.nn.sigmoid(gate_pre)
    inner = (gate_pre * sig * up_pre).astype(BF16)
    result = dot_t(inner, w_down).astype(BF16).astype(F32)
    grads_f = grads.astype(F32)
    grad_gate = jnp.sum(result * grads_f, axis=-1, keepdims=True)
    grad_expert = (gate * grads_f).astype(BF16)
    grad_inner = dot(grad_expert, w_down)
    grad_gate_pre = (grad_inner * up_pre * sig * (1.0 + gate_pre * (1.0 - sig))).astype(BF16)
    grad_up_pre = (grad_inner * (gate_pre * sig)).astype(BF16)
    grad_in = (dot_t(grad_gate_pre, w_gate) + dot_t(grad_up_pre, w_up)).astype(BF16)
    terms = jnp.concatenate(
        [
            t_dot(hidden, grad_gate_pre).astype(BF16),
            t_dot(hidden, grad_up_pre).astype(BF16),
            t_dot(grad_expert, inner).astype(BF16),
        ],
        axis=1,
    )
    return gate * result, grad_gate, grad_in.astype(F32), terms


def per_device(
    sizes,
    tokens,
    lengths,
    routes,
    cotangent,
    gain_one,
    w_query,
    key_matrix,
    value_matrix,
    w_out,
    gain_two,
    w_router,
    w_gate,
    w_up,
    w_down,
):
    ndp = sizes["dp"]
    rows = tokens.shape[0]
    local = w_gate.shape[0]
    width = w_gate.shape[2]
    me_dp = lax.axis_index("dp")
    position = jnp.arange(rows)
    length = lengths[0]
    live = (position < length)[:, None]
    expert_ids = jnp.arange(EXPERTS, dtype=jnp.int32)

    extra = jnp.concatenate([gain_one[:, None], gain_two[:, None], w_router], axis=1)
    extra = jnp.pad(extra, ((0, 0), (0, PAD - extra.shape[1])))
    first = gather_rows(jnp.concatenate([w_query, key_matrix, value_matrix, extra], axis=1), sizes)
    out_all = gather_rows(w_out, sizes)
    expert_mats = [
        lax.all_gather(
            jnp.concatenate([w_gate[j], w_up[j], w_down[j]], axis=1), ("z", "core"), axis=0, tiled=True
        )
        for j in range(local)
    ]
    grad_low = jnp.where(live, cotangent, jnp.zeros_like(cotangent))
    grad_far = jnp.concatenate(gather_axis(grad_low, "dp", ndp), axis=0)
    routes_far = jnp.concatenate(gather_axis(routes, "dp", ndp), axis=0)

    in_all = first[:, : QW + 2 * KW]
    gain_one_row = first[:, QW + 2 * KW].astype(F32)
    gain_two_row = first[:, QW + 2 * KW + 1].astype(F32)
    router = first[:, QW + 2 * KW + 2 : QW + 2 * KW + 2 + EXPERTS]

    tok = tokens.astype(F32)
    scale_one = rms_scale(tok)
    normed_one = tok * scale_one
    h_one = (normed_one * gain_one_row).astype(BF16)
    pre = dot(h_one, in_all)
    cosine, sine = rope_tables(rows)
    queries = rotate(pre[:, :QW].reshape(rows, QUERY_HEADS, HEAD_SIZE), cosine, sine).astype(BF16)
    keys = rotate(
        pre[:, QW : QW + KW].reshape(rows, KEY_VALUE_HEADS, HEAD_SIZE), cosine, sine
    ).astype(BF16)
    values = pre[:, QW + KW :].astype(BF16).reshape(rows, KEY_VALUE_HEADS, HEAD_SIZE)
    visible = (position[None, :] <= position[:, None]) & (position[None, :] < length)
    mixed_parts, probs_parts = [], []
    for g in range(KEY_VALUE_HEADS):
        scores = jnp.einsum(
            "qgd,sd->gqs", queries[:, g * GROUP : (g + 1) * GROUP], keys[:, g], preferred_element_type=F32
        ) * HEAD_SIZE ** (-0.5)
        scores = jnp.where(visible[None], scores, NEG_FILL)
        top = jnp.max(scores, axis=-1, keepdims=True)
        expon = jnp.exp(scores - top)
        probs = expon / jnp.sum(expon, axis=-1, keepdims=True)
        probs_parts.append(probs)
        mixed_parts.append(
            jnp.einsum("gqs,sd->qgd", probs.astype(BF16), values[:, g], preferred_element_type=F32)
        )
    mixed = jnp.concatenate(mixed_parts, axis=1).reshape(rows, QW).astype(BF16)
    residual = tok + dot(mixed, out_all)
    scale_two = rms_scale(residual)
    normed_two = residual * scale_two
    h_two = (normed_two * gain_two_row).astype(BF16)

    hidden = jnp.concatenate(gather_axis(h_two, "dp", ndp), axis=0)
    logits = dot(hidden, router)
    logit_exp = jnp.exp(logits - jnp.max(logits, axis=-1, keepdims=True))
    route_probs = logit_exp / jnp.sum(logit_exp, axis=-1, keepdims=True)
    named = jnp.any(routes_far[:, :, None] == expert_ids[None, None, :], axis=1)

    out_far = 0.0
    back_far = 0.0
    gate_grads, sums = [], []
    for j in range(local):
        pick = named & (expert_ids == me_dp * local + j)[None, :]
        gate = jnp.sum(jnp.where(pick, route_probs, 0.0), axis=-1, keepdims=True)
        out, grad_gate, grad_in, terms = expert_pass(hidden, grad_far, gate, expert_mats[j], width)
        out_far = out_far + out
        back_far = back_far + grad_in
        gate_grads.append(jnp.where(jnp.any(pick, axis=-1, keepdims=True), grad_gate, 0.0))
        sums.append(
            lax.psum_scatter(terms, ("z", "core"), scatter_dimension=0, tiled=True).astype(F32)
        )
    out_far = out_far.astype(BF16).reshape(ndp, rows, MODEL_WIDTH)
    back_far = back_far.astype(BF16).reshape(ndp, rows, MODEL_WIDTH)
    gates_far = jnp.concatenate(gate_grads, axis=1).reshape(ndp, rows, local)

    block = residual + out_far[0].astype(F32)
    grad_h_two = back_far[0].astype(F32)
    grad_route = jnp.zeros((rows, EXPERTS), F32)
    grad_route = lax.dynamic_update_slice_in_dim(grad_route, gates_far[0], me_dp * local, 1)
    for k in range(1, ndp):
        block = block + exchange(out_far[k], "dp", ndp, k).astype(F32)
        grad_h_two = grad_h_two + exchange(back_far[k], "dp", ndp, k).astype(F32)
        grad_route = lax.dynamic_update_slice_in_dim(
            grad_route, exchange(gates_far[k], "dp", ndp, k), (me_dp ^ k) * local, 1
        )
    block_out = block.astype(BF16)

    own_probs = route_probs[:rows]
    grad_logits = (
        own_probs * (grad_route - jnp.sum(own_probs * grad_route, axis=-1, keepdims=True))
    ).astype(BF16)
    grad_router = t_dot(h_two, grad_logits)
    grad_h_two = grad_h_two + dot_t(grad_logits, router)
    grad_gain_two = jnp.sum(normed_two * grad_h_two, axis=0)
    grad_resid = grad_low.astype(F32) + norm_back(normed_two, scale_two, grad_h_two * gain_two_row)
    grad_attn = grad_resid.astype(BF16)
    grad_out = scatter_rows(t_dot(mixed, grad_attn).astype(BF16), sizes)
    grad_mixed = dot_t(grad_attn, out_all).astype(BF16).reshape(rows, QUERY_HEADS, HEAD_SIZE)
    query_parts, key_parts, value_parts = [], [], []
    for g in range(KEY_VALUE_HEADS):
        heads = slice(g * GROUP, (g + 1) * GROUP)
        probs = probs_parts[g]
        grad_probs = jnp.einsum(
            "qgd,sd->gqs", grad_mixed[:, heads], values[:, g], preferred_element_type=F32
        )
        value_parts.append(
            jnp.einsum("gqs,qgd->sd", probs.astype(BF16), grad_mixed[:, heads], preferred_element_type=F32)
        )
        row_dot = jnp.sum(probs * grad_probs, axis=-1, keepdims=True)
        grad_scores = (probs * (grad_probs - row_dot)).astype(BF16)
        query_parts.append(
            jnp.einsum("gqs,sd->qgd", grad_scores, keys[:, g], preferred_element_type=F32)
            * HEAD_SIZE ** (-0.5)
        )
        key_parts.append(
            jnp.einsum("gqs,qgd->sd", grad_scores, queries[:, heads], preferred_element_type=F32)
            * HEAD_SIZE ** (-0.5)
        )
    grad_pre = jnp.concatenate(
        [
            rotate(jnp.concatenate(query_parts, axis=1), cosine, -sine).reshape(rows, QW).astype(BF16),
            rotate(jnp.stack(key_parts, axis=1), cosine, -sine).reshape(rows, KW).astype(BF16),
            jnp.stack(value_parts, axis=1).reshape(rows, KW).astype(BF16),
        ],
        axis=1,
    )
    grad_h_one = dot_t(grad_pre, in_all)
    grad_gain_one = jnp.sum(normed_one * grad_h_one, axis=0)
    grad_tokens = grad_resid + norm_back(normed_one, scale_one, grad_h_one * gain_one_row)
    last = jnp.concatenate([grad_gain_one[:, None], grad_gain_two[:, None], grad_router], axis=1)
    last = jnp.pad(last, ((0, 0), (0, PAD - last.shape[1]))).astype(BF16)
    grad_first = scatter_rows(
        jnp.concatenate([t_dot(h_one, grad_pre).astype(BF16), last], axis=1), sizes
    )
    base = QW + 2 * KW
    expert_sums = jnp.stack(sums, axis=0)
    return (
        block_out,
        grad_tokens,
        grad_first[:, base],
        grad_first[:, :QW],
        grad_first[:, QW : QW + KW],
        grad_first[:, QW + KW : base],
        grad_out,
        grad_first[:, base + 1],
        grad_first[:, base + 2 : base + 2 + EXPERTS],
        expert_sums[:, :, :width],
        expert_sums[:, :, width : 2 * width],
        expert_sums[:, :, 2 * width :],
    )


def solution(mesh):
    ndp, nf = mesh.shape["dp"], mesh.shape["fsdp"]
    sizes = {"dp": ndp, "z": nf // 2, "core": 2}
    split = Mesh(mesh.devices.reshape(ndp, nf // 2, 2), ("dp", "z", "core"))
    every = ("dp", "z", "core")
    rows = P(every, None)
    vector = P(every)
    expert = P("dp", ("z", "core"), None)

    def run(*args):
        return per_device(sizes, *args)

    return jax.shard_map(
        run,
        mesh=split,
        in_specs=(rows, vector, rows, rows, vector, rows, rows, rows, rows, vector, rows)
        + (expert,) * 3,
        out_specs=(rows, rows, vector, rows, rows, rows, rows, vector, rows) + (expert,) * 3,
        check_vma=False,
    )
```

```python
import functools

import jax
import jax.numpy as jnp
from jax import lax
from jax.experimental import pallas as pl
from jax.experimental.pallas import tpu as pltpu
from jax.sharding import Mesh
from jax.sharding import PartitionSpec as P

MODEL_WIDTH = 1536
QUERY_HEADS = 12
KEY_VALUE_HEADS = 2
HEAD_SIZE = 128
EXPERTS = 8
GROUP = QUERY_HEADS // KEY_VALUE_HEADS
QW = QUERY_HEADS * HEAD_SIZE
KW = KEY_VALUE_HEADS * HEAD_SIZE
PAD = 128
EPS = 1e-06
ROPE_BASE = 1500000.0
NEG_FILL = -1e30
F32 = jnp.float32
BF16 = jnp.bfloat16
CAP = 160
VMEM_LIMIT = 60 * 1024 * 1024
TILE = 256


def nn(a, b):
    return lax.dot_general(a, b, (((1,), (0,)), ((), ())), preferred_element_type=F32)


def nt(a, b):
    return lax.dot_general(a, b, (((1,), (1,)), ((), ())), preferred_element_type=F32)


def tn(a, b):
    return lax.dot_general(a, b, (((0,), (0,)), ((), ())), preferred_element_type=F32)


def route_softmax(router_rows, hidden):
    logits = nt(router_rows, hidden)[:EXPERTS]
    expon = jnp.exp(logits - jnp.max(logits, axis=0, keepdims=True))
    return expon / jnp.sum(expon, axis=0, keepdims=True)


def expert_kernel(ndp, rows, width, chained, *refs):
    it = iter(refs)
    take = lambda n: [next(it) for _ in range(n)]
    (expert_ref, router_ref, named_ref) = take(3)
    hid_in, cot_in = take(ndp), take(ndp)
    (w_in,) = take(1)
    prev_in = take(2) if chained else []
    out_hbm, back_hbm, gates_ref, terms_hbm = take(4)
    hid, cot, w, x, d, ge, inner, dg, du, pick, pick_t, slot_gate, slot_dot = take(13)
    (terms_buf,) = take(1)
    prev = take(2) if chained else []
    in_sem, out_sem = take(2)
    depth = MODEL_WIDTH
    tiles = depth // TILE

    loads = []
    for s in range(ndp):
        loads.append(pltpu.make_async_copy(hid_in[s], hid.at[s], in_sem.at[s]))
    for s in range(ndp):
        loads.append(pltpu.make_async_copy(cot_in[s], cot.at[s], in_sem.at[ndp + s]))
    loads.append(pltpu.make_async_copy(w_in, w, in_sem.at[2 * ndp]))
    for i in range(len(prev)):
        loads.append(pltpu.make_async_copy(prev_in[i], prev[i], in_sem.at[2 * ndp + 1 + i]))
    for load in loads:
        load.start()

    expert = expert_ref[0]
    which = lax.broadcasted_iota(jnp.int32, (EXPERTS, rows), 0) == expert
    earlier = (
        lax.broadcasted_iota(jnp.int32, (rows, rows), 0)
        < lax.broadcasted_iota(jnp.int32, (rows, rows), 1)
    ).astype(F32).astype(BF16)
    slot = lax.broadcasted_iota(jnp.int32, (CAP, rows), 0).astype(F32)
    for s in range(ndp):
        loads[s].wait()
        hidden = hid[s]
        probs = route_softmax(router_ref[...], hidden)
        named = named_ref[s]
        named_row = jnp.sum(jnp.where(which, named, 0.0), axis=0, keepdims=True)
        gate_row = jnp.sum(jnp.where(which, probs, 0.0), axis=0, keepdims=True)
        place = nn(named.astype(BF16), earlier)
        place_row = jnp.sum(jnp.where(which, place, 0.0), axis=0, keepdims=True)
        chosen = jnp.where((slot == place_row) & (named_row > 0.5), 1.0, 0.0)
        pick[s] = chosen.astype(BF16)
        pick_t[s] = jnp.transpose(chosen).astype(BF16)
        at = pl.ds(s * CAP, CAP)
        slot_gate[at, :] = jnp.broadcast_to(
            jnp.sum(chosen * gate_row, axis=1, keepdims=True), (CAP, 128)
        )
        x[at, :] = nn(pick[s], hidden).astype(BF16)
    for s in range(ndp):
        loads[ndp + s].wait()
        at = pl.ds(s * CAP, CAP)
        grads = nn(pick[s], cot[s])
        d[at, :] = grads.astype(BF16)
        ge[at, :] = (slot_gate[at, :1] * grads).astype(BF16)
    loads[2 * ndp].wait()

    def hidden_units(t, carry):
        at = pl.multiple_of(t * TILE, TILE)
        gate_pre = nn(x[...], w[:, pl.ds(at, TILE)])
        up_pre = nn(x[...], w[:, pl.ds(width + at, TILE)])
        grad_inner = nn(ge[...], w[:, pl.ds(2 * width + at, TILE)])
        sig = 1.0 / (1.0 + jnp.exp(-gate_pre))
        act = gate_pre * sig
        inner[:, pl.ds(at, TILE)] = (act * up_pre).astype(BF16)
        dg[:, pl.ds(at, TILE)] = (
            grad_inner * up_pre * sig * (1.0 + gate_pre * (1.0 - sig))
        ).astype(BF16)
        du[:, pl.ds(at, TILE)] = (grad_inner * act).astype(BF16)
        return carry

    lax.fori_loop(0, width // TILE, hidden_units, 0)
    slot_dot[...] = jnp.zeros_like(slot_dot)
    for i in range(len(prev)):
        loads[2 * ndp + 1 + i].wait()

    def stores(t):
        lane = pl.ds(pl.multiple_of(t * TILE, TILE), TILE)
        return (
            pltpu.make_async_copy(hid.at[:, :, lane], out_hbm.at[:, :, lane], out_sem.at[0, t]),
            pltpu.make_async_copy(cot.at[:, :, lane], back_hbm.at[:, :, lane], out_sem.at[1, t]),
            pltpu.make_async_copy(
                terms_buf.at[lane, :], terms_hbm.at[lane, :], out_sem.at[2, t]
            ),
        )

    def features(t, carry):
        at = pl.multiple_of(t * TILE, TILE)
        lane = pl.ds(at, TILE)
        result = nt(inner[...], w[lane, pl.ds(2 * width, width)]).astype(BF16).astype(F32)
        partial = jnp.sum(result * d[:, lane].astype(F32), axis=1, keepdims=True)
        slot_dot[...] += jnp.broadcast_to(partial, slot_dot.shape)
        gated = (slot_gate[:, :1] * result).astype(BF16)
        grad_in = (
            nt(dg[...], w[lane, pl.ds(0, width)]) + nt(du[...], w[lane, pl.ds(width, width)])
        ).astype(BF16)
        for s in range(ndp):
            part = slice(s * CAP, (s + 1) * CAP)
            sent = nn(pick_t[s], gated[part])
            back = nn(pick_t[s], grad_in[part])
            if prev:
                sent = sent + prev[0][s, :, lane].astype(F32)
                back = back + prev[1][s, :, lane].astype(F32)
            hid[s, :, lane] = sent.astype(BF16)
            cot[s, :, lane] = back.astype(BF16)
        x_t = jnp.transpose(x[:, lane])
        terms_buf[lane, pl.ds(0, width)] = nn(x_t, dg[...]).astype(BF16)
        terms_buf[lane, pl.ds(width, width)] = nn(x_t, du[...]).astype(BF16)
        ge_t = jnp.transpose(ge[:, lane])
        terms_buf[lane, pl.ds(2 * width, width)] = nn(ge_t, inner[...]).astype(BF16)
        for store in stores(t):
            store.start()
        return carry

    lax.fori_loop(0, tiles, features, 0)
    for s in range(ndp):
        part = slice(s * CAP, (s + 1) * CAP)
        gates_ref[s] = jnp.sum(
            pick[s].astype(F32) * slot_dot[part, :1], axis=0, keepdims=True
        )
    for t in range(tiles):
        for store in stores(t):
            store.wait()


def run_expert(expert, router_rows, named, hidden, grads, w_all, prev):
    ndp, rows = len(hidden), hidden[0].shape[0]
    width = w_all.shape[1] // 3
    slots = ndp * CAP
    depth = MODEL_WIDTH
    tiles = depth // TILE
    hbm = pl.BlockSpec(memory_space=pl.ANY)
    vmem = pl.BlockSpec(memory_space=pltpu.VMEM)
    smem = pl.BlockSpec(memory_space=pltpu.SMEM)
    chained = prev is not None
    far = jax.ShapeDtypeStruct((ndp, rows, depth), BF16)
    scratch = [
        pltpu.VMEM((ndp, rows, depth), BF16),
        pltpu.VMEM((ndp, rows, depth), BF16),
        pltpu.VMEM((depth, 3 * width), BF16),
        pltpu.VMEM((slots, depth), BF16),
        pltpu.VMEM((slots, depth), BF16),
        pltpu.VMEM((slots, depth), BF16),
        pltpu.VMEM((slots, width), BF16),
        pltpu.VMEM((slots, width), BF16),
        pltpu.VMEM((slots, width), BF16),
        pltpu.VMEM((ndp, CAP, rows), BF16),
        pltpu.VMEM((ndp, rows, CAP), BF16),
        pltpu.VMEM((slots, 128), F32),
        pltpu.VMEM((slots, 128), F32),
        pltpu.VMEM((depth, 3 * width), BF16),
    ]
    if chained:
        scratch += [pltpu.VMEM((ndp, rows, depth), BF16)] * 2
    scratch += [pltpu.SemaphoreType.DMA((2 * ndp + 3,)), pltpu.SemaphoreType.DMA((3, tiles))]
    flops = 2 * slots * depth * width * 9 + 8 * ndp * CAP * rows * depth
    return pl.pallas_call(
        functools.partial(expert_kernel, ndp, rows, width, chained),
        out_shape=(
            far,
            far,
            jax.ShapeDtypeStruct((ndp, 1, rows), F32),
            jax.ShapeDtypeStruct((depth, 3 * width), BF16),
        ),
        in_specs=[smem, vmem, vmem] + [hbm] * (2 * ndp + 1 + (2 if chained else 0)),
        out_specs=(hbm, hbm, vmem, hbm),
        scratch_shapes=scratch,
        compiler_params=pltpu.CompilerParams(vmem_limit_bytes=VMEM_LIMIT),
        cost_estimate=pl.CostEstimate(
            flops=flops, bytes_accessed=40 * 1024 * 1024, transcendentals=slots * width
        ),
        name="expert",
    )(expert, router_rows, named, *hidden, *grads, w_all, *(prev or ()))


def rms_scale(rows):
    return lax.rsqrt(jnp.mean(rows * rows, axis=-1, keepdims=True) + EPS)


def norm_back(normed, row_scale, grad):
    return row_scale * (grad - normed * jnp.mean(grad * normed, axis=-1, keepdims=True))


def rope_tables(rows):
    half = HEAD_SIZE // 2
    position = jnp.arange(rows).astype(F32)
    inverse = ROPE_BASE ** (-jnp.arange(half).astype(F32) / half)
    angles = position[:, None] * inverse[None, :]
    return jnp.cos(angles)[:, None, :], jnp.sin(angles)[:, None, :]


def rotate(vals, cosine, sine):
    half = vals.shape[-1] // 2
    a, b = vals[..., :half], vals[..., half:]
    return jnp.concatenate([a * cosine - b * sine, b * cosine + a * sine], axis=-1)


def exchange(block, axis, size, step):
    return lax.ppermute(block, axis, [(i, i ^ step) for i in range(size)])


def gather_axis(block, axis, size):
    return [block] + [exchange(block, axis, size, k) for k in range(1, size)]


def in_order(parts, axis):
    me = lax.axis_index(axis)
    whole = jnp.zeros((len(parts),) + parts[0].shape, parts[0].dtype)
    for k, part in enumerate(parts):
        whole = lax.dynamic_update_slice_in_dim(whole, part[None], me ^ k, 0)
    return whole


def gather_rows(block, sizes):
    along_z = in_order(gather_axis(block, "z", sizes["z"]), "z")
    along_dp = in_order(gather_axis(along_z, "dp", sizes["dp"]), "dp")
    both = in_order(gather_axis(along_dp, "core", 2), "core")
    whole = jnp.moveaxis(both, 0, 2)
    return whole.reshape(-1, block.shape[-1])


def scatter_rows(grads, sizes):
    ndp, nz = sizes["dp"], sizes["z"]
    blocks = grads.reshape(ndp, nz, 2, -1, grads.shape[-1])
    core, me_dp, me_z = lax.axis_index("core"), lax.axis_index("dp"), lax.axis_index("z")
    mine = lax.dynamic_index_in_dim(blocks, core, 2, keepdims=False)
    other = lax.dynamic_index_in_dim(blocks, 1 - core, 2, keepdims=False)
    half = (mine.astype(F32) + exchange(other, "core", 2, 1).astype(F32)).astype(BF16)
    total = lax.dynamic_index_in_dim(half, me_dp, 0, keepdims=False).astype(F32)
    for k in range(1, ndp):
        sent = lax.dynamic_index_in_dim(half, me_dp ^ k, 0, keepdims=False)
        total = total + exchange(sent, "dp", ndp, k).astype(F32)
    part = total.astype(BF16)
    final = lax.dynamic_index_in_dim(part, me_z, 0, keepdims=False).astype(F32)
    for k in range(1, nz):
        sent = lax.dynamic_index_in_dim(part, me_z ^ k, 0, keepdims=False)
        final = final + exchange(sent, "z", nz, k).astype(F32)
    return final


def dot(a, b):
    return jnp.dot(a, b, preferred_element_type=F32)


def dot_t(a, b):
    return lax.dot_general(a, b, (((1,), (1,)), ((), ())), preferred_element_type=F32)


def t_dot(a, b):
    return lax.dot_general(a, b, (((0,), (0,)), ((), ())), preferred_element_type=F32)


def per_device(
    sizes,
    tokens,
    lengths,
    routes,
    cotangent,
    gain_one,
    w_query,
    key_matrix,
    value_matrix,
    w_out,
    gain_two,
    w_router,
    w_gate,
    w_up,
    w_down,
):
    ndp = sizes["dp"]
    rows = tokens.shape[0]
    local = w_gate.shape[0]
    width = w_gate.shape[2]
    me_dp = lax.axis_index("dp")
    position = jnp.arange(rows)
    length = lengths[0]
    live = (position < length)[:, None]
    expert_ids = jnp.arange(EXPERTS, dtype=jnp.int32)

    extra = jnp.concatenate([gain_one[:, None], gain_two[:, None], w_router], axis=1)
    extra = jnp.pad(extra, ((0, 0), (0, PAD - extra.shape[1])))
    first = gather_rows(jnp.concatenate([w_query, key_matrix, value_matrix, extra], axis=1), sizes)
    out_all = gather_rows(w_out, sizes)
    expert_mats = [
        lax.all_gather(
            jnp.concatenate([w_gate[j], w_up[j], w_down[j]], axis=1), ("z", "core"), axis=0, tiled=True
        )
        for j in range(local)
    ]
    grad_low = jnp.where(live, cotangent, jnp.zeros_like(cotangent))
    grad_far = gather_axis(grad_low, "dp", ndp)
    named = jnp.any(routes[None, :, :] == expert_ids[:, None, None], axis=2).astype(F32)
    named_far = jnp.stack(gather_axis(named, "dp", ndp))

    in_all = first[:, : QW + 2 * KW]
    gain_one_row = first[:, QW + 2 * KW].astype(F32)
    gain_two_row = first[:, QW + 2 * KW + 1].astype(F32)
    router = first[:, QW + 2 * KW + 2 : QW + 2 * KW + 2 + EXPERTS]

    tok = tokens.astype(F32)
    scale_one = rms_scale(tok)
    normed_one = tok * scale_one
    h_one = (normed_one * gain_one_row).astype(BF16)
    pre = dot(h_one, in_all)
    cosine, sine = rope_tables(rows)
    queries = rotate(pre[:, :QW].reshape(rows, QUERY_HEADS, HEAD_SIZE), cosine, sine).astype(BF16)
    keys = rotate(
        pre[:, QW : QW + KW].reshape(rows, KEY_VALUE_HEADS, HEAD_SIZE), cosine, sine
    ).astype(BF16)
    values = pre[:, QW + KW :].astype(BF16).reshape(rows, KEY_VALUE_HEADS, HEAD_SIZE)
    visible = (position[None, :] <= position[:, None]) & (position[None, :] < length)
    mixed_parts, probs_parts = [], []
    for g in range(KEY_VALUE_HEADS):
        scores = jnp.einsum(
            "qgd,sd->gqs", queries[:, g * GROUP : (g + 1) * GROUP], keys[:, g], preferred_element_type=F32
        ) * HEAD_SIZE ** (-0.5)
        scores = jnp.where(visible[None], scores, NEG_FILL)
        top = jnp.max(scores, axis=-1, keepdims=True)
        expon = jnp.exp(scores - top)
        probs = expon / jnp.sum(expon, axis=-1, keepdims=True)
        probs_parts.append(probs)
        mixed_parts.append(
            jnp.einsum("gqs,sd->qgd", probs.astype(BF16), values[:, g], preferred_element_type=F32)
        )
    mixed = jnp.concatenate(mixed_parts, axis=1).reshape(rows, QW).astype(BF16)
    residual = tok + dot(mixed, out_all)
    scale_two = rms_scale(residual)
    normed_two = residual * scale_two
    h_two = (normed_two * gain_two_row).astype(BF16)

    hidden = gather_axis(h_two, "dp", ndp)
    router_rows = jnp.pad(router.T, ((0, 16 - EXPERTS), (0, 0)))
    own_probs = route_softmax(router_rows, h_two)

    prev = None
    gate_grads, sums = [], []
    for j in range(local):
        expert = (me_dp * local + j).astype(jnp.int32).reshape(1)
        out_far, back_far, grad_gate, terms = run_expert(
            expert, router_rows, named_far, hidden, grad_far, expert_mats[j], prev
        )
        prev = (out_far, back_far)
        gate_grads.append(grad_gate)
        sums.append(
            lax.psum_scatter(terms, ("z", "core"), scatter_dimension=0, tiled=True).astype(F32)
        )
    gates_far = jnp.concatenate(gate_grads, axis=1)

    block = residual + out_far[0].astype(F32)
    grad_h_two = back_far[0].astype(F32)
    grad_route = jnp.zeros((EXPERTS, rows), F32)
    grad_route = lax.dynamic_update_slice_in_dim(grad_route, gates_far[0], me_dp * local, 0)
    for k in range(1, ndp):
        block = block + exchange(out_far[k], "dp", ndp, k).astype(F32)
        grad_h_two = grad_h_two + exchange(back_far[k], "dp", ndp, k).astype(F32)
        grad_route = lax.dynamic_update_slice_in_dim(
            grad_route, exchange(gates_far[k], "dp", ndp, k), (me_dp ^ k) * local, 0
        )
    block_out = block.astype(BF16)

    grad_logits = (
        own_probs * (grad_route - jnp.sum(own_probs * grad_route, axis=0, keepdims=True))
    ).astype(BF16)
    grad_router = dot_t(h_two.T, grad_logits)
    grad_h_two = grad_h_two + t_dot(grad_logits, router.T)
    grad_gain_two = jnp.sum(normed_two * grad_h_two, axis=0)
    grad_resid = grad_low.astype(F32) + norm_back(normed_two, scale_two, grad_h_two * gain_two_row)
    grad_attn = grad_resid.astype(BF16)
    grad_out = scatter_rows(t_dot(mixed, grad_attn).astype(BF16), sizes)
    grad_mixed = dot_t(grad_attn, out_all).astype(BF16).reshape(rows, QUERY_HEADS, HEAD_SIZE)
    query_parts, key_parts, value_parts = [], [], []
    for g in range(KEY_VALUE_HEADS):
        heads = slice(g * GROUP, (g + 1) * GROUP)
        probs = probs_parts[g]
        grad_probs = jnp.einsum(
            "qgd,sd->gqs", grad_mixed[:, heads], values[:, g], preferred_element_type=F32
        )
        value_parts.append(
            jnp.einsum("gqs,qgd->sd", probs.astype(BF16), grad_mixed[:, heads], preferred_element_type=F32)
        )
        row_dot = jnp.sum(probs * grad_probs, axis=-1, keepdims=True)
        grad_scores = (probs * (grad_probs - row_dot)).astype(BF16)
        query_parts.append(
            jnp.einsum("gqs,sd->qgd", grad_scores, keys[:, g], preferred_element_type=F32)
            * HEAD_SIZE ** (-0.5)
        )
        key_parts.append(
            jnp.einsum("gqs,qgd->sd", grad_scores, queries[:, heads], preferred_element_type=F32)
            * HEAD_SIZE ** (-0.5)
        )
    grad_pre = jnp.concatenate(
        [
            rotate(jnp.concatenate(query_parts, axis=1), cosine, -sine).reshape(rows, QW).astype(BF16),
            rotate(jnp.stack(key_parts, axis=1), cosine, -sine).reshape(rows, KW).astype(BF16),
            jnp.stack(value_parts, axis=1).reshape(rows, KW).astype(BF16),
        ],
        axis=1,
    )
    grad_h_one = dot_t(grad_pre, in_all)
    grad_gain_one = jnp.sum(normed_one * grad_h_one, axis=0)
    grad_tokens = grad_resid + norm_back(normed_one, scale_one, grad_h_one * gain_one_row)
    last = jnp.concatenate([grad_gain_one[:, None], grad_gain_two[:, None], grad_router], axis=1)
    last = jnp.pad(last, ((0, 0), (0, PAD - last.shape[1]))).astype(BF16)
    grad_first = scatter_rows(
        jnp.concatenate([t_dot(h_one, grad_pre).astype(BF16), last], axis=1), sizes
    )
    base = QW + 2 * KW
    expert_sums = jnp.stack(sums, axis=0)
    return (
        block_out,
        grad_tokens,
        grad_first[:, base],
        grad_first[:, :QW],
        grad_first[:, QW : QW + KW],
        grad_first[:, QW + KW : base],
        grad_out,
        grad_first[:, base + 1],
        grad_first[:, base + 2 : base + 2 + EXPERTS],
        expert_sums[:, :, :width],
        expert_sums[:, :, width : 2 * width],
        expert_sums[:, :, 2 * width :],
    )


def solution(mesh):
    ndp, nf = mesh.shape["dp"], mesh.shape["fsdp"]
    sizes = {"dp": ndp, "z": nf // 2, "core": 2}
    split = Mesh(mesh.devices.reshape(ndp, nf // 2, 2), ("dp", "z", "core"))
    every = ("dp", "z", "core")
    rows = P(every, None)
    vector = P(every)
    expert = P("dp", ("z", "core"), None)

    def run(*args):
        return per_device(sizes, *args)

    return jax.shard_map(
        run,
        mesh=split,
        in_specs=(rows, vector, rows, rows, vector, rows, rows, rows, rows, vector, rows)
        + (expert,) * 3,
        out_specs=(rows, rows, vector, rows, rows, rows, rows, vector, rows) + (expert,) * 3,
        check_vma=False,
    )
```

```python
import functools

import jax
import jax.numpy as jnp
from jax import lax
from jax.experimental import pallas as pl
from jax.experimental.pallas import tpu as pltpu
from jax.sharding import Mesh
from jax.sharding import PartitionSpec as P

MODEL_WIDTH = 1536
QUERY_HEADS = 12
KEY_VALUE_HEADS = 2
HEAD_SIZE = 128
EXPERTS = 8
CAP = 160
GROUP = QUERY_HEADS // KEY_VALUE_HEADS
QW = QUERY_HEADS * HEAD_SIZE
KW = KEY_VALUE_HEADS * HEAD_SIZE
QKV = QW + 2 * KW
PAD = 128
FIRST = QKV + PAD
NOTE = 16
EPS = 1e-06
ROPE_BASE = 1500000.0
NEG_FILL = -1e30
SCALE = HEAD_SIZE ** (-0.5)
F32 = jnp.float32
BF16 = jnp.bfloat16
TILE = 256
MIB = 1024 * 1024
HBM = pl.BlockSpec(memory_space=pl.ANY)
VMEM = pl.BlockSpec(memory_space=pltpu.VMEM)
SMEM = pl.BlockSpec(memory_space=pltpu.SMEM)


def nn(a, b):
    return lax.dot_general(a, b, (((1,), (0,)), ((), ())), preferred_element_type=F32)


def nt(a, b):
    return lax.dot_general(a, b, (((1,), (1,)), ((), ())), preferred_element_type=F32)


def tn(a, b):
    return lax.dot_general(a, b, (((0,), (0,)), ((), ())), preferred_element_type=F32)


def shape(dims, dtype):
    return jax.ShapeDtypeStruct(dims, dtype)


def params(mib):
    return pltpu.CompilerParams(vmem_limit_bytes=mib * MIB)


def cost(flops, data, special=0):
    return pl.CostEstimate(flops=flops, bytes_accessed=data, transcendentals=special)


def exchange(block, axis, size, step):
    return lax.ppermute(block, axis, [(i, i ^ step) for i in range(size)])


def gather_axis(block, axis, size):
    return [block] + [exchange(block, axis, size, k) for k in range(1, size)]


def both_cores(parts):
    return [p for part in parts for p in (part, exchange(part, "core", 2, 1))]


def split_kernel(at, count, whole, *refs):
    *_, out, sem = refs
    copy = pltpu.make_async_copy(whole.at[:, :, pl.ds(at, count)], out, sem)
    copy.start()
    copy.wait()


def split_after(whole, at, count, before):
    dims = whole.shape[:2] + (count,)
    return pl.pallas_call(
        functools.partial(split_kernel, at, count),
        out_shape=shape(dims, whole.dtype),
        in_specs=[HBM] * (1 + len(before)),
        out_specs=HBM,
        scratch_shapes=[pltpu.SemaphoreType.DMA],
        cost_estimate=cost(0, 4 * dims[0] * dims[1] * dims[2]),
        name="columns",
    )(whole, *before)


def block_rows(sizes):
    return MODEL_WIDTH // (2 * sizes["dp"] * sizes["z"])


def by_blocks(sizes):
    return block_rows(sizes) % 16 == 0


def row_parts(parts, ids, sizes):
    if by_blocks(sizes):
        return parts
    columns = parts[0].shape[-1]
    whole = jnp.zeros((sizes["dp"], sizes["z"], 2, block_rows(sizes), columns), BF16)
    for i, part in enumerate(parts):
        k, c = divmod(i, 2)
        whole = lax.dynamic_update_slice(
            whole, part[None, :, None], (ids[0] ^ k, 0, ids[2] ^ c, 0, 0)
        )
    return [whole.reshape(MODEL_WIDTH, columns)]


def scatter_rows(terms, ids, sizes):
    ndp, nz = sizes["dp"], sizes["z"]
    if len(terms) == 1:
        blocks = terms[0].reshape(ndp, nz, 2, block_rows(sizes), -1)
        blocks = jnp.take(jnp.take(blocks, ids[0] ^ jnp.arange(ndp), 0), ids[1] ^ jnp.arange(nz), 1)
        terms = [lax.dynamic_index_in_dim(blocks, ids[2] ^ c, 2, keepdims=False) for c in range(2)]
    mine, other = terms
    got = exchange(other, "core", 2, 1)
    half = [(mine[k].astype(F32) + got[k].astype(F32)) for k in range(ndp)]
    total = half[0]
    for k in range(1, ndp):
        total = total + exchange(half[k].astype(BF16), "dp", ndp, k).astype(F32)
    final = total[0]
    for k in range(1, nz):
        final = final + exchange(total[k].astype(BF16), "z", nz, k).astype(F32)
    return final


def load_rows(ids, ndp, nz, parts, dest, sem):
    if len(parts) == 1:
        loads = [pltpu.make_async_copy(parts[0], dest, sem.at[0])]
        loads[0].start()
        return loads
    rows = MODEL_WIDTH // (ndp * nz * 2)
    loads = []
    for k in range(ndp):
        for c in range(2):
            for z in range(nz):
                block = ((ids[0] ^ k) * nz + z) * 2 + (ids[2] ^ c)
                place = pl.ds(pl.multiple_of(block * rows, rows), rows)
                n = (k * 2 + c) * nz + z
                loads.append(
                    pltpu.make_async_copy(parts[k * 2 + c].at[z], dest.at[place, :], sem.at[n])
                )
    for load in loads:
        load.start()
    return loads


def store_rows(ids, ndp, nz, source, dests, sem):
    if len(dests) == 1:
        store = pltpu.make_async_copy(source, dests[0], sem.at[0])
        store.start()
        store.wait()
        return
    rows = MODEL_WIDTH // (ndp * nz * 2)
    stores = []
    for k in range(ndp):
        for z in range(nz):
            for c, dest in enumerate(dests):
                block = ((ids[0] ^ k) * nz + (ids[1] ^ z)) * 2 + (ids[2] ^ c)
                place = pl.ds(pl.multiple_of(block * rows, rows), rows)
                n = (k * 2 + c) * nz + z
                stores.append(
                    pltpu.make_async_copy(source.at[place, :], dest.at[k, z], sem.at[n])
                )
    for store in stores:
        store.start()
    for store in stores:
        store.wait()


def split_shapes(columns, sizes):
    if by_blocks(sizes):
        return (shape((sizes["dp"], sizes["z"], block_rows(sizes), columns), BF16),) * 2
    return (shape((MODEL_WIDTH, columns), BF16),)


def rms_scale(rows):
    return lax.rsqrt(jnp.mean(rows * rows, axis=-1, keepdims=True) + EPS)


def norm_back(normed, row_scale, grad):
    return row_scale * (grad - normed * jnp.mean(grad * normed, axis=-1, keepdims=True))


def swapped(vals):
    return pltpu.roll(vals, HEAD_SIZE // 2, 1)


def head(h):
    return slice(h * HEAD_SIZE, (h + 1) * HEAD_SIZE)


def seen(rows, length):
    q = lax.broadcasted_iota(jnp.int32, (rows, rows), 0)
    s = lax.broadcasted_iota(jnp.int32, (rows, rows), 1)
    return (s <= q) & (s < length)


def attention_probs(query, key, visible):
    scores = jnp.where(visible, nt(query, key) * SCALE, NEG_FILL)
    expon = jnp.exp(scores - jnp.max(scores, axis=-1, keepdims=True))
    return expon / jnp.sum(expon, axis=-1, keepdims=True)


def route_softmax(router_rows, hidden):
    logits = nt(router_rows, hidden)[:EXPERTS]
    expon = jnp.exp(logits - jnp.max(logits, axis=0, keepdims=True))
    return expon / jnp.sum(expon, axis=0, keepdims=True)


def attend_kernel(ndp, nz, ids, tokens, cosine, sine, *refs):
    *parts, qkv, mixed, h_one, gains, router, w, sem = refs
    rows = tokens.shape[0]
    loads = load_rows(ids, ndp, nz, parts, w, sem)
    tok = tokens[...].astype(F32)
    normed = tok * rms_scale(tok)
    for load in loads:
        load.wait()
    extra = jnp.transpose(w[:, QKV:].astype(F32))
    gains[...] = extra[:8]
    router[...] = extra[2 : 2 + NOTE].astype(BF16)
    h_one[...] = (normed * extra[0:1]).astype(BF16)
    cos, sin = cosine[...], sine[...]
    for t in range(QKV // TILE):
        pre = nn(h_one[...], w[:, t * TILE : (t + 1) * TILE])
        for i in range(TILE // HEAD_SIZE):
            part = pre[:, head(i)]
            at = t * TILE + i * HEAD_SIZE
            if at < QW + KW:
                part = part * cos + swapped(part) * sin
            qkv[:, at : at + HEAD_SIZE] = part.astype(BF16)
    visible = seen(rows, ids[3])
    for h in range(QUERY_HEADS):
        g = h // GROUP
        probs = attention_probs(qkv[:, head(h)], qkv[:, head(QUERY_HEADS + g)], visible)
        values = qkv[:, head(QUERY_HEADS + KEY_VALUE_HEADS + g)]
        mixed[:, head(h)] = nn(probs.astype(BF16), values).astype(BF16)


def attend(ids, tokens, cosine, sine, parts, sizes):
    ndp, nz = sizes["dp"], sizes["z"]
    rows = tokens.shape[0]
    return pl.pallas_call(
        functools.partial(attend_kernel, ndp, nz),
        out_shape=(
            shape((rows, QKV), BF16),
            shape((rows, QW), BF16),
            shape((rows, MODEL_WIDTH), BF16),
            shape((8, MODEL_WIDTH), F32),
            shape((NOTE, MODEL_WIDTH), BF16),
        ),
        in_specs=[SMEM, VMEM, VMEM, VMEM] + [HBM] * len(parts),
        out_specs=(VMEM,) * 5,
        scratch_shapes=[
            pltpu.VMEM((MODEL_WIDTH, FIRST), BF16),
            pltpu.SemaphoreType.DMA((2 * ndp * nz,)),
        ],
        compiler_params=params(40),
        cost_estimate=cost(2 * rows * MODEL_WIDTH * QKV, 10 * MIB, 12 * rows * rows),
        name="attend",
    )(ids, tokens, cosine, sine, *parts)


def project_kernel(ndp, nz, ids, tokens, mixed, gains, *refs):
    *parts, residual, h_two, w, sem = refs
    loads = load_rows(ids, ndp, nz, parts, w, sem)
    for load in loads:
        load.wait()
    for t in range(MODEL_WIDTH // TILE):
        lane = slice(t * TILE, (t + 1) * TILE)
        residual[:, lane] = tokens[:, lane].astype(F32) + nn(mixed[...], w[:, lane])
    whole = residual[...]
    h_two[...] = (whole * rms_scale(whole) * gains[1:2]).astype(BF16)


def project(ids, tokens, mixed, gains, parts, sizes):
    ndp, nz = sizes["dp"], sizes["z"]
    rows = tokens.shape[0]
    return pl.pallas_call(
        functools.partial(project_kernel, ndp, nz),
        out_shape=(shape((rows, MODEL_WIDTH), F32), shape((rows, MODEL_WIDTH), BF16)),
        in_specs=[SMEM, VMEM, VMEM, VMEM] + [HBM] * len(parts),
        out_specs=(VMEM,) * 2,
        scratch_shapes=[
            pltpu.VMEM((QW, MODEL_WIDTH), BF16),
            pltpu.SemaphoreType.DMA((2 * ndp * nz,)),
        ],
        compiler_params=params(40),
        cost_estimate=cost(2 * rows * MODEL_WIDTH * QW, 8 * MIB),
        name="project",
    )(ids, tokens, mixed, gains, *parts)


def expert_kernel(ndp, rows, width, index, *refs):
    it = iter(refs)
    take = lambda n: [next(it) for _ in range(n)]
    (expert_ref, router_ref) = take(2)
    prev_gates = take(index)
    hid_in, cot_in = take(ndp), take(ndp)
    (w_in,) = take(1)
    prev_in = take(2) if index else []
    out_hbm, back_hbm, gates_ref, terms_hbm = take(4)
    hid, cot, w, x, d, ge, inner, dg, du, pick, pick_t, slot_gate, slot_dot = take(13)
    (terms_buf,) = take(1)
    prev = take(2) if index else []
    in_sem, out_sem = take(2)
    depth = MODEL_WIDTH
    tiles = depth // TILE

    loads = []
    for s in range(ndp):
        loads.append(pltpu.make_async_copy(hid_in[s], hid.at[s], in_sem.at[s]))
    for s in range(ndp):
        loads.append(pltpu.make_async_copy(cot_in[s], cot.at[s], in_sem.at[ndp + s]))
    loads.append(pltpu.make_async_copy(w_in, w, in_sem.at[2 * ndp]))
    for i in range(len(prev)):
        loads.append(pltpu.make_async_copy(prev_in[i], prev[i], in_sem.at[2 * ndp + 1 + i]))
    for load in loads:
        load.start()

    expert = expert_ref[0]
    which = lax.broadcasted_iota(jnp.int32, (EXPERTS, rows), 0) == expert
    earlier = (
        (
            lax.broadcasted_iota(jnp.int32, (rows, rows), 0)
            < lax.broadcasted_iota(jnp.int32, (rows, rows), 1)
        )
        .astype(F32)
        .astype(BF16)
    )
    slot = lax.broadcasted_iota(jnp.int32, (CAP, rows), 0).astype(F32)
    for s in range(ndp):
        loads[s].wait()
        loads[ndp + s].wait()
        hidden = hid[s]
        probs = route_softmax(router_ref[...], hidden)
        named = cot[s, rows : rows + NOTE, :rows]
        place = nn(named, earlier)[:EXPERTS]
        named = named[:EXPERTS].astype(F32)
        named_row = jnp.sum(jnp.where(which, named, 0.0), axis=0, keepdims=True)
        gate_row = jnp.sum(jnp.where(which, probs, 0.0), axis=0, keepdims=True)
        place_row = jnp.sum(jnp.where(which, place, 0.0), axis=0, keepdims=True)
        chosen = jnp.where((slot == place_row) & (named_row > 0.5), 1.0, 0.0)
        pick[s] = chosen.astype(BF16)
        pick_t[s] = jnp.transpose(chosen).astype(BF16)
        at = pl.ds(s * CAP, CAP)
        gate = jnp.sum(chosen * gate_row, axis=1, keepdims=True)
        slot_gate[at, :] = jnp.broadcast_to(gate, (CAP, 128))
        x[at, :] = nn(pick[s], hidden).astype(BF16)
        grads = nn(pick[s], cot[s, :rows])
        d[at, :] = grads.astype(BF16)
        ge[at, :] = (gate * grads).astype(BF16)
    loads[2 * ndp].wait()

    def hidden_units(t, carry):
        at = pl.multiple_of(t * TILE, TILE)
        gate_pre = nn(x[...], w[:, pl.ds(at, TILE)])
        up_pre = nn(x[...], w[:, pl.ds(width + at, TILE)])
        grad_inner = nn(ge[...], w[:, pl.ds(2 * width + at, TILE)])
        sig = 1.0 / (1.0 + jnp.exp(-gate_pre))
        act = gate_pre * sig
        inner[:, pl.ds(at, TILE)] = (act * up_pre).astype(BF16)
        dg[:, pl.ds(at, TILE)] = (
            grad_inner * up_pre * sig * (1.0 + gate_pre * (1.0 - sig))
        ).astype(BF16)
        du[:, pl.ds(at, TILE)] = (grad_inner * act).astype(BF16)
        return carry

    lax.fori_loop(0, width // TILE, hidden_units, 0)
    slot_dot[...] = jnp.zeros_like(slot_dot)
    for i in range(len(prev)):
        loads[2 * ndp + 1 + i].wait()

    def stores(t):
        lane = pl.ds(pl.multiple_of(t * TILE, TILE), TILE)
        body = pl.ds(0, rows)
        return (
            pltpu.make_async_copy(
                hid.at[:, :, lane], out_hbm.at[:, :, lane], out_sem.at[0, t]
            ),
            pltpu.make_async_copy(
                cot.at[:, body, lane], back_hbm.at[:, body, lane], out_sem.at[1, t]
            ),
            pltpu.make_async_copy(
                terms_buf.at[lane, :], terms_hbm.at[lane, :], out_sem.at[2, t]
            ),
        )

    def features(t, carry):
        lane = pl.ds(pl.multiple_of(t * TILE, TILE), TILE)
        result = nt(inner[...], w[lane, pl.ds(2 * width, width)]).astype(BF16).astype(F32)
        partial = jnp.sum(result * d[:, lane].astype(F32), axis=1, keepdims=True)
        slot_dot[...] += jnp.broadcast_to(partial, slot_dot.shape)
        gated = (slot_gate[:, :1] * result).astype(BF16)
        grad_in = (
            nt(dg[...], w[lane, pl.ds(0, width)]) + nt(du[...], w[lane, pl.ds(width, width)])
        ).astype(BF16)
        for s in range(ndp):
            part = slice(s * CAP, (s + 1) * CAP)
            sent = nn(pick_t[s], gated[part])
            back = nn(pick_t[s], grad_in[part])
            if prev:
                sent = sent + prev[0][s, :, lane].astype(F32)
                back = back + prev[1][s, :rows, lane].astype(F32)
            hid[s, :, lane] = sent.astype(BF16)
            cot[s, :rows, lane] = back.astype(BF16)
        x_t = jnp.transpose(x[:, lane])
        terms_buf[lane, pl.ds(0, width)] = nn(x_t, dg[...]).astype(BF16)
        terms_buf[lane, pl.ds(width, width)] = nn(x_t, du[...]).astype(BF16)
        ge_t = jnp.transpose(ge[:, lane])
        terms_buf[lane, pl.ds(2 * width, width)] = nn(ge_t, inner[...]).astype(BF16)
        for store in stores(t):
            store.start()
        return carry

    lax.fori_loop(0, tiles, features, 0)
    line = lax.broadcasted_iota(jnp.int32, (NOTE, 3 * rows), 0)
    for s in range(ndp):
        part = slice(s * CAP, (s + 1) * CAP)
        own = jnp.sum(pick[s].astype(F32) * slot_dot[part, :1], axis=0, keepdims=True)
        gates_ref[s] = own
        note = jnp.zeros((NOTE, 3 * rows), F32)
        for j, row in enumerate([p[s] for p in prev_gates] + [own]):
            high = row.astype(BF16).astype(F32)
            middle = (row - high).astype(BF16).astype(F32)
            low = row - high - middle
            note = jnp.where(line == j, jnp.concatenate([high, middle, low], axis=1), note)
        cot[s, rows : rows + NOTE, : 3 * rows] = note.astype(BF16)
    notes = pltpu.make_async_copy(
        cot.at[:, pl.ds(rows, NOTE), :], back_hbm.at[:, pl.ds(rows, NOTE), :], out_sem.at[3, 0]
    )
    notes.start()
    for t in range(tiles):
        for store in stores(t):
            store.wait()
    notes.wait()


def run_expert(index, expert, router, hidden, grads, w_all, prev, prev_gates):
    ndp, rows = len(hidden), hidden[0].shape[0]
    width = w_all.shape[1] // 3
    slots = ndp * CAP
    depth = MODEL_WIDTH
    tiles = depth // TILE
    scratch = [
        pltpu.VMEM((ndp, rows, depth), BF16),
        pltpu.VMEM((ndp, rows + NOTE, depth), BF16),
        pltpu.VMEM((depth, 3 * width), BF16),
        pltpu.VMEM((slots, depth), BF16),
        pltpu.VMEM((slots, depth), BF16),
        pltpu.VMEM((slots, depth), BF16),
        pltpu.VMEM((slots, width), BF16),
        pltpu.VMEM((slots, width), BF16),
        pltpu.VMEM((slots, width), BF16),
        pltpu.VMEM((ndp, CAP, rows), BF16),
        pltpu.VMEM((ndp, rows, CAP), BF16),
        pltpu.VMEM((slots, 128), F32),
        pltpu.VMEM((slots, 128), F32),
        pltpu.VMEM((depth, 3 * width), BF16),
    ]
    if index:
        scratch += [
            pltpu.VMEM((ndp, rows, depth), BF16),
            pltpu.VMEM((ndp, rows + NOTE, depth), BF16),
        ]
    scratch += [pltpu.SemaphoreType.DMA((2 * ndp + 3,)), pltpu.SemaphoreType.DMA((4, tiles))]
    flops = 2 * slots * depth * width * 9 + 8 * ndp * CAP * rows * depth
    return pl.pallas_call(
        functools.partial(expert_kernel, ndp, rows, width, index),
        out_shape=(
            shape((ndp, rows, depth), BF16),
            shape((ndp, rows + NOTE, depth), BF16),
            shape((ndp, 1, rows), F32),
            shape((depth, 3 * width), BF16),
        ),
        in_specs=[SMEM, VMEM]
        + [VMEM] * index
        + [HBM] * (2 * ndp + 1 + (2 if index else 0)),
        out_specs=(HBM, HBM, VMEM, HBM),
        scratch_shapes=scratch,
        compiler_params=params(60),
        cost_estimate=cost(flops, 40 * MIB, slots * width),
        name="expert",
    )(expert, router, *prev_gates, *hidden, *grads, w_all, *prev)


def project_back_kernel(
    ndp, nz, local, count, ids, residual, h_two, mixed, grads, gains, router, *refs
):
    backs, refs = refs[:ndp], refs[ndp:]
    parts, refs = refs[:count], refs[count:]
    _, _, grad_resid, grad_mixed, notes, *dests, w, terms, sem, out_sem = refs
    rows = residual.shape[0]
    loads = load_rows(ids, ndp, nz, parts, w, sem)
    expert = lax.broadcasted_iota(jnp.int32, (EXPERTS, rows), 0)
    grad_h = jnp.zeros((rows, MODEL_WIDTH), F32)
    grad_route = jnp.zeros((EXPERTS, rows), F32)
    for k in range(ndp):
        grad_h = grad_h + backs[k][:rows].astype(F32)
        note = backs[k][rows : rows + NOTE, : 3 * rows].astype(F32)
        whole = note[:, :rows] + note[:, rows : 2 * rows] + note[:, 2 * rows :]
        for j in range(local):
            at = (ids[0] ^ k) * local + j
            grad_route = grad_route + jnp.where(expert == at, whole[j : j + 1], 0.0)
    hidden = h_two[...]
    probs = route_softmax(router[...], hidden)
    grad_logits = probs * (grad_route - jnp.sum(probs * grad_route, axis=0, keepdims=True))
    grad_logits = jnp.concatenate([grad_logits, jnp.zeros_like(grad_logits)], axis=0)
    grad_logits = grad_logits.astype(BF16)
    grad_h = grad_h + tn(grad_logits, router[...])
    res = residual[...]
    scale = rms_scale(res)
    normed = res * scale
    notes[0:8] = jnp.broadcast_to(
        jnp.sum(normed * grad_h, axis=0, keepdims=True), (8, MODEL_WIDTH)
    )
    notes[8:16] = nn(grad_logits, hidden)[:EXPERTS]
    live = lax.broadcasted_iota(jnp.int32, (rows, 1), 0) < ids[3]
    final = jnp.where(live, grads[...].astype(F32), 0.0)
    total = final + norm_back(normed, scale, grad_h * gains[1:2])
    grad_resid[...] = total
    grad_attn = total.astype(BF16)
    mixed_t = jnp.transpose(mixed[...])
    for t in range(MODEL_WIDTH // TILE):
        lane = slice(t * TILE, (t + 1) * TILE)
        terms[:, lane] = nn(mixed_t, grad_attn[:, lane]).astype(BF16)
    for load in loads:
        load.wait()
    for t in range(QW // TILE):
        lane = slice(t * TILE, (t + 1) * TILE)
        grad_mixed[:, lane] = nt(grad_attn, w[lane, :]).astype(BF16)
    store_rows(ids, ndp, nz, terms, dests, out_sem)


def project_back(ids, residual, h_two, mixed, grads, gains, router, parts, backs, kept, sizes, local):
    ndp, nz = sizes["dp"], sizes["z"]
    rows = residual.shape[0]
    split = split_shapes(MODEL_WIDTH, sizes)
    given = 7 + ndp + len(parts)
    return pl.pallas_call(
        functools.partial(project_back_kernel, ndp, nz, local, len(parts)),
        out_shape=(
            shape(kept.shape, kept.dtype),
            shape((rows, MODEL_WIDTH), F32),
            shape((rows, QW), BF16),
            shape((16, MODEL_WIDTH), F32),
            *split,
        ),
        in_specs=[SMEM] + [VMEM] * (6 + ndp) + [HBM] * (len(parts) + 1),
        out_specs=(HBM, VMEM, VMEM, VMEM) + (HBM,) * len(split),
        scratch_shapes=[
            pltpu.VMEM((QW, MODEL_WIDTH), BF16),
            pltpu.VMEM((QW, MODEL_WIDTH), BF16),
            pltpu.SemaphoreType.DMA((2 * ndp * nz,)),
            pltpu.SemaphoreType.DMA((2 * ndp * nz,)),
        ],
        input_output_aliases={given: 0},
        compiler_params=params(50),
        cost_estimate=cost(4 * rows * MODEL_WIDTH * QW, 20 * MIB),
        name="project_back",
    )(ids, residual, h_two, mixed, grads, gains, router, *backs, *parts, kept)


def attend_back_kernel(
    ndp, nz, count, ids, tokens, cosine, sine, qkv, h_one, grad_mixed, grad_resid, gains, notes, *refs
):
    parts, refs = refs[:count], refs[count:]
    grad_tokens, *dests, w, terms, grad_pre, sem, out_sem = refs
    rows = tokens.shape[0]
    loads = load_rows(ids, ndp, nz, parts, w, sem)
    visible = seen(rows, ids[3])
    cos, sin = cosine[...], sine[...]
    for g in range(KEY_VALUE_HEADS):
        key = qkv[:, head(QUERY_HEADS + g)]
        value = qkv[:, head(QUERY_HEADS + KEY_VALUE_HEADS + g)]
        grad_key = jnp.zeros((rows, HEAD_SIZE), F32)
        grad_value = jnp.zeros((rows, HEAD_SIZE), F32)
        for h in range(g * GROUP, (g + 1) * GROUP):
            query, grad = qkv[:, head(h)], grad_mixed[:, head(h)]
            probs = attention_probs(query, key, visible)
            grad_probs = nt(grad, value)
            grad_value = grad_value + tn(probs.astype(BF16), grad)
            row_dot = jnp.sum(probs * grad_probs, axis=-1, keepdims=True)
            grad_scores = (probs * (grad_probs - row_dot)).astype(BF16)
            grad_query = nn(grad_scores, key) * SCALE
            grad_key = grad_key + tn(grad_scores, query)
            grad_pre[:, head(h)] = (grad_query * cos - swapped(grad_query) * sin).astype(BF16)
        grad_key = grad_key * SCALE
        grad_pre[:, head(QUERY_HEADS + g)] = (
            grad_key * cos - swapped(grad_key) * sin
        ).astype(BF16)
        grad_pre[:, head(QUERY_HEADS + KEY_VALUE_HEADS + g)] = grad_value.astype(BF16)
    h_one_t = jnp.transpose(h_one[...])
    for t in range(QKV // TILE):
        lane = slice(t * TILE, (t + 1) * TILE)
        terms[:, lane] = nn(h_one_t, grad_pre[:, lane]).astype(BF16)
    for load in loads:
        load.wait()
    tok = tokens[...].astype(F32)
    scale = rms_scale(tok)
    normed = tok * scale
    for t in range(MODEL_WIDTH // TILE):
        lane = slice(t * TILE, (t + 1) * TILE)
        grad_tokens[:, lane] = nt(grad_pre[...], w[lane, :QKV])
    grad_h = grad_tokens[...]
    grad_gain = jnp.sum(normed * grad_h, axis=0, keepdims=True)
    grad_tokens[...] = grad_resid[...] + norm_back(normed, scale, grad_h * gains[0:1])
    line = lax.broadcasted_iota(jnp.int32, (8, MODEL_WIDTH), 0)
    top = jnp.where(line == 0, grad_gain, jnp.where(line == 1, notes[0:8], 0.0))
    block = jnp.concatenate(
        [top, notes[8:16], jnp.zeros((PAD - 16, MODEL_WIDTH), F32)], axis=0
    )
    terms[:, QKV:] = jnp.transpose(block).astype(BF16)
    store_rows(ids, ndp, nz, terms, dests, out_sem)


def attend_back(
    ids, tokens, cosine, sine, qkv, h_one, grad_mixed, grad_resid, gains, notes, parts, sizes
):
    ndp, nz = sizes["dp"], sizes["z"]
    rows = tokens.shape[0]
    split = split_shapes(FIRST, sizes)
    return pl.pallas_call(
        functools.partial(attend_back_kernel, ndp, nz, len(parts)),
        out_shape=(shape((rows, MODEL_WIDTH), F32), *split),
        in_specs=[SMEM] + [VMEM] * 9 + [HBM] * len(parts),
        out_specs=(VMEM,) + (HBM,) * len(split),
        scratch_shapes=[
            pltpu.VMEM((MODEL_WIDTH, FIRST), BF16),
            pltpu.VMEM((MODEL_WIDTH, FIRST), BF16),
            pltpu.VMEM((rows, QKV), BF16),
            pltpu.SemaphoreType.DMA((2 * ndp * nz,)),
            pltpu.SemaphoreType.DMA((2 * ndp * nz,)),
        ],
        compiler_params=params(50),
        cost_estimate=cost(5 * rows * MODEL_WIDTH * QKV, 24 * MIB, 12 * rows * rows),
        name="attend_back",
    )(ids, tokens, cosine, sine, qkv, h_one, grad_mixed, grad_resid, gains, notes, *parts)


def rope_tables(rows):
    half = HEAD_SIZE // 2
    position = jnp.arange(rows).astype(F32)
    inverse = ROPE_BASE ** (-jnp.arange(half).astype(F32) / half)
    angles = position[:, None] * inverse[None, :]
    cosine, sine = jnp.cos(angles), jnp.sin(angles)
    return jnp.concatenate([cosine, cosine], axis=1), jnp.concatenate([-sine, sine], axis=1)


def per_device(
    sizes,
    tokens,
    lengths,
    routes,
    cotangent,
    gain_one,
    w_query,
    key_matrix,
    value_matrix,
    w_out,
    gain_two,
    w_router,
    w_gate,
    w_up,
    w_down,
):
    ndp = sizes["dp"]
    rows = tokens.shape[0]
    local, _, width = w_gate.shape
    me_dp = lax.axis_index("dp")
    length = lengths[0]
    ids = jnp.stack([me_dp, lax.axis_index("z"), lax.axis_index("core"), length]).astype(jnp.int32)
    live = (jnp.arange(rows) < length)[:, None]
    expert_ids = jnp.arange(EXPERTS, dtype=jnp.int32)

    extra = jnp.concatenate([gain_one[:, None], gain_two[:, None], w_router], axis=1)
    extra = jnp.pad(extra, ((0, 0), (0, PAD - extra.shape[1])))
    packed = jnp.concatenate([w_query, key_matrix, value_matrix, extra, w_out], axis=1)
    along_z = lax.all_gather(packed, "z", axis=0)
    named = jnp.any(routes[None, :, :] == expert_ids[:, None, None], axis=2).astype(BF16)
    named = jnp.pad(named, ((0, NOTE - EXPERTS), (0, MODEL_WIDTH - rows)))
    grad_low = jnp.where(live, cotangent, jnp.zeros_like(cotangent))
    grad_far = gather_axis(jnp.concatenate([grad_low, named], axis=0), "dp", ndp)
    expert_mats = [
        lax.all_gather(
            jnp.concatenate([w_gate[j], w_up[j], w_down[j]], axis=1), ("z", "core"), axis=0, tiled=True
        )
        for j in range(local)
    ]
    first = gather_axis(split_after(along_z, 0, FIRST, grad_far[1:]), "dp", ndp)
    second = gather_axis(split_after(along_z, FIRST, MODEL_WIDTH, first[1:]), "dp", ndp)
    first = row_parts(both_cores(first), ids, sizes)
    second = row_parts(both_cores(second), ids, sizes)

    cosine, sine = rope_tables(rows)
    qkv, mixed, h_one, gains, router = attend(ids, tokens, cosine, sine, first, sizes)
    residual, h_two = project(ids, tokens, mixed, gains, second, sizes)
    hidden = gather_axis(h_two, "dp", ndp)

    prev, gate_grads, sums = (), [], []
    for j in range(local):
        expert = (me_dp * local + j).astype(jnp.int32).reshape(1)
        out_far, back_far, grad_gate, terms = run_expert(
            j, expert, router, hidden, grad_far, expert_mats[j], prev, gate_grads
        )
        prev = (out_far, back_far)
        gate_grads.append(grad_gate)
        sums.append(
            lax.psum_scatter(terms, ("z", "core"), scatter_dimension=0, tiled=True).astype(F32)
        )
    backs = [back_far[0]] + [exchange(back_far[k], "dp", ndp, k) for k in range(1, ndp)]
    out_far, grad_resid, grad_mixed, notes, *terms = project_back(
        ids, residual, h_two, mixed, cotangent, gains, router, second, backs, out_far, sizes, local
    )
    grad_out = scatter_rows(terms, ids, sizes)
    grad_tokens, *terms = attend_back(
        ids, tokens, cosine, sine, qkv, h_one, grad_mixed, grad_resid, gains, notes, first, sizes
    )
    grad_first = scatter_rows(terms, ids, sizes)
    block = residual + out_far[0].astype(F32)
    for k in range(1, ndp):
        block = block + exchange(out_far[k], "dp", ndp, k).astype(F32)
    block_out = block.astype(BF16)

    expert_sums = jnp.stack(sums, axis=0)
    return (
        block_out,
        grad_tokens,
        grad_first[:, QKV],
        grad_first[:, :QW],
        grad_first[:, QW : QW + KW],
        grad_first[:, QW + KW : QKV],
        grad_out,
        grad_first[:, QKV + 1],
        grad_first[:, QKV + 8 : QKV + 8 + EXPERTS],
        expert_sums[:, :, :width],
        expert_sums[:, :, width : 2 * width],
        expert_sums[:, :, 2 * width :],
    )


def solution(mesh):
    ndp, nf = mesh.shape["dp"], mesh.shape["fsdp"]
    sizes = {"dp": ndp, "z": nf // 2, "core": 2}
    split = Mesh(mesh.devices.reshape(ndp, nf // 2, 2), ("dp", "z", "core"))
    every = ("dp", "z", "core")
    rows = P(every, None)
    vector = P(every)
    expert = P("dp", ("z", "core"), None)

    def run(*args):
        return per_device(sizes, *args)

    return jax.shard_map(
        run,
        mesh=split,
        in_specs=(rows, vector, rows, rows, vector, rows, rows, rows, rows, vector, rows)
        + (expert,) * 3,
        out_specs=(rows, rows, vector, rows, rows, rows, rows, vector, rows) + (expert,) * 3,
        check_vma=False,
    )
```

```python
import functools

import jax
import jax.numpy as jnp
from jax import lax
from jax.experimental import pallas as pl
from jax.experimental.pallas import tpu as pltpu
from jax.sharding import Mesh
from jax.sharding import PartitionSpec as P

MODEL_WIDTH = 1536
QUERY_HEADS = 12
KEY_VALUE_HEADS = 2
HEAD_SIZE = 128
EXPERTS = 8
CAP = 160
GROUP = QUERY_HEADS // KEY_VALUE_HEADS
QW = QUERY_HEADS * HEAD_SIZE
KW = KEY_VALUE_HEADS * HEAD_SIZE
QKV = QW + 2 * KW
PAD = 128
FIRST = QKV + PAD
NOTE = 32
ROUTER = 16
EPS = 1e-06
ROPE_BASE = 1500000.0
NEG_FILL = -1e30
SCALE = HEAD_SIZE ** (-0.5)
F32 = jnp.float32
BF16 = jnp.bfloat16
TILE = 256
MIB = 1024 * 1024
HBM = pl.BlockSpec(memory_space=pltpu.HBM)
VMEM = pl.BlockSpec(memory_space=pltpu.VMEM)
SMEM = pl.BlockSpec(memory_space=pltpu.SMEM)


def nn(a, b):
    return lax.dot_general(a, b, (((1,), (0,)), ((), ())), preferred_element_type=F32)


def nt(a, b):
    return lax.dot_general(a, b, (((1,), (1,)), ((), ())), preferred_element_type=F32)


def tn(a, b):
    return lax.dot_general(a, b, (((0,), (0,)), ((), ())), preferred_element_type=F32)


def shape(dims, dtype):
    return jax.ShapeDtypeStruct(dims, dtype)


def params(mib):
    return pltpu.CompilerParams(vmem_limit_bytes=mib * MIB)


def cost(flops, data, special=0):
    return pl.CostEstimate(flops=flops, bytes_accessed=data, transcendentals=special)


def exchange(block, axis, size, step):
    return lax.ppermute(block, axis, [(i, i ^ step) for i in range(size)])


def gather_dp(block, ndp):
    if ndp != 4:
        return [(k, 0, exchange(block, "dp", ndp, k) if k else block) for k in range(ndp)]
    half = block.shape[0] // 2
    side, up = exchange(block, "dp", ndp, 1), exchange(block, "dp", ndp, 2)
    return [
        (0, 0, block),
        (1, 0, side),
        (2, 0, up),
        (3, 0, exchange(side[:half], "dp", ndp, 2)),
        (3, half, exchange(up[half:], "dp", ndp, 1)),
    ]


def scatter_dp(slots, ndp):
    low = lambda part: part.astype(BF16)
    if ndp != 4:
        return [tuple(exchange(low(h), "dp", ndp, k) for h in slots[k]) for k in range(1, ndp)]
    add = lambda a, b: (a.astype(F32) + b.astype(F32)).astype(BF16)
    past_side = exchange(low(slots[3][0]), "dp", ndp, 1)
    past_up = exchange(low(slots[3][1]), "dp", ndp, 2)
    side = exchange(low(slots[1][0]), "dp", ndp, 1)
    up = exchange(low(slots[2][1]), "dp", ndp, 2)
    return [
        (side, exchange(add(slots[1][1], past_up), "dp", ndp, 1)),
        (exchange(add(slots[2][0], past_side), "dp", ndp, 2), up),
    ]


def both_cores(pieces):
    return [
        (k, c, start, exchange(piece, "core", 2, 1) if c else piece)
        for k, start, piece in pieces
        for c in range(2)
    ]


def stack_kernel(count, *refs):
    out = refs[-1]
    for i in range(count):
        out[i] = refs[i][...]


def stack_after(parts, before):
    dims = (len(parts),) + parts[0].shape
    return pl.pallas_call(
        functools.partial(stack_kernel, len(parts)),
        out_shape=shape(dims, parts[0].dtype),
        in_specs=[VMEM] * len(parts) + [HBM] * len(before),
        out_specs=VMEM,
        cost_estimate=cost(0, 4 * dims[0] * dims[1] * dims[2]),
        name="stack",
    )(*parts, *before)


def after_kernel(*refs):
    pass


def after(arrays, before):
    return pl.pallas_call(
        after_kernel,
        out_shape=tuple(shape(a.shape, a.dtype) for a in arrays),
        in_specs=[HBM] * (len(arrays) + len(before)),
        out_specs=(HBM,) * len(arrays),
        input_output_aliases={i: i for i in range(len(arrays))},
        name="after",
    )(*arrays, *before)


def block_rows(sizes):
    return MODEL_WIDTH // (2 * sizes["dp"] * sizes["z"])


def by_blocks(sizes):
    return block_rows(sizes) % 16 == 0


def gather_rows(block, before, ids, sizes):
    ndp, nz = sizes["dp"], sizes["z"]
    along_z = [block] + [exchange(block, "z", nz, k) for k in range(1, nz)]
    along_dp = gather_dp(stack_after(along_z, before), ndp)
    pieces = both_cores(along_dp)
    near = [piece for _, _, piece in along_dp[1:3]]
    if by_blocks(sizes):
        places = tuple((k, c, start, piece.shape[0]) for k, c, start, piece in pieces)
        return (places, [piece for *_, piece in pieces]), near
    columns = block.shape[-1]
    whole = jnp.zeros((ndp, nz, 2, block_rows(sizes), columns), BF16)
    for k, c, start, piece in pieces:
        order = ids[1] ^ jnp.arange(start, start + piece.shape[0])
        whole = whole.at[ids[0] ^ k, order, ids[2] ^ c].set(piece)
    return (None, [whole.reshape(MODEL_WIDTH, columns)]), near


def scatter_rows(terms, ids, sizes):
    ndp, nz = sizes["dp"], sizes["z"]
    if len(terms) == 1:
        blocks = terms[0].reshape(ndp, nz, 2, block_rows(sizes), -1)
        blocks = jnp.take(jnp.take(blocks, ids[0] ^ jnp.arange(ndp), 0), ids[1] ^ jnp.arange(nz), 1)
        terms = [lax.dynamic_index_in_dim(blocks, ids[2] ^ c, 2, keepdims=False) for c in range(2)]
    mine, other = terms
    got = exchange(other, "core", 2, 1)
    half = nz // 2
    slots = [
        tuple(mine[k, at].astype(F32) + got[k, at].astype(F32) for at in (slice(half), slice(half, nz)))
        for k in range(ndp)
    ]
    total = slots[0]
    for pair in scatter_dp(slots, ndp):
        total = tuple(t + p.astype(F32) for t, p in zip(total, pair))
    total = [total[z // half][z % half] for z in range(nz)]
    final = total[0]
    for z in range(1, nz):
        final = final + exchange(total[z].astype(BF16), "z", nz, z).astype(F32)
    return final


def load_rows(ids, ndp, nz, places, parts, dest, sem):
    if places is None:
        loads = [pltpu.make_async_copy(parts[0], dest, sem.at[0])]
        loads[0].start()
        return loads
    rows = MODEL_WIDTH // (ndp * nz * 2)
    loads = []
    for (k, c, start, count), part in zip(places, parts):
        for z in range(count):
            block = ((ids[0] ^ k) * nz + (ids[1] ^ (start + z))) * 2 + (ids[2] ^ c)
            place = pl.ds(pl.multiple_of(block * rows, rows), rows)
            copy = pltpu.make_async_copy(part.at[z], dest.at[place, :], sem.at[len(loads)])
            loads.append(copy)
    for load in loads:
        load.start()
    return loads


def store_rows(ids, ndp, nz, source, dests, sem):
    if len(dests) == 1:
        store = pltpu.make_async_copy(source, dests[0], sem.at[0])
        store.start()
        store.wait()
        return
    rows = MODEL_WIDTH // (ndp * nz * 2)
    stores = []
    for k in range(ndp):
        for z in range(nz):
            for c, dest in enumerate(dests):
                block = ((ids[0] ^ k) * nz + (ids[1] ^ z)) * 2 + (ids[2] ^ c)
                place = pl.ds(pl.multiple_of(block * rows, rows), rows)
                n = (k * 2 + c) * nz + z
                stores.append(
                    pltpu.make_async_copy(source.at[place, :], dest.at[k, z], sem.at[n])
                )
    for store in stores:
        store.start()
    for store in stores:
        store.wait()


def split_shapes(columns, sizes):
    if by_blocks(sizes):
        return (shape((sizes["dp"], sizes["z"], block_rows(sizes), columns), BF16),) * 2
    return (shape((MODEL_WIDTH, columns), BF16),)


def rms_scale(rows):
    return lax.rsqrt(jnp.mean(rows * rows, axis=-1, keepdims=True) + EPS)


def norm_back(normed, row_scale, grad):
    return row_scale * (grad - normed * jnp.mean(grad * normed, axis=-1, keepdims=True))


def swapped(vals):
    return pltpu.roll(vals, HEAD_SIZE // 2, 1)


def head(h):
    return slice(h * HEAD_SIZE, (h + 1) * HEAD_SIZE)


def seen(rows, length):
    q = lax.broadcasted_iota(jnp.int32, (rows, rows), 0)
    s = lax.broadcasted_iota(jnp.int32, (rows, rows), 1)
    return (s <= q) & (s < length)


def attention_probs(query, key, visible):
    scores = jnp.where(visible, nt(query, key) * SCALE, NEG_FILL)
    expon = jnp.exp(scores - jnp.max(scores, axis=-1, keepdims=True))
    return expon / jnp.sum(expon, axis=-1, keepdims=True)


def route_softmax(router_rows, hidden):
    logits = nt(router_rows, hidden)[:EXPERTS]
    expon = jnp.exp(logits - jnp.max(logits, axis=0, keepdims=True))
    return expon / jnp.sum(expon, axis=0, keepdims=True)


def attend_kernel(ndp, nz, places, ids, tokens, cosine, sine, *refs):
    *parts, qkv, mixed, h_one, gains, router, w, sem = refs
    rows = tokens.shape[0]
    loads = load_rows(ids, ndp, nz, places, parts, w, sem)
    tok = tokens[...].astype(F32)
    normed = tok * rms_scale(tok)
    for load in loads:
        load.wait()
    extra = jnp.transpose(w[:, QKV:].astype(F32))
    gains[...] = extra[:8]
    router[...] = extra[2 : 2 + ROUTER].astype(BF16)
    h_one[...] = (normed * extra[0:1]).astype(BF16)
    cos, sin = cosine[...], sine[...]
    for t in range(QKV // TILE):
        pre = nn(h_one[...], w[:, t * TILE : (t + 1) * TILE])
        for i in range(TILE // HEAD_SIZE):
            part = pre[:, head(i)]
            at = t * TILE + i * HEAD_SIZE
            if at < QW + KW:
                part = part * cos + swapped(part) * sin
            qkv[:, at : at + HEAD_SIZE] = part.astype(BF16)
    visible = seen(rows, ids[3])
    for h in range(QUERY_HEADS):
        g = h // GROUP
        probs = attention_probs(qkv[:, head(h)], qkv[:, head(QUERY_HEADS + g)], visible)
        values = qkv[:, head(QUERY_HEADS + KEY_VALUE_HEADS + g)]
        mixed[:, head(h)] = nn(probs.astype(BF16), values).astype(BF16)


def attend(ids, tokens, cosine, sine, weights, sizes):
    places, parts = weights
    ndp, nz = sizes["dp"], sizes["z"]
    rows = tokens.shape[0]
    return pl.pallas_call(
        functools.partial(attend_kernel, ndp, nz, places),
        out_shape=(
            shape((rows, QKV), BF16),
            shape((rows, QW), BF16),
            shape((rows, MODEL_WIDTH), BF16),
            shape((8, MODEL_WIDTH), F32),
            shape((ROUTER, MODEL_WIDTH), BF16),
        ),
        in_specs=[SMEM, VMEM, VMEM, VMEM] + [HBM] * len(parts),
        out_specs=(VMEM,) * 5,
        scratch_shapes=[
            pltpu.VMEM((MODEL_WIDTH, FIRST), BF16),
            pltpu.SemaphoreType.DMA((2 * ndp * nz,)),
        ],
        compiler_params=params(28),
        cost_estimate=cost(2 * rows * MODEL_WIDTH * QKV, 10 * MIB, 12 * rows * rows),
        name="attend",
    )(ids, tokens, cosine, sine, *parts)


def project_kernel(ndp, nz, places, ids, tokens, mixed, gains, *refs):
    *parts, residual, h_two, w, sem = refs
    loads = load_rows(ids, ndp, nz, places, parts, w, sem)
    for load in loads:
        load.wait()
    for t in range(MODEL_WIDTH // TILE):
        lane = slice(t * TILE, (t + 1) * TILE)
        residual[:, lane] = tokens[:, lane].astype(F32) + nn(mixed[...], w[:, lane])
    whole = residual[...]
    h_two[...] = (whole * rms_scale(whole) * gains[1:2]).astype(BF16)


def project(ids, tokens, mixed, gains, weights, sizes):
    places, parts = weights
    ndp, nz = sizes["dp"], sizes["z"]
    rows = tokens.shape[0]
    return pl.pallas_call(
        functools.partial(project_kernel, ndp, nz, places),
        out_shape=(shape((rows, MODEL_WIDTH), F32), shape((rows, MODEL_WIDTH), BF16)),
        in_specs=[SMEM, VMEM, VMEM, VMEM] + [HBM] * len(parts),
        out_specs=(VMEM,) * 2,
        scratch_shapes=[
            pltpu.VMEM((QW, MODEL_WIDTH), BF16),
            pltpu.SemaphoreType.DMA((2 * ndp * nz,)),
        ],
        compiler_params=params(28),
        cost_estimate=cost(2 * rows * MODEL_WIDTH * QW, 8 * MIB),
        name="project",
    )(ids, tokens, mixed, gains, *parts)


def expert_kernel(ndp, rows, width, index, last, near, far, *refs):
    it = iter(refs)
    take = lambda n: [next(it) for _ in range(n)]
    (expert_ref, router_ref) = take(2)
    prev_gates = take(index)
    hid_in, cot_in = take(len(near)), take(len(far))
    (w_in,) = take(1)
    prev_in = take(2) if index else []
    out_hbm, back_hbm = (take(2 * ndp), take(2 * ndp)) if last else (take(1), take(1))
    gates_ref, terms_hbm = take(2)
    hid, cot, w, x, d, ge, inner, dg, du, pick, pick_t, slot_gate, slot_dot = take(13)
    (terms_buf,) = take(1)
    prev = take(2) if index else []
    in_sem, out_sem = take(2)
    depth = MODEL_WIDTH
    tiles = depth // TILE

    loads = {}

    def load(name, source, dest):
        copy = pltpu.make_async_copy(source, dest, in_sem.at[len(loads)])
        copy.start()
        loads[name] = copy

    for i, (k, start, count) in enumerate(near):
        load(("hid", i), hid_in[i], hid.at[k, pl.ds(start, count), :])
    for i, (k, start, count) in enumerate(far):
        load(("cot", i), cot_in[i], cot.at[k, pl.ds(start, count), :])
    load("w", w_in, w)
    for i in range(len(prev)):
        load(("prev", i), prev_in[i], prev[i])

    expert = expert_ref[0]
    which = lax.broadcasted_iota(jnp.int32, (EXPERTS, rows), 0) == expert
    earlier = (
        (
            lax.broadcasted_iota(jnp.int32, (rows, rows), 0)
            < lax.broadcasted_iota(jnp.int32, (rows, rows), 1)
        )
        .astype(F32)
        .astype(BF16)
    )
    slot = lax.broadcasted_iota(jnp.int32, (CAP, rows), 0).astype(F32)
    for s in range(ndp):
        for i, piece in enumerate(near):
            if piece[0] == s:
                loads["hid", i].wait()
        for i, piece in enumerate(far):
            if piece[0] == s:
                loads["cot", i].wait()
        hidden = hid[s]
        probs = route_softmax(router_ref[...], hidden)
        named = cot[s, rows : rows + NOTE, :rows]
        place = nn(named, earlier)[:EXPERTS]
        named = named[:EXPERTS].astype(F32)
        named_row = jnp.sum(jnp.where(which, named, 0.0), axis=0, keepdims=True)
        gate_row = jnp.sum(jnp.where(which, probs, 0.0), axis=0, keepdims=True)
        place_row = jnp.sum(jnp.where(which, place, 0.0), axis=0, keepdims=True)
        chosen = jnp.where((slot == place_row) & (named_row > 0.5), 1.0, 0.0)
        pick[s] = chosen.astype(BF16)
        pick_t[s] = jnp.transpose(chosen).astype(BF16)
        at = pl.ds(s * CAP, CAP)
        gate = jnp.sum(chosen * gate_row, axis=1, keepdims=True)
        slot_gate[at, :] = jnp.broadcast_to(gate, (CAP, 128))
        x[at, :] = nn(pick[s], hidden).astype(BF16)
        grads = nn(pick[s], cot[s, :rows])
        d[at, :] = grads.astype(BF16)
        ge[at, :] = (gate * grads).astype(BF16)
    loads["w"].wait()

    def hidden_units(t, carry):
        at = pl.multiple_of(t * TILE, TILE)
        gate_pre = nn(x[...], w[:, pl.ds(at, TILE)])
        up_pre = nn(x[...], w[:, pl.ds(width + at, TILE)])
        grad_inner = nn(ge[...], w[:, pl.ds(2 * width + at, TILE)])
        sig = 1.0 / (1.0 + jnp.exp(-gate_pre))
        act = gate_pre * sig
        inner[:, pl.ds(at, TILE)] = (act * up_pre).astype(BF16)
        dg[:, pl.ds(at, TILE)] = (
            grad_inner * up_pre * sig * (1.0 + gate_pre * (1.0 - sig))
        ).astype(BF16)
        du[:, pl.ds(at, TILE)] = (grad_inner * act).astype(BF16)
        return carry

    lax.fori_loop(0, width // TILE, hidden_units, 0)
    slot_dot[...] = jnp.zeros_like(slot_dot)
    for i in range(len(prev)):
        loads["prev", i].wait()

    half, noted = rows // 2, (rows + NOTE) // 2

    def stores(t):
        lane = pl.ds(pl.multiple_of(t * TILE, TILE), TILE)
        copies = [(terms_buf.at[lane, :], terms_hbm.at[lane, :])]
        if not last:
            body = pl.ds(0, rows)
            copies.append((hid.at[:, :, lane], out_hbm[0].at[:, :, lane]))
            copies.append((cot.at[:, body, lane], back_hbm[0].at[:, body, lane]))
        else:
            for i in range(2 * ndp):
                first = pl.ds(i % 2 * half, half)
                copies.append((hid.at[i // 2, first, lane], out_hbm[i].at[:, lane]))
                body = pl.ds(0, noted if i % 2 == 0 else rows - noted)
                taken = pl.ds(i % 2 * noted, noted if i % 2 == 0 else rows - noted)
                copies.append((cot.at[i // 2, taken, lane], back_hbm[i].at[body, lane]))
        return [
            pltpu.make_async_copy(source, dest, out_sem.at[i, t])
            for i, (source, dest) in enumerate(copies)
        ]

    def features(t, carry):
        lane = pl.ds(pl.multiple_of(t * TILE, TILE), TILE)
        result = nt(inner[...], w[lane, pl.ds(2 * width, width)]).astype(BF16).astype(F32)
        partial = jnp.sum(result * d[:, lane].astype(F32), axis=1, keepdims=True)
        slot_dot[...] += jnp.broadcast_to(partial, slot_dot.shape)
        gated = (slot_gate[:, :1] * result).astype(BF16)
        grad_in = (
            nt(dg[...], w[lane, pl.ds(0, width)]) + nt(du[...], w[lane, pl.ds(width, width)])
        ).astype(BF16)
        for s in range(ndp):
            part = slice(s * CAP, (s + 1) * CAP)
            sent = nn(pick_t[s], gated[part])
            back = nn(pick_t[s], grad_in[part])
            if prev:
                sent = sent + prev[0][s, :, lane].astype(F32)
                back = back + prev[1][s, :rows, lane].astype(F32)
            hid[s, :, lane] = sent.astype(BF16)
            cot[s, :rows, lane] = back.astype(BF16)
        x_t = jnp.transpose(x[:, lane])
        terms_buf[lane, pl.ds(0, width)] = nn(x_t, dg[...]).astype(BF16)
        terms_buf[lane, pl.ds(width, width)] = nn(x_t, du[...]).astype(BF16)
        ge_t = jnp.transpose(ge[:, lane])
        terms_buf[lane, pl.ds(2 * width, width)] = nn(ge_t, inner[...]).astype(BF16)
        for store in stores(t):
            store.start()
        return carry

    lax.fori_loop(0, tiles, features, 0)
    line = lax.broadcasted_iota(jnp.int32, (NOTE, 3 * rows), 0)
    notes = []
    for s in range(ndp):
        part = slice(s * CAP, (s + 1) * CAP)
        own = jnp.sum(pick[s].astype(F32) * slot_dot[part, :1], axis=0, keepdims=True)
        gates_ref[s] = own
        if not last:
            continue
        note = jnp.zeros((NOTE, 3 * rows), F32)
        for j, row in enumerate([p[s] for p in prev_gates] + [own]):
            high = row.astype(BF16).astype(F32)
            middle = (row - high).astype(BF16).astype(F32)
            low = row - high - middle
            at = expert - index + j
            note = jnp.where(line == at, jnp.concatenate([high, middle, low], axis=1), note)
        cot[s, rows : rows + NOTE, : 3 * rows] = note.astype(BF16)
        notes.append(
            pltpu.make_async_copy(
                cot.at[s, pl.ds(rows, NOTE), :],
                back_hbm[2 * s + 1].at[pl.ds(rows - noted, NOTE), :],
                out_sem.at[4 * ndp + 1, s],
            )
        )
        notes[-1].start()
    for t in range(tiles):
        for store in stores(t):
            store.wait()
    for note in notes:
        note.wait()


def run_expert(index, last, expert, router, hidden, grads, w_all, prev, prev_gates, ndp):
    rows = hidden[0][2].shape[0]
    near, far = (tuple((k, at, p.shape[0]) for k, at, p in group) for group in (hidden, grads))
    width = w_all.shape[1] // 3
    slots = ndp * CAP
    depth = MODEL_WIDTH
    tiles = depth // TILE
    scratch = [
        pltpu.VMEM((ndp, rows, depth), BF16),
        pltpu.VMEM((ndp, rows + NOTE, depth), BF16),
        pltpu.VMEM((depth, 3 * width), BF16),
        pltpu.VMEM((slots, depth), BF16),
        pltpu.VMEM((slots, depth), BF16),
        pltpu.VMEM((slots, depth), BF16),
        pltpu.VMEM((slots, width), BF16),
        pltpu.VMEM((slots, width), BF16),
        pltpu.VMEM((slots, width), BF16),
        pltpu.VMEM((ndp, CAP, rows), BF16),
        pltpu.VMEM((ndp, rows, CAP), BF16),
        pltpu.VMEM((slots, 128), F32),
        pltpu.VMEM((slots, 128), F32),
        pltpu.VMEM((depth, 3 * width), BF16),
    ]
    if index:
        scratch += [
            pltpu.VMEM((ndp, rows, depth), BF16),
            pltpu.VMEM((ndp, rows + NOTE, depth), BF16),
        ]
    scratch += [
        pltpu.SemaphoreType.DMA((len(near) + len(far) + 3,)),
        pltpu.SemaphoreType.DMA((4 * ndp + 2, max(tiles, ndp))),
    ]
    sent = [shape((ndp, rows, depth), BF16), shape((ndp, rows + NOTE, depth), BF16)]
    if last:
        sent = [shape((rows // 2, depth), BF16)] * (2 * ndp)
        sent += [shape(((rows + NOTE) // 2, depth), BF16)] * (2 * ndp)
    flops = 2 * slots * depth * width * 9 + 8 * ndp * CAP * rows * depth
    return pl.pallas_call(
        functools.partial(expert_kernel, ndp, rows, width, index, last, near, far),
        out_shape=(
            *sent,
            shape((ndp, 1, rows), F32),
            shape((depth, 3 * width), BF16),
        ),
        in_specs=[SMEM, VMEM]
        + [VMEM] * len(prev_gates)
        + [HBM] * (len(near) + len(far) + 1 + len(prev)),
        out_specs=(HBM,) * len(sent) + (VMEM, HBM),
        scratch_shapes=scratch,
        compiler_params=params(60),
        cost_estimate=cost(flops, 40 * MIB, slots * width),
        name="expert",
    )(
        expert,
        router,
        *prev_gates,
        *(piece for *_, piece in hidden),
        *(piece for *_, piece in grads),
        w_all,
        *prev,
    )


def project_back_kernel(
    ndp, nz, local, places, count, pairs, ids, residual, h_two, mixed, grads, gains, router, *refs
):
    backs, refs = refs[: 2 * pairs], refs[2 * pairs :]
    parts, refs = refs[:count], refs[count:]
    grad_resid, grad_mixed, notes, *dests, w, terms, sem, out_sem = refs
    rows = residual.shape[0]
    loads = load_rows(ids, ndp, nz, places, parts, w, sem)
    upper, lower = backs[0][...].astype(F32), backs[1][...].astype(F32)
    for i in range(1, pairs):
        upper = upper + backs[2 * i][...].astype(F32)
        lower = lower + backs[2 * i + 1][...].astype(F32)
    body = rows - upper.shape[0]
    grad_h = jnp.concatenate([upper, lower[:body]], axis=0)
    note = lower[body : body + EXPERTS, : 3 * rows]
    grad_route = note[:, :rows] + note[:, rows : 2 * rows] + note[:, 2 * rows :]
    hidden = h_two[...]
    probs = route_softmax(router[...], hidden)
    grad_logits = probs * (grad_route - jnp.sum(probs * grad_route, axis=0, keepdims=True))
    grad_logits = jnp.concatenate([grad_logits, jnp.zeros_like(grad_logits)], axis=0)
    grad_logits = grad_logits.astype(BF16)
    grad_h = grad_h + tn(grad_logits, router[...])
    res = residual[...]
    scale = rms_scale(res)
    normed = res * scale
    notes[0:8] = jnp.broadcast_to(
        jnp.sum(normed * grad_h, axis=0, keepdims=True), (8, MODEL_WIDTH)
    )
    notes[8:16] = nn(grad_logits, hidden)[:EXPERTS]
    live = lax.broadcasted_iota(jnp.int32, (rows, 1), 0) < ids[3]
    final = jnp.where(live, grads[...].astype(F32), 0.0)
    total = final + norm_back(normed, scale, grad_h * gains[1:2])
    grad_resid[...] = total
    grad_attn = total.astype(BF16)
    mixed_t = jnp.transpose(mixed[...])
    for t in range(MODEL_WIDTH // TILE):
        lane = slice(t * TILE, (t + 1) * TILE)
        terms[:, lane] = nn(mixed_t, grad_attn[:, lane]).astype(BF16)
    for load in loads:
        load.wait()
    for t in range(QW // TILE):
        lane = slice(t * TILE, (t + 1) * TILE)
        grad_mixed[:, lane] = nt(grad_attn, w[lane, :]).astype(BF16)
    store_rows(ids, ndp, nz, terms, dests, out_sem)


def project_back(ids, residual, h_two, mixed, grads, gains, router, weights, backs, sizes, local):
    places, parts = weights
    ndp, nz = sizes["dp"], sizes["z"]
    rows = residual.shape[0]
    split = split_shapes(MODEL_WIDTH, sizes)
    return pl.pallas_call(
        functools.partial(
            project_back_kernel, ndp, nz, local, places, len(parts), len(backs) // 2
        ),
        out_shape=(
            shape((rows, MODEL_WIDTH), F32),
            shape((rows, QW), BF16),
            shape((16, MODEL_WIDTH), F32),
            *split,
        ),
        in_specs=[SMEM] + [VMEM] * (6 + len(backs)) + [HBM] * len(parts),
        out_specs=(VMEM, VMEM, VMEM) + (HBM,) * len(split),
        scratch_shapes=[
            pltpu.VMEM((QW, MODEL_WIDTH), BF16),
            pltpu.VMEM((QW, MODEL_WIDTH), BF16),
            pltpu.SemaphoreType.DMA((2 * ndp * nz,)),
            pltpu.SemaphoreType.DMA((2 * ndp * nz,)),
        ],
        compiler_params=params(50),
        cost_estimate=cost(4 * rows * MODEL_WIDTH * QW, 20 * MIB),
        name="project_back",
    )(ids, residual, h_two, mixed, grads, gains, router, *backs, *parts)


def attend_back_kernel(
    ndp, nz, places, count, unread, ids, tokens, cosine, sine, qkv, h_one, grad_mixed, grad_resid, gains, notes, *refs
):
    parts, refs = refs[:count], refs[count:]
    grad_tokens, *dests, w, terms, grad_pre, sem, out_sem = refs[unread:]
    rows = tokens.shape[0]
    loads = load_rows(ids, ndp, nz, places, parts, w, sem)
    visible = seen(rows, ids[3])
    cos, sin = cosine[...], sine[...]
    for g in range(KEY_VALUE_HEADS):
        key = qkv[:, head(QUERY_HEADS + g)]
        value = qkv[:, head(QUERY_HEADS + KEY_VALUE_HEADS + g)]
        grad_key = jnp.zeros((rows, HEAD_SIZE), F32)
        grad_value = jnp.zeros((rows, HEAD_SIZE), F32)
        for h in range(g * GROUP, (g + 1) * GROUP):
            query, grad = qkv[:, head(h)], grad_mixed[:, head(h)]
            probs = attention_probs(query, key, visible)
            grad_probs = nt(grad, value)
            grad_value = grad_value + tn(probs.astype(BF16), grad)
            row_dot = jnp.sum(probs * grad_probs, axis=-1, keepdims=True)
            grad_scores = (probs * (grad_probs - row_dot)).astype(BF16)
            grad_query = nn(grad_scores, key) * SCALE
            grad_key = grad_key + tn(grad_scores, query)
            grad_pre[:, head(h)] = (grad_query * cos - swapped(grad_query) * sin).astype(BF16)
        grad_key = grad_key * SCALE
        grad_pre[:, head(QUERY_HEADS + g)] = (
            grad_key * cos - swapped(grad_key) * sin
        ).astype(BF16)
        grad_pre[:, head(QUERY_HEADS + KEY_VALUE_HEADS + g)] = grad_value.astype(BF16)
    h_one_t = jnp.transpose(h_one[...])
    for t in range(QKV // TILE):
        lane = slice(t * TILE, (t + 1) * TILE)
        terms[:, lane] = nn(h_one_t, grad_pre[:, lane]).astype(BF16)
    for load in loads:
        load.wait()
    tok = tokens[...].astype(F32)
    scale = rms_scale(tok)
    normed = tok * scale
    for t in range(MODEL_WIDTH // TILE):
        lane = slice(t * TILE, (t + 1) * TILE)
        grad_tokens[:, lane] = nt(grad_pre[...], w[lane, :QKV])
    grad_h = grad_tokens[...]
    grad_gain = jnp.sum(normed * grad_h, axis=0, keepdims=True)
    grad_tokens[...] = grad_resid[...] + norm_back(normed, scale, grad_h * gains[0:1])
    line = lax.broadcasted_iota(jnp.int32, (8, MODEL_WIDTH), 0)
    top = jnp.where(line == 0, grad_gain, jnp.where(line == 1, notes[0:8], 0.0))
    block = jnp.concatenate(
        [top, notes[8:16], jnp.zeros((PAD - 16, MODEL_WIDTH), F32)], axis=0
    )
    terms[:, QKV:] = jnp.transpose(block).astype(BF16)
    store_rows(ids, ndp, nz, terms, dests, out_sem)


def attend_back(
    ids, tokens, cosine, sine, qkv, h_one, grad_mixed, grad_resid, gains, notes, weights, before, sizes
):
    places, parts = weights
    ndp, nz = sizes["dp"], sizes["z"]
    rows = tokens.shape[0]
    split = split_shapes(FIRST, sizes)
    return pl.pallas_call(
        functools.partial(attend_back_kernel, ndp, nz, places, len(parts), len(before)),
        out_shape=(shape((rows, MODEL_WIDTH), F32), *split),
        in_specs=[SMEM] + [VMEM] * 9 + [HBM] * (len(parts) + len(before)),
        out_specs=(VMEM,) + (HBM,) * len(split),
        scratch_shapes=[
            pltpu.VMEM((MODEL_WIDTH, FIRST), BF16),
            pltpu.VMEM((MODEL_WIDTH, FIRST), BF16),
            pltpu.VMEM((rows, QKV), BF16),
            pltpu.SemaphoreType.DMA((2 * ndp * nz,)),
            pltpu.SemaphoreType.DMA((2 * ndp * nz,)),
        ],
        compiler_params=params(50),
        cost_estimate=cost(5 * rows * MODEL_WIDTH * QKV, 24 * MIB, 12 * rows * rows),
        name="attend_back",
    )(ids, tokens, cosine, sine, qkv, h_one, grad_mixed, grad_resid, gains, notes, *parts, *before)


def rope_tables(rows):
    half = HEAD_SIZE // 2
    position = jnp.arange(rows).astype(F32)
    inverse = ROPE_BASE ** (-jnp.arange(half).astype(F32) / half)
    angles = position[:, None] * inverse[None, :]
    cosine, sine = jnp.cos(angles), jnp.sin(angles)
    return jnp.concatenate([cosine, cosine], axis=1), jnp.concatenate([-sine, sine], axis=1)


def per_device(
    sizes,
    tokens,
    lengths,
    routes,
    cotangent,
    gain_one,
    w_query,
    key_matrix,
    value_matrix,
    w_out,
    gain_two,
    w_router,
    w_gate,
    w_up,
    w_down,
):
    ndp = sizes["dp"]
    rows = tokens.shape[0]
    local, _, width = w_gate.shape
    me_dp = lax.axis_index("dp")
    length = lengths[0]
    ids = jnp.stack([me_dp, lax.axis_index("z"), lax.axis_index("core"), length]).astype(jnp.int32)
    live = (jnp.arange(rows) < length)[:, None]
    expert_ids = jnp.arange(EXPERTS, dtype=jnp.int32)

    extra = jnp.concatenate([gain_one[:, None], gain_two[:, None], w_router], axis=1)
    extra = jnp.pad(extra, ((0, 0), (0, PAD - extra.shape[1])))
    first = jnp.concatenate([w_query, key_matrix, value_matrix, extra], axis=1)
    named = jnp.any(routes[None, :, :] == expert_ids[:, None, None], axis=2).astype(BF16)
    named = jnp.pad(named, ((0, NOTE - EXPERTS), (0, MODEL_WIDTH - rows)))
    grad_low = jnp.where(live, cotangent, jnp.zeros_like(cotangent))
    grad_far = gather_dp(jnp.concatenate([grad_low, named], axis=0), ndp)
    expert_mats = [
        lax.all_gather(
            jnp.concatenate([w_gate[j], w_up[j], w_down[j]], axis=1), ("z", "core"), axis=0, tiled=True
        )
        for j in range(local)
    ]
    first, near = gather_rows(first, [piece for *_, piece in grad_far[1:3]], ids, sizes)
    second, _ = gather_rows(w_out, near, ids, sizes)

    cosine, sine = rope_tables(rows)
    qkv, mixed, h_one, gains, router = attend(ids, tokens, cosine, sine, first, sizes)
    residual, h_two = project(ids, tokens, mixed, gains, second, sizes)
    hidden = gather_dp(h_two, ndp)

    prev, gate_grads, sums = (), [], []
    for j in range(local):
        expert = (me_dp * local + j).astype(jnp.int32).reshape(1)
        *prev, grad_gate, terms = run_expert(
            j,
            j == local - 1,
            expert,
            router,
            hidden,
            grad_far,
            expert_mats[j],
            prev,
            gate_grads,
            ndp,
        )
        gate_grads.append(grad_gate)
        sums.append(lax.psum_scatter(terms, ("z", "core"), scatter_dimension=0, tiled=True))
    outs, backs = prev[: 2 * ndp], prev[2 * ndp :]
    pairs = lambda flat: [tuple(flat[2 * k : 2 * k + 2]) for k in range(len(flat) // 2)]
    got = scatter_dp(pairs(backs), ndp)
    backs = list(backs[:2]) + [part for pair in got for part in pair]
    outs = list(outs[:2]) + list(after(outs[2:], backs[2:]))
    grad_resid, grad_mixed, notes, *terms = project_back(
        ids, residual, h_two, mixed, cotangent, gains, router, second, backs, sizes, local
    )
    grad_out = scatter_rows(terms, ids, sizes)
    grad_tokens, *terms = attend_back(
        ids, tokens, cosine, sine, qkv, h_one, grad_mixed, grad_resid, gains, notes, first, sums[:-1], sizes
    )
    grad_first = scatter_rows(terms, ids, sizes)
    block = tuple(part.astype(F32) for part in outs[:2])
    for pair in scatter_dp(pairs(outs), ndp):
        block = tuple(total + part.astype(F32) for total, part in zip(block, pair))
    block_out = (residual + jnp.concatenate(block, axis=0)).astype(BF16)

    expert_sums = jnp.stack(sums, axis=0).astype(F32)
    return (
        block_out,
        grad_tokens,
        grad_first[:, QKV],
        grad_first[:, :QW],
        grad_first[:, QW : QW + KW],
        grad_first[:, QW + KW : QKV],
        grad_out,
        grad_first[:, QKV + 1],
        grad_first[:, QKV + 8 : QKV + 8 + EXPERTS],
        expert_sums[:, :, :width],
        expert_sums[:, :, width : 2 * width],
        expert_sums[:, :, 2 * width :],
    )


def solution(mesh):
    ndp, nf = mesh.shape["dp"], mesh.shape["fsdp"]
    sizes = {"dp": ndp, "z": nf // 2, "core": 2}
    split = Mesh(mesh.devices.reshape(ndp, nf // 2, 2), ("dp", "z", "core"))
    every = ("dp", "z", "core")
    rows = P(every, None)
    vector = P(every)
    expert = P("dp", ("z", "core"), None)

    def run(*args):
        return per_device(sizes, *args)

    return jax.shard_map(
        run,
        mesh=split,
        in_specs=(rows, vector, rows, rows, vector, rows, rows, rows, rows, vector, rows)
        + (expert,) * 3,
        out_specs=(rows, rows, vector, rows, rows, rows, rows, vector, rows) + (expert,) * 3,
        check_vma=False,
    )
```

```python
import functools

import jax
import jax.numpy as jnp
from jax import lax
from jax.experimental import pallas as pl
from jax.experimental.pallas import tpu as pltpu
from jax.sharding import Mesh
from jax.sharding import PartitionSpec as P

MODEL_WIDTH = 1536
QUERY_HEADS = 12
KEY_VALUE_HEADS = 2
HEAD_SIZE = 128
EXPERTS = 8
CAP = 160
GROUP = QUERY_HEADS // KEY_VALUE_HEADS
QW = QUERY_HEADS * HEAD_SIZE
KW = KEY_VALUE_HEADS * HEAD_SIZE
QKV = QW + 2 * KW
PAD = 128
FIRST = QKV + PAD
NOTE = 32
ROUTER = 16
EPS = 1e-06
ROPE_BASE = 1500000.0
NEG_FILL = -1e30
SCALE = HEAD_SIZE ** (-0.5)
F32 = jnp.float32
BF16 = jnp.bfloat16
TILE = 256
MIB = 1024 * 1024
HBM = pl.BlockSpec(memory_space=pltpu.HBM)
VMEM = pl.BlockSpec(memory_space=pltpu.VMEM)
SMEM = pl.BlockSpec(memory_space=pltpu.SMEM)


def nn(a, b):
    return lax.dot_general(a, b, (((1,), (0,)), ((), ())), preferred_element_type=F32)


def nt(a, b):
    return lax.dot_general(a, b, (((1,), (1,)), ((), ())), preferred_element_type=F32)


def tn(a, b):
    return lax.dot_general(a, b, (((0,), (0,)), ((), ())), preferred_element_type=F32)


def shape(dims, dtype):
    return jax.ShapeDtypeStruct(dims, dtype)


def params(mib):
    return pltpu.CompilerParams(vmem_limit_bytes=mib * MIB)


def cost(flops, data, special=0):
    return pl.CostEstimate(flops=flops, bytes_accessed=data, transcendentals=special)


def exchange(block, axis, size, step):
    return lax.ppermute(block, axis, [(i, i ^ step) for i in range(size)])


def start_dp(block, ndp):
    return [exchange(block, "dp", ndp, k) for k in ((1, 2) if ndp == 4 else range(1, ndp))]


def pass_on(block, near, ndp, before=()):
    if ndp != 4:
        return [(k, 0, piece) for k, piece in enumerate([block] + near)]
    side, up = after(near, before) if before else near
    half = block.shape[0] // 2
    return [
        (0, 0, block),
        (1, 0, side),
        (2, 0, up),
        (3, 0, exchange(side[:half], "dp", ndp, 2)),
        (3, half, exchange(up[half:], "dp", ndp, 1)),
    ]


def gather_halves(halves, ndp):
    top, low = halves
    at = top.shape[0]
    if ndp != 4:
        return [
            (k, i * at, exchange(half, "dp", ndp, k) if k else half)
            for k in range(ndp)
            for i, half in enumerate(halves)
        ]
    side_top, up_low = exchange(top, "dp", ndp, 1), exchange(low, "dp", ndp, 2)
    side_low, up_top = exchange(low, "dp", ndp, 1), exchange(top, "dp", ndp, 2)
    return [
        (0, 0, top),
        (0, at, low),
        (1, 0, side_top),
        (2, at, up_low),
        (1, at, side_low),
        (2, 0, up_top),
        (3, 0, exchange(side_top, "dp", ndp, 2)),
        (3, at, exchange(up_low, "dp", ndp, 1)),
    ]


def scatter_dp(slots, ndp, before=()):
    low = lambda part: part.astype(BF16)
    if ndp != 4:
        return [tuple(exchange(low(h), "dp", ndp, k) for h in slots[k]) for k in range(1, ndp)]
    add = lambda a, b: (a.astype(F32) + b.astype(F32)).astype(BF16)
    past_side = exchange(low(slots[3][0]), "dp", ndp, 1)
    past_up = exchange(low(slots[3][1]), "dp", ndp, 2)
    side = exchange(low(slots[1][0]), "dp", ndp, 1)
    up = exchange(low(slots[2][1]), "dp", ndp, 2)
    if before:
        past_side, past_up = after([past_side, past_up], before)
    return [
        (side, exchange(add(slots[1][1], past_up), "dp", ndp, 1)),
        (exchange(add(slots[2][0], past_side), "dp", ndp, 2), up),
    ]


def both_cores(pieces):
    return [
        (k, c, start, exchange(piece, "core", 2, 1) if c else piece)
        for k, start, piece in pieces
        for c in range(2)
    ]


def stack_kernel(count, *refs):
    for i in range(count):
        refs[-1][i] = refs[i][...]


def stack_after(parts, before):
    dims = (len(parts),) + parts[0].shape
    return pl.pallas_call(
        functools.partial(stack_kernel, len(parts)),
        out_shape=shape(dims, parts[0].dtype),
        in_specs=[VMEM] * len(parts) + [HBM] * len(before),
        out_specs=VMEM,
        cost_estimate=cost(0, 4 * dims[0] * dims[1] * dims[2]),
        name="stack",
    )(*parts, *before)


def pack_kernel(index, *refs):
    width = refs[0].shape[2]
    for i in range(3):
        refs[-1][:, i * width : (i + 1) * width] = refs[i][index]


def pack_after(index, mats, before):
    _, rows, width = mats[0].shape
    return pl.pallas_call(
        functools.partial(pack_kernel, index),
        out_shape=shape((rows, 3 * width), BF16),
        in_specs=[VMEM] * 3 + [HBM] * len(before),
        out_specs=VMEM,
        name="pack",
    )(*mats, *before)


def finish_kernel(count, *refs):
    outs = refs[-3:]
    width = outs[0].shape[2]
    for j in range(count):
        for i in range(3):
            outs[i][j] = refs[j][:, i * width : (i + 1) * width].astype(F32)


def finish_after(sums, before):
    rows, width = sums[0].shape[0], sums[0].shape[1] // 3
    return pl.pallas_call(
        functools.partial(finish_kernel, len(sums)),
        out_shape=(shape((len(sums), rows, width), F32),) * 3,
        in_specs=[VMEM] * len(sums) + [HBM] * len(before),
        out_specs=(VMEM,) * 3,
        name="finish",
    )(*sums, *before)


def after_kernel(*refs):
    pass


def after(arrays, before):
    return pl.pallas_call(
        after_kernel,
        out_shape=tuple(shape(a.shape, a.dtype) for a in arrays),
        in_specs=[HBM] * (len(arrays) + len(before)),
        out_specs=(HBM,) * len(arrays),
        input_output_aliases={i: i for i in range(len(arrays))},
        name="after",
    )(*arrays, *before)


def block_rows(sizes):
    return MODEL_WIDTH // (2 * sizes["dp"] * sizes["z"])


def by_blocks(sizes):
    return block_rows(sizes) % 16 == 0


def gather_rows(block, along_dp, ids, sizes):
    ndp, nz = sizes["dp"], sizes["z"]
    pieces = both_cores(along_dp)
    if by_blocks(sizes):
        places = tuple((k, c, start, piece.shape[0]) for k, c, start, piece in pieces)
        return places, [piece for *_, piece in pieces]
    columns = block.shape[-1]
    whole = jnp.zeros((ndp, nz, 2, block_rows(sizes), columns), BF16)
    for k, c, start, piece in pieces:
        order = ids[1] ^ jnp.arange(start, start + piece.shape[0])
        whole = whole.at[ids[0] ^ k, order, ids[2] ^ c].set(piece)
    return None, [whole.reshape(MODEL_WIDTH, columns)]


def scatter_rows(terms, ids, sizes, before=()):
    ndp, nz = sizes["dp"], sizes["z"]
    if len(terms) == 1:
        blocks = terms[0].reshape(ndp, nz, 2, block_rows(sizes), -1)
        blocks = jnp.take(jnp.take(blocks, ids[0] ^ jnp.arange(ndp), 0), ids[1] ^ jnp.arange(nz), 1)
        terms = [lax.dynamic_index_in_dim(blocks, ids[2] ^ c, 2, keepdims=False) for c in range(2)]
    mine, other = terms
    got = exchange(other, "core", 2, 1)
    if before:
        (got,) = after([got], before)
    half = nz // 2
    slots = [
        tuple(mine[k, at].astype(F32) + got[k, at].astype(F32) for at in (slice(half), slice(half, nz)))
        for k in range(ndp)
    ]
    total = slots[0]
    for pair in scatter_dp(slots, ndp):
        total = tuple(t + p.astype(F32) for t, p in zip(total, pair))
    total = [total[z // half][z % half] for z in range(nz)]
    got = [exchange(total[z].astype(BF16), "z", nz, z) for z in range(1, nz)]
    return total[0] + sum(part.astype(F32) for part in got), got


def load_rows(ids, ndp, nz, places, parts, dest, sem):
    if places is None:
        loads = [pltpu.make_async_copy(parts[0], dest, sem.at[0])]
        loads[0].start()
        return loads
    rows = MODEL_WIDTH // (ndp * nz * 2)
    loads = []
    for (k, c, start, count), part in zip(places, parts):
        for z in range(count):
            block = ((ids[0] ^ k) * nz + (ids[1] ^ (start + z))) * 2 + (ids[2] ^ c)
            place = pl.ds(pl.multiple_of(block * rows, rows), rows)
            copy = pltpu.make_async_copy(part.at[z], dest.at[place, :], sem.at[len(loads)])
            loads.append(copy)
    for load in loads:
        load.start()
    return loads


def store_rows(ids, ndp, nz, source, dests, sem):
    if len(dests) == 1:
        store = pltpu.make_async_copy(source, dests[0], sem.at[0])
        store.start()
        store.wait()
        return
    rows = MODEL_WIDTH // (ndp * nz * 2)
    stores = []
    for k in range(ndp):
        for z in range(nz):
            for c, dest in enumerate(dests):
                block = ((ids[0] ^ k) * nz + (ids[1] ^ z)) * 2 + (ids[2] ^ c)
                place = pl.ds(pl.multiple_of(block * rows, rows), rows)
                n = (k * 2 + c) * nz + z
                stores.append(
                    pltpu.make_async_copy(source.at[place, :], dest.at[k, z], sem.at[n])
                )
    for store in stores:
        store.start()
    for store in stores:
        store.wait()


def split_shapes(columns, sizes):
    if by_blocks(sizes):
        return (shape((sizes["dp"], sizes["z"], block_rows(sizes), columns), BF16),) * 2
    return (shape((MODEL_WIDTH, columns), BF16),)


def rms_scale(rows):
    return lax.rsqrt(jnp.mean(rows * rows, axis=-1, keepdims=True) + EPS)


def norm_back(normed, row_scale, grad):
    return row_scale * (grad - normed * jnp.mean(grad * normed, axis=-1, keepdims=True))


def swapped(vals):
    return pltpu.roll(vals, HEAD_SIZE // 2, 1)


def head(h):
    return slice(h * HEAD_SIZE, (h + 1) * HEAD_SIZE)


def seen(rows, length):
    q = lax.broadcasted_iota(jnp.int32, (rows, rows), 0)
    s = lax.broadcasted_iota(jnp.int32, (rows, rows), 1)
    return (s <= q) & (s < length)


def attention_probs(query, key, visible):
    scores = jnp.where(visible, nt(query, key) * SCALE, NEG_FILL)
    expon = jnp.exp(scores - jnp.max(scores, axis=-1, keepdims=True))
    return expon / jnp.sum(expon, axis=-1, keepdims=True)


def route_softmax(router_rows, hidden):
    logits = nt(router_rows, hidden)[:EXPERTS]
    expon = jnp.exp(logits - jnp.max(logits, axis=0, keepdims=True))
    return expon / jnp.sum(expon, axis=0, keepdims=True)


def attend_kernel(ndp, nz, places, ids, tokens, cosine, sine, *refs):
    *parts, qkv, mixed, h_one, gains, router, w, sem = refs
    rows = tokens.shape[0]
    loads = load_rows(ids, ndp, nz, places, parts, w, sem)
    tok = tokens[...].astype(F32)
    normed = tok * rms_scale(tok)
    for load in loads:
        load.wait()
    extra = jnp.transpose(w[:, QKV:].astype(F32))
    gains[...] = extra[:8]
    router[...] = extra[2 : 2 + ROUTER].astype(BF16)
    h_one[...] = (normed * extra[0:1]).astype(BF16)
    cos, sin = cosine[...], sine[...]
    for t in range(QKV // TILE):
        pre = nn(h_one[...], w[:, t * TILE : (t + 1) * TILE])
        for i in range(TILE // HEAD_SIZE):
            part = pre[:, head(i)]
            at = t * TILE + i * HEAD_SIZE
            if at < QW + KW:
                part = part * cos + swapped(part) * sin
            qkv[:, at : at + HEAD_SIZE] = part.astype(BF16)
    visible = seen(rows, ids[3])
    for h in range(QUERY_HEADS):
        g = h // GROUP
        probs = attention_probs(qkv[:, head(h)], qkv[:, head(QUERY_HEADS + g)], visible)
        values = qkv[:, head(QUERY_HEADS + KEY_VALUE_HEADS + g)]
        mixed[:, head(h)] = nn(probs.astype(BF16), values).astype(BF16)


def attend(ids, tokens, cosine, sine, weights, sizes):
    places, parts = weights
    ndp, nz = sizes["dp"], sizes["z"]
    rows = tokens.shape[0]
    return pl.pallas_call(
        functools.partial(attend_kernel, ndp, nz, places),
        out_shape=(
            shape((rows, QKV), BF16),
            shape((rows, QW), BF16),
            shape((rows, MODEL_WIDTH), BF16),
            shape((8, MODEL_WIDTH), F32),
            shape((ROUTER, MODEL_WIDTH), BF16),
        ),
        in_specs=[SMEM, VMEM, VMEM, VMEM] + [HBM] * len(parts),
        out_specs=(VMEM,) * 5,
        scratch_shapes=[
            pltpu.VMEM((MODEL_WIDTH, FIRST), BF16),
            pltpu.SemaphoreType.DMA((2 * ndp * nz,)),
        ],
        compiler_params=params(28),
        cost_estimate=cost(2 * rows * MODEL_WIDTH * QKV, 10 * MIB, 12 * rows * rows),
        name="attend",
    )(ids, tokens, cosine, sine, *parts)


def project_kernel(ndp, nz, places, ids, tokens, mixed, gains, *refs):
    *parts, residual, top, low, w, sem = refs
    loads = load_rows(ids, ndp, nz, places, parts, w, sem)
    for load in loads:
        load.wait()
    for t in range(MODEL_WIDTH // TILE):
        lane = slice(t * TILE, (t + 1) * TILE)
        residual[:, lane] = tokens[:, lane].astype(F32) + nn(mixed[...], w[:, lane])
    whole = residual[...]
    h_two = (whole * rms_scale(whole) * gains[1:2]).astype(BF16)
    half = top.shape[0]
    top[...], low[...] = h_two[:half], h_two[half:]


def project(ids, tokens, mixed, gains, weights, sizes):
    places, parts = weights
    ndp, nz = sizes["dp"], sizes["z"]
    rows = tokens.shape[0]
    return pl.pallas_call(
        functools.partial(project_kernel, ndp, nz, places),
        out_shape=(shape((rows, MODEL_WIDTH), F32),)
        + (shape((rows // 2, MODEL_WIDTH), BF16),) * 2,
        in_specs=[SMEM, VMEM, VMEM, VMEM] + [HBM] * len(parts),
        out_specs=(VMEM,) * 3,
        scratch_shapes=[
            pltpu.VMEM((QW, MODEL_WIDTH), BF16),
            pltpu.SemaphoreType.DMA((2 * ndp * nz,)),
        ],
        compiler_params=params(28),
        cost_estimate=cost(2 * rows * MODEL_WIDTH * QW, 8 * MIB),
        name="project",
    )(ids, tokens, mixed, gains, *parts)


def expert_kernel(ndp, rows, width, index, last, near, far, *refs):
    it = iter(refs)
    take = lambda n: [next(it) for _ in range(n)]
    (expert_ref, router_ref) = take(2)
    prev_gates = take(index)
    hid_in, cot_in = take(len(near)), take(len(far))
    (w_in,) = take(1)
    prev_in = take(2) if index else []
    out_hbm, back_hbm = (take(2 * ndp), take(2 * ndp)) if last else (take(1), take(1))
    gates_ref, terms_hbm = take(2)
    hid, cot, w, x, d, ge, inner, dg, du, pick, pick_t, slot_gate, slot_dot = take(13)
    (terms_buf,) = take(1)
    prev = take(2) if index else []
    in_sem, out_sem = take(2)
    depth = MODEL_WIDTH
    tiles = depth // TILE

    loads = {}

    def load(name, source, dest):
        copy = pltpu.make_async_copy(source, dest, in_sem.at[len(loads)])
        copy.start()
        loads[name] = copy

    for i, (k, start, count) in enumerate(near):
        load(("hid", i), hid_in[i], hid.at[k, pl.ds(start, count), :])
    for i, (k, start, count) in enumerate(far):
        load(("cot", i), cot_in[i], cot.at[k, pl.ds(start, count), :])
    load("w", w_in, w)
    for i in range(len(prev)):
        load(("prev", i), prev_in[i], prev[i])

    expert = expert_ref[0]
    which = lax.broadcasted_iota(jnp.int32, (EXPERTS, rows), 0) == expert
    earlier = (
        (
            lax.broadcasted_iota(jnp.int32, (rows, rows), 0)
            < lax.broadcasted_iota(jnp.int32, (rows, rows), 1)
        )
        .astype(F32)
        .astype(BF16)
    )
    slot = lax.broadcasted_iota(jnp.int32, (CAP, rows), 0).astype(F32)
    for s in range(ndp):
        for i, piece in enumerate(near):
            if piece[0] == s:
                loads["hid", i].wait()
        for i, piece in enumerate(far):
            if piece[0] == s:
                loads["cot", i].wait()
        hidden = hid[s]
        probs = route_softmax(router_ref[...], hidden)
        named = cot[s, rows : rows + NOTE, :rows]
        place = nn(named, earlier)[:EXPERTS]
        named = named[:EXPERTS].astype(F32)
        named_row = jnp.sum(jnp.where(which, named, 0.0), axis=0, keepdims=True)
        gate_row = jnp.sum(jnp.where(which, probs, 0.0), axis=0, keepdims=True)
        place_row = jnp.sum(jnp.where(which, place, 0.0), axis=0, keepdims=True)
        chosen = jnp.where((slot == place_row) & (named_row > 0.5), 1.0, 0.0)
        pick[s] = chosen.astype(BF16)
        pick_t[s] = jnp.transpose(chosen).astype(BF16)
        at = pl.ds(s * CAP, CAP)
        gate = jnp.sum(chosen * gate_row, axis=1, keepdims=True)
        slot_gate[at, :] = jnp.broadcast_to(gate, (CAP, 128))
        x[at, :] = nn(pick[s], hidden).astype(BF16)
        grads = nn(pick[s], cot[s, :rows])
        d[at, :] = grads.astype(BF16)
        ge[at, :] = (gate * grads).astype(BF16)
    loads["w"].wait()

    def hidden_units(t, carry):
        at = pl.multiple_of(t * TILE, TILE)
        gate_pre = nn(x[...], w[:, pl.ds(at, TILE)])
        up_pre = nn(x[...], w[:, pl.ds(width + at, TILE)])
        grad_inner = nn(ge[...], w[:, pl.ds(2 * width + at, TILE)])
        sig = 1.0 / (1.0 + jnp.exp(-gate_pre))
        act = gate_pre * sig
        inner[:, pl.ds(at, TILE)] = (act * up_pre).astype(BF16)
        dg[:, pl.ds(at, TILE)] = (
            grad_inner * up_pre * sig * (1.0 + gate_pre * (1.0 - sig))
        ).astype(BF16)
        du[:, pl.ds(at, TILE)] = (grad_inner * act).astype(BF16)
        return carry

    lax.fori_loop(0, width // TILE, hidden_units, 0)
    slot_dot[...] = jnp.zeros_like(slot_dot)
    for i in range(len(prev)):
        loads["prev", i].wait()

    half, noted = rows // 2, (rows + NOTE) // 2

    def stores(t):
        lane = pl.ds(pl.multiple_of(t * TILE, TILE), TILE)
        copies = [(terms_buf.at[lane, :], terms_hbm.at[lane, :])]
        if not last:
            body = pl.ds(0, rows)
            copies.append((hid.at[:, :, lane], out_hbm[0].at[:, :, lane]))
            copies.append((cot.at[:, body, lane], back_hbm[0].at[:, body, lane]))
        else:
            for i in range(2 * ndp):
                first = pl.ds(i % 2 * half, half)
                copies.append((hid.at[i // 2, first, lane], out_hbm[i].at[:, lane]))
                body = pl.ds(0, noted if i % 2 == 0 else rows - noted)
                taken = pl.ds(i % 2 * noted, noted if i % 2 == 0 else rows - noted)
                copies.append((cot.at[i // 2, taken, lane], back_hbm[i].at[body, lane]))
        return [
            pltpu.make_async_copy(source, dest, out_sem.at[i, t])
            for i, (source, dest) in enumerate(copies)
        ]

    def features(t, carry):
        lane = pl.ds(pl.multiple_of(t * TILE, TILE), TILE)
        result = nt(inner[...], w[lane, pl.ds(2 * width, width)]).astype(BF16).astype(F32)
        partial = jnp.sum(result * d[:, lane].astype(F32), axis=1, keepdims=True)
        slot_dot[...] += jnp.broadcast_to(partial, slot_dot.shape)
        gated = (slot_gate[:, :1] * result).astype(BF16)
        grad_in = (
            nt(dg[...], w[lane, pl.ds(0, width)]) + nt(du[...], w[lane, pl.ds(width, width)])
        ).astype(BF16)
        for s in range(ndp):
            part = slice(s * CAP, (s + 1) * CAP)
            sent = nn(pick_t[s], gated[part])
            back = nn(pick_t[s], grad_in[part])
            if prev:
                sent = sent + prev[0][s, :, lane].astype(F32)
                back = back + prev[1][s, :rows, lane].astype(F32)
            hid[s, :, lane] = sent.astype(BF16)
            cot[s, :rows, lane] = back.astype(BF16)
        x_t = jnp.transpose(x[:, lane])
        terms_buf[lane, pl.ds(0, width)] = nn(x_t, dg[...]).astype(BF16)
        terms_buf[lane, pl.ds(width, width)] = nn(x_t, du[...]).astype(BF16)
        ge_t = jnp.transpose(ge[:, lane])
        terms_buf[lane, pl.ds(2 * width, width)] = nn(ge_t, inner[...]).astype(BF16)
        for store in stores(t):
            store.start()
        return carry

    lax.fori_loop(0, tiles, features, 0)
    line = lax.broadcasted_iota(jnp.int32, (NOTE, 3 * rows), 0)
    notes = []
    for s in range(ndp):
        part = slice(s * CAP, (s + 1) * CAP)
        own = jnp.sum(pick[s].astype(F32) * slot_dot[part, :1], axis=0, keepdims=True)
        gates_ref[s] = own
        if not last:
            continue
        note = jnp.zeros((NOTE, 3 * rows), F32)
        for j, row in enumerate([p[s] for p in prev_gates] + [own]):
            high = row.astype(BF16).astype(F32)
            middle = (row - high).astype(BF16).astype(F32)
            low = row - high - middle
            at = expert - index + j
            note = jnp.where(line == at, jnp.concatenate([high, middle, low], axis=1), note)
        cot[s, rows : rows + NOTE, : 3 * rows] = note.astype(BF16)
        notes.append(
            pltpu.make_async_copy(
                cot.at[s, pl.ds(rows, NOTE), :],
                back_hbm[2 * s + 1].at[pl.ds(rows - noted, NOTE), :],
                out_sem.at[4 * ndp + 1, s],
            )
        )
        notes[-1].start()
    for t in range(tiles):
        for store in stores(t):
            store.wait()
    for note in notes:
        note.wait()


def run_expert(index, last, expert, router, hidden, grads, w_all, prev, prev_gates, ndp):
    rows = 2 * hidden[0][2].shape[0]
    near, far = (tuple((k, at, p.shape[0]) for k, at, p in group) for group in (hidden, grads))
    width = w_all.shape[1] // 3
    slots = ndp * CAP
    depth = MODEL_WIDTH
    tiles = depth // TILE
    scratch = [
        pltpu.VMEM((ndp, rows, depth), BF16),
        pltpu.VMEM((ndp, rows + NOTE, depth), BF16),
        pltpu.VMEM((depth, 3 * width), BF16),
        pltpu.VMEM((slots, depth), BF16),
        pltpu.VMEM((slots, depth), BF16),
        pltpu.VMEM((slots, depth), BF16),
        pltpu.VMEM((slots, width), BF16),
        pltpu.VMEM((slots, width), BF16),
        pltpu.VMEM((slots, width), BF16),
        pltpu.VMEM((ndp, CAP, rows), BF16),
        pltpu.VMEM((ndp, rows, CAP), BF16),
        pltpu.VMEM((slots, 128), F32),
        pltpu.VMEM((slots, 128), F32),
        pltpu.VMEM((depth, 3 * width), BF16),
    ]
    if index:
        scratch += [
            pltpu.VMEM((ndp, rows, depth), BF16),
            pltpu.VMEM((ndp, rows + NOTE, depth), BF16),
        ]
    scratch += [
        pltpu.SemaphoreType.DMA((len(near) + len(far) + 3,)),
        pltpu.SemaphoreType.DMA((4 * ndp + 2, max(tiles, ndp))),
    ]
    sent = [shape((ndp, rows, depth), BF16), shape((ndp, rows + NOTE, depth), BF16)]
    if last:
        sent = [shape((rows // 2, depth), BF16)] * (2 * ndp)
        sent += [shape(((rows + NOTE) // 2, depth), BF16)] * (2 * ndp)
    flops = 2 * slots * depth * width * 9 + 8 * ndp * CAP * rows * depth
    return pl.pallas_call(
        functools.partial(expert_kernel, ndp, rows, width, index, last, near, far),
        out_shape=(
            *sent,
            shape((ndp, 1, rows), F32),
            shape((depth, 3 * width), BF16),
        ),
        in_specs=[SMEM, VMEM]
        + [VMEM] * len(prev_gates)
        + [HBM] * (len(near) + len(far) + 1 + len(prev)),
        out_specs=(HBM,) * len(sent) + (VMEM, HBM),
        scratch_shapes=scratch,
        compiler_params=params(60),
        cost_estimate=cost(flops, 40 * MIB, slots * width),
        name="expert",
    )(
        expert,
        router,
        *prev_gates,
        *(piece for *_, piece in hidden),
        *(piece for *_, piece in grads),
        w_all,
        *prev,
    )


def project_back_kernel(
    ndp, nz, local, places, count, pairs, ids, residual, top, low, mixed, grads, gains, router, *refs
):
    backs, refs = refs[: 2 * pairs], refs[2 * pairs :]
    parts, refs = refs[:count], refs[count:]
    grad_resid, grad_mixed, notes, *dests, w, terms, sem, out_sem = refs
    rows = residual.shape[0]
    loads = load_rows(ids, ndp, nz, places, parts, w, sem)
    upper, lower = backs[0][...].astype(F32), backs[1][...].astype(F32)
    for i in range(1, pairs):
        upper = upper + backs[2 * i][...].astype(F32)
        lower = lower + backs[2 * i + 1][...].astype(F32)
    body = rows - upper.shape[0]
    grad_h = jnp.concatenate([upper, lower[:body]], axis=0)
    note = lower[body : body + EXPERTS, : 3 * rows]
    grad_route = note[:, :rows] + note[:, rows : 2 * rows] + note[:, 2 * rows :]
    hidden = jnp.concatenate([top[...], low[...]], axis=0)
    probs = route_softmax(router[...], hidden)
    grad_logits = probs * (grad_route - jnp.sum(probs * grad_route, axis=0, keepdims=True))
    grad_logits = jnp.concatenate([grad_logits, jnp.zeros_like(grad_logits)], axis=0)
    grad_logits = grad_logits.astype(BF16)
    grad_h = grad_h + tn(grad_logits, router[...])
    res = residual[...]
    scale = rms_scale(res)
    normed = res * scale
    notes[0:8] = jnp.broadcast_to(
        jnp.sum(normed * grad_h, axis=0, keepdims=True), (8, MODEL_WIDTH)
    )
    notes[8:16] = nn(grad_logits, hidden)[:EXPERTS]
    live = lax.broadcasted_iota(jnp.int32, (rows, 1), 0) < ids[3]
    final = jnp.where(live, grads[...].astype(F32), 0.0)
    total = final + norm_back(normed, scale, grad_h * gains[1:2])
    grad_resid[...] = total
    grad_attn = total.astype(BF16)
    mixed_t = jnp.transpose(mixed[...])
    for t in range(MODEL_WIDTH // TILE):
        lane = slice(t * TILE, (t + 1) * TILE)
        terms[:, lane] = nn(mixed_t, grad_attn[:, lane]).astype(BF16)
    for load in loads:
        load.wait()
    for t in range(QW // TILE):
        lane = slice(t * TILE, (t + 1) * TILE)
        grad_mixed[:, lane] = nt(grad_attn, w[lane, :]).astype(BF16)
    store_rows(ids, ndp, nz, terms, dests, out_sem)


def project_back(ids, residual, h_two, mixed, grads, gains, router, weights, backs, sizes, local):
    places, parts = weights
    ndp, nz = sizes["dp"], sizes["z"]
    rows = residual.shape[0]
    split = split_shapes(MODEL_WIDTH, sizes)
    return pl.pallas_call(
        functools.partial(
            project_back_kernel, ndp, nz, local, places, len(parts), len(backs) // 2
        ),
        out_shape=(
            shape((rows, MODEL_WIDTH), F32),
            shape((rows, QW), BF16),
            shape((16, MODEL_WIDTH), F32),
            *split,
        ),
        in_specs=[SMEM] + [VMEM] * (7 + len(backs)) + [HBM] * len(parts),
        out_specs=(VMEM, VMEM, VMEM) + (HBM,) * len(split),
        scratch_shapes=[
            pltpu.VMEM((QW, MODEL_WIDTH), BF16),
            pltpu.VMEM((QW, MODEL_WIDTH), BF16),
            pltpu.SemaphoreType.DMA((2 * ndp * nz,)),
            pltpu.SemaphoreType.DMA((2 * ndp * nz,)),
        ],
        compiler_params=params(50),
        cost_estimate=cost(4 * rows * MODEL_WIDTH * QW, 20 * MIB),
        name="project_back",
    )(ids, residual, *h_two, mixed, grads, gains, router, *backs, *parts)


def attend_back_kernel(
    ndp, nz, places, count, unread, ids, tokens, cosine, sine, qkv, h_one, grad_mixed, grad_resid, gains, notes, *refs
):
    parts, refs = refs[:count], refs[count:]
    grad_tokens, *dests, w, terms, grad_pre, sem, out_sem = refs[unread:]
    rows = tokens.shape[0]
    loads = load_rows(ids, ndp, nz, places, parts, w, sem)
    visible = seen(rows, ids[3])
    cos, sin = cosine[...], sine[...]
    for g in range(KEY_VALUE_HEADS):
        key = qkv[:, head(QUERY_HEADS + g)]
        value = qkv[:, head(QUERY_HEADS + KEY_VALUE_HEADS + g)]
        grad_key = jnp.zeros((rows, HEAD_SIZE), F32)
        grad_value = jnp.zeros((rows, HEAD_SIZE), F32)
        for h in range(g * GROUP, (g + 1) * GROUP):
            query, grad = qkv[:, head(h)], grad_mixed[:, head(h)]
            probs = attention_probs(query, key, visible)
            grad_probs = nt(grad, value)
            grad_value = grad_value + tn(probs.astype(BF16), grad)
            row_dot = jnp.sum(probs * grad_probs, axis=-1, keepdims=True)
            grad_scores = (probs * (grad_probs - row_dot)).astype(BF16)
            grad_query = nn(grad_scores, key) * SCALE
            grad_key = grad_key + tn(grad_scores, query)
            grad_pre[:, head(h)] = (grad_query * cos - swapped(grad_query) * sin).astype(BF16)
        grad_key = grad_key * SCALE
        grad_pre[:, head(QUERY_HEADS + g)] = (
            grad_key * cos - swapped(grad_key) * sin
        ).astype(BF16)
        grad_pre[:, head(QUERY_HEADS + KEY_VALUE_HEADS + g)] = grad_value.astype(BF16)
    h_one_t = jnp.transpose(h_one[...])
    for t in range(QKV // TILE):
        lane = slice(t * TILE, (t + 1) * TILE)
        terms[:, lane] = nn(h_one_t, grad_pre[:, lane]).astype(BF16)
    for load in loads:
        load.wait()
    tok = tokens[...].astype(F32)
    scale = rms_scale(tok)
    normed = tok * scale
    for t in range(MODEL_WIDTH // TILE):
        lane = slice(t * TILE, (t + 1) * TILE)
        grad_tokens[:, lane] = nt(grad_pre[...], w[lane, :QKV])
    grad_h = grad_tokens[...]
    grad_gain = jnp.sum(normed * grad_h, axis=0, keepdims=True)
    grad_tokens[...] = grad_resid[...] + norm_back(normed, scale, grad_h * gains[0:1])
    line = lax.broadcasted_iota(jnp.int32, (8, MODEL_WIDTH), 0)
    top = jnp.where(line == 0, grad_gain, jnp.where(line == 1, notes[0:8], 0.0))
    block = jnp.concatenate(
        [top, notes[8:16], jnp.zeros((PAD - 16, MODEL_WIDTH), F32)], axis=0
    )
    terms[:, QKV:] = jnp.transpose(block).astype(BF16)
    store_rows(ids, ndp, nz, terms, dests, out_sem)


def attend_back(
    ids, tokens, cosine, sine, qkv, h_one, grad_mixed, grad_resid, gains, notes, weights, before, sizes
):
    places, parts = weights
    ndp, nz = sizes["dp"], sizes["z"]
    rows = tokens.shape[0]
    split = split_shapes(FIRST, sizes)
    return pl.pallas_call(
        functools.partial(attend_back_kernel, ndp, nz, places, len(parts), len(before)),
        out_shape=(shape((rows, MODEL_WIDTH), F32), *split),
        in_specs=[SMEM] + [VMEM] * 9 + [HBM] * (len(parts) + len(before)),
        out_specs=(VMEM,) + (HBM,) * len(split),
        scratch_shapes=[
            pltpu.VMEM((MODEL_WIDTH, FIRST), BF16),
            pltpu.VMEM((MODEL_WIDTH, FIRST), BF16),
            pltpu.VMEM((rows, QKV), BF16),
            pltpu.SemaphoreType.DMA((2 * ndp * nz,)),
            pltpu.SemaphoreType.DMA((2 * ndp * nz,)),
        ],
        compiler_params=params(50),
        cost_estimate=cost(5 * rows * MODEL_WIDTH * QKV, 24 * MIB, 12 * rows * rows),
        name="attend_back",
    )(ids, tokens, cosine, sine, qkv, h_one, grad_mixed, grad_resid, gains, notes, *parts, *before)


def rope_tables(rows):
    half = HEAD_SIZE // 2
    position = jnp.arange(rows).astype(F32)
    inverse = ROPE_BASE ** (-jnp.arange(half).astype(F32) / half)
    angles = position[:, None] * inverse[None, :]
    cosine, sine = jnp.cos(angles), jnp.sin(angles)
    return jnp.concatenate([cosine, cosine], axis=1), jnp.concatenate([-sine, sine], axis=1)


def per_device(
    sizes,
    tokens,
    lengths,
    routes,
    cotangent,
    gain_one,
    w_query,
    key_matrix,
    value_matrix,
    w_out,
    gain_two,
    w_router,
    w_gate,
    w_up,
    w_down,
):
    ndp = sizes["dp"]
    rows = tokens.shape[0]
    local, _, width = w_gate.shape
    me_dp = lax.axis_index("dp")
    length = lengths[0]
    ids = jnp.stack([me_dp, lax.axis_index("z"), lax.axis_index("core"), length]).astype(jnp.int32)
    live = (jnp.arange(rows) < length)[:, None]
    expert_ids = jnp.arange(EXPERTS, dtype=jnp.int32)

    extra = jnp.concatenate([gain_one[:, None], gain_two[:, None], w_router], axis=1)
    extra = jnp.pad(extra, ((0, 0), (0, PAD - extra.shape[1])))
    first = jnp.concatenate([w_query, key_matrix, value_matrix, extra], axis=1)
    named = jnp.any(routes[None, :, :] == expert_ids[:, None, None], axis=2).astype(BF16)
    named = jnp.pad(named, ((0, NOTE - EXPERTS), (0, MODEL_WIDTH - rows)))
    grad_low = jnp.where(live, cotangent, jnp.zeros_like(cotangent))
    grad_low = jnp.concatenate([grad_low, named], axis=0)
    grad_near = start_dp(grad_low, ndp)

    nz = sizes["z"]
    first_z = [first] + [exchange(first, "z", nz, k) for k in range(1, nz)]
    first_block = stack_after(first_z, grad_near)
    first_dp = pass_on(first_block, start_dp(first_block, ndp), ndp)
    packed = [
        pack_after(j, (w_gate, w_up, w_down), first_z[1:] + grad_near) for j in range(local)
    ]
    expert_mats = [lax.all_gather(p, ("z", "core"), axis=0, tiled=True) for p in packed]

    second_z = [w_out] + [exchange(w_out, "z", nz, k) for k in range(1, nz)]
    second_block = stack_after(second_z, [piece for *_, piece in first_dp[1:]])
    second_near = start_dp(second_block, ndp)

    cosine, sine = rope_tables(rows)
    weights_in = gather_rows(first, first_dp, ids, sizes)
    qkv, mixed, h_one, gains, router = attend(ids, tokens, cosine, sine, weights_in, sizes)
    second_dp = pass_on(second_block, second_near, ndp, [mixed])
    weights_out = gather_rows(w_out, second_dp, ids, sizes)
    grad_far = pass_on(grad_low, grad_near, ndp, [piece for *_, piece in second_dp[3:]])
    residual, *h_two = project(ids, tokens, mixed, gains, weights_out, sizes)
    hidden = gather_halves(h_two, ndp)

    prev, gate_grads, sums = (), [], []
    for j in range(local):
        expert = (me_dp * local + j).astype(jnp.int32).reshape(1)
        *prev, grad_gate, terms = run_expert(
            j,
            j == local - 1,
            expert,
            router,
            hidden,
            grad_far,
            expert_mats[j],
            prev,
            gate_grads,
            ndp,
        )
        gate_grads.append(grad_gate)
        sums.append(lax.psum_scatter(terms, ("z", "core"), scatter_dimension=0, tiled=True))
    outs, backs = prev[: 2 * ndp], prev[2 * ndp :]
    pairs = lambda flat: [tuple(flat[2 * k : 2 * k + 2]) for k in range(len(flat) // 2)]
    got = scatter_dp(pairs(backs), ndp)
    backs = list(backs[:2]) + [part for pair in got for part in pair]
    outs = list(outs[:2]) + list(after(outs[2:], backs[2:]))
    grad_resid, grad_mixed, notes, *terms = project_back(
        ids, residual, h_two, mixed, cotangent, gains, router, weights_out, backs, sizes, local
    )
    grad_tokens, *terms_in = attend_back(
        ids, tokens, cosine, sine, qkv, h_one, grad_mixed, grad_resid, gains, notes, weights_in, sums[:-1], sizes
    )
    out_pairs = scatter_dp(pairs(outs), ndp, terms_in[:1])
    grad_out, late = scatter_rows(terms, ids, sizes, terms_in[:1])
    grad_first, _ = scatter_rows(terms_in, ids, sizes)
    block = tuple(part.astype(F32) for part in outs[:2])
    for pair in out_pairs:
        block = tuple(total + part.astype(F32) for total, part in zip(block, pair))
    block_out = (residual + jnp.concatenate(block, axis=0)).astype(BF16)

    expert_sums = finish_after(sums, late)
    return (
        block_out,
        grad_tokens,
        grad_first[:, QKV],
        grad_first[:, :QW],
        grad_first[:, QW : QW + KW],
        grad_first[:, QW + KW : QKV],
        grad_out,
        grad_first[:, QKV + 1],
        grad_first[:, QKV + 8 : QKV + 8 + EXPERTS],
        *expert_sums,
    )


def solution(mesh):
    ndp, nf = mesh.shape["dp"], mesh.shape["fsdp"]
    sizes = {"dp": ndp, "z": nf // 2, "core": 2}
    split = Mesh(mesh.devices.reshape(ndp, nf // 2, 2), ("dp", "z", "core"))
    every = ("dp", "z", "core")
    rows = P(every, None)
    vector = P(every)
    expert = P("dp", ("z", "core"), None)

    def run(*args):
        return per_device(sizes, *args)

    return jax.shard_map(
        run,
        mesh=split,
        in_specs=(rows, vector, rows, rows, vector, rows, rows, rows, rows, vector, rows)
        + (expert,) * 3,
        out_specs=(rows, rows, vector, rows, rows, rows, rows, vector, rows) + (expert,) * 3,
        check_vma=False,
    )
```

```python
import functools

import jax
import jax.numpy as jnp
from jax import lax
from jax.experimental import pallas as pl
from jax.experimental.pallas import tpu as pltpu
from jax.sharding import Mesh
from jax.sharding import PartitionSpec as P

MODEL_WIDTH = 1536
QUERY_HEADS = 12
KEY_VALUE_HEADS = 2
HEAD_SIZE = 128
EXPERTS = 8
CAP = 160
GROUP = QUERY_HEADS // KEY_VALUE_HEADS
QW = QUERY_HEADS * HEAD_SIZE
KW = KEY_VALUE_HEADS * HEAD_SIZE
QKV = QW + 2 * KW
PAD = 128
FIRST = QKV + PAD
NOTE = 32
ROUTER = 16
EPS = 1e-06
ROPE_BASE = 1500000.0
NEG_FILL = -1e30
SCALE = HEAD_SIZE ** (-0.5)
F32 = jnp.float32
BF16 = jnp.bfloat16
TILE = 256
MIB = 1024 * 1024
HBM = pl.BlockSpec(memory_space=pltpu.HBM)
VMEM = pl.BlockSpec(memory_space=pltpu.VMEM)
SMEM = pl.BlockSpec(memory_space=pltpu.SMEM)


def nn(a, b):
    return lax.dot_general(a, b, (((1,), (0,)), ((), ())), preferred_element_type=F32)


def nt(a, b):
    return lax.dot_general(a, b, (((1,), (1,)), ((), ())), preferred_element_type=F32)


def tn(a, b):
    return lax.dot_general(a, b, (((0,), (0,)), ((), ())), preferred_element_type=F32)


def shape(dims, dtype):
    return jax.ShapeDtypeStruct(dims, dtype)


def params(mib):
    return pltpu.CompilerParams(vmem_limit_bytes=mib * MIB)


def cost(flops, data, special=0):
    return pl.CostEstimate(flops=flops, bytes_accessed=data, transcendentals=special)


def exchange(block, axis, size, step):
    return lax.ppermute(block, axis, [(i, i ^ step) for i in range(size)])


def start_dp(block, ndp):
    return [exchange(block, "dp", ndp, k) for k in ((1, 2) if ndp == 4 else range(1, ndp))]


def pass_on(block, near, ndp, before=()):
    if ndp != 4:
        return [(k, 0, piece) for k, piece in enumerate([block] + near)]
    side, up = after(near, before) if before else near
    half = block.shape[0] // 2
    return [
        (0, 0, block),
        (1, 0, side),
        (2, 0, up),
        (3, 0, exchange(side[:half], "dp", ndp, 2)),
        (3, half, exchange(up[half:], "dp", ndp, 1)),
    ]


def gather_direct(block, ndp):
    return [(k, 0, exchange(block, "dp", ndp, k) if k else block) for k in range(ndp)]


def gather_halves(halves, ndp):
    top, low = halves
    at = top.shape[0]
    if ndp != 4:
        return [
            (k, i * at, exchange(half, "dp", ndp, k) if k else half)
            for k in range(ndp)
            for i, half in enumerate(halves)
        ]
    side_top, up_low = exchange(top, "dp", ndp, 1), exchange(low, "dp", ndp, 2)
    side_low, up_top = exchange(low, "dp", ndp, 1), exchange(top, "dp", ndp, 2)
    return [
        (0, 0, top),
        (0, at, low),
        (1, 0, side_top),
        (2, at, up_low),
        (1, at, side_low),
        (2, 0, up_top),
        (3, 0, exchange(side_top, "dp", ndp, 2)),
        (3, at, exchange(up_low, "dp", ndp, 1)),
    ]


def scatter_dp(slots, ndp):
    low = lambda part: part.astype(BF16)
    if ndp != 4:
        return [tuple(exchange(low(h), "dp", ndp, k) for h in slots[k]) for k in range(1, ndp)]
    add = lambda a, b: (a.astype(F32) + b.astype(F32)).astype(BF16)
    past_side = exchange(low(slots[3][0]), "dp", ndp, 1)
    past_up = exchange(low(slots[3][1]), "dp", ndp, 2)
    side = exchange(low(slots[1][0]), "dp", ndp, 1)
    up = exchange(low(slots[2][1]), "dp", ndp, 2)
    return [
        (side, exchange(add(slots[1][1], past_up), "dp", ndp, 1)),
        (exchange(add(slots[2][0], past_side), "dp", ndp, 2), up),
    ]


def both_cores(pieces):
    return [
        (k, c, start, exchange(piece, "core", 2, 1) if c else piece)
        for k, start, piece in pieces
        for c in range(2)
    ]


def stack_kernel(count, *refs):
    for i in range(count):
        refs[-1][i] = refs[i][...]


def stack_after(parts, before):
    dims = (len(parts),) + parts[0].shape
    return pl.pallas_call(
        functools.partial(stack_kernel, len(parts)),
        out_shape=shape(dims, parts[0].dtype),
        in_specs=[VMEM] * len(parts) + [HBM] * len(before),
        out_specs=VMEM,
        compiler_params=params(60),
        cost_estimate=cost(0, 4 * dims[0] * dims[1] * dims[2]),
        name="stack",
    )(*parts, *before)


def pack_kernel(index, *refs):
    width = refs[0].shape[2]
    for i in range(3):
        refs[-1][:, i * width : (i + 1) * width] = refs[i][index]


def pack(index, mats):
    _, rows, width = mats[0].shape
    return pl.pallas_call(
        functools.partial(pack_kernel, index),
        out_shape=shape((rows, 3 * width), BF16),
        in_specs=[VMEM] * 3,
        out_specs=VMEM,
        compiler_params=params(60),
        name="pack",
    )(*mats)


def finish_kernel(count, *refs):
    outs = refs[-3:]
    width = outs[0].shape[2]
    for j in range(count):
        for i in range(3):
            outs[i][j] = refs[j][:, i * width : (i + 1) * width].astype(F32)


def finish_after(sums, before):
    rows, width = sums[0].shape[0], sums[0].shape[1] // 3
    return pl.pallas_call(
        functools.partial(finish_kernel, len(sums)),
        out_shape=(shape((len(sums), rows, width), F32),) * 3,
        in_specs=[VMEM] * len(sums) + [HBM] * len(before),
        out_specs=(VMEM,) * 3,
        compiler_params=params(60),
        name="finish",
    )(*sums, *before)


def after_kernel(*refs):
    pass


def after(arrays, before):
    return pl.pallas_call(
        after_kernel,
        out_shape=tuple(shape(a.shape, a.dtype) for a in arrays),
        in_specs=[HBM] * (len(arrays) + len(before)),
        out_specs=(HBM,) * len(arrays),
        input_output_aliases={i: i for i in range(len(arrays))},
        name="after",
    )(*arrays, *before)


def block_rows(sizes):
    return MODEL_WIDTH // (2 * sizes["dp"] * sizes["z"])


def by_blocks(sizes):
    return block_rows(sizes) % 16 == 0


def gather_rows(block, along_dp, ids, sizes):
    ndp, nz = sizes["dp"], sizes["z"]
    pieces = both_cores(along_dp)
    if by_blocks(sizes):
        places = tuple((k, c, start, piece.shape[0]) for k, c, start, piece in pieces)
        return places, [piece for *_, piece in pieces]
    columns = block.shape[-1]
    whole = jnp.zeros((ndp, nz, 2, block_rows(sizes), columns), BF16)
    for k, c, start, piece in pieces:
        order = ids[1] ^ jnp.arange(start, start + piece.shape[0])
        whole = whole.at[ids[0] ^ k, order, ids[2] ^ c].set(piece)
    return None, [whole.reshape(MODEL_WIDTH, columns)]


def split_cores(columns, ids, sizes):
    rows = columns.shape[0]
    blocks = columns.reshape(rows, sizes["dp"] * sizes["z"], 2, block_rows(sizes))
    halves = [lax.dynamic_index_in_dim(blocks, ids[2] ^ c, 2, keepdims=False) for c in range(2)]
    return [half.reshape(rows, MODEL_WIDTH // 2) for half in halves]


def share_cores(columns, ids, sizes):
    mine, other = split_cores(columns, ids, sizes)
    return [mine, exchange(other, "core", 2, 1)]


def scatter_rows(terms, sizes):
    ndp, nz = sizes["dp"], sizes["z"]
    blocks = terms.reshape(ndp, nz, block_rows(sizes), terms.shape[1])
    got = lax.all_to_all(blocks, "dp", split_axis=0, concat_axis=0, tiled=True)
    part = jnp.sum(got.astype(F32), axis=0).astype(BF16)
    got = lax.all_to_all(part, "z", split_axis=0, concat_axis=0, tiled=True)
    return jnp.sum(got.astype(F32), axis=0), got


def load_rows(ids, ndp, nz, places, parts, dest, sem):
    if places is None:
        loads = [pltpu.make_async_copy(parts[0], dest, sem.at[0])]
        loads[0].start()
        return loads
    rows = MODEL_WIDTH // (ndp * nz * 2)
    loads = []
    for (k, c, start, count), part in zip(places, parts):
        for z in range(count):
            block = ((ids[0] ^ k) * nz + (ids[1] ^ (start + z))) * 2 + (ids[2] ^ c)
            place = pl.ds(pl.multiple_of(block * rows, rows), rows)
            copy = pltpu.make_async_copy(part.at[z], dest.at[place, :], sem.at[len(loads)])
            loads.append(copy)
    for load in loads:
        load.start()
    return loads


def rms_scale(rows):
    return lax.rsqrt(jnp.mean(rows * rows, axis=-1, keepdims=True) + EPS)


def norm_back(normed, row_scale, grad):
    return row_scale * (grad - normed * jnp.mean(grad * normed, axis=-1, keepdims=True))


def swapped(vals):
    return pltpu.roll(vals, HEAD_SIZE // 2, 1)


def head(h):
    return slice(h * HEAD_SIZE, (h + 1) * HEAD_SIZE)


def seen(rows, length):
    q = lax.broadcasted_iota(jnp.int32, (rows, rows), 0)
    s = lax.broadcasted_iota(jnp.int32, (rows, rows), 1)
    return (s <= q) & (s < length)


def attention_probs(query, key, visible):
    scores = jnp.where(visible, nt(query, key) * SCALE, NEG_FILL)
    expon = jnp.exp(scores - jnp.max(scores, axis=-1, keepdims=True))
    return expon / jnp.sum(expon, axis=-1, keepdims=True)


def route_softmax(router_rows, hidden):
    logits = nt(router_rows, hidden)[:EXPERTS]
    expon = jnp.exp(logits - jnp.max(logits, axis=0, keepdims=True))
    return expon / jnp.sum(expon, axis=0, keepdims=True)


def attend_kernel(ndp, nz, places, ids, tokens, cosine, sine, *refs):
    *parts, qkv, mixed, h_one, gains, router, w, sem = refs
    rows = tokens.shape[0]
    loads = load_rows(ids, ndp, nz, places, parts, w, sem)
    tok = tokens[...].astype(F32)
    normed = tok * rms_scale(tok)
    for load in loads:
        load.wait()
    extra = jnp.transpose(w[:, QKV:].astype(F32))
    gains[...] = extra[:8]
    router[...] = extra[2 : 2 + ROUTER].astype(BF16)
    h_one[...] = (normed * extra[0:1]).astype(BF16)
    cos, sin = cosine[...], sine[...]
    for t in range(QKV // TILE):
        pre = nn(h_one[...], w[:, t * TILE : (t + 1) * TILE])
        for i in range(TILE // HEAD_SIZE):
            part = pre[:, head(i)]
            at = t * TILE + i * HEAD_SIZE
            if at < QW + KW:
                part = part * cos + swapped(part) * sin
            qkv[:, at : at + HEAD_SIZE] = part.astype(BF16)
    visible = seen(rows, ids[3])
    for h in range(QUERY_HEADS):
        g = h // GROUP
        probs = attention_probs(qkv[:, head(h)], qkv[:, head(QUERY_HEADS + g)], visible)
        values = qkv[:, head(QUERY_HEADS + KEY_VALUE_HEADS + g)]
        mixed[:, head(h)] = nn(probs.astype(BF16), values).astype(BF16)


def attend(ids, tokens, cosine, sine, weights, sizes):
    places, parts = weights
    ndp, nz = sizes["dp"], sizes["z"]
    rows = tokens.shape[0]
    return pl.pallas_call(
        functools.partial(attend_kernel, ndp, nz, places),
        out_shape=(
            shape((rows, QKV), BF16),
            shape((rows, QW), BF16),
            shape((rows, MODEL_WIDTH), BF16),
            shape((8, MODEL_WIDTH), F32),
            shape((ROUTER, MODEL_WIDTH), BF16),
        ),
        in_specs=[SMEM, VMEM, VMEM, VMEM] + [HBM] * len(parts),
        out_specs=(VMEM,) * 5,
        scratch_shapes=[
            pltpu.VMEM((MODEL_WIDTH, FIRST), BF16),
            pltpu.SemaphoreType.DMA((2 * ndp * nz,)),
        ],
        compiler_params=params(60),
        cost_estimate=cost(2 * rows * MODEL_WIDTH * QKV, 10 * MIB, 12 * rows * rows),
        name="attend",
    )(ids, tokens, cosine, sine, *parts)


def project_kernel(ndp, nz, places, ids, tokens, mixed, gains, *refs):
    *parts, residual, top, low, w, sem = refs
    loads = load_rows(ids, ndp, nz, places, parts, w, sem)
    for load in loads:
        load.wait()
    for t in range(MODEL_WIDTH // TILE):
        lane = slice(t * TILE, (t + 1) * TILE)
        residual[:, lane] = tokens[:, lane].astype(F32) + nn(mixed[...], w[:, lane])
    whole = residual[...]
    h_two = (whole * rms_scale(whole) * gains[1:2]).astype(BF16)
    half = top.shape[0]
    top[...], low[...] = h_two[:half], h_two[half:]


def project(ids, tokens, mixed, gains, weights, sizes):
    places, parts = weights
    ndp, nz = sizes["dp"], sizes["z"]
    rows = tokens.shape[0]
    return pl.pallas_call(
        functools.partial(project_kernel, ndp, nz, places),
        out_shape=(shape((rows, MODEL_WIDTH), F32),)
        + (shape((rows // 2, MODEL_WIDTH), BF16),) * 2,
        in_specs=[SMEM, VMEM, VMEM, VMEM] + [HBM] * len(parts),
        out_specs=(VMEM,) * 3,
        scratch_shapes=[
            pltpu.VMEM((QW, MODEL_WIDTH), BF16),
            pltpu.SemaphoreType.DMA((2 * ndp * nz,)),
        ],
        compiler_params=params(60),
        cost_estimate=cost(2 * rows * MODEL_WIDTH * QW, 8 * MIB),
        name="project",
    )(ids, tokens, mixed, gains, *parts)


def expert_kernel(ndp, rows, width, index, last, near, far, unread, *refs):
    it = iter(refs)
    take = lambda n: [next(it) for _ in range(n)]
    (expert_ref, router_ref) = take(2)
    prev_gates = take(index)
    hid_in, cot_in = take(len(near)), take(len(far))
    (w_in,) = take(1)
    prev_in = take(2) if index else []
    take(unread)
    (out_hbm,), back_hbm = take(1), take(2 * ndp if last else 1)
    gates_ref, terms_hbm = take(2)
    hid, cot, w, x, d, ge, inner, dg, du, pick, pick_t, slot_gate, slot_dot = take(13)
    (terms_buf,) = take(1)
    prev = take(2) if index else []
    in_sem, out_sem = take(2)
    depth = MODEL_WIDTH
    tiles = depth // TILE

    loads = {}

    def load(name, source, dest):
        copy = pltpu.make_async_copy(source, dest, in_sem.at[len(loads)])
        copy.start()
        loads[name] = copy

    for i, (k, start, count) in enumerate(near):
        load(("hid", i), hid_in[i], hid.at[k, pl.ds(start, count), :])
    for i, (k, start, count) in enumerate(far):
        load(("cot", i), cot_in[i], cot.at[k, pl.ds(start, count), :])
    load("w", w_in, w)
    for i in range(len(prev)):
        load(("prev", i), prev_in[i], prev[i])

    expert, me = expert_ref[0], expert_ref[1]
    which = lax.broadcasted_iota(jnp.int32, (EXPERTS, rows), 0) == expert
    earlier = (
        (
            lax.broadcasted_iota(jnp.int32, (rows, rows), 0)
            < lax.broadcasted_iota(jnp.int32, (rows, rows), 1)
        )
        .astype(F32)
        .astype(BF16)
    )
    slot = lax.broadcasted_iota(jnp.int32, (CAP, rows), 0).astype(F32)
    for s in range(ndp):
        for i, piece in enumerate(near):
            if piece[0] == s:
                loads["hid", i].wait()
        for i, piece in enumerate(far):
            if piece[0] == s:
                loads["cot", i].wait()
        hidden = hid[s]
        probs = route_softmax(router_ref[...], hidden)
        named = cot[s, rows : rows + NOTE, :rows]
        place = nn(named, earlier)[:EXPERTS]
        named = named[:EXPERTS].astype(F32)
        named_row = jnp.sum(jnp.where(which, named, 0.0), axis=0, keepdims=True)
        gate_row = jnp.sum(jnp.where(which, probs, 0.0), axis=0, keepdims=True)
        place_row = jnp.sum(jnp.where(which, place, 0.0), axis=0, keepdims=True)
        chosen = jnp.where((slot == place_row) & (named_row > 0.5), 1.0, 0.0)
        pick[s] = chosen.astype(BF16)
        pick_t[s] = jnp.transpose(chosen).astype(BF16)
        at = pl.ds(s * CAP, CAP)
        gate = jnp.sum(chosen * gate_row, axis=1, keepdims=True)
        slot_gate[at, :] = jnp.broadcast_to(gate, (CAP, 128))
        x[at, :] = nn(pick[s], hidden).astype(BF16)
        grads = nn(pick[s], cot[s, :rows])
        d[at, :] = grads.astype(BF16)
        ge[at, :] = (gate * grads).astype(BF16)
    loads["w"].wait()

    def hidden_units(t, carry):
        at = pl.multiple_of(t * TILE, TILE)
        gate_pre = nn(x[...], w[:, pl.ds(at, TILE)])
        up_pre = nn(x[...], w[:, pl.ds(width + at, TILE)])
        grad_inner = nn(ge[...], w[:, pl.ds(2 * width + at, TILE)])
        sig = 1.0 / (1.0 + jnp.exp(-gate_pre))
        act = gate_pre * sig
        inner[:, pl.ds(at, TILE)] = (act * up_pre).astype(BF16)
        dg[:, pl.ds(at, TILE)] = (
            grad_inner * up_pre * sig * (1.0 + gate_pre * (1.0 - sig))
        ).astype(BF16)
        du[:, pl.ds(at, TILE)] = (grad_inner * act).astype(BF16)
        return carry

    lax.fori_loop(0, width // TILE, hidden_units, 0)
    slot_dot[...] = jnp.zeros_like(slot_dot)
    for i in range(len(prev)):
        loads["prev", i].wait()

    noted = (rows + NOTE) // 2

    def stores(t):
        lane = pl.ds(pl.multiple_of(t * TILE, TILE), TILE)
        copies = [(terms_buf.at[lane, :], terms_hbm.at[lane, :])]
        if not last:
            body = pl.ds(0, rows)
            copies.append((hid.at[:, :, lane], out_hbm.at[:, :, lane]))
            copies.append((cot.at[:, body, lane], back_hbm[0].at[:, body, lane]))
        else:
            for k in range(ndp):
                copies.append((hid.at[k, :, lane], out_hbm.at[me ^ k, :, lane]))
            for i in range(2 * ndp):
                body = pl.ds(0, noted if i % 2 == 0 else rows - noted)
                taken = pl.ds(i % 2 * noted, noted if i % 2 == 0 else rows - noted)
                copies.append((cot.at[i // 2, taken, lane], back_hbm[i].at[body, lane]))
        return [
            pltpu.make_async_copy(source, dest, out_sem.at[i, t])
            for i, (source, dest) in enumerate(copies)
        ]

    def features(t, carry):
        lane = pl.ds(pl.multiple_of(t * TILE, TILE), TILE)
        result = nt(inner[...], w[lane, pl.ds(2 * width, width)]).astype(BF16).astype(F32)
        partial = jnp.sum(result * d[:, lane].astype(F32), axis=1, keepdims=True)
        slot_dot[...] += jnp.broadcast_to(partial, slot_dot.shape)
        gated = (slot_gate[:, :1] * result).astype(BF16)
        grad_in = (
            nt(dg[...], w[lane, pl.ds(0, width)]) + nt(du[...], w[lane, pl.ds(width, width)])
        ).astype(BF16)
        for s in range(ndp):
            part = slice(s * CAP, (s + 1) * CAP)
            sent = nn(pick_t[s], gated[part])
            back = nn(pick_t[s], grad_in[part])
            if prev:
                sent = sent + prev[0][s, :, lane].astype(F32)
                back = back + prev[1][s, :rows, lane].astype(F32)
            hid[s, :, lane] = sent.astype(BF16)
            cot[s, :rows, lane] = back.astype(BF16)
        x_t = jnp.transpose(x[:, lane])
        terms_buf[lane, pl.ds(0, width)] = nn(x_t, dg[...]).astype(BF16)
        terms_buf[lane, pl.ds(width, width)] = nn(x_t, du[...]).astype(BF16)
        ge_t = jnp.transpose(ge[:, lane])
        terms_buf[lane, pl.ds(2 * width, width)] = nn(ge_t, inner[...]).astype(BF16)
        for store in stores(t):
            store.start()
        return carry

    lax.fori_loop(0, tiles, features, 0)
    line = lax.broadcasted_iota(jnp.int32, (NOTE, 3 * rows), 0)
    notes = []
    for s in range(ndp):
        part = slice(s * CAP, (s + 1) * CAP)
        own = jnp.sum(pick[s].astype(F32) * slot_dot[part, :1], axis=0, keepdims=True)
        gates_ref[s] = own
        if not last:
            continue
        note = jnp.zeros((NOTE, 3 * rows), F32)
        for j, row in enumerate([p[s] for p in prev_gates] + [own]):
            high = row.astype(BF16).astype(F32)
            middle = (row - high).astype(BF16).astype(F32)
            low = row - high - middle
            at = expert - index + j
            note = jnp.where(line == at, jnp.concatenate([high, middle, low], axis=1), note)
        cot[s, rows : rows + NOTE, : 3 * rows] = note.astype(BF16)
        notes.append(
            pltpu.make_async_copy(
                cot.at[s, pl.ds(rows, NOTE), :],
                back_hbm[2 * s + 1].at[pl.ds(rows - noted, NOTE), :],
                out_sem.at[4 * ndp + 1, s],
            )
        )
        notes[-1].start()
    for t in range(tiles):
        for store in stores(t):
            store.wait()
    for note in notes:
        note.wait()


def run_expert(index, last, expert, router, hidden, grads, w_all, prev, prev_gates, ndp, before):
    rows = 2 * hidden[0][2].shape[0]
    near, far = (tuple((k, at, p.shape[0]) for k, at, p in group) for group in (hidden, grads))
    width = w_all.shape[1] // 3
    slots = ndp * CAP
    depth = MODEL_WIDTH
    tiles = depth // TILE
    scratch = [
        pltpu.VMEM((ndp, rows, depth), BF16),
        pltpu.VMEM((ndp, rows + NOTE, depth), BF16),
        pltpu.VMEM((depth, 3 * width), BF16),
        pltpu.VMEM((slots, depth), BF16),
        pltpu.VMEM((slots, depth), BF16),
        pltpu.VMEM((slots, depth), BF16),
        pltpu.VMEM((slots, width), BF16),
        pltpu.VMEM((slots, width), BF16),
        pltpu.VMEM((slots, width), BF16),
        pltpu.VMEM((ndp, CAP, rows), BF16),
        pltpu.VMEM((ndp, rows, CAP), BF16),
        pltpu.VMEM((slots, 128), F32),
        pltpu.VMEM((slots, 128), F32),
        pltpu.VMEM((depth, 3 * width), BF16),
    ]
    if index:
        scratch += [
            pltpu.VMEM((ndp, rows, depth), BF16),
            pltpu.VMEM((ndp, rows + NOTE, depth), BF16),
        ]
    scratch += [
        pltpu.SemaphoreType.DMA((len(near) + len(far) + 3,)),
        pltpu.SemaphoreType.DMA((4 * ndp + 2, max(tiles, ndp))),
    ]
    sent = [shape((ndp, rows, depth), BF16), shape((ndp, rows + NOTE, depth), BF16)]
    if last:
        sent = sent[:1] + [shape(((rows + NOTE) // 2, depth), BF16)] * (2 * ndp)
    flops = 2 * slots * depth * width * 9 + 8 * ndp * CAP * rows * depth
    return pl.pallas_call(
        functools.partial(
            expert_kernel, ndp, rows, width, index, last, near, far, len(before)
        ),
        out_shape=(
            *sent,
            shape((ndp, 1, rows), F32),
            shape((depth, 3 * width), BF16),
        ),
        in_specs=[SMEM, VMEM]
        + [VMEM] * len(prev_gates)
        + [HBM] * (len(near) + len(far) + 1 + len(prev) + len(before)),
        out_specs=(HBM,) * len(sent) + (VMEM, HBM),
        scratch_shapes=scratch,
        compiler_params=params(60),
        cost_estimate=cost(flops, 40 * MIB, slots * width),
        name="expert",
    )(
        expert,
        router,
        *prev_gates,
        *(piece for *_, piece in hidden),
        *(piece for *_, piece in grads),
        w_all,
        *prev,
        *before,
    )


def back_kernel(
    ndp,
    nz,
    places,
    count,
    pairs,
    ids,
    residual,
    top,
    low,
    grads,
    gains,
    router,
    cosine,
    sine,
    qkv,
    *refs,
):
    backs, refs = refs[: 2 * pairs], refs[2 * pairs :]
    parts, refs = refs[:count], refs[count:]
    grad_resid, grad_attn, grad_pre, notes, w, grad_mixed, sem = refs
    rows = residual.shape[0]
    loads = load_rows(ids, ndp, nz, places, parts, w, sem)
    upper, lower = backs[0][...].astype(F32), backs[1][...].astype(F32)
    for i in range(1, pairs):
        upper = upper + backs[2 * i][...].astype(F32)
        lower = lower + backs[2 * i + 1][...].astype(F32)
    body = rows - upper.shape[0]
    grad_h = jnp.concatenate([upper, lower[:body]], axis=0)
    note = lower[body : body + EXPERTS, : 3 * rows]
    grad_route = note[:, :rows] + note[:, rows : 2 * rows] + note[:, 2 * rows :]
    hidden = jnp.concatenate([top[...], low[...]], axis=0)
    probs = route_softmax(router[...], hidden)
    grad_logits = probs * (grad_route - jnp.sum(probs * grad_route, axis=0, keepdims=True))
    grad_logits = jnp.concatenate([grad_logits, jnp.zeros_like(grad_logits)], axis=0)
    grad_logits = grad_logits.astype(BF16)
    grad_h = grad_h + tn(grad_logits, router[...])
    res = residual[...]
    scale = rms_scale(res)
    normed = res * scale
    notes[0:8] = jnp.broadcast_to(
        jnp.sum(normed * grad_h, axis=0, keepdims=True), (8, MODEL_WIDTH)
    )
    notes[8:16] = nn(grad_logits, hidden)[:EXPERTS]
    live = lax.broadcasted_iota(jnp.int32, (rows, 1), 0) < ids[3]
    final = jnp.where(live, grads[...].astype(F32), 0.0)
    total = final + norm_back(normed, scale, grad_h * gains[1:2])
    grad_resid[...] = total
    grad_attn[...] = total.astype(BF16)
    for load in loads:
        load.wait()
    for t in range(QW // TILE):
        lane = slice(t * TILE, (t + 1) * TILE)
        grad_mixed[:, lane] = nt(grad_attn[...], w[lane, :]).astype(BF16)
    visible = seen(rows, ids[3])
    cos, sin = cosine[...], sine[...]
    for g in range(KEY_VALUE_HEADS):
        key = qkv[:, head(QUERY_HEADS + g)]
        value = qkv[:, head(QUERY_HEADS + KEY_VALUE_HEADS + g)]
        grad_key = jnp.zeros((rows, HEAD_SIZE), F32)
        grad_value = jnp.zeros((rows, HEAD_SIZE), F32)
        for h in range(g * GROUP, (g + 1) * GROUP):
            query, grad = qkv[:, head(h)], grad_mixed[:, head(h)]
            probs = attention_probs(query, key, visible)
            grad_probs = nt(grad, value)
            grad_value = grad_value + tn(probs.astype(BF16), grad)
            row_dot = jnp.sum(probs * grad_probs, axis=-1, keepdims=True)
            grad_scores = (probs * (grad_probs - row_dot)).astype(BF16)
            grad_query = nn(grad_scores, key) * SCALE
            grad_key = grad_key + tn(grad_scores, query)
            grad_pre[:, head(h)] = (grad_query * cos - swapped(grad_query) * sin).astype(BF16)
        grad_key = grad_key * SCALE
        grad_pre[:, head(QUERY_HEADS + g)] = (
            grad_key * cos - swapped(grad_key) * sin
        ).astype(BF16)
        grad_pre[:, head(QUERY_HEADS + KEY_VALUE_HEADS + g)] = grad_value.astype(BF16)


def back(ids, residual, h_two, grads, gains, router, cosine, sine, qkv, backs, weights, sizes):
    ndp, nz = sizes["dp"], sizes["z"]
    places, parts = weights
    rows = residual.shape[0]
    return pl.pallas_call(
        functools.partial(back_kernel, ndp, nz, places, len(parts), len(backs) // 2),
        out_shape=(
            shape((rows, MODEL_WIDTH), F32),
            shape((rows, MODEL_WIDTH), BF16),
            shape((rows, QKV), BF16),
            shape((16, MODEL_WIDTH), F32),
        ),
        in_specs=[SMEM] + [VMEM] * (9 + len(backs)) + [HBM] * len(parts),
        out_specs=(VMEM,) * 4,
        scratch_shapes=[
            pltpu.VMEM((QW, MODEL_WIDTH), BF16),
            pltpu.VMEM((rows, QW), BF16),
            pltpu.SemaphoreType.DMA((2 * ndp * nz,)),
        ],
        compiler_params=params(60),
        cost_estimate=cost(3 * rows * MODEL_WIDTH * QW, 16 * MIB, 12 * rows * rows),
        name="back",
    )(ids, residual, *h_two, grads, gains, router, cosine, sine, qkv, *backs, *parts)


def tokens_back_kernel(ndp, nz, places, ids, tokens, gains, grad_pre, grad_resid, *refs):
    *parts, grad_tokens, w, sem = refs
    loads = load_rows(ids, ndp, nz, places, parts, w, sem)
    tok = tokens[...].astype(F32)
    scale = rms_scale(tok)
    normed = tok * scale
    for load in loads:
        load.wait()
    for t in range(MODEL_WIDTH // TILE):
        lane = slice(t * TILE, (t + 1) * TILE)
        grad_tokens[:, lane] = nt(grad_pre[...], w[lane, :QKV])
    grad_h = grad_tokens[...]
    grad_tokens[...] = grad_resid[...] + norm_back(normed, scale, grad_h * gains[0:1])


def tokens_back(ids, tokens, gains, grad_pre, grad_resid, weights, sizes):
    ndp, nz = sizes["dp"], sizes["z"]
    places, parts = weights
    rows = tokens.shape[0]
    return pl.pallas_call(
        functools.partial(tokens_back_kernel, ndp, nz, places),
        out_shape=shape((rows, MODEL_WIDTH), F32),
        in_specs=[SMEM] + [VMEM] * 4 + [HBM] * len(parts),
        out_specs=VMEM,
        scratch_shapes=[
            pltpu.VMEM((MODEL_WIDTH, FIRST), BF16),
            pltpu.SemaphoreType.DMA((2 * ndp * nz,)),
        ],
        compiler_params=params(60),
        cost_estimate=cost(2 * rows * MODEL_WIDTH * QKV, 12 * MIB),
        name="tokens_back",
    )(ids, tokens, gains, grad_pre, grad_resid, *parts)


def terms_kernel(*refs):
    out_terms, in_terms = refs[-2:]
    mixed, grad_attn, h_one, grad_pre, notes = (refs[2 * i : 2 * i + 2] for i in range(5))
    both = lambda pair: jnp.concatenate([pair[0][...], pair[1][...]], axis=0)
    left, right = jnp.transpose(both(mixed)), both(grad_attn)
    for t in range(MODEL_WIDTH // TILE):
        lane = slice(t * TILE, (t + 1) * TILE)
        out_terms[:, lane] = nn(left, right[:, lane]).astype(BF16)
    left, right = jnp.transpose(both(h_one)), both(grad_pre)
    for t in range(QKV // TILE):
        lane = slice(t * TILE, (t + 1) * TILE)
        in_terms[:, lane] = nn(left, right[:, lane]).astype(BF16)
    note = notes[0][...] + notes[1][...]
    block = jnp.concatenate([note, jnp.zeros((PAD - 16, note.shape[1]), F32)], axis=0)
    in_terms[:, QKV:] = jnp.transpose(block).astype(BF16)


def weight_terms(pairs, before):
    half = MODEL_WIDTH // 2
    arrays = [array for pair in pairs for array in pair]
    return pl.pallas_call(
        terms_kernel,
        out_shape=(shape((half, MODEL_WIDTH), BF16), shape((half, FIRST), BF16)),
        in_specs=[VMEM] * len(arrays) + [HBM] * len(before),
        out_specs=(VMEM,) * 2,
        compiler_params=params(60),
        cost_estimate=cost(2 * MODEL_WIDTH * pairs[0][0].shape[0] * (QW + QKV), 10 * MIB),
        name="weight_terms",
    )(*arrays, *before)


def rope_tables(rows):
    half = HEAD_SIZE // 2
    position = jnp.arange(rows).astype(F32)
    inverse = ROPE_BASE ** (-jnp.arange(half).astype(F32) / half)
    angles = position[:, None] * inverse[None, :]
    cosine, sine = jnp.cos(angles), jnp.sin(angles)
    return jnp.concatenate([cosine, cosine], axis=1), jnp.concatenate([-sine, sine], axis=1)


def per_device(
    sizes,
    tokens,
    lengths,
    routes,
    cotangent,
    gain_one,
    w_query,
    key_matrix,
    value_matrix,
    w_out,
    gain_two,
    w_router,
    w_gate,
    w_up,
    w_down,
):
    ndp = sizes["dp"]
    rows = tokens.shape[0]
    local, _, width = w_gate.shape
    me_dp = lax.axis_index("dp")
    length = lengths[0]
    ids = jnp.stack([me_dp, lax.axis_index("z"), lax.axis_index("core"), length]).astype(jnp.int32)
    live = (jnp.arange(rows) < length)[:, None]
    expert_ids = jnp.arange(EXPERTS, dtype=jnp.int32)

    extra = jnp.concatenate([gain_one[:, None], gain_two[:, None], w_router], axis=1)
    extra = jnp.pad(extra, ((0, 0), (0, PAD - extra.shape[1])))
    first = jnp.concatenate([w_query, key_matrix, value_matrix, extra], axis=1)
    named = jnp.any(routes[None, :, :] == expert_ids[:, None, None], axis=2).astype(BF16)
    named = jnp.pad(named, ((0, NOTE - EXPERTS), (0, MODEL_WIDTH - rows)))
    grad_low = jnp.where(live, cotangent, jnp.zeros_like(cotangent))
    grad_low = jnp.concatenate([grad_low, named], axis=0)
    grad_near = start_dp(grad_low, ndp)

    nz = sizes["z"]
    first_z = [first] + [exchange(first, "z", nz, k) for k in range(1, nz)]
    first_block = stack_after(first_z, grad_near)
    second_z = [w_out] + [exchange(w_out, "z", nz, k) for k in range(1, nz)]
    first_dp = pass_on(first_block, start_dp(first_block, ndp), ndp, second_z[1:])
    packed = [pack(j, (w_gate, w_up, w_down)) for j in range(local)]
    packed = after(packed, [first_block])
    expert_mats = [lax.all_gather(p, ("z", "core"), axis=0, tiled=True) for p in packed]
    second_block = stack_after(second_z, [piece for *_, piece in first_dp[1:]])
    second_dp = gather_direct(second_block, ndp)

    cosine, sine = rope_tables(rows)
    weights_in = gather_rows(first, first_dp, ids, sizes)
    qkv, mixed, h_one, gains, router = attend(ids, tokens, cosine, sine, weights_in, sizes)
    second_far = after([piece for *_, piece in second_dp[1:]], [mixed])
    second_dp = [(k, 0, piece) for k, piece in enumerate([second_block, *second_far])]
    grad_far = pass_on(grad_low, grad_near, ndp, second_far)
    weights_out = gather_rows(w_out, second_dp, ids, sizes)
    residual, *h_two = project(ids, tokens, mixed, gains, weights_out, sizes)
    hidden = gather_halves(h_two, ndp)
    mixed, h_one = (share_cores(x, ids, sizes) for x in after([mixed, h_one], [residual]))

    prev, gate_grads, sums = (), [], []
    for j in range(local):
        expert = jnp.stack([me_dp * local + j, me_dp]).astype(jnp.int32)
        *prev, grad_gate, terms = run_expert(
            j,
            j == local - 1,
            expert,
            router,
            hidden,
            grad_far,
            expert_mats[j],
            prev,
            gate_grads,
            ndp,
            [mixed[1], h_one[1]],
        )
        gate_grads.append(grad_gate)
        sums.append(lax.psum_scatter(terms, ("z", "core"), scatter_dimension=0, tiled=True))
    outs, *backs = prev
    pairs = [tuple(backs[2 * k : 2 * k + 2]) for k in range(ndp)]
    backs = [part for pair in pairs[:1] + scatter_dp(pairs, ndp) for part in pair]
    (outs,) = after([outs], backs[2:])
    outs = lax.all_to_all(outs, "dp", split_axis=0, concat_axis=0, tiled=True)
    block_out = (residual + jnp.sum(outs.astype(F32), axis=0)).astype(BF16)

    grad_resid, grad_attn, grad_pre, notes = back(
        ids, residual, h_two, cotangent, gains, router, cosine, sine, qkv, backs, weights_out, sizes
    )
    grad_tokens = tokens_back(ids, tokens, gains, grad_pre, grad_resid, weights_in, sizes)
    pairs = (
        mixed,
        (grad_attn, exchange(grad_attn, "core", 2, 1)),
        h_one,
        (grad_pre, exchange(grad_pre, "core", 2, 1)),
        share_cores(notes, ids, sizes),
    )
    out_terms, in_terms = weight_terms(pairs, sums[:-1])
    grad_out, _ = scatter_rows(out_terms, sizes)
    grad_first, late = scatter_rows(in_terms, sizes)
    grad_in = grad_first[:, :QKV]
    own_rows = jnp.concatenate([w_query, key_matrix, value_matrix], axis=1)
    grad_gain_one = jnp.sum(grad_in * own_rows.astype(F32), axis=1) / gain_one.astype(F32)
    expert_sums = finish_after(sums, [late])
    return (
        block_out,
        grad_tokens,
        grad_gain_one,
        grad_in[:, :QW],
        grad_in[:, QW : QW + KW],
        grad_in[:, QW + KW :],
        grad_out,
        grad_first[:, QKV],
        grad_first[:, QKV + 8 : QKV + 8 + EXPERTS],
        *expert_sums,
    )


def solution(mesh):
    ndp, nf = mesh.shape["dp"], mesh.shape["fsdp"]
    sizes = {"dp": ndp, "z": nf // 2, "core": 2}
    split = Mesh(mesh.devices.reshape(ndp, nf // 2, 2), ("dp", "z", "core"))
    every = ("dp", "z", "core")
    rows = P(every, None)
    vector = P(every)
    expert = P("dp", ("z", "core"), None)

    def run(*args):
        return per_device(sizes, *args)

    return jax.shard_map(
        run,
        mesh=split,
        in_specs=(rows, vector, rows, rows, vector, rows, rows, rows, rows, vector, rows)
        + (expert,) * 3,
        out_specs=(rows, rows, vector, rows, rows, rows, rows, vector, rows) + (expert,) * 3,
        check_vma=False,
    )
```

```python
import functools

import jax
import jax.numpy as jnp
from jax import lax
from jax.experimental import pallas as pl
from jax.experimental.pallas import tpu as pltpu
from jax.sharding import Mesh
from jax.sharding import PartitionSpec as P

MODEL_WIDTH = 1536
QUERY_HEADS = 12
KEY_VALUE_HEADS = 2
HEAD_SIZE = 128
EXPERTS = 8
CAP = 160
GROUP = QUERY_HEADS // KEY_VALUE_HEADS
QW = QUERY_HEADS * HEAD_SIZE
KW = KEY_VALUE_HEADS * HEAD_SIZE
QKV = QW + 2 * KW
PAD = 128
FIRST = QKV + PAD
NOTE = 32
ROUTER = 16
EPS = 1e-06
ROPE_BASE = 1500000.0
NEG_FILL = -1e30
SCALE = HEAD_SIZE ** (-0.5)
F32 = jnp.float32
BF16 = jnp.bfloat16
TILE = 256
MIB = 1024 * 1024
HBM = pl.BlockSpec(memory_space=pltpu.HBM)
VMEM = pl.BlockSpec(memory_space=pltpu.VMEM)
SMEM = pl.BlockSpec(memory_space=pltpu.SMEM)


def nn(a, b):
    return lax.dot_general(a, b, (((1,), (0,)), ((), ())), preferred_element_type=F32)


def nt(a, b):
    return lax.dot_general(a, b, (((1,), (1,)), ((), ())), preferred_element_type=F32)


def tn(a, b):
    return lax.dot_general(a, b, (((0,), (0,)), ((), ())), preferred_element_type=F32)


def shape(dims, dtype):
    return jax.ShapeDtypeStruct(dims, dtype)


def params(mib):
    return pltpu.CompilerParams(vmem_limit_bytes=mib * MIB)


def cost(flops, data, special=0):
    return pl.CostEstimate(flops=flops, bytes_accessed=data, transcendentals=special)


def exchange(block, axis, size, step):
    return lax.ppermute(block, axis, [(i, i ^ step) for i in range(size)])


def start_dp(block, ndp):
    return [exchange(block, "dp", ndp, k) for k in ((1, 2) if ndp == 4 else range(1, ndp))]


def pass_on(block, near, ndp, before=()):
    if ndp != 4:
        return [(k, 0, piece) for k, piece in enumerate([block] + near)]
    side, up = after(near, before) if before else near
    half = block.shape[0] // 2
    return [
        (0, 0, block),
        (1, 0, side),
        (2, 0, up),
        (3, 0, exchange(side[:half], "dp", ndp, 2)),
        (3, half, exchange(up[half:], "dp", ndp, 1)),
    ]


def gather_direct(block, ndp):
    return [(k, 0, exchange(block, "dp", ndp, k) if k else block) for k in range(ndp)]


def gather_halves(halves, ndp):
    top, low = halves
    at = top.shape[0]
    if ndp != 4:
        return [
            (k, i * at, exchange(half, "dp", ndp, k) if k else half)
            for k in range(ndp)
            for i, half in enumerate(halves)
        ]
    side_top, up_low = exchange(top, "dp", ndp, 1), exchange(low, "dp", ndp, 2)
    side_low, up_top = exchange(low, "dp", ndp, 1), exchange(top, "dp", ndp, 2)
    return [
        (0, 0, top),
        (0, at, low),
        (1, 0, side_top),
        (2, at, up_low),
        (1, at, side_low),
        (2, 0, up_top),
        (3, 0, exchange(side_top, "dp", ndp, 2)),
        (3, at, exchange(up_low, "dp", ndp, 1)),
    ]


def scatter_dp(slots, ndp, before=()):
    if ndp != 4:
        whole = [jnp.concatenate(slot, axis=0) for slot in slots[1:]]
        return [exchange(part, "dp", ndp, k + 1) for k, part in enumerate(whole)]
    past = [exchange(slots[3][0], "dp", ndp, 1), exchange(slots[3][1], "dp", ndp, 2)]
    if before:
        past = after(past, before)
    add = lambda a, b: (a.astype(F32) + b.astype(F32)).astype(BF16)
    side = jnp.concatenate([slots[1][0], add(slots[1][1], past[1])], axis=0)
    up = jnp.concatenate([add(slots[2][0], past[0]), slots[2][1]], axis=0)
    return [exchange(side, "dp", ndp, 1), exchange(up, "dp", ndp, 2)]


def both_cores(pieces):
    return [
        (k, c, start, exchange(piece, "core", 2, 1) if c else piece)
        for k, start, piece in pieces
        for c in range(2)
    ]


def stack_kernel(count, *refs):
    for i in range(count):
        refs[-1][i] = refs[i][...]


def stack_after(parts, before):
    dims = (len(parts),) + parts[0].shape
    return pl.pallas_call(
        functools.partial(stack_kernel, len(parts)),
        out_shape=shape(dims, parts[0].dtype),
        in_specs=[VMEM] * len(parts) + [HBM] * len(before),
        out_specs=VMEM,
        compiler_params=params(60),
        cost_estimate=cost(0, 4 * dims[0] * dims[1] * dims[2]),
        name="stack",
    )(*parts, *before)


def pack_kernel(index, *refs):
    width = refs[0].shape[2]
    for i in range(3):
        refs[-1][:, i * width : (i + 1) * width] = refs[i][index]


def pack(index, mats):
    _, rows, width = mats[0].shape
    return pl.pallas_call(
        functools.partial(pack_kernel, index),
        out_shape=shape((rows, 3 * width), BF16),
        in_specs=[VMEM] * 3,
        out_specs=VMEM,
        compiler_params=params(60),
        name="pack",
    )(*mats)


def finish_kernel(count, *refs):
    outs = refs[-3:]
    width = outs[0].shape[2]
    for j in range(count):
        for i in range(3):
            outs[i][j] = refs[j][:, i * width : (i + 1) * width].astype(F32)


def finish_after(sums, before):
    rows, width = sums[0].shape[0], sums[0].shape[1] // 3
    return pl.pallas_call(
        functools.partial(finish_kernel, len(sums)),
        out_shape=(shape((len(sums), rows, width), F32),) * 3,
        in_specs=[VMEM] * len(sums) + [HBM] * len(before),
        out_specs=(VMEM,) * 3,
        compiler_params=params(60),
        name="finish",
    )(*sums, *before)


def after_kernel(*refs):
    pass


def after(arrays, before):
    return pl.pallas_call(
        after_kernel,
        out_shape=tuple(shape(a.shape, a.dtype) for a in arrays),
        in_specs=[HBM] * (len(arrays) + len(before)),
        out_specs=(HBM,) * len(arrays),
        input_output_aliases={i: i for i in range(len(arrays))},
        name="after",
    )(*arrays, *before)


def block_rows(sizes):
    return MODEL_WIDTH // (2 * sizes["dp"] * sizes["z"])


def by_blocks(sizes):
    return block_rows(sizes) % 16 == 0


def gather_rows(block, along_dp, ids, sizes):
    ndp, nz = sizes["dp"], sizes["z"]
    pieces = both_cores(along_dp)
    if by_blocks(sizes):
        places = tuple((k, c, start, piece.shape[0]) for k, c, start, piece in pieces)
        return places, [piece for *_, piece in pieces]
    columns = block.shape[-1]
    whole = jnp.zeros((ndp, nz, 2, block_rows(sizes), columns), BF16)
    for k, c, start, piece in pieces:
        order = ids[1] ^ jnp.arange(start, start + piece.shape[0])
        whole = whole.at[ids[0] ^ k, order, ids[2] ^ c].set(piece)
    return None, [whole.reshape(MODEL_WIDTH, columns)]


def split_cores(columns, ids, sizes):
    ndp, nz = sizes["dp"], sizes["z"]
    rows = columns.shape[0]
    blocks = columns.reshape(rows, ndp, nz, 2, block_rows(sizes))
    blocks = jnp.take(jnp.take(blocks, ids[0] ^ jnp.arange(ndp), 1), ids[1] ^ jnp.arange(nz), 2)
    halves = [lax.dynamic_index_in_dim(blocks, ids[2] ^ c, 3, keepdims=False) for c in range(2)]
    return [half.reshape(rows, MODEL_WIDTH // 2) for half in halves]


def turn_kernel(ndp, nz, count, ids, *refs):
    block = MODEL_WIDTH // (2 * ndp * nz)
    turned = refs[-1]
    for i in range(count):
        turned[...] = jnp.transpose(refs[i][...])
        for k in range(ndp):
            for z in range(nz):
                for c in range(2):
                    at = ((ids[0] ^ k) * nz + (ids[1] ^ z)) * 2 + (ids[2] ^ c)
                    place = pl.ds(pl.multiple_of(at * block, block), block)
                    dest = refs[-1 - 2 * count + 2 * i + c]
                    dest[(k * nz + z) * block : (k * nz + z + 1) * block] = turned[place, :]


def turn(arrays, before, ids, sizes):
    if not by_blocks(sizes):
        return [[half.T for half in split_cores(array, ids, sizes)] for array in arrays]
    rows = arrays[0].shape[0]
    halves = pl.pallas_call(
        functools.partial(turn_kernel, sizes["dp"], sizes["z"], len(arrays)),
        out_shape=(shape((MODEL_WIDTH // 2, rows), BF16),) * (2 * len(arrays)),
        in_specs=[SMEM] + [VMEM] * len(arrays) + [HBM] * len(before),
        out_specs=(VMEM,) * (2 * len(arrays)),
        scratch_shapes=[pltpu.VMEM((MODEL_WIDTH, rows), BF16)],
        compiler_params=params(60),
        name="turn",
    )(ids, *arrays, *before)
    return [halves[2 * i : 2 * i + 2] for i in range(len(arrays))]


def scatter_rows(own, slots, sizes, before=()):
    ndp, nz = sizes["dp"], sizes["z"]
    total = own
    for part in scatter_dp([None, *slots], ndp, before):
        total = total + part.astype(F32)
    rows = block_rows(sizes)
    blocks = [total[z * rows : (z + 1) * rows] for z in range(nz)]
    got = [exchange(blocks[z].astype(BF16), "z", nz, z) for z in range(1, nz)]
    return blocks[0] + sum(part.astype(F32) for part in got), got


def load_rows(ids, ndp, nz, places, parts, dest, sem):
    if places is None:
        loads = [pltpu.make_async_copy(parts[0], dest, sem.at[0])]
        loads[0].start()
        return loads
    rows = MODEL_WIDTH // (ndp * nz * 2)
    loads = []
    for (k, c, start, count), part in zip(places, parts):
        for z in range(count):
            block = ((ids[0] ^ k) * nz + (ids[1] ^ (start + z))) * 2 + (ids[2] ^ c)
            place = pl.ds(pl.multiple_of(block * rows, rows), rows)
            copy = pltpu.make_async_copy(part.at[z], dest.at[place, :], sem.at[len(loads)])
            loads.append(copy)
    for load in loads:
        load.start()
    return loads


def rms_scale(rows):
    return lax.rsqrt(jnp.mean(rows * rows, axis=-1, keepdims=True) + EPS)


def norm_back(normed, row_scale, grad):
    return row_scale * (grad - normed * jnp.mean(grad * normed, axis=-1, keepdims=True))


def swapped(vals):
    return pltpu.roll(vals, HEAD_SIZE // 2, 1)


def head(h):
    return slice(h * HEAD_SIZE, (h + 1) * HEAD_SIZE)


def seen(rows, length):
    q = lax.broadcasted_iota(jnp.int32, (rows, rows), 0)
    s = lax.broadcasted_iota(jnp.int32, (rows, rows), 1)
    return (s <= q) & (s < length)


def attention_probs(query, key, visible):
    scores = jnp.where(visible, nt(query, key) * SCALE, NEG_FILL)
    expon = jnp.exp(scores - jnp.max(scores, axis=-1, keepdims=True))
    return expon / jnp.sum(expon, axis=-1, keepdims=True)


def route_softmax(router_rows, hidden):
    logits = nt(router_rows, hidden)[:EXPERTS]
    expon = jnp.exp(logits - jnp.max(logits, axis=0, keepdims=True))
    return expon / jnp.sum(expon, axis=0, keepdims=True)


def attend_kernel(ndp, nz, places, ids, tokens, cosine, sine, *refs):
    *parts, qkv, mixed, h_one, gains, router, w, sem = refs
    rows = tokens.shape[0]
    loads = load_rows(ids, ndp, nz, places, parts, w, sem)
    tok = tokens[...].astype(F32)
    normed = tok * rms_scale(tok)
    for load in loads:
        load.wait()
    extra = jnp.transpose(w[:, QKV:].astype(F32))
    gains[...] = extra[:8]
    router[...] = extra[2 : 2 + ROUTER].astype(BF16)
    h_one[...] = (normed * extra[0:1]).astype(BF16)
    cos, sin = cosine[...], sine[...]
    for t in range(QKV // TILE):
        pre = nn(h_one[...], w[:, t * TILE : (t + 1) * TILE])
        for i in range(TILE // HEAD_SIZE):
            part = pre[:, head(i)]
            at = t * TILE + i * HEAD_SIZE
            if at < QW + KW:
                part = part * cos + swapped(part) * sin
            qkv[:, at : at + HEAD_SIZE] = part.astype(BF16)
    visible = seen(rows, ids[3])
    for h in range(QUERY_HEADS):
        g = h // GROUP
        probs = attention_probs(qkv[:, head(h)], qkv[:, head(QUERY_HEADS + g)], visible)
        values = qkv[:, head(QUERY_HEADS + KEY_VALUE_HEADS + g)]
        mixed[:, head(h)] = nn(probs.astype(BF16), values).astype(BF16)


def attend(ids, tokens, cosine, sine, weights, sizes):
    places, parts = weights
    ndp, nz = sizes["dp"], sizes["z"]
    rows = tokens.shape[0]
    return pl.pallas_call(
        functools.partial(attend_kernel, ndp, nz, places),
        out_shape=(
            shape((rows, QKV), BF16),
            shape((rows, QW), BF16),
            shape((rows, MODEL_WIDTH), BF16),
            shape((8, MODEL_WIDTH), F32),
            shape((ROUTER, MODEL_WIDTH), BF16),
        ),
        in_specs=[SMEM, VMEM, VMEM, VMEM] + [HBM] * len(parts),
        out_specs=(VMEM,) * 5,
        scratch_shapes=[
            pltpu.VMEM((MODEL_WIDTH, FIRST), BF16),
            pltpu.SemaphoreType.DMA((2 * ndp * nz,)),
        ],
        compiler_params=params(60),
        cost_estimate=cost(2 * rows * MODEL_WIDTH * QKV, 10 * MIB, 12 * rows * rows),
        name="attend",
    )(ids, tokens, cosine, sine, *parts)


def project_kernel(ndp, nz, places, ids, tokens, mixed, gains, *refs):
    *parts, residual, top, low, w, sem = refs
    loads = load_rows(ids, ndp, nz, places, parts, w, sem)
    for load in loads:
        load.wait()
    for t in range(MODEL_WIDTH // TILE):
        lane = slice(t * TILE, (t + 1) * TILE)
        residual[:, lane] = tokens[:, lane].astype(F32) + nn(mixed[...], w[:, lane])
    whole = residual[...]
    h_two = (whole * rms_scale(whole) * gains[1:2]).astype(BF16)
    half = top.shape[0]
    top[...], low[...] = h_two[:half], h_two[half:]


def project(ids, tokens, mixed, gains, weights, sizes):
    places, parts = weights
    ndp, nz = sizes["dp"], sizes["z"]
    rows = tokens.shape[0]
    return pl.pallas_call(
        functools.partial(project_kernel, ndp, nz, places),
        out_shape=(shape((rows, MODEL_WIDTH), F32),)
        + (shape((rows // 2, MODEL_WIDTH), BF16),) * 2,
        in_specs=[SMEM, VMEM, VMEM, VMEM] + [HBM] * len(parts),
        out_specs=(VMEM,) * 3,
        scratch_shapes=[
            pltpu.VMEM((QW, MODEL_WIDTH), BF16),
            pltpu.SemaphoreType.DMA((2 * ndp * nz,)),
        ],
        compiler_params=params(60),
        cost_estimate=cost(2 * rows * MODEL_WIDTH * QW, 8 * MIB),
        name="project",
    )(ids, tokens, mixed, gains, *parts)


def expert_kernel(ndp, rows, width, index, last, near, far, unread, *refs):
    it = iter(refs)
    take = lambda n: [next(it) for _ in range(n)]
    (expert_ref, router_ref) = take(2)
    prev_gates = take(index)
    hid_in, cot_in = take(len(near)), take(len(far))
    (w_in,) = take(1)
    prev_in = take(2) if index else []
    take(unread)
    (out_hbm,), back_hbm = take(1), take(2 * ndp if last else 1)
    gates_ref, terms_hbm = take(2)
    hid, cot, w, x, d, ge, inner, dg, du, pick, pick_t, slot_gate, slot_dot = take(13)
    (terms_buf,) = take(1)
    prev = take(2) if index else []
    in_sem, out_sem = take(2)
    depth = MODEL_WIDTH
    tiles = depth // TILE

    loads = {}

    def load(name, source, dest):
        copy = pltpu.make_async_copy(source, dest, in_sem.at[len(loads)])
        copy.start()
        loads[name] = copy

    for i, (k, start, count) in enumerate(near):
        load(("hid", i), hid_in[i], hid.at[k, pl.ds(start, count), :])
    for i, (k, start, count) in enumerate(far):
        load(("cot", i), cot_in[i], cot.at[k, pl.ds(start, count), :])
    load("w", w_in, w)
    for i in range(len(prev)):
        load(("prev", i), prev_in[i], prev[i])

    expert, me = expert_ref[0], expert_ref[1]
    which = lax.broadcasted_iota(jnp.int32, (EXPERTS, rows), 0) == expert
    earlier = (
        (
            lax.broadcasted_iota(jnp.int32, (rows, rows), 0)
            < lax.broadcasted_iota(jnp.int32, (rows, rows), 1)
        )
        .astype(F32)
        .astype(BF16)
    )
    slot = lax.broadcasted_iota(jnp.int32, (CAP, rows), 0).astype(F32)
    for s in range(ndp):
        for i, piece in enumerate(near):
            if piece[0] == s:
                loads["hid", i].wait()
        for i, piece in enumerate(far):
            if piece[0] == s:
                loads["cot", i].wait()
        hidden = hid[s]
        probs = route_softmax(router_ref[...], hidden)
        named = cot[s, rows : rows + NOTE, :rows]
        place = nn(named, earlier)[:EXPERTS]
        named = named[:EXPERTS].astype(F32)
        named_row = jnp.sum(jnp.where(which, named, 0.0), axis=0, keepdims=True)
        gate_row = jnp.sum(jnp.where(which, probs, 0.0), axis=0, keepdims=True)
        place_row = jnp.sum(jnp.where(which, place, 0.0), axis=0, keepdims=True)
        chosen = jnp.where((slot == place_row) & (named_row > 0.5), 1.0, 0.0)
        pick[s] = chosen.astype(BF16)
        pick_t[s] = jnp.transpose(chosen).astype(BF16)
        at = pl.ds(s * CAP, CAP)
        gate = jnp.sum(chosen * gate_row, axis=1, keepdims=True)
        slot_gate[at, :] = jnp.broadcast_to(gate, (CAP, 128))
        x[at, :] = nn(pick[s], hidden).astype(BF16)
        grads = nn(pick[s], cot[s, :rows])
        d[at, :] = grads.astype(BF16)
        ge[at, :] = (gate * grads).astype(BF16)
    loads["w"].wait()

    def hidden_units(t, carry):
        at = pl.multiple_of(t * TILE, TILE)
        gate_pre = nn(x[...], w[:, pl.ds(at, TILE)])
        up_pre = nn(x[...], w[:, pl.ds(width + at, TILE)])
        grad_inner = nn(ge[...], w[:, pl.ds(2 * width + at, TILE)])
        sig = 1.0 / (1.0 + jnp.exp(-gate_pre))
        act = gate_pre * sig
        inner[:, pl.ds(at, TILE)] = (act * up_pre).astype(BF16)
        dg[:, pl.ds(at, TILE)] = (
            grad_inner * up_pre * sig * (1.0 + gate_pre * (1.0 - sig))
        ).astype(BF16)
        du[:, pl.ds(at, TILE)] = (grad_inner * act).astype(BF16)
        return carry

    lax.fori_loop(0, width // TILE, hidden_units, 0)
    slot_dot[...] = jnp.zeros_like(slot_dot)
    for i in range(len(prev)):
        loads["prev", i].wait()

    noted = (rows + NOTE) // 2

    def stores(t):
        lane = pl.ds(pl.multiple_of(t * TILE, TILE), TILE)
        copies = [(terms_buf.at[lane, :], terms_hbm.at[lane, :])]
        if not last:
            body = pl.ds(0, rows)
            copies.append((hid.at[:, :, lane], out_hbm.at[:, :, lane]))
            copies.append((cot.at[:, body, lane], back_hbm[0].at[:, body, lane]))
        else:
            for k in range(ndp):
                copies.append((hid.at[k, :, lane], out_hbm.at[me ^ k, :, lane]))
            for i in range(2 * ndp):
                body = pl.ds(0, noted if i % 2 == 0 else rows - noted)
                taken = pl.ds(i % 2 * noted, noted if i % 2 == 0 else rows - noted)
                copies.append((cot.at[i // 2, taken, lane], back_hbm[i].at[body, lane]))
        return [
            pltpu.make_async_copy(source, dest, out_sem.at[i, t])
            for i, (source, dest) in enumerate(copies)
        ]

    def features(t, carry):
        lane = pl.ds(pl.multiple_of(t * TILE, TILE), TILE)
        result = nt(inner[...], w[lane, pl.ds(2 * width, width)]).astype(BF16).astype(F32)
        partial = jnp.sum(result * d[:, lane].astype(F32), axis=1, keepdims=True)
        slot_dot[...] += jnp.broadcast_to(partial, slot_dot.shape)
        gated = (slot_gate[:, :1] * result).astype(BF16)
        grad_in = (
            nt(dg[...], w[lane, pl.ds(0, width)]) + nt(du[...], w[lane, pl.ds(width, width)])
        ).astype(BF16)
        for s in range(ndp):
            part = slice(s * CAP, (s + 1) * CAP)
            sent = nn(pick_t[s], gated[part])
            back = nn(pick_t[s], grad_in[part])
            if prev:
                sent = sent + prev[0][s, :, lane].astype(F32)
                back = back + prev[1][s, :rows, lane].astype(F32)
            hid[s, :, lane] = sent.astype(BF16)
            cot[s, :rows, lane] = back.astype(BF16)
        x_t = jnp.transpose(x[:, lane])
        terms_buf[lane, pl.ds(0, width)] = nn(x_t, dg[...]).astype(BF16)
        terms_buf[lane, pl.ds(width, width)] = nn(x_t, du[...]).astype(BF16)
        ge_t = jnp.transpose(ge[:, lane])
        terms_buf[lane, pl.ds(2 * width, width)] = nn(ge_t, inner[...]).astype(BF16)
        for store in stores(t):
            store.start()
        return carry

    lax.fori_loop(0, tiles, features, 0)
    line = lax.broadcasted_iota(jnp.int32, (NOTE, 3 * rows), 0)
    notes = []
    for s in range(ndp):
        part = slice(s * CAP, (s + 1) * CAP)
        own = jnp.sum(pick[s].astype(F32) * slot_dot[part, :1], axis=0, keepdims=True)
        gates_ref[s] = own
        if not last:
            continue
        note = jnp.zeros((NOTE, 3 * rows), F32)
        for j, row in enumerate([p[s] for p in prev_gates] + [own]):
            high = row.astype(BF16).astype(F32)
            middle = (row - high).astype(BF16).astype(F32)
            low = row - high - middle
            at = expert - index + j
            note = jnp.where(line == at, jnp.concatenate([high, middle, low], axis=1), note)
        cot[s, rows : rows + NOTE, : 3 * rows] = note.astype(BF16)
        notes.append(
            pltpu.make_async_copy(
                cot.at[s, pl.ds(rows, NOTE), :],
                back_hbm[2 * s + 1].at[pl.ds(rows - noted, NOTE), :],
                out_sem.at[4 * ndp + 1, s],
            )
        )
        notes[-1].start()
    for t in range(tiles):
        for store in stores(t):
            store.wait()
    for note in notes:
        note.wait()


def run_expert(index, last, expert, router, hidden, grads, w_all, prev, prev_gates, ndp, before):
    rows = 2 * hidden[0][2].shape[0]
    near, far = (tuple((k, at, p.shape[0]) for k, at, p in group) for group in (hidden, grads))
    width = w_all.shape[1] // 3
    slots = ndp * CAP
    depth = MODEL_WIDTH
    tiles = depth // TILE
    scratch = [
        pltpu.VMEM((ndp, rows, depth), BF16),
        pltpu.VMEM((ndp, rows + NOTE, depth), BF16),
        pltpu.VMEM((depth, 3 * width), BF16),
        pltpu.VMEM((slots, depth), BF16),
        pltpu.VMEM((slots, depth), BF16),
        pltpu.VMEM((slots, depth), BF16),
        pltpu.VMEM((slots, width), BF16),
        pltpu.VMEM((slots, width), BF16),
        pltpu.VMEM((slots, width), BF16),
        pltpu.VMEM((ndp, CAP, rows), BF16),
        pltpu.VMEM((ndp, rows, CAP), BF16),
        pltpu.VMEM((slots, 128), F32),
        pltpu.VMEM((slots, 128), F32),
        pltpu.VMEM((depth, 3 * width), BF16),
    ]
    if index:
        scratch += [
            pltpu.VMEM((ndp, rows, depth), BF16),
            pltpu.VMEM((ndp, rows + NOTE, depth), BF16),
        ]
    scratch += [
        pltpu.SemaphoreType.DMA((len(near) + len(far) + 3,)),
        pltpu.SemaphoreType.DMA((4 * ndp + 2, max(tiles, ndp))),
    ]
    sent = [shape((ndp, rows, depth), BF16), shape((ndp, rows + NOTE, depth), BF16)]
    if last:
        sent = sent[:1] + [shape(((rows + NOTE) // 2, depth), BF16)] * (2 * ndp)
    flops = 2 * slots * depth * width * 9 + 8 * ndp * CAP * rows * depth
    return pl.pallas_call(
        functools.partial(
            expert_kernel, ndp, rows, width, index, last, near, far, len(before)
        ),
        out_shape=(
            *sent,
            shape((ndp, 1, rows), F32),
            shape((depth, 3 * width), BF16),
        ),
        in_specs=[SMEM, VMEM]
        + [VMEM] * len(prev_gates)
        + [HBM] * (len(near) + len(far) + 1 + len(prev) + len(before)),
        out_specs=(HBM,) * len(sent) + (VMEM, HBM),
        scratch_shapes=scratch,
        compiler_params=params(60),
        cost_estimate=cost(flops, 40 * MIB, slots * width),
        name="expert",
    )(
        expert,
        router,
        *prev_gates,
        *(piece for *_, piece in hidden),
        *(piece for *_, piece in grads),
        w_all,
        *prev,
        *before,
    )


def back_kernel(
    ndp,
    nz,
    places,
    count,
    given,
    unread,
    ids,
    residual,
    top,
    low,
    grads,
    gains,
    router,
    cosine,
    sine,
    qkv,
    *refs,
):
    backs, refs = refs[:given], refs[given:]
    parts, refs = refs[:count], refs[count:]
    grad_resid, grad_attn, grad_pre, notes, w, grad_mixed, sem = refs[unread:]
    rows = residual.shape[0]
    loads = load_rows(ids, ndp, nz, places, parts, w, sem)
    whole = jnp.concatenate([backs[0][...], backs[1][...]], axis=0).astype(F32)
    for part in backs[2:]:
        whole = whole + part[...].astype(F32)
    grad_h = whole[:rows]
    note = whole[rows : rows + EXPERTS, : 3 * rows]
    grad_route = note[:, :rows] + note[:, rows : 2 * rows] + note[:, 2 * rows :]
    hidden = jnp.concatenate([top[...], low[...]], axis=0)
    probs = route_softmax(router[...], hidden)
    grad_logits = probs * (grad_route - jnp.sum(probs * grad_route, axis=0, keepdims=True))
    grad_logits = jnp.concatenate([grad_logits, jnp.zeros_like(grad_logits)], axis=0)
    grad_logits = grad_logits.astype(BF16)
    grad_h = grad_h + tn(grad_logits, router[...])
    res = residual[...]
    scale = rms_scale(res)
    normed = res * scale
    notes[0:8] = jnp.broadcast_to(
        jnp.sum(normed * grad_h, axis=0, keepdims=True), (8, MODEL_WIDTH)
    )
    notes[8:16] = nn(grad_logits, hidden)[:EXPERTS]
    live = lax.broadcasted_iota(jnp.int32, (rows, 1), 0) < ids[3]
    final = jnp.where(live, grads[...].astype(F32), 0.0)
    total = final + norm_back(normed, scale, grad_h * gains[1:2])
    grad_resid[...] = total
    grad_attn[...] = total.astype(BF16)
    for load in loads:
        load.wait()
    for t in range(QW // TILE):
        lane = slice(t * TILE, (t + 1) * TILE)
        grad_mixed[:, lane] = nt(grad_attn[...], w[lane, :]).astype(BF16)
    visible = seen(rows, ids[3])
    cos, sin = cosine[...], sine[...]
    for g in range(KEY_VALUE_HEADS):
        key = qkv[:, head(QUERY_HEADS + g)]
        value = qkv[:, head(QUERY_HEADS + KEY_VALUE_HEADS + g)]
        grad_key = jnp.zeros((rows, HEAD_SIZE), F32)
        grad_value = jnp.zeros((rows, HEAD_SIZE), F32)
        for h in range(g * GROUP, (g + 1) * GROUP):
            query, grad = qkv[:, head(h)], grad_mixed[:, head(h)]
            probs = attention_probs(query, key, visible)
            grad_probs = nt(grad, value)
            grad_value = grad_value + tn(probs.astype(BF16), grad)
            row_dot = jnp.sum(probs * grad_probs, axis=-1, keepdims=True)
            grad_scores = (probs * (grad_probs - row_dot)).astype(BF16)
            grad_query = nn(grad_scores, key) * SCALE
            grad_key = grad_key + tn(grad_scores, query)
            grad_pre[:, head(h)] = (grad_query * cos - swapped(grad_query) * sin).astype(BF16)
        grad_key = grad_key * SCALE
        grad_pre[:, head(QUERY_HEADS + g)] = (
            grad_key * cos - swapped(grad_key) * sin
        ).astype(BF16)
        grad_pre[:, head(QUERY_HEADS + KEY_VALUE_HEADS + g)] = grad_value.astype(BF16)


def back(
    ids, residual, h_two, grads, gains, router, cosine, sine, qkv, backs, weights, before, sizes
):
    ndp, nz = sizes["dp"], sizes["z"]
    places, parts = weights
    rows = residual.shape[0]
    return pl.pallas_call(
        functools.partial(
            back_kernel, ndp, nz, places, len(parts), len(backs), len(before)
        ),
        out_shape=(
            shape((rows, MODEL_WIDTH), F32),
            shape((rows, MODEL_WIDTH), BF16),
            shape((rows, QKV), BF16),
            shape((16, MODEL_WIDTH), F32),
        ),
        in_specs=[SMEM] + [VMEM] * (9 + len(backs)) + [HBM] * (len(parts) + len(before)),
        out_specs=(VMEM,) * 4,
        scratch_shapes=[
            pltpu.VMEM((QW, MODEL_WIDTH), BF16),
            pltpu.VMEM((rows, QW), BF16),
            pltpu.SemaphoreType.DMA((2 * ndp * nz,)),
        ],
        compiler_params=params(60),
        cost_estimate=cost(3 * rows * MODEL_WIDTH * QW, 16 * MIB, 12 * rows * rows),
        name="back",
    )(ids, residual, *h_two, grads, gains, router, cosine, sine, qkv, *backs, *parts, *before)


def tokens_back_kernel(ndp, nz, places, ids, tokens, gains, grad_pre, grad_resid, *refs):
    *parts, grad_tokens, w, sem = refs
    loads = load_rows(ids, ndp, nz, places, parts, w, sem)
    tok = tokens[...].astype(F32)
    scale = rms_scale(tok)
    normed = tok * scale
    for load in loads:
        load.wait()
    for t in range(MODEL_WIDTH // TILE):
        lane = slice(t * TILE, (t + 1) * TILE)
        grad_tokens[:, lane] = nt(grad_pre[...], w[lane, :QKV])
    grad_h = grad_tokens[...]
    grad_tokens[...] = grad_resid[...] + norm_back(normed, scale, grad_h * gains[0:1])


def tokens_back(ids, tokens, gains, grad_pre, grad_resid, weights, sizes):
    ndp, nz = sizes["dp"], sizes["z"]
    places, parts = weights
    rows = tokens.shape[0]
    return pl.pallas_call(
        functools.partial(tokens_back_kernel, ndp, nz, places),
        out_shape=shape((rows, MODEL_WIDTH), F32),
        in_specs=[SMEM] + [VMEM] * 4 + [HBM] * len(parts),
        out_specs=VMEM,
        scratch_shapes=[
            pltpu.VMEM((MODEL_WIDTH, FIRST), BF16),
            pltpu.SemaphoreType.DMA((2 * ndp * nz,)),
        ],
        compiler_params=params(60),
        cost_estimate=cost(2 * rows * MODEL_WIDTH * QKV, 12 * MIB),
        name="tokens_back",
    )(ids, tokens, gains, grad_pre, grad_resid, *parts)


def terms_kernel(ndp, nz, selected, ids, *refs):
    count = 2 * ndp - 1
    note_rows = refs[-1]
    outs, ins = refs[-1 - 2 * count : -1 - count], refs[-1 - count : -1]
    mixed, grad_attn, h_one, grad_pre, notes = (refs[2 * i : 2 * i + 2] for i in range(5))
    both = lambda pair, axis: jnp.concatenate([pair[0][...], pair[1][...]], axis=axis)
    slot = MODEL_WIDTH // (2 * ndp)

    def put(dests, lane, value):
        dests[0][:, lane] = value[:slot]
        for i in range(1, count):
            at = slot + (i - 1) * (slot // 2)
            dests[i][:, lane] = value[at : at + slot // 2].astype(BF16)

    for dests, left, right in ((outs, mixed, grad_attn), (ins, h_one, grad_pre)):
        left, right = both(left, 1), both(right, 0)
        for t in range(right.shape[1] // TILE):
            lane = slice(t * TILE, (t + 1) * TILE)
            put(dests, lane, nn(left, right[:, lane]))
    note = notes[0][...] + notes[1][...]
    block = jnp.concatenate([note, jnp.zeros((PAD - 16, note.shape[1]), F32)], axis=0)
    if selected:
        put(ins, slice(QKV, FIRST), jnp.transpose(block))
        return
    note_rows[...] = jnp.transpose(block)
    rows = MODEL_WIDTH // (2 * ndp * nz)
    taken = []
    for k in range(ndp):
        for z in range(nz):
            at = ((ids[0] ^ k) * nz + (ids[1] ^ z)) * 2 + ids[2]
            taken.append(note_rows[pl.ds(pl.multiple_of(at * rows, rows), rows), :])
    put(ins, slice(QKV, FIRST), jnp.concatenate(taken, axis=0))


def weight_terms(ids, pairs, before, sizes):
    ndp, nz = sizes["dp"], sizes["z"]
    slot = MODEL_WIDTH // (2 * ndp)
    arrays = [array for pair in pairs for array in pair]
    selected = arrays[-1].shape[1] != MODEL_WIDTH
    results = [
        part
        for columns in (MODEL_WIDTH, FIRST)
        for part in [shape((slot, columns), F32)]
        + [shape((slot // 2, columns), BF16)] * (2 * ndp - 2)
    ]
    found = pl.pallas_call(
        functools.partial(terms_kernel, ndp, nz, selected),
        out_shape=tuple(results),
        in_specs=[SMEM] + [VMEM] * len(arrays) + [HBM] * len(before),
        out_specs=(VMEM,) * len(results),
        scratch_shapes=[pltpu.VMEM((MODEL_WIDTH, PAD), F32)],
        compiler_params=params(60),
        cost_estimate=cost(2 * MODEL_WIDTH * pairs[0][0].shape[1] * (QW + QKV), 10 * MIB),
        name="weight_terms",
    )(ids, *arrays, *before)
    half = len(found) // 2
    return [
        (group[0], [tuple(group[i : i + 2]) for i in range(1, half, 2)])
        for group in (found[:half], found[half:])
    ]


def rope_tables(rows):
    half = HEAD_SIZE // 2
    position = jnp.arange(rows).astype(F32)
    inverse = ROPE_BASE ** (-jnp.arange(half).astype(F32) / half)
    angles = position[:, None] * inverse[None, :]
    cosine, sine = jnp.cos(angles), jnp.sin(angles)
    return jnp.concatenate([cosine, cosine], axis=1), jnp.concatenate([-sine, sine], axis=1)


def per_device(
    sizes,
    tokens,
    lengths,
    routes,
    cotangent,
    gain_one,
    w_query,
    key_matrix,
    value_matrix,
    w_out,
    gain_two,
    w_router,
    w_gate,
    w_up,
    w_down,
):
    ndp = sizes["dp"]
    rows = tokens.shape[0]
    local, _, width = w_gate.shape
    me_dp = lax.axis_index("dp")
    length = lengths[0]
    ids = jnp.stack([me_dp, lax.axis_index("z"), lax.axis_index("core"), length]).astype(jnp.int32)
    live = (jnp.arange(rows) < length)[:, None]
    expert_ids = jnp.arange(EXPERTS, dtype=jnp.int32)

    extra = jnp.concatenate([gain_one[:, None], gain_two[:, None], w_router], axis=1)
    extra = jnp.pad(extra, ((0, 0), (0, PAD - extra.shape[1])))
    first = jnp.concatenate([w_query, key_matrix, value_matrix, extra], axis=1)
    named = jnp.any(routes[None, :, :] == expert_ids[:, None, None], axis=2).astype(BF16)
    named = jnp.pad(named, ((0, NOTE - EXPERTS), (0, MODEL_WIDTH - rows)))
    grad_low = jnp.where(live, cotangent, jnp.zeros_like(cotangent))
    grad_low = jnp.concatenate([grad_low, named], axis=0)
    grad_near = start_dp(grad_low, ndp)

    nz = sizes["z"]
    first_z = [first] + [exchange(first, "z", nz, k) for k in range(1, nz)]
    first_block = stack_after(first_z, grad_near)
    second_z = [w_out] + [exchange(w_out, "z", nz, k) for k in range(1, nz)]
    first_near = start_dp(first_block, ndp)
    first_dp = pass_on(first_block, first_near, ndp, second_z[1:])
    packed = [pack(j, (w_gate, w_up, w_down)) for j in range(local)]
    packed = after(packed, [first_block])
    expert_mats = [lax.all_gather(p, ("z", "core"), axis=0, tiled=True) for p in packed]
    second_block = stack_after(second_z, [piece for *_, piece in first_dp[1:3]])
    second_dp = gather_direct(second_block, ndp)

    cosine, sine = rope_tables(rows)
    weights_in = gather_rows(first, first_dp, ids, sizes)
    qkv, mixed, h_one, gains, router = attend(ids, tokens, cosine, sine, weights_in, sizes)
    second_far = after([piece for *_, piece in second_dp[1:]], [mixed])
    second_dp = [(k, 0, piece) for k, piece in enumerate([second_block, *second_far])]
    grad_far = pass_on(grad_low, grad_near, ndp, second_far)
    weights_out = gather_rows(w_out, second_dp, ids, sizes)
    residual, *h_two = project(ids, tokens, mixed, gains, weights_out, sizes)
    hidden = gather_halves(h_two, ndp)
    turned = turn([mixed, h_one], [hidden[2][2]], ids, sizes)
    mixed, h_one = ([mine, exchange(other, "core", 2, 1)] for mine, other in turned)

    prev, gate_grads, sums = (), [], []
    for j in range(local):
        expert = jnp.stack([me_dp * local + j, me_dp]).astype(jnp.int32)
        *prev, grad_gate, terms = run_expert(
            j,
            j == local - 1,
            expert,
            router,
            hidden,
            grad_far,
            expert_mats[j],
            prev,
            gate_grads,
            ndp,
            [*mixed, *h_one],
        )
        gate_grads.append(grad_gate)
        sums.append(lax.psum_scatter(terms, ("z", "core"), scatter_dimension=0, tiled=True))
    outs, *backs = prev
    pairs = [tuple(backs[2 * k : 2 * k + 2]) for k in range(ndp)]
    backs = [*pairs[0], *scatter_dp(pairs, ndp)]
    (sent,) = after([outs], backs[2:])
    outs = lax.all_to_all(sent, "dp", split_axis=0, concat_axis=0, tiled=True)
    block_out = (residual + jnp.sum(outs.astype(F32), axis=0)).astype(BF16)

    grad_resid, grad_attn, grad_pre, notes = back(
        ids,
        residual,
        h_two,
        cotangent,
        gains,
        router,
        cosine,
        sine,
        qkv,
        backs,
        weights_out,
        [sent],
        sizes,
    )
    grad_tokens = tokens_back(ids, tokens, gains, grad_pre, grad_resid, weights_in, sizes)
    if not by_blocks(sizes):
        notes = split_cores(notes, ids, sizes)
        notes = notes[0], exchange(notes[1], "core", 2, 1)
    else:
        notes = notes, exchange(notes, "core", 2, 1)
    pairs = (
        mixed,
        (grad_attn, exchange(grad_attn, "core", 2, 1)),
        h_one,
        (grad_pre, exchange(grad_pre, "core", 2, 1)),
        notes,
    )
    out_terms, in_terms = weight_terms(ids, pairs, sums[:-1], sizes)
    grad_out, _ = scatter_rows(*out_terms, sizes)
    grad_first, late = scatter_rows(*in_terms, sizes, [grad_tokens])
    grad_in = grad_first[:, :QKV]
    own_rows = jnp.concatenate([w_query, key_matrix, value_matrix], axis=1)
    grad_gain_one = jnp.sum(grad_in * own_rows.astype(F32), axis=1) / gain_one.astype(F32)
    expert_sums = finish_after(sums, late[:1])
    return (
        block_out,
        grad_tokens,
        grad_gain_one,
        grad_in[:, :QW],
        grad_in[:, QW : QW + KW],
        grad_in[:, QW + KW :],
        grad_out,
        grad_first[:, QKV],
        grad_first[:, QKV + 8 : QKV + 8 + EXPERTS],
        *expert_sums,
    )


def solution(mesh):
    ndp, nf = mesh.shape["dp"], mesh.shape["fsdp"]
    sizes = {"dp": ndp, "z": nf // 2, "core": 2}
    split = Mesh(mesh.devices.reshape(ndp, nf // 2, 2), ("dp", "z", "core"))
    every = ("dp", "z", "core")
    rows = P(every, None)
    vector = P(every)
    expert = P("dp", ("z", "core"), None)

    def run(*args):
        return per_device(sizes, *args)

    return jax.shard_map(
        run,
        mesh=split,
        in_specs=(rows, vector, rows, rows, vector, rows, rows, rows, rows, vector, rows)
        + (expert,) * 3,
        out_specs=(rows, rows, vector, rows, rows, rows, rows, vector, rows) + (expert,) * 3,
        check_vma=False,
    )
```

```python
import functools

import jax
import jax.numpy as jnp
from jax import lax
from jax.experimental import pallas as pl
from jax.experimental.pallas import tpu as pltpu
from jax.sharding import Mesh
from jax.sharding import PartitionSpec as P

MODEL_WIDTH = 1536
QUERY_HEADS = 12
KEY_VALUE_HEADS = 2
HEAD_SIZE = 128
EXPERTS = 8
CAP = 160
GROUP = QUERY_HEADS // KEY_VALUE_HEADS
QW = QUERY_HEADS * HEAD_SIZE
KW = KEY_VALUE_HEADS * HEAD_SIZE
QKV = QW + 2 * KW
PAD = 128
FIRST = QKV + PAD
NOTE = 32
ROUTER = 16
EPS = 1e-06
ROPE_BASE = 1500000.0
NEG_FILL = -1e30
SCALE = HEAD_SIZE ** (-0.5)
F32 = jnp.float32
BF16 = jnp.bfloat16
TILE = 256
MIB = 1024 * 1024
HBM = pl.BlockSpec(memory_space=pltpu.HBM)
VMEM = pl.BlockSpec(memory_space=pltpu.VMEM)
SMEM = pl.BlockSpec(memory_space=pltpu.SMEM)


def nn(a, b):
    return lax.dot_general(a, b, (((1,), (0,)), ((), ())), preferred_element_type=F32)


def nt(a, b):
    return lax.dot_general(a, b, (((1,), (1,)), ((), ())), preferred_element_type=F32)


def tn(a, b):
    return lax.dot_general(a, b, (((0,), (0,)), ((), ())), preferred_element_type=F32)


def shape(dims, dtype):
    return jax.ShapeDtypeStruct(dims, dtype)


def params(mib):
    return pltpu.CompilerParams(vmem_limit_bytes=mib * MIB)


def cost(flops, data, special=0):
    return pl.CostEstimate(flops=flops, bytes_accessed=data, transcendentals=special)


def exchange(block, axis, size, step):
    return lax.ppermute(block, axis, [(i, i ^ step) for i in range(size)])


def start_dp(block, ndp):
    return [exchange(block, "dp", ndp, k) for k in ((1, 2) if ndp == 4 else range(1, ndp))]


def pass_on(block, near, ndp, before=()):
    if ndp != 4:
        return [(k, 0, piece) for k, piece in enumerate([block] + near)]
    side, up = after(near, before) if before else near
    half = block.shape[0] // 2
    return [
        (0, 0, block),
        (1, 0, side),
        (2, 0, up),
        (3, 0, exchange(side[:half], "dp", ndp, 2)),
        (3, half, exchange(up[half:], "dp", ndp, 1)),
    ]


def gather_direct(block, ndp):
    return [(k, 0, exchange(block, "dp", ndp, k) if k else block) for k in range(ndp)]


def gather_halves(halves, ndp):
    top, low = halves
    at = top.shape[0]
    if ndp != 4:
        return [
            (k, i * at, exchange(half, "dp", ndp, k) if k else half)
            for k in range(ndp)
            for i, half in enumerate(halves)
        ]
    side_top, up_low = exchange(top, "dp", ndp, 1), exchange(low, "dp", ndp, 2)
    side_low, up_top = exchange(low, "dp", ndp, 1), exchange(top, "dp", ndp, 2)
    return [
        (0, 0, top),
        (0, at, low),
        (1, 0, side_top),
        (2, at, up_low),
        (1, at, side_low),
        (2, 0, up_top),
        (3, 0, exchange(side_top, "dp", ndp, 2)),
        (3, at, exchange(up_low, "dp", ndp, 1)),
    ]


def scatter_dp(slots, ndp, before=()):
    if ndp != 4:
        whole = [jnp.concatenate(slot, axis=0) for slot in slots[1:]]
        return [exchange(part, "dp", ndp, k + 1) for k, part in enumerate(whole)]
    past = [exchange(slots[3][0], "dp", ndp, 1), exchange(slots[3][1], "dp", ndp, 2)]
    if before:
        past = after(past, before)
    add = lambda a, b: (a.astype(F32) + b.astype(F32)).astype(BF16)
    side = jnp.concatenate([slots[1][0], add(slots[1][1], past[1])], axis=0)
    up = jnp.concatenate([add(slots[2][0], past[0]), slots[2][1]], axis=0)
    return [exchange(side, "dp", ndp, 1), exchange(up, "dp", ndp, 2)]


def both_cores(pieces):
    return [
        (k, c, start, exchange(piece, "core", 2, 1) if c else piece)
        for k, start, piece in pieces
        for c in range(2)
    ]


def stack_kernel(count, *refs):
    for i in range(count):
        refs[-1][i] = refs[i][...]


def stack_after(parts, before):
    dims = (len(parts),) + parts[0].shape
    return pl.pallas_call(
        functools.partial(stack_kernel, len(parts)),
        out_shape=shape(dims, parts[0].dtype),
        in_specs=[VMEM] * len(parts) + [HBM] * len(before),
        out_specs=VMEM,
        compiler_params=params(60),
        cost_estimate=cost(0, 4 * dims[0] * dims[1] * dims[2]),
        name="stack",
    )(*parts, *before)


def pack_kernel(index, *refs):
    width = refs[0].shape[2]
    for i in range(3):
        refs[-1][:, i * width : (i + 1) * width] = refs[i][index]


def pack(index, mats):
    _, rows, width = mats[0].shape
    return pl.pallas_call(
        functools.partial(pack_kernel, index),
        out_shape=shape((rows, 3 * width), BF16),
        in_specs=[VMEM] * 3,
        out_specs=VMEM,
        compiler_params=params(60),
        name="pack",
    )(*mats)


def finish_kernel(count, *refs):
    outs = refs[-3:]
    width = outs[0].shape[2]
    for j in range(count):
        for i in range(3):
            outs[i][j] = refs[j][:, i * width : (i + 1) * width].astype(F32)


def finish_after(sums, before):
    rows, width = sums[0].shape[0], sums[0].shape[1] // 3
    return pl.pallas_call(
        functools.partial(finish_kernel, len(sums)),
        out_shape=(shape((len(sums), rows, width), F32),) * 3,
        in_specs=[VMEM] * len(sums) + [HBM] * len(before),
        out_specs=(VMEM,) * 3,
        compiler_params=params(60),
        name="finish",
    )(*sums, *before)


def after_kernel(*refs):
    pass


def after(arrays, before):
    return pl.pallas_call(
        after_kernel,
        out_shape=tuple(shape(a.shape, a.dtype) for a in arrays),
        in_specs=[HBM] * (len(arrays) + len(before)),
        out_specs=(HBM,) * len(arrays),
        input_output_aliases={i: i for i in range(len(arrays))},
        name="after",
    )(*arrays, *before)


def block_rows(sizes):
    return MODEL_WIDTH // (2 * sizes["dp"] * sizes["z"])


def by_blocks(sizes):
    return block_rows(sizes) % 16 == 0


def gather_rows(block, along_dp, ids, sizes):
    ndp, nz = sizes["dp"], sizes["z"]
    pieces = both_cores(along_dp)
    if by_blocks(sizes):
        places = tuple((k, c, start, piece.shape[0]) for k, c, start, piece in pieces)
        return places, [piece for *_, piece in pieces]
    columns = block.shape[-1]
    whole = jnp.zeros((ndp, nz, 2, block_rows(sizes), columns), BF16)
    for k, c, start, piece in pieces:
        order = ids[1] ^ jnp.arange(start, start + piece.shape[0])
        whole = whole.at[ids[0] ^ k, order, ids[2] ^ c].set(piece)
    return None, [whole.reshape(MODEL_WIDTH, columns)]


def split_cores(columns, ids, sizes):
    ndp, nz = sizes["dp"], sizes["z"]
    rows = columns.shape[0]
    blocks = columns.reshape(rows, ndp, nz, 2, block_rows(sizes))
    blocks = jnp.take(jnp.take(blocks, ids[0] ^ jnp.arange(ndp), 1), ids[1] ^ jnp.arange(nz), 2)
    halves = [lax.dynamic_index_in_dim(blocks, ids[2] ^ c, 3, keepdims=False) for c in range(2)]
    return [half.reshape(rows, MODEL_WIDTH // 2) for half in halves]


def turn_kernel(ndp, nz, count, ids, *refs):
    block = MODEL_WIDTH // (2 * ndp * nz)
    turned = refs[-1]
    for i in range(count):
        turned[...] = jnp.transpose(refs[i][...])
        for k in range(ndp):
            for z in range(nz):
                for c in range(2):
                    at = ((ids[0] ^ k) * nz + (ids[1] ^ z)) * 2 + (ids[2] ^ c)
                    place = pl.ds(pl.multiple_of(at * block, block), block)
                    dest = refs[-1 - 2 * count + 2 * i + c]
                    dest[(k * nz + z) * block : (k * nz + z + 1) * block] = turned[place, :]


def turn(arrays, before, ids, sizes):
    if not by_blocks(sizes):
        return [[half.T for half in split_cores(array, ids, sizes)] for array in arrays]
    rows = arrays[0].shape[0]
    halves = pl.pallas_call(
        functools.partial(turn_kernel, sizes["dp"], sizes["z"], len(arrays)),
        out_shape=(shape((MODEL_WIDTH // 2, rows), BF16),) * (2 * len(arrays)),
        in_specs=[SMEM] + [VMEM] * len(arrays) + [HBM] * len(before),
        out_specs=(VMEM,) * (2 * len(arrays)),
        scratch_shapes=[pltpu.VMEM((MODEL_WIDTH, rows), BF16)],
        compiler_params=params(60),
        name="turn",
    )(ids, *arrays, *before)
    return [halves[2 * i : 2 * i + 2] for i in range(len(arrays))]


def scatter_rows(own, slots, sizes, before=()):
    ndp, nz = sizes["dp"], sizes["z"]
    total = own
    for part in scatter_dp([None, *slots], ndp, before):
        total = total + part.astype(F32)
    rows = block_rows(sizes)
    blocks = [total[z * rows : (z + 1) * rows] for z in range(nz)]
    got = [exchange(blocks[z].astype(BF16), "z", nz, z) for z in range(1, nz)]
    return blocks[0], got


def load_rows(ids, ndp, nz, places, parts, dest, sem):
    if places is None:
        loads = [pltpu.make_async_copy(parts[0], dest, sem.at[0])]
        loads[0].start()
        return loads
    rows = MODEL_WIDTH // (ndp * nz * 2)
    loads = []
    for (k, c, start, count), part in zip(places, parts):
        for z in range(count):
            block = ((ids[0] ^ k) * nz + (ids[1] ^ (start + z))) * 2 + (ids[2] ^ c)
            place = pl.ds(pl.multiple_of(block * rows, rows), rows)
            copy = pltpu.make_async_copy(part.at[z], dest.at[place, :], sem.at[len(loads)])
            loads.append(copy)
    for load in loads:
        load.start()
    return loads


def start_all(pairs, sem):
    copies = [pltpu.make_async_copy(a, b, sem.at[i]) for i, (a, b) in enumerate(pairs)]
    for copy in copies:
        copy.start()
    return copies


def wait_all(copies):
    for copy in copies:
        copy.wait()


def rms_scale(rows):
    return lax.rsqrt(jnp.mean(rows * rows, axis=-1, keepdims=True) + EPS)


def norm_back(normed, row_scale, grad):
    return row_scale * (grad - normed * jnp.mean(grad * normed, axis=-1, keepdims=True))


def swapped(vals):
    return pltpu.roll(vals, HEAD_SIZE // 2, 1)


def head(h):
    return slice(h * HEAD_SIZE, (h + 1) * HEAD_SIZE)


def seen(rows, length):
    q = lax.broadcasted_iota(jnp.int32, (rows, rows), 0)
    s = lax.broadcasted_iota(jnp.int32, (rows, rows), 1)
    return (s <= q) & (s < length)


def attention_probs(query, key, visible):
    scores = jnp.where(visible, nt(query, key) * SCALE, NEG_FILL)
    expon = jnp.exp(scores - jnp.max(scores, axis=-1, keepdims=True))
    return expon / jnp.sum(expon, axis=-1, keepdims=True)


def route_softmax(router_rows, hidden):
    logits = nt(router_rows, hidden)[:EXPERTS]
    expon = jnp.exp(logits - jnp.max(logits, axis=0, keepdims=True))
    return expon / jnp.sum(expon, axis=0, keepdims=True)


def attend_kernel(ndp, nz, places, count, ids, tokens, cosine, sine, *refs):
    parts = refs[:count]
    qkv, mixed, h_one, gains, router, w, sem = refs[-7:]
    rows = tokens.shape[0]
    loads = load_rows(ids, ndp, nz, places, parts, w, sem)
    tok = tokens[...].astype(F32)
    normed = tok * rms_scale(tok)
    for load in loads:
        load.wait()
    extra = jnp.transpose(w[:, QKV:].astype(F32))
    gains[...] = extra[:8]
    router[...] = extra[2 : 2 + ROUTER].astype(BF16)
    h_one[...] = (normed * extra[0:1]).astype(BF16)
    cos, sin = cosine[...], sine[...]
    for t in range(QKV // TILE):
        pre = nn(h_one[...], w[:, t * TILE : (t + 1) * TILE])
        for i in range(TILE // HEAD_SIZE):
            part = pre[:, head(i)]
            at = t * TILE + i * HEAD_SIZE
            if at < QW + KW:
                part = part * cos + swapped(part) * sin
            qkv[:, at : at + HEAD_SIZE] = part.astype(BF16)
    visible = seen(rows, ids[3])
    for h in range(QUERY_HEADS):
        g = h // GROUP
        probs = attention_probs(qkv[:, head(h)], qkv[:, head(QUERY_HEADS + g)], visible)
        values = qkv[:, head(QUERY_HEADS + KEY_VALUE_HEADS + g)]
        mixed[:, head(h)] = nn(probs.astype(BF16), values).astype(BF16)


def attend(ids, tokens, cosine, sine, weights, before, sizes):
    places, parts = weights
    ndp, nz = sizes["dp"], sizes["z"]
    rows = tokens.shape[0]
    return pl.pallas_call(
        functools.partial(attend_kernel, ndp, nz, places, len(parts)),
        out_shape=(
            shape((rows, QKV), BF16),
            shape((rows, QW), BF16),
            shape((rows, MODEL_WIDTH), BF16),
            shape((8, MODEL_WIDTH), F32),
            shape((ROUTER, MODEL_WIDTH), BF16),
        ),
        in_specs=[SMEM, VMEM, VMEM, VMEM] + [HBM] * (len(parts) + len(before)),
        out_specs=(VMEM,) * 5,
        scratch_shapes=[
            pltpu.VMEM((MODEL_WIDTH, FIRST), BF16),
            pltpu.SemaphoreType.DMA((2 * ndp * nz,)),
        ],
        compiler_params=params(60),
        cost_estimate=cost(2 * rows * MODEL_WIDTH * QKV, 10 * MIB, 12 * rows * rows),
        name="attend",
    )(ids, tokens, cosine, sine, *parts, *before)


def project_kernel(ndp, nz, places, ids, tokens, mixed, gains, *refs):
    *parts, residual, top, low, w, sem = refs
    loads = load_rows(ids, ndp, nz, places, parts, w, sem)
    for load in loads:
        load.wait()
    for t in range(MODEL_WIDTH // TILE):
        lane = slice(t * TILE, (t + 1) * TILE)
        residual[:, lane] = tokens[:, lane].astype(F32) + nn(mixed[...], w[:, lane])
    whole = residual[...]
    h_two = (whole * rms_scale(whole) * gains[1:2]).astype(BF16)
    half = top.shape[0]
    top[...], low[...] = h_two[:half], h_two[half:]


def project(ids, tokens, mixed, gains, weights, sizes):
    places, parts = weights
    ndp, nz = sizes["dp"], sizes["z"]
    rows = tokens.shape[0]
    return pl.pallas_call(
        functools.partial(project_kernel, ndp, nz, places),
        out_shape=(shape((rows, MODEL_WIDTH), F32),)
        + (shape((rows // 2, MODEL_WIDTH), BF16),) * 2,
        in_specs=[SMEM, VMEM, VMEM, VMEM] + [HBM] * len(parts),
        out_specs=(VMEM,) * 3,
        scratch_shapes=[
            pltpu.VMEM((QW, MODEL_WIDTH), BF16),
            pltpu.SemaphoreType.DMA((2 * ndp * nz,)),
        ],
        compiler_params=params(60),
        cost_estimate=cost(2 * rows * MODEL_WIDTH * QW, 8 * MIB),
        name="project",
    )(ids, tokens, mixed, gains, *parts)


def expert_kernel(ndp, rows, width, index, last, near, far, unread, *refs):
    it = iter(refs)
    take = lambda n: [next(it) for _ in range(n)]
    (expert_ref, router_ref) = take(2)
    prev_gates = take(index)
    hid_in, cot_in = take(len(near)), take(len(far))
    (w_in,) = take(1)
    prev_in = take(2) if index else []
    take(unread)
    (out_hbm,), back_hbm = take(1), take(2 * ndp if last else 1)
    gates_ref, terms_hbm = take(2)
    hid, cot, w, x, d, ge, inner, dg, du, pick, pick_t, slot_gate, slot_dot = take(13)
    (terms_buf,) = take(1)
    prev = take(2) if index else []
    in_sem, out_sem = take(2)
    depth = MODEL_WIDTH
    tiles = depth // TILE

    loads = {}

    def load(name, source, dest):
        copy = pltpu.make_async_copy(source, dest, in_sem.at[len(loads)])
        copy.start()
        loads[name] = copy

    for i, (k, start, count) in enumerate(near):
        load(("hid", i), hid_in[i], hid.at[k, pl.ds(start, count), :])
    for i, (k, start, count) in enumerate(far):
        load(("cot", i), cot_in[i], cot.at[k, pl.ds(start, count), :])
    load("w", w_in, w)
    for i in range(len(prev)):
        load(("prev", i), prev_in[i], prev[i])

    expert, me = expert_ref[0], expert_ref[1]
    which = lax.broadcasted_iota(jnp.int32, (EXPERTS, rows), 0) == expert
    earlier = (
        (
            lax.broadcasted_iota(jnp.int32, (rows, rows), 0)
            < lax.broadcasted_iota(jnp.int32, (rows, rows), 1)
        )
        .astype(F32)
        .astype(BF16)
    )
    slot = lax.broadcasted_iota(jnp.int32, (CAP, rows), 0).astype(F32)
    for s in range(ndp):
        for i, piece in enumerate(near):
            if piece[0] == s:
                loads["hid", i].wait()
        for i, piece in enumerate(far):
            if piece[0] == s:
                loads["cot", i].wait()
        hidden = hid[s]
        probs = route_softmax(router_ref[...], hidden)
        named = cot[s, rows : rows + NOTE, :rows]
        place = nn(named, earlier)[:EXPERTS]
        named = named[:EXPERTS].astype(F32)
        named_row = jnp.sum(jnp.where(which, named, 0.0), axis=0, keepdims=True)
        gate_row = jnp.sum(jnp.where(which, probs, 0.0), axis=0, keepdims=True)
        place_row = jnp.sum(jnp.where(which, place, 0.0), axis=0, keepdims=True)
        chosen = jnp.where((slot == place_row) & (named_row > 0.5), 1.0, 0.0)
        pick[s] = chosen.astype(BF16)
        pick_t[s] = jnp.transpose(chosen).astype(BF16)
        at = pl.ds(s * CAP, CAP)
        gate = jnp.sum(chosen * gate_row, axis=1, keepdims=True)
        slot_gate[at, :] = jnp.broadcast_to(gate, (CAP, 128))
        x[at, :] = nn(pick[s], hidden).astype(BF16)
        grads = nn(pick[s], cot[s, :rows])
        d[at, :] = grads.astype(BF16)
        ge[at, :] = (gate * grads).astype(BF16)
    loads["w"].wait()

    def hidden_units(t, carry):
        at = pl.multiple_of(t * TILE, TILE)
        gate_pre = nn(x[...], w[:, pl.ds(at, TILE)])
        up_pre = nn(x[...], w[:, pl.ds(width + at, TILE)])
        grad_inner = nn(ge[...], w[:, pl.ds(2 * width + at, TILE)])
        sig = 1.0 / (1.0 + jnp.exp(-gate_pre))
        act = gate_pre * sig
        inner[:, pl.ds(at, TILE)] = (act * up_pre).astype(BF16)
        dg[:, pl.ds(at, TILE)] = (
            grad_inner * up_pre * sig * (1.0 + gate_pre * (1.0 - sig))
        ).astype(BF16)
        du[:, pl.ds(at, TILE)] = (grad_inner * act).astype(BF16)
        return carry

    lax.fori_loop(0, width // TILE, hidden_units, 0)
    slot_dot[...] = jnp.zeros_like(slot_dot)
    for i in range(len(prev)):
        loads["prev", i].wait()

    noted = (rows + NOTE) // 2

    def stores(t):
        lane = pl.ds(pl.multiple_of(t * TILE, TILE), TILE)
        copies = [(terms_buf.at[lane, :], terms_hbm.at[lane, :])]
        if not last:
            body = pl.ds(0, rows)
            copies.append((hid.at[:, :, lane], out_hbm.at[:, :, lane]))
            copies.append((cot.at[:, body, lane], back_hbm[0].at[:, body, lane]))
        else:
            for k in range(ndp):
                copies.append((hid.at[k, :, lane], out_hbm.at[me ^ k, :, lane]))
            for i in range(2 * ndp):
                body = pl.ds(0, noted if i % 2 == 0 else rows - noted)
                taken = pl.ds(i % 2 * noted, noted if i % 2 == 0 else rows - noted)
                copies.append((cot.at[i // 2, taken, lane], back_hbm[i].at[body, lane]))
        return [
            pltpu.make_async_copy(source, dest, out_sem.at[i, t])
            for i, (source, dest) in enumerate(copies)
        ]

    def features(t, carry):
        lane = pl.ds(pl.multiple_of(t * TILE, TILE), TILE)
        result = nt(inner[...], w[lane, pl.ds(2 * width, width)]).astype(BF16).astype(F32)
        partial = jnp.sum(result * d[:, lane].astype(F32), axis=1, keepdims=True)
        slot_dot[...] += jnp.broadcast_to(partial, slot_dot.shape)
        gated = (slot_gate[:, :1] * result).astype(BF16)
        grad_in = (
            nt(dg[...], w[lane, pl.ds(0, width)]) + nt(du[...], w[lane, pl.ds(width, width)])
        ).astype(BF16)
        for s in range(ndp):
            part = slice(s * CAP, (s + 1) * CAP)
            sent = nn(pick_t[s], gated[part])
            back = nn(pick_t[s], grad_in[part])
            if prev:
                sent = sent + prev[0][s, :, lane].astype(F32)
                back = back + prev[1][s, :rows, lane].astype(F32)
            hid[s, :, lane] = sent.astype(BF16)
            cot[s, :rows, lane] = back.astype(BF16)
        x_t = jnp.transpose(x[:, lane])
        terms_buf[lane, pl.ds(0, width)] = nn(x_t, dg[...]).astype(BF16)
        terms_buf[lane, pl.ds(width, width)] = nn(x_t, du[...]).astype(BF16)
        ge_t = jnp.transpose(ge[:, lane])
        terms_buf[lane, pl.ds(2 * width, width)] = nn(ge_t, inner[...]).astype(BF16)
        for store in stores(t):
            store.start()
        return carry

    lax.fori_loop(0, tiles, features, 0)
    line = lax.broadcasted_iota(jnp.int32, (NOTE, 3 * rows), 0)
    notes = []
    for s in range(ndp):
        part = slice(s * CAP, (s + 1) * CAP)
        own = jnp.sum(pick[s].astype(F32) * slot_dot[part, :1], axis=0, keepdims=True)
        gates_ref[s] = own
        if not last:
            continue
        note = jnp.zeros((NOTE, 3 * rows), F32)
        for j, row in enumerate([p[s] for p in prev_gates] + [own]):
            high = row.astype(BF16).astype(F32)
            middle = (row - high).astype(BF16).astype(F32)
            low = row - high - middle
            at = expert - index + j
            note = jnp.where(line == at, jnp.concatenate([high, middle, low], axis=1), note)
        cot[s, rows : rows + NOTE, : 3 * rows] = note.astype(BF16)
        notes.append(
            pltpu.make_async_copy(
                cot.at[s, pl.ds(rows, NOTE), :],
                back_hbm[2 * s + 1].at[pl.ds(rows - noted, NOTE), :],
                out_sem.at[4 * ndp + 1, s],
            )
        )
        notes[-1].start()
    for t in range(tiles):
        for store in stores(t):
            store.wait()
    for note in notes:
        note.wait()


def run_expert(index, last, expert, router, hidden, grads, w_all, prev, prev_gates, ndp, before):
    rows = 2 * hidden[0][2].shape[0]
    near, far = (tuple((k, at, p.shape[0]) for k, at, p in group) for group in (hidden, grads))
    width = w_all.shape[1] // 3
    slots = ndp * CAP
    depth = MODEL_WIDTH
    tiles = depth // TILE
    scratch = [
        pltpu.VMEM((ndp, rows, depth), BF16),
        pltpu.VMEM((ndp, rows + NOTE, depth), BF16),
        pltpu.VMEM((depth, 3 * width), BF16),
        pltpu.VMEM((slots, depth), BF16),
        pltpu.VMEM((slots, depth), BF16),
        pltpu.VMEM((slots, depth), BF16),
        pltpu.VMEM((slots, width), BF16),
        pltpu.VMEM((slots, width), BF16),
        pltpu.VMEM((slots, width), BF16),
        pltpu.VMEM((ndp, CAP, rows), BF16),
        pltpu.VMEM((ndp, rows, CAP), BF16),
        pltpu.VMEM((slots, 128), F32),
        pltpu.VMEM((slots, 128), F32),
        pltpu.VMEM((depth, 3 * width), BF16),
    ]
    if index:
        scratch += [
            pltpu.VMEM((ndp, rows, depth), BF16),
            pltpu.VMEM((ndp, rows + NOTE, depth), BF16),
        ]
    scratch += [
        pltpu.SemaphoreType.DMA((len(near) + len(far) + 3,)),
        pltpu.SemaphoreType.DMA((4 * ndp + 2, max(tiles, ndp))),
    ]
    sent = [shape((ndp, rows, depth), BF16), shape((ndp, rows + NOTE, depth), BF16)]
    if last:
        sent = sent[:1] + [shape(((rows + NOTE) // 2, depth), BF16)] * (2 * ndp)
    flops = 2 * slots * depth * width * 9 + 8 * ndp * CAP * rows * depth
    return pl.pallas_call(
        functools.partial(
            expert_kernel, ndp, rows, width, index, last, near, far, len(before)
        ),
        out_shape=(
            *sent,
            shape((ndp, 1, rows), F32),
            shape((depth, 3 * width), BF16),
        ),
        in_specs=[SMEM, VMEM]
        + [VMEM] * len(prev_gates)
        + [HBM] * (len(near) + len(far) + 1 + len(prev) + len(before)),
        out_specs=(HBM,) * len(sent) + (VMEM, HBM),
        scratch_shapes=scratch,
        compiler_params=params(60),
        cost_estimate=cost(flops, 40 * MIB, slots * width),
        name="expert",
    )(
        expert,
        router,
        *prev_gates,
        *(piece for *_, piece in hidden),
        *(piece for *_, piece in grads),
        w_all,
        *prev,
        *before,
    )


def back_kernel(ndp, nz, places, count, given, unread, ids, gains, router, cosine, sine, *refs):
    refs = list(refs)
    take = lambda n: [refs.pop(0) for _ in range(n)]
    data, backs, parts = take(5), take(given), take(count)
    take(unread)
    out_resid, out_attn, out_pre, notes = take(4)
    residual, top, low, grads, qkv = held = take(5)
    got = take(given)
    w, grad_mixed, grad_resid, grad_attn, grad_pre, sem, data_sem, out_sem = refs
    rows = residual.shape[0]
    fetched = start_all(list(zip(backs + data[1:3] + data[:1] + data[3:], got + held[1:3] + held[:1] + held[3:])), data_sem)
    loads = load_rows(ids, ndp, nz, places, parts, w, sem)
    wait_all(fetched[:given])
    whole = jnp.concatenate([got[0][...], got[1][...]], axis=0).astype(F32)
    for part in got[2:]:
        whole = whole + part[...].astype(F32)
    grad_h = whole[:rows]
    note = whole[rows : rows + EXPERTS, : 3 * rows]
    grad_route = note[:, :rows] + note[:, rows : 2 * rows] + note[:, 2 * rows :]
    wait_all(fetched[given : given + 4])
    hidden = jnp.concatenate([top[...], low[...]], axis=0)
    probs = route_softmax(router[...], hidden)
    grad_logits = probs * (grad_route - jnp.sum(probs * grad_route, axis=0, keepdims=True))
    grad_logits = jnp.concatenate([grad_logits, jnp.zeros_like(grad_logits)], axis=0)
    grad_logits = grad_logits.astype(BF16)
    grad_h = grad_h + tn(grad_logits, router[...])
    res = residual[...]
    scale = rms_scale(res)
    normed = res * scale
    notes[0:8] = jnp.broadcast_to(
        jnp.sum(normed * grad_h, axis=0, keepdims=True), (8, MODEL_WIDTH)
    )
    notes[8:16] = nn(grad_logits, hidden)[:EXPERTS]
    live = lax.broadcasted_iota(jnp.int32, (rows, 1), 0) < ids[3]
    final = jnp.where(live, grads[...].astype(F32), 0.0)
    total = final + norm_back(normed, scale, grad_h * gains[1:2])
    grad_resid[...] = total
    grad_attn[...] = total.astype(BF16)
    stores = start_all([(grad_attn, out_attn), (grad_resid, out_resid)], out_sem)
    wait_all(loads)
    for t in range(QW // TILE):
        lane = slice(t * TILE, (t + 1) * TILE)
        grad_mixed[:, lane] = nt(grad_attn[...], w[lane, :]).astype(BF16)
    wait_all(fetched[given + 4 :])
    visible = seen(rows, ids[3])
    cos, sin = cosine[...], sine[...]
    for g in range(KEY_VALUE_HEADS):
        key = qkv[:, head(QUERY_HEADS + g)]
        value = qkv[:, head(QUERY_HEADS + KEY_VALUE_HEADS + g)]
        grad_key = jnp.zeros((rows, HEAD_SIZE), F32)
        grad_value = jnp.zeros((rows, HEAD_SIZE), F32)
        for h in range(g * GROUP, (g + 1) * GROUP):
            query, grad = qkv[:, head(h)], grad_mixed[:, head(h)]
            probs = attention_probs(query, key, visible)
            grad_probs = nt(grad, value)
            grad_value = grad_value + tn(probs.astype(BF16), grad)
            row_dot = jnp.sum(probs * grad_probs, axis=-1, keepdims=True)
            grad_scores = (probs * (grad_probs - row_dot)).astype(BF16)
            grad_query = nn(grad_scores, key) * SCALE
            grad_key = grad_key + tn(grad_scores, query)
            grad_pre[:, head(h)] = (grad_query * cos - swapped(grad_query) * sin).astype(BF16)
        grad_key = grad_key * SCALE
        grad_pre[:, head(QUERY_HEADS + g)] = (
            grad_key * cos - swapped(grad_key) * sin
        ).astype(BF16)
        grad_pre[:, head(QUERY_HEADS + KEY_VALUE_HEADS + g)] = grad_value.astype(BF16)
    last = pltpu.make_async_copy(grad_pre, out_pre, out_sem.at[2])
    last.start()
    wait_all(stores + [last])


def back(
    ids, residual, h_two, grads, gains, router, cosine, sine, qkv, backs, weights, before, sizes
):
    ndp, nz = sizes["dp"], sizes["z"]
    places, parts = weights
    rows = residual.shape[0]
    data = [residual, *h_two, grads, qkv]
    made = [
        shape((rows, MODEL_WIDTH), F32),
        shape((rows, MODEL_WIDTH), BF16),
        shape((rows, QKV), BF16),
    ]
    room = lambda array: pltpu.VMEM(array.shape, array.dtype)
    return pl.pallas_call(
        functools.partial(
            back_kernel, ndp, nz, places, len(parts), len(backs), len(before)
        ),
        out_shape=(*made, shape((16, MODEL_WIDTH), F32)),
        in_specs=[SMEM]
        + [VMEM] * 4
        + [HBM] * (len(data) + len(backs) + len(parts) + len(before)),
        out_specs=(HBM, HBM, HBM, VMEM),
        scratch_shapes=[
            *(room(array) for array in data + backs),
            pltpu.VMEM((QW, MODEL_WIDTH), BF16),
            pltpu.VMEM((rows, QW), BF16),
            *(room(array) for array in made),
            pltpu.SemaphoreType.DMA((2 * ndp * nz,)),
            pltpu.SemaphoreType.DMA((len(data) + len(backs),)),
            pltpu.SemaphoreType.DMA((3,)),
        ],
        compiler_params=params(60),
        cost_estimate=cost(3 * rows * MODEL_WIDTH * QW, 16 * MIB, 12 * rows * rows),
        name="back",
    )(ids, gains, router, cosine, sine, *data, *backs, *parts, *before)


def tokens_back_kernel(ndp, nz, places, count, ids, tokens, gains, grad_pre, grad_resid, *refs):
    parts = refs[:count]
    grad_tokens, w, sem = refs[-3:]
    loads = load_rows(ids, ndp, nz, places, parts, w, sem)
    tok = tokens[...].astype(F32)
    scale = rms_scale(tok)
    normed = tok * scale
    for load in loads:
        load.wait()
    for t in range(MODEL_WIDTH // TILE):
        lane = slice(t * TILE, (t + 1) * TILE)
        grad_tokens[:, lane] = nt(grad_pre[...], w[lane, :QKV])
    grad_h = grad_tokens[...]
    grad_tokens[...] = grad_resid[...] + norm_back(normed, scale, grad_h * gains[0:1])


def tokens_back(ids, tokens, gains, grad_pre, grad_resid, weights, before, sizes):
    ndp, nz = sizes["dp"], sizes["z"]
    places, parts = weights
    rows = tokens.shape[0]
    return pl.pallas_call(
        functools.partial(tokens_back_kernel, ndp, nz, places, len(parts)),
        out_shape=shape((rows, MODEL_WIDTH), F32),
        in_specs=[SMEM] + [VMEM] * 4 + [HBM] * (len(parts) + len(before)),
        out_specs=VMEM,
        scratch_shapes=[
            pltpu.VMEM((MODEL_WIDTH, FIRST), BF16),
            pltpu.SemaphoreType.DMA((2 * ndp * nz,)),
        ],
        compiler_params=params(60),
        cost_estimate=cost(2 * rows * MODEL_WIDTH * QKV, 12 * MIB),
        name="tokens_back",
    )(ids, tokens, gains, grad_pre, grad_resid, *parts, *before)


def terms_kernel(ndp, nz, noted, unread, ids, *refs):
    refs = list(refs)
    take = lambda n: [refs.pop(0) for _ in range(n)]
    notes, given = take(2 if noted else 0), take(4)
    take(unread)
    count = 2 * ndp - 1
    outs, held, dests = take(count), take(4), take(count)
    note_rows, in_sem, out_sem = refs
    wait_all(start_all(list(zip(given, held)), in_sem))
    left = jnp.concatenate([held[0][...], held[1][...]], axis=1)
    right = jnp.concatenate([held[2][...], held[3][...]], axis=0)
    slot = MODEL_WIDTH // (2 * ndp)
    stores = []

    def put(lane, value):
        dests[0][:, lane] = value[:slot]
        for i in range(1, count):
            at = slot + (i - 1) * (slot // 2)
            dests[i][:, lane] = value[at : at + slot // 2].astype(BF16)
        pairs = [(dests[i].at[:, lane], outs[i].at[:, lane]) for i in range(count)]
        stores.extend(start_all(pairs, out_sem.at[len(stores) // count]))

    if noted:
        note = notes[0][...] + notes[1][...]
        block = jnp.concatenate([note, jnp.zeros((PAD - 16, note.shape[1]), F32)], axis=0)
        block = jnp.transpose(block)
    if noted == 1:
        note_rows[...] = block
        rows = MODEL_WIDTH // (2 * ndp * nz)
        taken = []
        for k in range(ndp):
            for z in range(nz):
                at = ((ids[0] ^ k) * nz + (ids[1] ^ z)) * 2 + ids[2]
                taken.append(note_rows[pl.ds(pl.multiple_of(at * rows, rows), rows), :])
        block = jnp.concatenate(taken, axis=0)
    if noted:
        put(slice(right.shape[1], right.shape[1] + PAD), block)
    for t in range(right.shape[1] // TILE):
        lane = slice(t * TILE, (t + 1) * TILE)
        put(lane, nn(left, right[:, lane]))
    wait_all(stores)


def weight_terms(ids, left, right, notes, before, sizes):
    ndp, nz = sizes["dp"], sizes["z"]
    slot = MODEL_WIDTH // (2 * ndp)
    columns = right[0].shape[1] + (PAD if notes else 0)
    noted = 0 if not notes else 1 if notes[0].shape[1] == MODEL_WIDTH else 2
    made = [shape((slot, columns), F32)] + [shape((slot // 2, columns), BF16)] * (2 * ndp - 2)
    room = lambda array: pltpu.VMEM(array.shape, array.dtype)
    arrays = [*left, *right]
    found = pl.pallas_call(
        functools.partial(terms_kernel, ndp, nz, noted, len(before)),
        out_shape=tuple(made),
        in_specs=[SMEM] + [VMEM] * len(notes) + [HBM] * (4 + len(before)),
        out_specs=(HBM,) * len(made),
        scratch_shapes=[
            *(room(array) for array in arrays + made),
            pltpu.VMEM((MODEL_WIDTH, PAD), F32),
            pltpu.SemaphoreType.DMA((4,)),
            pltpu.SemaphoreType.DMA((columns // TILE + 1, len(made))),
        ],
        compiler_params=params(60),
        cost_estimate=cost(2 * MODEL_WIDTH * left[0].shape[1] * columns, 5 * MIB),
        name="weight_terms",
    )(ids, *notes, *arrays, *before)
    return found[0], [tuple(found[i : i + 2]) for i in range(1, len(found), 2)]


def settle_kernel(count, *refs):
    own, got = refs[0], refs[1 : 1 + count]
    mats = refs[1 + count : 4 + count]
    outs, small = refs[-4:-1], refs[-1]
    total = own[...]
    for part in got:
        total = total + part[...].astype(F32)
    dot, at = jnp.zeros((total.shape[0], 1), F32), 0
    for mat, out in zip(mats, outs):
        width = mat.shape[1]
        part = total[:, at : at + width]
        out[...] = part
        dot = dot + jnp.sum(part * mat[...].astype(F32), axis=1, keepdims=True)
        at += width
    lane = lax.broadcasted_iota(jnp.int32, small.shape, 1)
    small[...] = jnp.where(lane == PAD - 1, dot, total[:, at:])


def settle(own, got, mats):
    rows = own.shape[0]
    return pl.pallas_call(
        functools.partial(settle_kernel, len(got)),
        out_shape=tuple(shape(mat.shape, F32) for mat in mats) + (shape((rows, PAD), F32),),
        in_specs=[VMEM] * (1 + len(got) + 3),
        out_specs=(VMEM,) * 4,
        compiler_params=params(60),
        name="settle",
    )(own, *got, *mats)


def rope_tables(rows):
    half = HEAD_SIZE // 2
    position = jnp.arange(rows).astype(F32)
    inverse = ROPE_BASE ** (-jnp.arange(half).astype(F32) / half)
    angles = position[:, None] * inverse[None, :]
    cosine, sine = jnp.cos(angles), jnp.sin(angles)
    return jnp.concatenate([cosine, cosine], axis=1), jnp.concatenate([-sine, sine], axis=1)


def per_device(
    sizes,
    tokens,
    lengths,
    routes,
    cotangent,
    gain_one,
    w_query,
    key_matrix,
    value_matrix,
    w_out,
    gain_two,
    w_router,
    w_gate,
    w_up,
    w_down,
):
    ndp = sizes["dp"]
    rows = tokens.shape[0]
    local, _, width = w_gate.shape
    me_dp = lax.axis_index("dp")
    length = lengths[0]
    ids = jnp.stack([me_dp, lax.axis_index("z"), lax.axis_index("core"), length]).astype(jnp.int32)
    live = (jnp.arange(rows) < length)[:, None]
    expert_ids = jnp.arange(EXPERTS, dtype=jnp.int32)

    extra = jnp.concatenate([gain_one[:, None], gain_two[:, None], w_router], axis=1)
    extra = jnp.pad(extra, ((0, 0), (0, PAD - extra.shape[1])))
    first = jnp.concatenate([w_query, key_matrix, value_matrix, extra], axis=1)
    named = jnp.any(routes[None, :, :] == expert_ids[:, None, None], axis=2).astype(BF16)
    named = jnp.pad(named, ((0, NOTE - EXPERTS), (0, MODEL_WIDTH - rows)))
    grad_low = jnp.where(live, cotangent, jnp.zeros_like(cotangent))
    grad_low = jnp.concatenate([grad_low, named], axis=0)
    (grad_low,) = after([grad_low], [first])
    grad_near = start_dp(grad_low, ndp)

    nz = sizes["z"]
    first_z = [first] + [exchange(first, "z", nz, k) for k in range(1, nz)]
    first_block = stack_after(first_z, grad_near)
    second_z = [w_out] + [exchange(w_out, "z", nz, k) for k in range(1, nz)]
    first_near = start_dp(first_block, ndp)
    first_dp = pass_on(first_block, first_near, ndp, second_z[1:])
    packed = [pack(j, (w_gate, w_up, w_down)) for j in range(local)]
    packed = after(packed, [first_block])
    expert_mats = [lax.all_gather(p, ("z", "core"), axis=0, tiled=True) for p in packed]
    second_block = stack_after(second_z, [piece for *_, piece in first_dp[1:3]])
    second_dp = gather_direct(second_block, ndp)

    cosine, sine = rope_tables(rows)
    weights_in = gather_rows(first, first_dp, ids, sizes)
    qkv, mixed, h_one, gains, router = attend(
        ids, tokens, cosine, sine, weights_in, [p for *_, p in second_dp[1:3]], sizes
    )
    second_far = after([piece for *_, piece in second_dp[1:]], [mixed])
    second_dp = [(k, 0, piece) for k, piece in enumerate([second_block, *second_far])]
    grad_far = pass_on(grad_low, grad_near, ndp, second_far)
    weights_out = gather_rows(w_out, second_dp, ids, sizes)
    residual, *h_two = project(ids, tokens, mixed, gains, weights_out, sizes)
    hidden = gather_halves(h_two, ndp)
    turned = turn([mixed, h_one], [hidden[2][2]], ids, sizes)
    mixed, h_one = ([mine, exchange(other, "core", 2, 1)] for mine, other in turned)

    prev, gate_grads, sums = (), [], []
    for j in range(local):
        expert = jnp.stack([me_dp * local + j, me_dp]).astype(jnp.int32)
        *prev, grad_gate, terms = run_expert(
            j,
            j == local - 1,
            expert,
            router,
            hidden,
            grad_far,
            expert_mats[j],
            prev,
            gate_grads,
            ndp,
            [*mixed, *h_one],
        )
        gate_grads.append(grad_gate)
        sums.append(lax.psum_scatter(terms, ("z", "core"), scatter_dimension=0, tiled=True))
    outs, *backs = prev
    pairs = [tuple(backs[2 * k : 2 * k + 2]) for k in range(ndp)]
    backs = [*pairs[0], *scatter_dp(pairs, ndp)]
    (sent,) = after([outs], backs[2:])
    outs = lax.all_to_all(sent, "dp", split_axis=0, concat_axis=0, tiled=True)
    grad_resid, grad_attn, grad_pre, notes = back(
        ids,
        residual,
        h_two,
        cotangent,
        gains,
        router,
        cosine,
        sine,
        qkv,
        backs,
        weights_out,
        [sent],
        sizes,
    )
    if not by_blocks(sizes):
        notes = split_cores(notes, ids, sizes)
        notes = notes[0], exchange(notes[1], "core", 2, 1)
    else:
        notes = notes, exchange(notes, "core", 2, 1)
    grad_attn = grad_attn, exchange(grad_attn, "core", 2, 1)
    grad_pre = grad_pre, exchange(grad_pre, "core", 2, 1)
    out_terms = weight_terms(ids, mixed, grad_attn, (), grad_pre[1:], sizes)
    in_terms = weight_terms(ids, h_one, grad_pre, notes, sums[:-1] + [out_terms[0]], sizes)
    grad_tokens = tokens_back(
        ids, tokens, gains, grad_pre[0], grad_resid, weights_in, in_terms[:1], sizes
    )
    (outs,) = after([outs], in_terms[:1])
    block_out = (residual + jnp.sum(outs.astype(F32), axis=0)).astype(BF16)
    own, late = scatter_rows(*out_terms, sizes, in_terms[:1])
    grad_out = own + sum(part.astype(F32) for part in late)
    own, got = scatter_rows(*in_terms, sizes, [grad_tokens])
    *grad_in, small = settle(own, got, (w_query, key_matrix, value_matrix))
    expert_sums = finish_after(sums, late[:1])
    return (
        block_out,
        grad_tokens,
        small[:, PAD - 1] / gain_one.astype(F32),
        *grad_in,
        grad_out,
        small[:, 0],
        small[:, 8 : 8 + EXPERTS],
        *expert_sums,
    )


def solution(mesh):
    ndp, nf = mesh.shape["dp"], mesh.shape["fsdp"]
    sizes = {"dp": ndp, "z": nf // 2, "core": 2}
    split = Mesh(mesh.devices.reshape(ndp, nf // 2, 2), ("dp", "z", "core"))
    every = ("dp", "z", "core")
    rows = P(every, None)
    vector = P(every)
    expert = P("dp", ("z", "core"), None)

    def run(*args):
        return per_device(sizes, *args)

    return jax.shard_map(
        run,
        mesh=split,
        in_specs=(rows, vector, rows, rows, vector, rows, rows, rows, rows, vector, rows)
        + (expert,) * 3,
        out_specs=(rows, rows, vector, rows, rows, rows, rows, vector, rows) + (expert,) * 3,
        check_vma=False,
    )
```

```python
import functools

import jax
import jax.numpy as jnp
from jax import lax
from jax.experimental import pallas as pl
from jax.experimental.pallas import tpu as pltpu
from jax.sharding import Mesh
from jax.sharding import PartitionSpec as P

MODEL_WIDTH = 1536
QUERY_HEADS = 12
KEY_VALUE_HEADS = 2
HEAD_SIZE = 128
EXPERTS = 8
CAP = 160
GROUP = QUERY_HEADS // KEY_VALUE_HEADS
QW = QUERY_HEADS * HEAD_SIZE
KW = KEY_VALUE_HEADS * HEAD_SIZE
QKV = QW + 2 * KW
PAD = 128
FIRST = QKV + PAD
NOTE = 32
ROUTER = 16
EPS = 1e-06
ROPE_BASE = 1500000.0
NEG_FILL = -1e30
SCALE = HEAD_SIZE ** (-0.5)
F32 = jnp.float32
BF16 = jnp.bfloat16
TILE = 256
MIB = 1024 * 1024
HBM = pl.BlockSpec(memory_space=pltpu.HBM)
VMEM = pl.BlockSpec(memory_space=pltpu.VMEM)
SMEM = pl.BlockSpec(memory_space=pltpu.SMEM)


def nn(a, b):
    return lax.dot_general(a, b, (((1,), (0,)), ((), ())), preferred_element_type=F32)


def nt(a, b):
    return lax.dot_general(a, b, (((1,), (1,)), ((), ())), preferred_element_type=F32)


def tn(a, b):
    return lax.dot_general(a, b, (((0,), (0,)), ((), ())), preferred_element_type=F32)


def shape(dims, dtype):
    return jax.ShapeDtypeStruct(dims, dtype)


def params(mib):
    return pltpu.CompilerParams(vmem_limit_bytes=mib * MIB)


def cost(flops, data, special=0):
    return pl.CostEstimate(flops=flops, bytes_accessed=data, transcendentals=special)


def exchange(block, axis, size, step):
    return lax.ppermute(block, axis, [(i, i ^ step) for i in range(size)])


def start_dp(block, ndp):
    return [exchange(block, "dp", ndp, k) for k in ((1, 2) if ndp == 4 else range(1, ndp))]


def pass_on(block, near, ndp, before=()):
    if ndp != 4:
        return [(k, 0, piece) for k, piece in enumerate([block] + near)]
    side, up = after(near, before) if before else near
    half = block.shape[0] // 2
    return [
        (0, 0, block),
        (1, 0, side),
        (2, 0, up),
        (3, 0, exchange(side[:half], "dp", ndp, 2)),
        (3, half, exchange(up[half:], "dp", ndp, 1)),
    ]


def gather_direct(block, ndp):
    return [(k, 0, exchange(block, "dp", ndp, k) if k else block) for k in range(ndp)]


def gather_halves(halves, ndp):
    top, low = halves
    at = top.shape[0]
    if ndp != 4:
        return [
            (k, i * at, exchange(half, "dp", ndp, k) if k else half)
            for k in range(ndp)
            for i, half in enumerate(halves)
        ]
    side_top, up_low = exchange(top, "dp", ndp, 1), exchange(low, "dp", ndp, 2)
    side_low, up_top = exchange(low, "dp", ndp, 1), exchange(top, "dp", ndp, 2)
    return [
        (0, 0, top),
        (0, at, low),
        (1, 0, side_top),
        (2, at, up_low),
        (1, at, side_low),
        (2, 0, up_top),
        (3, 0, exchange(side_top, "dp", ndp, 2)),
        (3, at, exchange(up_low, "dp", ndp, 1)),
    ]


def scatter_dp(slots, ndp, before=()):
    if ndp != 4:
        whole = [jnp.concatenate(slot, axis=0) for slot in slots[1:]]
        return [exchange(part, "dp", ndp, k + 1) for k, part in enumerate(whole)]
    past = [exchange(slots[3][0], "dp", ndp, 1), exchange(slots[3][1], "dp", ndp, 2)]
    if before:
        past = after(past, before)
    add = lambda a, b: (a.astype(F32) + b.astype(F32)).astype(BF16)
    side = jnp.concatenate([slots[1][0], add(slots[1][1], past[1])], axis=0)
    up = jnp.concatenate([add(slots[2][0], past[0]), slots[2][1]], axis=0)
    return [exchange(side, "dp", ndp, 1), exchange(up, "dp", ndp, 2)]


def both_cores(pieces):
    return [
        (k, c, start, exchange(piece, "core", 2, 1) if c else piece)
        for k, start, piece in pieces
        for c in range(2)
    ]


def stack_kernel(count, at, *refs):
    for i in range(count):
        refs[-2][i] = refs[i][:, :at]
        refs[-1][i] = refs[i][:, at:]


def stack_after(parts, at, before):
    rows, columns = parts[0].shape
    split = [(len(parts), rows, width) for width in (at, columns - at)]
    return pl.pallas_call(
        functools.partial(stack_kernel, len(parts), at),
        out_shape=tuple(shape(dims, parts[0].dtype) for dims in split),
        in_specs=[VMEM] * len(parts) + [HBM] * len(before),
        out_specs=(VMEM,) * 2,
        compiler_params=params(60),
        cost_estimate=cost(0, 4 * len(parts) * rows * columns),
        name="stack",
    )(*parts, *before)


def pack_kernel(index, *refs):
    width = refs[0].shape[2]
    for i in range(3):
        refs[-1][:, i * width : (i + 1) * width] = refs[i][index]


def pack(index, mats):
    _, rows, width = mats[0].shape
    return pl.pallas_call(
        functools.partial(pack_kernel, index),
        out_shape=shape((rows, 3 * width), BF16),
        in_specs=[VMEM] * 3,
        out_specs=VMEM,
        compiler_params=params(60),
        name="pack",
    )(*mats)


def finish_kernel(count, *refs):
    outs = refs[-3:]
    width = outs[0].shape[2]
    for j in range(count):
        for i in range(3):
            outs[i][j] = refs[j][:, i * width : (i + 1) * width].astype(F32)


def finish_after(sums, before):
    rows, width = sums[0].shape[0], sums[0].shape[1] // 3
    return pl.pallas_call(
        functools.partial(finish_kernel, len(sums)),
        out_shape=(shape((len(sums), rows, width), F32),) * 3,
        in_specs=[VMEM] * len(sums) + [HBM] * len(before),
        out_specs=(VMEM,) * 3,
        compiler_params=params(60),
        name="finish",
    )(*sums, *before)


def after_kernel(*refs):
    pass


def after(arrays, before):
    return pl.pallas_call(
        after_kernel,
        out_shape=tuple(shape(a.shape, a.dtype) for a in arrays),
        in_specs=[HBM] * (len(arrays) + len(before)),
        out_specs=(HBM,) * len(arrays),
        input_output_aliases={i: i for i in range(len(arrays))},
        name="after",
    )(*arrays, *before)


def block_rows(sizes):
    return MODEL_WIDTH // (2 * sizes["dp"] * sizes["z"])


def by_blocks(sizes):
    return block_rows(sizes) % 16 == 0


def gather_rows(along_dp, ids, sizes):
    ndp, nz = sizes["dp"], sizes["z"]
    pieces = both_cores(along_dp)
    if by_blocks(sizes):
        places = tuple((k, c, start, piece.shape[0]) for k, c, start, piece in pieces)
        return places, [piece for *_, piece in pieces]
    columns = pieces[0][3].shape[-1]
    whole = jnp.zeros((ndp, nz, 2, block_rows(sizes), columns), BF16)
    for k, c, start, piece in pieces:
        order = ids[1] ^ jnp.arange(start, start + piece.shape[0])
        whole = whole.at[ids[0] ^ k, order, ids[2] ^ c].set(piece)
    return None, [whole.reshape(MODEL_WIDTH, columns)]


def split_cores(columns, ids, sizes):
    ndp, nz = sizes["dp"], sizes["z"]
    rows = columns.shape[0]
    blocks = columns.reshape(rows, ndp, nz, 2, block_rows(sizes))
    blocks = jnp.take(jnp.take(blocks, ids[0] ^ jnp.arange(ndp), 1), ids[1] ^ jnp.arange(nz), 2)
    halves = [lax.dynamic_index_in_dim(blocks, ids[2] ^ c, 3, keepdims=False) for c in range(2)]
    return [half.reshape(rows, MODEL_WIDTH // 2) for half in halves]


def turn_kernel(ndp, nz, count, ids, *refs):
    block = MODEL_WIDTH // (2 * ndp * nz)
    turned = refs[-1]
    for i in range(count):
        turned[...] = jnp.transpose(refs[i][...])
        for k in range(ndp):
            for z in range(nz):
                for c in range(2):
                    at = ((ids[0] ^ k) * nz + (ids[1] ^ z)) * 2 + (ids[2] ^ c)
                    place = pl.ds(pl.multiple_of(at * block, block), block)
                    dest = refs[-1 - 2 * count + 2 * i + c]
                    dest[(k * nz + z) * block : (k * nz + z + 1) * block] = turned[place, :]


def turn(arrays, before, ids, sizes):
    if not by_blocks(sizes):
        return [[half.T for half in split_cores(array, ids, sizes)] for array in arrays]
    rows = arrays[0].shape[0]
    halves = pl.pallas_call(
        functools.partial(turn_kernel, sizes["dp"], sizes["z"], len(arrays)),
        out_shape=(shape((MODEL_WIDTH // 2, rows), BF16),) * (2 * len(arrays)),
        in_specs=[SMEM] + [VMEM] * len(arrays) + [HBM] * len(before),
        out_specs=(VMEM,) * (2 * len(arrays)),
        scratch_shapes=[pltpu.VMEM((MODEL_WIDTH, rows), BF16)],
        compiler_params=params(60),
        name="turn",
    )(ids, *arrays, *before)
    return [halves[2 * i : 2 * i + 2] for i in range(len(arrays))]


def scatter_rows(own, slots, sizes, before=()):
    ndp, nz = sizes["dp"], sizes["z"]
    total = own
    for part in scatter_dp([None, *slots], ndp, before):
        total = total + part.astype(F32)
    rows = block_rows(sizes)
    blocks = [total[z * rows : (z + 1) * rows] for z in range(nz)]
    got = [exchange(blocks[z].astype(BF16), "z", nz, z) for z in range(1, nz)]
    return blocks[0], got


def load_rows(ids, ndp, nz, places, parts, dest, sem):
    if places is None:
        loads = [pltpu.make_async_copy(parts[0], dest, sem.at[0])]
        loads[0].start()
        return loads
    rows = MODEL_WIDTH // (ndp * nz * 2)
    loads = []
    for (k, c, start, count), part in zip(places, parts):
        for z in range(count):
            block = ((ids[0] ^ k) * nz + (ids[1] ^ (start + z))) * 2 + (ids[2] ^ c)
            place = pl.ds(pl.multiple_of(block * rows, rows), rows)
            copy = pltpu.make_async_copy(part.at[z], dest.at[place, :], sem.at[len(loads)])
            loads.append(copy)
    for load in loads:
        load.start()
    return loads


def start_all(pairs, sem):
    copies = [pltpu.make_async_copy(a, b, sem.at[i]) for i, (a, b) in enumerate(pairs)]
    for copy in copies:
        copy.start()
    return copies


def wait_all(copies):
    for copy in copies:
        copy.wait()


def rms_scale(rows):
    return lax.rsqrt(jnp.mean(rows * rows, axis=-1, keepdims=True) + EPS)


def norm_back(normed, row_scale, grad):
    return row_scale * (grad - normed * jnp.mean(grad * normed, axis=-1, keepdims=True))


def swapped(vals):
    return pltpu.roll(vals, HEAD_SIZE // 2, 1)


def head(h):
    return slice(h * HEAD_SIZE, (h + 1) * HEAD_SIZE)


def seen(rows, length):
    q = lax.broadcasted_iota(jnp.int32, (rows, rows), 0)
    s = lax.broadcasted_iota(jnp.int32, (rows, rows), 1)
    return (s <= q) & (s < length)


def attention_probs(query, key, visible):
    scores = jnp.where(visible, nt(query, key) * SCALE, NEG_FILL)
    expon = jnp.exp(scores - jnp.max(scores, axis=-1, keepdims=True))
    return expon / jnp.sum(expon, axis=-1, keepdims=True)


def route_softmax(router_rows, hidden):
    logits = nt(router_rows, hidden)[:EXPERTS]
    expon = jnp.exp(logits - jnp.max(logits, axis=0, keepdims=True))
    return expon / jnp.sum(expon, axis=0, keepdims=True)


def attend_kernel(ndp, nz, places, count, ids, tokens, cosine, sine, *refs):
    parts = refs[:count]
    qkv, mixed, h_one, gains, router, w, sem = refs[-7:]
    rows = tokens.shape[0]
    loads = load_rows(ids, ndp, nz, places, parts, w, sem)
    tok = tokens[...].astype(F32)
    normed = tok * rms_scale(tok)
    for load in loads:
        load.wait()
    extra = jnp.transpose(w[:, QKV:].astype(F32))
    gains[...] = extra[:8]
    router[...] = extra[2 : 2 + ROUTER].astype(BF16)
    h_one[...] = (normed * extra[0:1]).astype(BF16)
    cos, sin = cosine[...], sine[...]
    for t in range(QKV // TILE):
        pre = nn(h_one[...], w[:, t * TILE : (t + 1) * TILE])
        for i in range(TILE // HEAD_SIZE):
            part = pre[:, head(i)]
            at = t * TILE + i * HEAD_SIZE
            if at < QW + KW:
                part = part * cos + swapped(part) * sin
            qkv[:, at : at + HEAD_SIZE] = part.astype(BF16)
    visible = seen(rows, ids[3])
    for h in range(QUERY_HEADS):
        g = h // GROUP
        probs = attention_probs(qkv[:, head(h)], qkv[:, head(QUERY_HEADS + g)], visible)
        values = qkv[:, head(QUERY_HEADS + KEY_VALUE_HEADS + g)]
        mixed[:, head(h)] = nn(probs.astype(BF16), values).astype(BF16)


def attend(ids, tokens, cosine, sine, weights, before, sizes):
    places, parts = weights
    ndp, nz = sizes["dp"], sizes["z"]
    rows = tokens.shape[0]
    return pl.pallas_call(
        functools.partial(attend_kernel, ndp, nz, places, len(parts)),
        out_shape=(
            shape((rows, QKV), BF16),
            shape((rows, QW), BF16),
            shape((rows, MODEL_WIDTH), BF16),
            shape((8, MODEL_WIDTH), F32),
            shape((ROUTER, MODEL_WIDTH), BF16),
        ),
        in_specs=[SMEM, VMEM, VMEM, VMEM] + [HBM] * (len(parts) + len(before)),
        out_specs=(VMEM,) * 5,
        scratch_shapes=[
            pltpu.VMEM((MODEL_WIDTH, FIRST), BF16),
            pltpu.SemaphoreType.DMA((2 * ndp * nz,)),
        ],
        compiler_params=params(60),
        cost_estimate=cost(2 * rows * MODEL_WIDTH * QKV, 10 * MIB, 12 * rows * rows),
        name="attend",
    )(ids, tokens, cosine, sine, *parts, *before)


def project_kernel(ndp, nz, places, ids, tokens, mixed, gains, *refs):
    *parts, residual, top, low, w, sem = refs
    loads = load_rows(ids, ndp, nz, places, parts, w, sem)
    for load in loads:
        load.wait()
    for t in range(MODEL_WIDTH // TILE):
        lane = slice(t * TILE, (t + 1) * TILE)
        residual[:, lane] = tokens[:, lane].astype(F32) + nn(mixed[...], w[:, lane])
    whole = residual[...]
    h_two = (whole * rms_scale(whole) * gains[1:2]).astype(BF16)
    half = top.shape[0]
    top[...], low[...] = h_two[:half], h_two[half:]


def project(ids, tokens, mixed, gains, weights, sizes):
    places, parts = weights
    ndp, nz = sizes["dp"], sizes["z"]
    rows = tokens.shape[0]
    return pl.pallas_call(
        functools.partial(project_kernel, ndp, nz, places),
        out_shape=(shape((rows, MODEL_WIDTH), F32),)
        + (shape((rows // 2, MODEL_WIDTH), BF16),) * 2,
        in_specs=[SMEM, VMEM, VMEM, VMEM] + [HBM] * len(parts),
        out_specs=(VMEM,) * 3,
        scratch_shapes=[
            pltpu.VMEM((QW, MODEL_WIDTH), BF16),
            pltpu.SemaphoreType.DMA((2 * ndp * nz,)),
        ],
        compiler_params=params(60),
        cost_estimate=cost(2 * rows * MODEL_WIDTH * QW, 8 * MIB),
        name="project",
    )(ids, tokens, mixed, gains, *parts)


def expert_kernel(ndp, rows, width, index, last, near, far, unread, *refs):
    it = iter(refs)
    take = lambda n: [next(it) for _ in range(n)]
    (expert_ref, router_ref) = take(2)
    prev_gates = take(index)
    hid_in, cot_in = take(len(near)), take(len(far))
    (w_in,) = take(1)
    prev_in = take(2) if index else []
    take(unread)
    (out_hbm,), back_hbm = take(1), take(2 * ndp if last else 1)
    gates_ref, terms_hbm = take(2)
    hid, cot, w, x, d, ge, inner, dg, du, pick, pick_t, slot_gate, slot_dot = take(13)
    (terms_buf,) = take(1)
    prev = take(2) if index else []
    in_sem, out_sem = take(2)
    depth = MODEL_WIDTH
    tiles = depth // TILE

    loads = {}

    def load(name, source, dest):
        copy = pltpu.make_async_copy(source, dest, in_sem.at[len(loads)])
        copy.start()
        loads[name] = copy

    for i, (k, start, count) in enumerate(near):
        load(("hid", i), hid_in[i], hid.at[k, pl.ds(start, count), :])
    for i, (k, start, count) in enumerate(far):
        load(("cot", i), cot_in[i], cot.at[k, pl.ds(start, count), :])
    load("w", w_in, w)
    for i in range(len(prev)):
        load(("prev", i), prev_in[i], prev[i])

    expert, me = expert_ref[0], expert_ref[1]
    which = lax.broadcasted_iota(jnp.int32, (EXPERTS, rows), 0) == expert
    earlier = (
        (
            lax.broadcasted_iota(jnp.int32, (rows, rows), 0)
            < lax.broadcasted_iota(jnp.int32, (rows, rows), 1)
        )
        .astype(F32)
        .astype(BF16)
    )
    slot = lax.broadcasted_iota(jnp.int32, (CAP, rows), 0).astype(F32)
    for s in range(ndp):
        for i, piece in enumerate(near):
            if piece[0] == s:
                loads["hid", i].wait()
        for i, piece in enumerate(far):
            if piece[0] == s:
                loads["cot", i].wait()
        hidden = hid[s]
        probs = route_softmax(router_ref[...], hidden)
        named = cot[s, rows : rows + NOTE, :rows]
        place = nn(named, earlier)[:EXPERTS]
        named = named[:EXPERTS].astype(F32)
        named_row = jnp.sum(jnp.where(which, named, 0.0), axis=0, keepdims=True)
        gate_row = jnp.sum(jnp.where(which, probs, 0.0), axis=0, keepdims=True)
        place_row = jnp.sum(jnp.where(which, place, 0.0), axis=0, keepdims=True)
        chosen = jnp.where((slot == place_row) & (named_row > 0.5), 1.0, 0.0)
        pick[s] = chosen.astype(BF16)
        pick_t[s] = jnp.transpose(chosen).astype(BF16)
        at = pl.ds(s * CAP, CAP)
        gate = jnp.sum(chosen * gate_row, axis=1, keepdims=True)
        slot_gate[at, :] = jnp.broadcast_to(gate, (CAP, 128))
        x[at, :] = nn(pick[s], hidden).astype(BF16)
        grads = nn(pick[s], cot[s, :rows])
        d[at, :] = grads.astype(BF16)
        ge[at, :] = (gate * grads).astype(BF16)
    loads["w"].wait()

    def hidden_units(t, carry):
        at = pl.multiple_of(t * TILE, TILE)
        gate_pre = nn(x[...], w[:, pl.ds(at, TILE)])
        up_pre = nn(x[...], w[:, pl.ds(width + at, TILE)])
        grad_inner = nn(ge[...], w[:, pl.ds(2 * width + at, TILE)])
        sig = 1.0 / (1.0 + jnp.exp(-gate_pre))
        act = gate_pre * sig
        inner[:, pl.ds(at, TILE)] = (act * up_pre).astype(BF16)
        dg[:, pl.ds(at, TILE)] = (
            grad_inner * up_pre * sig * (1.0 + gate_pre * (1.0 - sig))
        ).astype(BF16)
        du[:, pl.ds(at, TILE)] = (grad_inner * act).astype(BF16)
        return carry

    lax.fori_loop(0, width // TILE, hidden_units, 0)
    slot_dot[...] = jnp.zeros_like(slot_dot)
    for i in range(len(prev)):
        loads["prev", i].wait()

    noted = (rows + NOTE) // 2

    def stores(t):
        lane = pl.ds(pl.multiple_of(t * TILE, TILE), TILE)
        copies = [(terms_buf.at[lane, :], terms_hbm.at[lane, :])]
        if not last:
            body = pl.ds(0, rows)
            copies.append((hid.at[:, :, lane], out_hbm.at[:, :, lane]))
            copies.append((cot.at[:, body, lane], back_hbm[0].at[:, body, lane]))
        else:
            for k in range(ndp):
                copies.append((hid.at[k, :, lane], out_hbm.at[me ^ k, :, lane]))
            for i in range(2 * ndp):
                body = pl.ds(0, noted if i % 2 == 0 else rows - noted)
                taken = pl.ds(i % 2 * noted, noted if i % 2 == 0 else rows - noted)
                copies.append((cot.at[i // 2, taken, lane], back_hbm[i].at[body, lane]))
        return [
            pltpu.make_async_copy(source, dest, out_sem.at[i, t])
            for i, (source, dest) in enumerate(copies)
        ]

    def features(t, carry):
        lane = pl.ds(pl.multiple_of(t * TILE, TILE), TILE)
        result = nt(inner[...], w[lane, pl.ds(2 * width, width)]).astype(BF16).astype(F32)
        partial = jnp.sum(result * d[:, lane].astype(F32), axis=1, keepdims=True)
        slot_dot[...] += jnp.broadcast_to(partial, slot_dot.shape)
        gated = (slot_gate[:, :1] * result).astype(BF16)
        grad_in = (
            nt(dg[...], w[lane, pl.ds(0, width)]) + nt(du[...], w[lane, pl.ds(width, width)])
        ).astype(BF16)
        for s in range(ndp):
            part = slice(s * CAP, (s + 1) * CAP)
            sent = nn(pick_t[s], gated[part])
            back = nn(pick_t[s], grad_in[part])
            if prev:
                sent = sent + prev[0][s, :, lane].astype(F32)
                back = back + prev[1][s, :rows, lane].astype(F32)
            hid[s, :, lane] = sent.astype(BF16)
            cot[s, :rows, lane] = back.astype(BF16)
        x_t = jnp.transpose(x[:, lane])
        terms_buf[lane, pl.ds(0, width)] = nn(x_t, dg[...]).astype(BF16)
        terms_buf[lane, pl.ds(width, width)] = nn(x_t, du[...]).astype(BF16)
        ge_t = jnp.transpose(ge[:, lane])
        terms_buf[lane, pl.ds(2 * width, width)] = nn(ge_t, inner[...]).astype(BF16)
        for store in stores(t):
            store.start()
        return carry

    lax.fori_loop(0, tiles, features, 0)
    line = lax.broadcasted_iota(jnp.int32, (NOTE, 3 * rows), 0)
    notes = []
    for s in range(ndp):
        part = slice(s * CAP, (s + 1) * CAP)
        own = jnp.sum(pick[s].astype(F32) * slot_dot[part, :1], axis=0, keepdims=True)
        gates_ref[s] = own
        if not last:
            continue
        note = jnp.zeros((NOTE, 3 * rows), F32)
        for j, row in enumerate([p[s] for p in prev_gates] + [own]):
            high = row.astype(BF16).astype(F32)
            middle = (row - high).astype(BF16).astype(F32)
            low = row - high - middle
            at = expert - index + j
            note = jnp.where(line == at, jnp.concatenate([high, middle, low], axis=1), note)
        cot[s, rows : rows + NOTE, : 3 * rows] = note.astype(BF16)
        notes.append(
            pltpu.make_async_copy(
                cot.at[s, pl.ds(rows, NOTE), :],
                back_hbm[2 * s + 1].at[pl.ds(rows - noted, NOTE), :],
                out_sem.at[4 * ndp + 1, s],
            )
        )
        notes[-1].start()
    for t in range(tiles):
        for store in stores(t):
            store.wait()
    for note in notes:
        note.wait()


def run_expert(index, last, expert, router, hidden, grads, w_all, prev, prev_gates, ndp, before):
    rows = 2 * hidden[0][2].shape[0]
    near, far = (tuple((k, at, p.shape[0]) for k, at, p in group) for group in (hidden, grads))
    width = w_all.shape[1] // 3
    slots = ndp * CAP
    depth = MODEL_WIDTH
    tiles = depth // TILE
    scratch = [
        pltpu.VMEM((ndp, rows, depth), BF16),
        pltpu.VMEM((ndp, rows + NOTE, depth), BF16),
        pltpu.VMEM((depth, 3 * width), BF16),
        pltpu.VMEM((slots, depth), BF16),
        pltpu.VMEM((slots, depth), BF16),
        pltpu.VMEM((slots, depth), BF16),
        pltpu.VMEM((slots, width), BF16),
        pltpu.VMEM((slots, width), BF16),
        pltpu.VMEM((slots, width), BF16),
        pltpu.VMEM((ndp, CAP, rows), BF16),
        pltpu.VMEM((ndp, rows, CAP), BF16),
        pltpu.VMEM((slots, 128), F32),
        pltpu.VMEM((slots, 128), F32),
        pltpu.VMEM((depth, 3 * width), BF16),
    ]
    if index:
        scratch += [
            pltpu.VMEM((ndp, rows, depth), BF16),
            pltpu.VMEM((ndp, rows + NOTE, depth), BF16),
        ]
    scratch += [
        pltpu.SemaphoreType.DMA((len(near) + len(far) + 3,)),
        pltpu.SemaphoreType.DMA((4 * ndp + 2, max(tiles, ndp))),
    ]
    sent = [shape((ndp, rows, depth), BF16), shape((ndp, rows + NOTE, depth), BF16)]
    if last:
        sent = sent[:1] + [shape(((rows + NOTE) // 2, depth), BF16)] * (2 * ndp)
    flops = 2 * slots * depth * width * 9 + 8 * ndp * CAP * rows * depth
    return pl.pallas_call(
        functools.partial(
            expert_kernel, ndp, rows, width, index, last, near, far, len(before)
        ),
        out_shape=(
            *sent,
            shape((ndp, 1, rows), F32),
            shape((depth, 3 * width), BF16),
        ),
        in_specs=[SMEM, VMEM]
        + [VMEM] * len(prev_gates)
        + [HBM] * (len(near) + len(far) + 1 + len(prev) + len(before)),
        out_specs=(HBM,) * len(sent) + (VMEM, HBM),
        scratch_shapes=scratch,
        compiler_params=params(60),
        cost_estimate=cost(flops, 40 * MIB, slots * width),
        name="expert",
    )(
        expert,
        router,
        *prev_gates,
        *(piece for *_, piece in hidden),
        *(piece for *_, piece in grads),
        w_all,
        *prev,
        *before,
    )


def back_kernel(ndp, nz, places, count, given, unread, ids, gains, router, cosine, sine, *refs):
    refs = list(refs)
    take = lambda n: [refs.pop(0) for _ in range(n)]
    data, backs, parts = take(5), take(given), take(count)
    take(unread)
    out_resid, out_attn, out_pre, notes = take(4)
    residual, top, low, grads, qkv = held = take(5)
    got = take(given)
    w, grad_mixed, grad_resid, grad_attn, grad_pre, sem, data_sem, out_sem = refs
    rows = residual.shape[0]
    fetched = start_all(list(zip(backs + data[1:3] + data[:1] + data[3:], got + held[1:3] + held[:1] + held[3:])), data_sem)
    loads = load_rows(ids, ndp, nz, places, parts, w, sem)
    wait_all(fetched[:given])
    whole = jnp.concatenate([got[0][...], got[1][...]], axis=0).astype(F32)
    for part in got[2:]:
        whole = whole + part[...].astype(F32)
    grad_h = whole[:rows]
    note = whole[rows : rows + EXPERTS, : 3 * rows]
    grad_route = note[:, :rows] + note[:, rows : 2 * rows] + note[:, 2 * rows :]
    wait_all(fetched[given : given + 4])
    hidden = jnp.concatenate([top[...], low[...]], axis=0)
    probs = route_softmax(router[...], hidden)
    grad_logits = probs * (grad_route - jnp.sum(probs * grad_route, axis=0, keepdims=True))
    grad_logits = jnp.concatenate([grad_logits, jnp.zeros_like(grad_logits)], axis=0)
    grad_logits = grad_logits.astype(BF16)
    grad_h = grad_h + tn(grad_logits, router[...])
    res = residual[...]
    scale = rms_scale(res)
    normed = res * scale
    notes[0:8] = jnp.broadcast_to(
        jnp.sum(normed * grad_h, axis=0, keepdims=True), (8, MODEL_WIDTH)
    )
    notes[8:16] = nn(grad_logits, hidden)[:EXPERTS]
    live = lax.broadcasted_iota(jnp.int32, (rows, 1), 0) < ids[3]
    final = jnp.where(live, grads[...].astype(F32), 0.0)
    total = final + norm_back(normed, scale, grad_h * gains[1:2])
    grad_resid[...] = total
    grad_attn[...] = total.astype(BF16)
    stores = start_all([(grad_attn, out_attn), (grad_resid, out_resid)], out_sem)
    wait_all(loads)
    for t in range(QW // TILE):
        lane = slice(t * TILE, (t + 1) * TILE)
        grad_mixed[:, lane] = nt(grad_attn[...], w[lane, :]).astype(BF16)
    wait_all(fetched[given + 4 :])
    visible = seen(rows, ids[3])
    cos, sin = cosine[...], sine[...]
    for g in range(KEY_VALUE_HEADS):
        key = qkv[:, head(QUERY_HEADS + g)]
        value = qkv[:, head(QUERY_HEADS + KEY_VALUE_HEADS + g)]
        grad_key = jnp.zeros((rows, HEAD_SIZE), F32)
        grad_value = jnp.zeros((rows, HEAD_SIZE), F32)
        for h in range(g * GROUP, (g + 1) * GROUP):
            query, grad = qkv[:, head(h)], grad_mixed[:, head(h)]
            probs = attention_probs(query, key, visible)
            grad_probs = nt(grad, value)
            grad_value = grad_value + tn(probs.astype(BF16), grad)
            row_dot = jnp.sum(probs * grad_probs, axis=-1, keepdims=True)
            grad_scores = (probs * (grad_probs - row_dot)).astype(BF16)
            grad_query = nn(grad_scores, key) * SCALE
            grad_key = grad_key + tn(grad_scores, query)
            grad_pre[:, head(h)] = (grad_query * cos - swapped(grad_query) * sin).astype(BF16)
        grad_key = grad_key * SCALE
        grad_pre[:, head(QUERY_HEADS + g)] = (
            grad_key * cos - swapped(grad_key) * sin
        ).astype(BF16)
        grad_pre[:, head(QUERY_HEADS + KEY_VALUE_HEADS + g)] = grad_value.astype(BF16)
    last = pltpu.make_async_copy(grad_pre, out_pre, out_sem.at[2])
    last.start()
    wait_all(stores + [last])


def back(
    ids, residual, h_two, grads, gains, router, cosine, sine, qkv, backs, weights, before, sizes
):
    ndp, nz = sizes["dp"], sizes["z"]
    places, parts = weights
    rows = residual.shape[0]
    data = [residual, *h_two, grads, qkv]
    made = [
        shape((rows, MODEL_WIDTH), F32),
        shape((rows, MODEL_WIDTH), BF16),
        shape((rows, QKV), BF16),
    ]
    room = lambda array: pltpu.VMEM(array.shape, array.dtype)
    return pl.pallas_call(
        functools.partial(
            back_kernel, ndp, nz, places, len(parts), len(backs), len(before)
        ),
        out_shape=(*made, shape((16, MODEL_WIDTH), F32)),
        in_specs=[SMEM]
        + [VMEM] * 4
        + [HBM] * (len(data) + len(backs) + len(parts) + len(before)),
        out_specs=(HBM, HBM, HBM, VMEM),
        scratch_shapes=[
            *(room(array) for array in data + backs),
            pltpu.VMEM((QW, MODEL_WIDTH), BF16),
            pltpu.VMEM((rows, QW), BF16),
            *(room(array) for array in made),
            pltpu.SemaphoreType.DMA((2 * ndp * nz,)),
            pltpu.SemaphoreType.DMA((len(data) + len(backs),)),
            pltpu.SemaphoreType.DMA((3,)),
        ],
        compiler_params=params(60),
        cost_estimate=cost(3 * rows * MODEL_WIDTH * QW, 16 * MIB, 12 * rows * rows),
        name="back",
    )(ids, gains, router, cosine, sine, *data, *backs, *parts, *before)


def tokens_back_kernel(ndp, nz, places, count, ids, tokens, gains, grad_pre, grad_resid, *refs):
    parts = refs[:count]
    grad_tokens, w, sem = refs[-3:]
    loads = load_rows(ids, ndp, nz, places, parts, w, sem)
    tok = tokens[...].astype(F32)
    scale = rms_scale(tok)
    normed = tok * scale
    for load in loads:
        load.wait()
    for t in range(MODEL_WIDTH // TILE):
        lane = slice(t * TILE, (t + 1) * TILE)
        grad_tokens[:, lane] = nt(grad_pre[...], w[lane, :QKV])
    grad_h = grad_tokens[...]
    grad_tokens[...] = grad_resid[...] + norm_back(normed, scale, grad_h * gains[0:1])


def tokens_back(ids, tokens, gains, grad_pre, grad_resid, weights, before, sizes):
    ndp, nz = sizes["dp"], sizes["z"]
    places, parts = weights
    rows = tokens.shape[0]
    return pl.pallas_call(
        functools.partial(tokens_back_kernel, ndp, nz, places, len(parts)),
        out_shape=shape((rows, MODEL_WIDTH), F32),
        in_specs=[SMEM] + [VMEM] * 4 + [HBM] * (len(parts) + len(before)),
        out_specs=VMEM,
        scratch_shapes=[
            pltpu.VMEM((MODEL_WIDTH, FIRST), BF16),
            pltpu.SemaphoreType.DMA((2 * ndp * nz,)),
        ],
        compiler_params=params(60),
        cost_estimate=cost(2 * rows * MODEL_WIDTH * QKV, 12 * MIB),
        name="tokens_back",
    )(ids, tokens, gains, grad_pre, grad_resid, *parts, *before)


def terms_kernel(ndp, nz, noted, unread, ids, *refs):
    refs = list(refs)
    take = lambda n: [refs.pop(0) for _ in range(n)]
    notes, given = take(2 if noted else 0), take(4)
    take(unread)
    count = 2 * ndp - 1
    outs, held, dests = take(count), take(4), take(count)
    note_rows, in_sem, out_sem = refs
    wait_all(start_all(list(zip(given, held)), in_sem))
    left = jnp.concatenate([held[0][...], held[1][...]], axis=1)
    right = jnp.concatenate([held[2][...], held[3][...]], axis=0)
    slot = MODEL_WIDTH // (2 * ndp)
    stores = []

    def put(lane, value):
        dests[0][:, lane] = value[:slot]
        for i in range(1, count):
            at = slot + (i - 1) * (slot // 2)
            dests[i][:, lane] = value[at : at + slot // 2].astype(BF16)
        pairs = [(dests[i].at[:, lane], outs[i].at[:, lane]) for i in range(count)]
        stores.extend(start_all(pairs, out_sem.at[len(stores) // count]))

    if noted:
        note = notes[0][...] + notes[1][...]
        block = jnp.concatenate([note, jnp.zeros((PAD - 16, note.shape[1]), F32)], axis=0)
        block = jnp.transpose(block)
    if noted == 1:
        note_rows[...] = block
        rows = MODEL_WIDTH // (2 * ndp * nz)
        taken = []
        for k in range(ndp):
            for z in range(nz):
                at = ((ids[0] ^ k) * nz + (ids[1] ^ z)) * 2 + ids[2]
                taken.append(note_rows[pl.ds(pl.multiple_of(at * rows, rows), rows), :])
        block = jnp.concatenate(taken, axis=0)
    if noted:
        put(slice(right.shape[1], right.shape[1] + PAD), block)
    for t in range(right.shape[1] // TILE):
        lane = slice(t * TILE, (t + 1) * TILE)
        put(lane, nn(left, right[:, lane]))
    wait_all(stores)


def weight_terms(ids, left, right, notes, before, sizes):
    ndp, nz = sizes["dp"], sizes["z"]
    slot = MODEL_WIDTH // (2 * ndp)
    columns = right[0].shape[1] + (PAD if notes else 0)
    noted = 0 if not notes else 1 if notes[0].shape[1] == MODEL_WIDTH else 2
    made = [shape((slot, columns), F32)] + [shape((slot // 2, columns), BF16)] * (2 * ndp - 2)
    room = lambda array: pltpu.VMEM(array.shape, array.dtype)
    arrays = [*left, *right]
    found = pl.pallas_call(
        functools.partial(terms_kernel, ndp, nz, noted, len(before)),
        out_shape=tuple(made),
        in_specs=[SMEM] + [VMEM] * len(notes) + [HBM] * (4 + len(before)),
        out_specs=(HBM,) * len(made),
        scratch_shapes=[
            *(room(array) for array in arrays + made),
            pltpu.VMEM((MODEL_WIDTH, PAD), F32),
            pltpu.SemaphoreType.DMA((4,)),
            pltpu.SemaphoreType.DMA((columns // TILE + 1, len(made))),
        ],
        compiler_params=params(60),
        cost_estimate=cost(2 * MODEL_WIDTH * left[0].shape[1] * columns, 5 * MIB),
        name="weight_terms",
    )(ids, *notes, *arrays, *before)
    return found[0], [tuple(found[i : i + 2]) for i in range(1, len(found), 2)]


def settle_kernel(count, *refs):
    own, got = refs[0], refs[1 : 1 + count]
    mats = refs[1 + count : 4 + count]
    outs, small = refs[-4:-1], refs[-1]
    total = own[...]
    for part in got:
        total = total + part[...].astype(F32)
    dot, at = jnp.zeros((total.shape[0], 1), F32), 0
    for mat, out in zip(mats, outs):
        width = mat.shape[1]
        part = total[:, at : at + width]
        out[...] = part
        dot = dot + jnp.sum(part * mat[...].astype(F32), axis=1, keepdims=True)
        at += width
    lane = lax.broadcasted_iota(jnp.int32, small.shape, 1)
    small[...] = jnp.where(lane == PAD - 1, dot, total[:, at:])


def settle(own, got, mats):
    rows = own.shape[0]
    return pl.pallas_call(
        functools.partial(settle_kernel, len(got)),
        out_shape=tuple(shape(mat.shape, F32) for mat in mats) + (shape((rows, PAD), F32),),
        in_specs=[VMEM] * (1 + len(got) + 3),
        out_specs=(VMEM,) * 4,
        compiler_params=params(60),
        name="settle",
    )(own, *got, *mats)


def rope_tables(rows):
    half = HEAD_SIZE // 2
    position = jnp.arange(rows).astype(F32)
    inverse = ROPE_BASE ** (-jnp.arange(half).astype(F32) / half)
    angles = position[:, None] * inverse[None, :]
    cosine, sine = jnp.cos(angles), jnp.sin(angles)
    return jnp.concatenate([cosine, cosine], axis=1), jnp.concatenate([-sine, sine], axis=1)


def per_device(
    sizes,
    tokens,
    lengths,
    routes,
    cotangent,
    gain_one,
    w_query,
    key_matrix,
    value_matrix,
    w_out,
    gain_two,
    w_router,
    w_gate,
    w_up,
    w_down,
):
    ndp = sizes["dp"]
    rows = tokens.shape[0]
    local, _, width = w_gate.shape
    me_dp = lax.axis_index("dp")
    length = lengths[0]
    ids = jnp.stack([me_dp, lax.axis_index("z"), lax.axis_index("core"), length]).astype(jnp.int32)
    live = (jnp.arange(rows) < length)[:, None]
    expert_ids = jnp.arange(EXPERTS, dtype=jnp.int32)

    extra = jnp.concatenate([gain_one[:, None], gain_two[:, None], w_router], axis=1)
    extra = jnp.pad(extra, ((0, 0), (0, PAD - extra.shape[1])))
    attention = jnp.concatenate([w_query, key_matrix, value_matrix, extra, w_out], axis=1)
    named = jnp.any(routes[None, :, :] == expert_ids[:, None, None], axis=2).astype(BF16)
    named = jnp.pad(named, ((0, NOTE - EXPERTS), (0, MODEL_WIDTH - rows)))
    grad_low = jnp.where(live, cotangent, jnp.zeros_like(cotangent))
    grad_low = jnp.concatenate([grad_low, named], axis=0)
    grad_near = start_dp(grad_low, ndp)

    nz = sizes["z"]
    along_z = [attention] + [exchange(attention, "z", nz, k) for k in range(1, nz)]
    first, second = stack_after(along_z, FIRST, grad_near)
    packed = after([pack(j, (w_gate, w_up, w_down)) for j in range(local)], [first])
    expert_mats = [lax.all_gather(p, ("z", "core"), axis=0, tiled=True) for p in packed]
    first_dp = pass_on(first, start_dp(first, ndp), ndp)
    (second,) = after([second], [piece for *_, piece in first_dp[1:]])
    second_dp = gather_direct(second, ndp)

    cosine, sine = rope_tables(rows)
    weights_in = gather_rows(first_dp, ids, sizes)
    qkv, mixed, h_one, gains, router = attend(ids, tokens, cosine, sine, weights_in, [], sizes)
    second_far = after([piece for *_, piece in second_dp[1:]], [mixed])
    second_dp = [(k, 0, piece) for k, piece in enumerate([second, *second_far])]
    grad_far = pass_on(grad_low, grad_near, ndp, second_far)
    weights_out = gather_rows(second_dp, ids, sizes)
    residual, *h_two = project(ids, tokens, mixed, gains, weights_out, sizes)
    hidden = gather_halves(h_two, ndp)
    turned = turn([mixed, h_one], [hidden[2][2]], ids, sizes)
    mixed, h_one = ([mine, exchange(other, "core", 2, 1)] for mine, other in turned)

    prev, gate_grads, sums = (), [], []
    for j in range(local):
        expert = jnp.stack([me_dp * local + j, me_dp]).astype(jnp.int32)
        *prev, grad_gate, terms = run_expert(
            j,
            j == local - 1,
            expert,
            router,
            hidden,
            grad_far,
            expert_mats[j],
            prev,
            gate_grads,
            ndp,
            [*mixed, *h_one],
        )
        gate_grads.append(grad_gate)
        sums.append(lax.psum_scatter(terms, ("z", "core"), scatter_dimension=0, tiled=True))
    outs, *backs = prev
    pairs = [tuple(backs[2 * k : 2 * k + 2]) for k in range(ndp)]
    backs = [*pairs[0], *scatter_dp(pairs, ndp)]
    (sent,) = after([outs], backs[2:])
    outs = lax.all_to_all(sent, "dp", split_axis=0, concat_axis=0, tiled=True)
    grad_resid, grad_attn, grad_pre, notes = back(
        ids,
        residual,
        h_two,
        cotangent,
        gains,
        router,
        cosine,
        sine,
        qkv,
        backs,
        weights_out,
        [sent],
        sizes,
    )
    if not by_blocks(sizes):
        notes = split_cores(notes, ids, sizes)
        notes = notes[0], exchange(notes[1], "core", 2, 1)
    else:
        notes = notes, exchange(notes, "core", 2, 1)
    grad_attn = grad_attn, exchange(grad_attn, "core", 2, 1)
    grad_pre = grad_pre, exchange(grad_pre, "core", 2, 1)
    out_terms = weight_terms(ids, mixed, grad_attn, (), grad_pre[1:], sizes)
    in_terms = weight_terms(ids, h_one, grad_pre, notes, sums[:-1] + [out_terms[0]], sizes)
    grad_tokens = tokens_back(
        ids, tokens, gains, grad_pre[0], grad_resid, weights_in, in_terms[:1], sizes
    )
    (outs,) = after([outs], out_terms[:1])
    block_out = (residual + jnp.sum(outs.astype(F32), axis=0)).astype(BF16)
    own, late = scatter_rows(*out_terms, sizes, in_terms[:1])
    grad_out = own + sum(part.astype(F32) for part in late)
    own, got = scatter_rows(*in_terms, sizes, [grad_tokens])
    *grad_in, small = settle(own, got, (w_query, key_matrix, value_matrix))
    expert_sums = finish_after(sums, late[:1])
    return (
        block_out,
        grad_tokens,
        small[:, PAD - 1] / gain_one.astype(F32),
        *grad_in,
        grad_out,
        small[:, 0],
        small[:, 8 : 8 + EXPERTS],
        *expert_sums,
    )


def solution(mesh):
    ndp, nf = mesh.shape["dp"], mesh.shape["fsdp"]
    sizes = {"dp": ndp, "z": nf // 2, "core": 2}
    split = Mesh(mesh.devices.reshape(ndp, nf // 2, 2), ("dp", "z", "core"))
    every = ("dp", "z", "core")
    rows = P(every, None)
    vector = P(every)
    expert = P("dp", ("z", "core"), None)

    def run(*args):
        return per_device(sizes, *args)

    return jax.shard_map(
        run,
        mesh=split,
        in_specs=(rows, vector, rows, rows, vector, rows, rows, rows, rows, vector, rows)
        + (expert,) * 3,
        out_specs=(rows, rows, vector, rows, rows, rows, rows, vector, rows) + (expert,) * 3,
        check_vma=False,
    )
```

```python
import functools

import jax
import jax.numpy as jnp
from jax import lax
from jax.experimental import pallas as pl
from jax.experimental.pallas import tpu as pltpu
from jax.sharding import Mesh
from jax.sharding import PartitionSpec as P

MODEL_WIDTH = 1536
QUERY_HEADS = 12
KEY_VALUE_HEADS = 2
HEAD_SIZE = 128
EXPERTS = 8
CAP = 160
GROUP = QUERY_HEADS // KEY_VALUE_HEADS
QW = QUERY_HEADS * HEAD_SIZE
KW = KEY_VALUE_HEADS * HEAD_SIZE
QKV = QW + 2 * KW
PAD = 128
FIRST = QKV + PAD
NOTE = 32
ROUTER = 16
EPS = 1e-06
ROPE_BASE = 1500000.0
NEG_FILL = -1e30
SCALE = HEAD_SIZE ** (-0.5)
F32 = jnp.float32
BF16 = jnp.bfloat16
TILE = 256
ROW_TILE = 384
MIB = 1024 * 1024
HBM = pl.BlockSpec(memory_space=pltpu.HBM)
VMEM = pl.BlockSpec(memory_space=pltpu.VMEM)
SMEM = pl.BlockSpec(memory_space=pltpu.SMEM)


def nn(a, b):
    return lax.dot_general(a, b, (((1,), (0,)), ((), ())), preferred_element_type=F32)


def nt(a, b):
    return lax.dot_general(a, b, (((1,), (1,)), ((), ())), preferred_element_type=F32)


def tn(a, b):
    return lax.dot_general(a, b, (((0,), (0,)), ((), ())), preferred_element_type=F32)


def shape(dims, dtype):
    return jax.ShapeDtypeStruct(dims, dtype)


def params(mib):
    return pltpu.CompilerParams(vmem_limit_bytes=mib * MIB)


def cost(flops, data, special=0):
    return pl.CostEstimate(flops=flops, bytes_accessed=data, transcendentals=special)


def exchange(block, axis, size, step):
    return lax.ppermute(block, axis, [(i, i ^ step) for i in range(size)])


def start_dp(block, ndp):
    return [exchange(block, "dp", ndp, k) for k in ((1, 2) if ndp == 4 else range(1, ndp))]


def pass_on(block, near, ndp, before=()):
    if ndp != 4:
        return [(k, 0, piece) for k, piece in enumerate([block] + near)]
    side, up = after(near, before) if before else near
    half = block.shape[0] // 2
    return [
        (0, 0, block),
        (1, 0, side),
        (2, 0, up),
        (3, 0, exchange(side[:half], "dp", ndp, 2)),
        (3, half, exchange(up[half:], "dp", ndp, 1)),
    ]


def gather_direct(block, ndp):
    return [(k, 0, exchange(block, "dp", ndp, k) if k else block) for k in range(ndp)]


def gather_halves(halves, ndp):
    top, low = halves
    at = top.shape[0]
    if ndp != 4:
        return [
            (k, i * at, exchange(half, "dp", ndp, k) if k else half)
            for k in range(ndp)
            for i, half in enumerate(halves)
        ]
    side_top, up_low = exchange(top, "dp", ndp, 1), exchange(low, "dp", ndp, 2)
    side_low, up_top = exchange(low, "dp", ndp, 1), exchange(top, "dp", ndp, 2)
    return [
        (0, 0, top),
        (0, at, low),
        (1, 0, side_top),
        (2, at, up_low),
        (1, at, side_low),
        (2, 0, up_top),
        (3, 0, exchange(side_top, "dp", ndp, 2)),
        (3, at, exchange(up_low, "dp", ndp, 1)),
    ]


def scatter_dp(slots, ndp, before=()):
    if ndp != 4:
        whole = [jnp.concatenate(slot, axis=0) for slot in slots[1:]]
        return [exchange(part, "dp", ndp, k + 1) for k, part in enumerate(whole)]
    past = [exchange(slots[3][0], "dp", ndp, 1), exchange(slots[3][1], "dp", ndp, 2)]
    if before:
        past = after(past, before)
    add = lambda a, b: (a.astype(F32) + b.astype(F32)).astype(BF16)
    side = jnp.concatenate([slots[1][0], add(slots[1][1], past[1])], axis=0)
    up = jnp.concatenate([add(slots[2][0], past[0]), slots[2][1]], axis=0)
    return [exchange(side, "dp", ndp, 1), exchange(up, "dp", ndp, 2)]


def both_cores(pieces):
    return [
        (k, c, start, exchange(piece, "core", 2, 1) if c else piece)
        for k, start, piece in pieces
        for c in range(2)
    ]


def stack_kernel(count, *refs):
    for i in range(count):
        refs[-1][i] = refs[i][...]


def stack_after(parts, before):
    dims = (len(parts),) + parts[0].shape
    return pl.pallas_call(
        functools.partial(stack_kernel, len(parts)),
        out_shape=shape(dims, parts[0].dtype),
        in_specs=[VMEM] * len(parts) + [HBM] * len(before),
        out_specs=VMEM,
        compiler_params=params(60),
        cost_estimate=cost(0, 4 * dims[0] * dims[1] * dims[2]),
        name="stack",
    )(*parts, *before)


def pack_kernel(index, *refs):
    width = refs[0].shape[2]
    for i in range(3):
        refs[-1][:, i * width : (i + 1) * width] = refs[i][index]


def pack(index, mats):
    _, rows, width = mats[0].shape
    return pl.pallas_call(
        functools.partial(pack_kernel, index),
        out_shape=shape((rows, 3 * width), BF16),
        in_specs=[VMEM] * 3,
        out_specs=VMEM,
        compiler_params=params(60),
        name="pack",
    )(*mats)


def finish_kernel(count, *refs):
    outs = refs[-3:]
    width = outs[0].shape[2]
    for j in range(count):
        for i in range(3):
            outs[i][j] = refs[j][:, i * width : (i + 1) * width].astype(F32)


def finish_after(sums, before):
    rows, width = sums[0].shape[0], sums[0].shape[1] // 3
    return pl.pallas_call(
        functools.partial(finish_kernel, len(sums)),
        out_shape=(shape((len(sums), rows, width), F32),) * 3,
        in_specs=[VMEM] * len(sums) + [HBM] * len(before),
        out_specs=(VMEM,) * 3,
        compiler_params=params(60),
        name="finish",
    )(*sums, *before)


def after_kernel(*refs):
    pass


def after(arrays, before):
    return pl.pallas_call(
        after_kernel,
        out_shape=tuple(shape(a.shape, a.dtype) for a in arrays),
        in_specs=[HBM] * (len(arrays) + len(before)),
        out_specs=(HBM,) * len(arrays),
        input_output_aliases={i: i for i in range(len(arrays))},
        name="after",
    )(*arrays, *before)


def block_rows(sizes):
    return MODEL_WIDTH // (2 * sizes["dp"] * sizes["z"])


def by_blocks(sizes):
    return block_rows(sizes) % 16 == 0


def gather_rows(along_dp, turned, ids, sizes):
    ndp, nz = sizes["dp"], sizes["z"]
    pieces = both_cores(along_dp)
    if by_blocks(sizes):
        places = tuple((k, c, start, piece.shape[0], turned) for k, c, start, piece in pieces)
        return places, [piece for *_, piece in pieces]
    columns = pieces[0][3].shape[-1]
    whole = jnp.zeros((ndp, nz, 2, block_rows(sizes), columns), BF16)
    for k, c, start, piece in pieces:
        order = (ids[1] if turned else 0) ^ jnp.arange(start, start + piece.shape[0])
        whole = whole.at[ids[0] ^ k, order, ids[2] ^ c].set(piece)
    return None, [whole.reshape(MODEL_WIDTH, columns)]


def split_cores(columns, ids, sizes):
    ndp, nz = sizes["dp"], sizes["z"]
    rows = columns.shape[0]
    blocks = columns.reshape(rows, ndp, nz, 2, block_rows(sizes))
    blocks = jnp.take(jnp.take(blocks, ids[0] ^ jnp.arange(ndp), 1), ids[1] ^ jnp.arange(nz), 2)
    halves = [lax.dynamic_index_in_dim(blocks, ids[2] ^ c, 3, keepdims=False) for c in range(2)]
    return [half.reshape(rows, MODEL_WIDTH // 2) for half in halves]


def turn_kernel(ndp, nz, count, ids, *refs):
    block = MODEL_WIDTH // (2 * ndp * nz)
    turned = refs[-1]
    for i in range(count):
        turned[...] = jnp.transpose(refs[i][...])
        for k in range(ndp):
            for z in range(nz):
                for c in range(2):
                    at = ((ids[0] ^ k) * nz + (ids[1] ^ z)) * 2 + (ids[2] ^ c)
                    place = pl.ds(pl.multiple_of(at * block, block), block)
                    dest = refs[-1 - 2 * count + 2 * i + c]
                    dest[(k * nz + z) * block : (k * nz + z + 1) * block] = turned[place, :]


def turn(arrays, before, ids, sizes):
    if not by_blocks(sizes):
        return [[half.T for half in split_cores(array, ids, sizes)] for array in arrays]
    rows = arrays[0].shape[0]
    halves = pl.pallas_call(
        functools.partial(turn_kernel, sizes["dp"], sizes["z"], len(arrays)),
        out_shape=(shape((MODEL_WIDTH // 2, rows), BF16),) * (2 * len(arrays)),
        in_specs=[SMEM] + [VMEM] * len(arrays) + [HBM] * len(before),
        out_specs=(VMEM,) * (2 * len(arrays)),
        scratch_shapes=[pltpu.VMEM((MODEL_WIDTH, rows), BF16)],
        compiler_params=params(60),
        name="turn",
    )(ids, *arrays, *before)
    return [halves[2 * i : 2 * i + 2] for i in range(len(arrays))]


def scatter_rows(own, slots, sizes, before=(), last=()):
    ndp, nz = sizes["dp"], sizes["z"]
    total = own
    for part in scatter_dp([None, *slots], ndp, before):
        total = total + part.astype(F32)
    rows = block_rows(sizes)
    blocks = [total[z * rows : (z + 1) * rows] for z in range(nz)]
    sent = [blocks[z].astype(BF16) for z in range(1, nz)]
    sent = after(sent, last) if last else sent
    return blocks[0], [exchange(part, "z", nz, z + 1) for z, part in enumerate(sent)]


def load_rows(ids, ndp, nz, places, parts, dest, sem):
    if places is None:
        loads = [pltpu.make_async_copy(parts[0], dest, sem.at[0])]
        loads[0].start()
        return loads
    rows = MODEL_WIDTH // (ndp * nz * 2)
    loads = []
    for (k, c, start, count, turned), part in zip(places, parts):
        for z in range(count):
            at_z = ids[1] ^ (start + z) if turned else start + z
            block = ((ids[0] ^ k) * nz + at_z) * 2 + (ids[2] ^ c)
            place = pl.ds(pl.multiple_of(block * rows, rows), rows)
            copy = pltpu.make_async_copy(part.at[z], dest.at[place, :], sem.at[len(loads)])
            loads.append(copy)
    for load in loads:
        load.start()
    return loads


def start_all(pairs, sem):
    copies = [pltpu.make_async_copy(a, b, sem.at[i]) for i, (a, b) in enumerate(pairs)]
    for copy in copies:
        copy.start()
    return copies


def wait_all(copies):
    for copy in copies:
        copy.wait()


def rms_scale(rows):
    return lax.rsqrt(jnp.mean(rows * rows, axis=-1, keepdims=True) + EPS)


def norm_back(normed, row_scale, grad):
    return row_scale * (grad - normed * jnp.mean(grad * normed, axis=-1, keepdims=True))


def swapped(vals):
    return pltpu.roll(vals, HEAD_SIZE // 2, 1)


def head(h):
    return slice(h * HEAD_SIZE, (h + 1) * HEAD_SIZE)


def seen(rows, length):
    q = lax.broadcasted_iota(jnp.int32, (rows, rows), 0)
    s = lax.broadcasted_iota(jnp.int32, (rows, rows), 1)
    return (s <= q) & (s < length)


def attention_probs(query, key, visible):
    scores = jnp.where(visible, nt(query, key) * SCALE, NEG_FILL)
    expon = jnp.exp(scores - jnp.max(scores, axis=-1, keepdims=True))
    return expon / jnp.sum(expon, axis=-1, keepdims=True)


def route_softmax(router_rows, hidden):
    logits = nt(router_rows, hidden)[:EXPERTS]
    expon = jnp.exp(logits - jnp.max(logits, axis=0, keepdims=True))
    return expon / jnp.sum(expon, axis=0, keepdims=True)


def attend_kernel(ndp, nz, places, count, ids, tokens, cosine, sine, *refs):
    parts = refs[:count]
    qkv, mixed, h_one, gains, router, w, sem = refs[-7:]
    rows = tokens.shape[0]
    loads = load_rows(ids, ndp, nz, places, parts, w, sem)
    tok = tokens[...].astype(F32)
    normed = tok * rms_scale(tok)
    for load in loads:
        load.wait()
    extra = jnp.transpose(w[:, QKV:].astype(F32))
    gains[...] = extra[:8]
    router[...] = extra[2 : 2 + ROUTER].astype(BF16)
    h_one[...] = (normed * extra[0:1]).astype(BF16)
    cos, sin = cosine[...], sine[...]
    for t in range(QKV // TILE):
        pre = nn(h_one[...], w[:, t * TILE : (t + 1) * TILE])
        for i in range(TILE // HEAD_SIZE):
            part = pre[:, head(i)]
            at = t * TILE + i * HEAD_SIZE
            if at < QW + KW:
                part = part * cos + swapped(part) * sin
            qkv[:, at : at + HEAD_SIZE] = part.astype(BF16)
    visible = seen(rows, ids[3])
    for h in range(QUERY_HEADS):
        g = h // GROUP
        probs = attention_probs(qkv[:, head(h)], qkv[:, head(QUERY_HEADS + g)], visible)
        values = qkv[:, head(QUERY_HEADS + KEY_VALUE_HEADS + g)]
        mixed[:, head(h)] = nn(probs.astype(BF16), values).astype(BF16)


def attend(ids, tokens, cosine, sine, weights, before, sizes):
    places, parts = weights
    ndp, nz = sizes["dp"], sizes["z"]
    rows = tokens.shape[0]
    return pl.pallas_call(
        functools.partial(attend_kernel, ndp, nz, places, len(parts)),
        out_shape=(
            shape((rows, QKV), BF16),
            shape((rows, QW), BF16),
            shape((rows, MODEL_WIDTH), BF16),
            shape((8, MODEL_WIDTH), F32),
            shape((ROUTER, MODEL_WIDTH), BF16),
        ),
        in_specs=[SMEM, VMEM, VMEM, VMEM] + [HBM] * (len(parts) + len(before)),
        out_specs=(VMEM,) * 5,
        scratch_shapes=[
            pltpu.VMEM((MODEL_WIDTH, FIRST), BF16),
            pltpu.SemaphoreType.DMA((2 * ndp * nz,)),
        ],
        compiler_params=params(60),
        cost_estimate=cost(2 * rows * MODEL_WIDTH * QKV, 10 * MIB, 12 * rows * rows),
        name="attend",
    )(ids, tokens, cosine, sine, *parts, *before)


def project_kernel(ndp, nz, places, ids, tokens, mixed, gains, *refs):
    *parts, residual, top, low, w, sem = refs
    loads = load_rows(ids, ndp, nz, places, parts, w, sem)
    for load in loads:
        load.wait()
    for t in range(MODEL_WIDTH // TILE):
        lane = slice(t * TILE, (t + 1) * TILE)
        residual[:, lane] = tokens[:, lane].astype(F32) + nn(mixed[...], w[:, lane])
    whole = residual[...]
    h_two = (whole * rms_scale(whole) * gains[1:2]).astype(BF16)
    half = top.shape[0]
    top[...], low[...] = h_two[:half], h_two[half:]


def project(ids, tokens, mixed, gains, weights, sizes):
    places, parts = weights
    ndp, nz = sizes["dp"], sizes["z"]
    rows = tokens.shape[0]
    return pl.pallas_call(
        functools.partial(project_kernel, ndp, nz, places),
        out_shape=(shape((rows, MODEL_WIDTH), F32),)
        + (shape((rows // 2, MODEL_WIDTH), BF16),) * 2,
        in_specs=[SMEM, VMEM, VMEM, VMEM] + [HBM] * len(parts),
        out_specs=(VMEM,) * 3,
        scratch_shapes=[
            pltpu.VMEM((QW, MODEL_WIDTH), BF16),
            pltpu.SemaphoreType.DMA((2 * ndp * nz,)),
        ],
        compiler_params=params(60),
        cost_estimate=cost(2 * rows * MODEL_WIDTH * QW, 8 * MIB),
        name="project",
    )(ids, tokens, mixed, gains, *parts)


def expert_kernel(ndp, rows, width, index, last, near, far, unread, *refs):
    it = iter(refs)
    take = lambda n: [next(it) for _ in range(n)]
    (expert_ref, router_ref) = take(2)
    prev_gates = take(index)
    hid_in, cot_in = take(len(near)), take(len(far))
    (w_in,) = take(1)
    prev_in = take(2) if index else []
    take(unread)
    (out_hbm,), back_hbm = take(1), take(2 * ndp if last else 1)
    gates_ref, *terms_hbm = take(3 if last else 2)
    hid, cot, w, x, d, ge, inner, dg, du, pick, pick_t, slot_gate, slot_dot = take(13)
    (terms_buf,) = take(1)
    prev = take(2) if index else []
    in_sem, out_sem = take(2)
    depth = MODEL_WIDTH
    tiles = depth // ROW_TILE

    loads = {}

    def load(name, source, dest):
        copy = pltpu.make_async_copy(source, dest, in_sem.at[len(loads)])
        copy.start()
        loads[name] = copy

    for i, (k, start, count) in enumerate(near):
        load(("hid", i), hid_in[i], hid.at[k, pl.ds(start, count), :])
    for i, (k, start, count) in enumerate(far):
        load(("cot", i), cot_in[i], cot.at[k, pl.ds(start, count), :])
    load("w", w_in, w)
    for i in range(len(prev)):
        load(("prev", i), prev_in[i], prev[i])

    expert, me, core = expert_ref[0], expert_ref[1], expert_ref[2]
    which = lax.broadcasted_iota(jnp.int32, (EXPERTS, rows), 0) == expert
    earlier = (
        (
            lax.broadcasted_iota(jnp.int32, (rows, rows), 0)
            < lax.broadcasted_iota(jnp.int32, (rows, rows), 1)
        )
        .astype(F32)
        .astype(BF16)
    )
    slot = lax.broadcasted_iota(jnp.int32, (CAP, rows), 0).astype(F32)
    for s in range(ndp):
        for i, piece in enumerate(near):
            if piece[0] == s:
                loads["hid", i].wait()
        for i, piece in enumerate(far):
            if piece[0] == s:
                loads["cot", i].wait()
        hidden = hid[s]
        probs = route_softmax(router_ref[...], hidden)
        named = cot[s, rows : rows + NOTE, :rows]
        place = nn(named, earlier)[:EXPERTS]
        named = named[:EXPERTS].astype(F32)
        named_row = jnp.sum(jnp.where(which, named, 0.0), axis=0, keepdims=True)
        gate_row = jnp.sum(jnp.where(which, probs, 0.0), axis=0, keepdims=True)
        place_row = jnp.sum(jnp.where(which, place, 0.0), axis=0, keepdims=True)
        chosen = jnp.where((slot == place_row) & (named_row > 0.5), 1.0, 0.0)
        pick[s] = chosen.astype(BF16)
        pick_t[s] = jnp.transpose(chosen).astype(BF16)
        at = pl.ds(s * CAP, CAP)
        gate = jnp.sum(chosen * gate_row, axis=1, keepdims=True)
        slot_gate[at, :] = jnp.broadcast_to(gate, (CAP, 128))
        x[at, :] = nn(pick[s], hidden).astype(BF16)
        grads = nn(pick[s], cot[s, :rows])
        d[at, :] = grads.astype(BF16)
        ge[at, :] = (gate * grads).astype(BF16)
    loads["w"].wait()

    def hidden_units(t, carry):
        at = pl.multiple_of(t * TILE, TILE)
        gate_pre = nn(x[...], w[:, pl.ds(at, TILE)])
        up_pre = nn(x[...], w[:, pl.ds(width + at, TILE)])
        grad_inner = nn(ge[...], w[:, pl.ds(2 * width + at, TILE)])
        sig = 1.0 / (1.0 + jnp.exp(-gate_pre))
        act = gate_pre * sig
        inner[:, pl.ds(at, TILE)] = (act * up_pre).astype(BF16)
        dg[:, pl.ds(at, TILE)] = (
            grad_inner * up_pre * sig * (1.0 + gate_pre * (1.0 - sig))
        ).astype(BF16)
        du[:, pl.ds(at, TILE)] = (grad_inner * act).astype(BF16)
        return carry

    lax.fori_loop(0, width // TILE, hidden_units, 0)
    slot_dot[...] = jnp.zeros_like(slot_dot)
    for i in range(len(prev)):
        loads["prev", i].wait()

    noted = (rows + NOTE) // 2

    def stores(t):
        lane = pl.ds(pl.multiple_of(t * ROW_TILE, ROW_TILE), ROW_TILE)
        copies = []
        if not last:
            copies.append((terms_buf.at[lane, :], terms_hbm[0].at[lane, :]))
        else:
            block = terms_hbm[0].shape[1]
            per_tile = ROW_TILE // (2 * block)
            for i in range(per_tile):
                z = t * per_tile + i
                for c in range(2):
                    at = pl.multiple_of((z * 2 + (core ^ c)) * block, block)
                    copies.append((terms_buf.at[pl.ds(at, block), :], terms_hbm[c].at[z]))
        if not last:
            body = pl.ds(0, rows)
            copies.append((hid.at[:, :, lane], out_hbm.at[:, :, lane]))
            copies.append((cot.at[:, body, lane], back_hbm[0].at[:, body, lane]))
        else:
            for k in range(ndp):
                copies.append((hid.at[k, :, lane], out_hbm.at[me ^ k, :, lane]))
            for i in range(2 * ndp):
                body = pl.ds(0, noted if i % 2 == 0 else rows - noted)
                taken = pl.ds(i % 2 * noted, noted if i % 2 == 0 else rows - noted)
                copies.append((cot.at[i // 2, taken, lane], back_hbm[i].at[body, lane]))
        return [
            pltpu.make_async_copy(source, dest, out_sem.at[i, t])
            for i, (source, dest) in enumerate(copies)
        ]

    def features(t, carry):
        lane = pl.ds(pl.multiple_of(t * ROW_TILE, ROW_TILE), ROW_TILE)
        result = nt(inner[...], w[lane, pl.ds(2 * width, width)]).astype(BF16).astype(F32)
        partial = jnp.sum(result * d[:, lane].astype(F32), axis=1, keepdims=True)
        slot_dot[...] += jnp.broadcast_to(partial, slot_dot.shape)
        gated = (slot_gate[:, :1] * result).astype(BF16)
        grad_in = (
            nt(dg[...], w[lane, pl.ds(0, width)]) + nt(du[...], w[lane, pl.ds(width, width)])
        ).astype(BF16)
        for s in range(ndp):
            part = slice(s * CAP, (s + 1) * CAP)
            sent = nn(pick_t[s], gated[part])
            back = nn(pick_t[s], grad_in[part])
            if prev:
                sent = sent + prev[0][s, :, lane].astype(F32)
                back = back + prev[1][s, :rows, lane].astype(F32)
            hid[s, :, lane] = sent.astype(BF16)
            cot[s, :rows, lane] = back.astype(BF16)
        x_t = jnp.transpose(x[:, lane])
        terms_buf[lane, pl.ds(0, width)] = nn(x_t, dg[...]).astype(BF16)
        terms_buf[lane, pl.ds(width, width)] = nn(x_t, du[...]).astype(BF16)
        ge_t = jnp.transpose(ge[:, lane])
        terms_buf[lane, pl.ds(2 * width, width)] = nn(ge_t, inner[...]).astype(BF16)
        for store in stores(t):
            store.start()
        return carry

    lax.fori_loop(0, tiles, features, 0)
    line = lax.broadcasted_iota(jnp.int32, (NOTE, 3 * rows), 0)
    notes = []
    for s in range(ndp):
        part = slice(s * CAP, (s + 1) * CAP)
        own = jnp.sum(pick[s].astype(F32) * slot_dot[part, :1], axis=0, keepdims=True)
        gates_ref[s] = own
        if not last:
            continue
        note = jnp.zeros((NOTE, 3 * rows), F32)
        for j, row in enumerate([p[s] for p in prev_gates] + [own]):
            high = row.astype(BF16).astype(F32)
            middle = (row - high).astype(BF16).astype(F32)
            low = row - high - middle
            at = expert - index + j
            note = jnp.where(line == at, jnp.concatenate([high, middle, low], axis=1), note)
        cot[s, rows : rows + NOTE, : 3 * rows] = note.astype(BF16)
        notes.append(
            pltpu.make_async_copy(
                cot.at[s, pl.ds(rows, NOTE), :],
                back_hbm[2 * s + 1].at[pl.ds(rows - noted, NOTE), :],
                out_sem.at[out_sem.shape[0] - 1, s],
            )
        )
        notes[-1].start()
    for t in range(tiles):
        for store in stores(t):
            store.wait()
    for note in notes:
        note.wait()


def run_expert(index, last, expert, router, hidden, grads, w_all, prev, prev_gates, ndp, block, before):
    rows = 2 * hidden[0][2].shape[0]
    near, far = (tuple((k, at, p.shape[0]) for k, at, p in group) for group in (hidden, grads))
    width = w_all.shape[1] // 3
    slots = ndp * CAP
    depth = MODEL_WIDTH
    tiles = depth // ROW_TILE
    per_tile = ROW_TILE // block
    scratch = [
        pltpu.VMEM((ndp, rows, depth), BF16),
        pltpu.VMEM((ndp, rows + NOTE, depth), BF16),
        pltpu.VMEM((depth, 3 * width), BF16),
        pltpu.VMEM((slots, depth), BF16),
        pltpu.VMEM((slots, depth), BF16),
        pltpu.VMEM((slots, depth), BF16),
        pltpu.VMEM((slots, width), BF16),
        pltpu.VMEM((slots, width), BF16),
        pltpu.VMEM((slots, width), BF16),
        pltpu.VMEM((ndp, CAP, rows), BF16),
        pltpu.VMEM((ndp, rows, CAP), BF16),
        pltpu.VMEM((slots, 128), F32),
        pltpu.VMEM((slots, 128), F32),
        pltpu.VMEM((depth, 3 * width), BF16),
    ]
    if index:
        scratch += [
            pltpu.VMEM((ndp, rows, depth), BF16),
            pltpu.VMEM((ndp, rows + NOTE, depth), BF16),
        ]
    scratch += [
        pltpu.SemaphoreType.DMA((len(near) + len(far) + 3,)),
        pltpu.SemaphoreType.DMA((3 * ndp + 2 + per_tile, max(tiles, ndp))),
    ]
    made = [shape((depth, 3 * width), BF16)]
    sent = [shape((ndp, rows, depth), BF16), shape((ndp, rows + NOTE, depth), BF16)]
    if last:
        made = [shape((depth // (2 * block), block, 3 * width), BF16)] * 2
        sent = sent[:1] + [shape(((rows + NOTE) // 2, depth), BF16)] * (2 * ndp)
    flops = 2 * slots * depth * width * 9 + 8 * ndp * CAP * rows * depth
    return pl.pallas_call(
        functools.partial(
            expert_kernel, ndp, rows, width, index, last, near, far, len(before)
        ),
        out_shape=(
            *sent,
            shape((ndp, 1, rows), F32),
            *made,
        ),
        in_specs=[SMEM, VMEM]
        + [VMEM] * len(prev_gates)
        + [HBM] * (len(near) + len(far) + 1 + len(prev) + len(before)),
        out_specs=(HBM,) * len(sent) + (VMEM,) + (HBM,) * len(made),
        scratch_shapes=scratch,
        compiler_params=params(60),
        cost_estimate=cost(flops, 40 * MIB, slots * width),
        name="expert",
    )(
        expert,
        router,
        *prev_gates,
        *(piece for *_, piece in hidden),
        *(piece for *_, piece in grads),
        w_all,
        *prev,
        *before,
    )


def back_kernel(ndp, nz, places, count, given, unread, ids, gains, router, cosine, sine, *refs):
    refs = list(refs)
    take = lambda n: [refs.pop(0) for _ in range(n)]
    data, backs, parts = take(5), take(given), take(count)
    take(unread)
    out_resid, out_attn, out_pre, notes = take(4)
    residual, top, low, grads, qkv = held = take(5)
    got = take(given)
    w, grad_mixed, grad_resid, grad_attn, grad_pre, sem, data_sem, out_sem = refs
    rows = residual.shape[0]
    fetched = start_all(list(zip(backs + data[1:3] + data[:1] + data[3:], got + held[1:3] + held[:1] + held[3:])), data_sem)
    loads = load_rows(ids, ndp, nz, places, parts, w, sem)
    wait_all(fetched[:given])
    whole = jnp.concatenate([got[0][...], got[1][...]], axis=0).astype(F32)
    for part in got[2:]:
        whole = whole + part[...].astype(F32)
    grad_h = whole[:rows]
    note = whole[rows : rows + EXPERTS, : 3 * rows]
    grad_route = note[:, :rows] + note[:, rows : 2 * rows] + note[:, 2 * rows :]
    wait_all(fetched[given : given + 4])
    hidden = jnp.concatenate([top[...], low[...]], axis=0)
    probs = route_softmax(router[...], hidden)
    grad_logits = probs * (grad_route - jnp.sum(probs * grad_route, axis=0, keepdims=True))
    grad_logits = jnp.concatenate([grad_logits, jnp.zeros_like(grad_logits)], axis=0)
    grad_logits = grad_logits.astype(BF16)
    grad_h = grad_h + tn(grad_logits, router[...])
    res = residual[...]
    scale = rms_scale(res)
    normed = res * scale
    notes[0:8] = jnp.broadcast_to(
        jnp.sum(normed * grad_h, axis=0, keepdims=True), (8, MODEL_WIDTH)
    )
    notes[8:16] = nn(grad_logits, hidden)[:EXPERTS]
    live = lax.broadcasted_iota(jnp.int32, (rows, 1), 0) < ids[3]
    final = jnp.where(live, grads[...].astype(F32), 0.0)
    total = final + norm_back(normed, scale, grad_h * gains[1:2])
    grad_resid[...] = total
    grad_attn[...] = total.astype(BF16)
    stores = start_all([(grad_attn, out_attn), (grad_resid, out_resid)], out_sem)
    wait_all(loads)
    for t in range(QW // TILE):
        lane = slice(t * TILE, (t + 1) * TILE)
        grad_mixed[:, lane] = nt(grad_attn[...], w[lane, :]).astype(BF16)
    wait_all(fetched[given + 4 :])
    visible = seen(rows, ids[3])
    cos, sin = cosine[...], sine[...]
    for g in range(KEY_VALUE_HEADS):
        key = qkv[:, head(QUERY_HEADS + g)]
        value = qkv[:, head(QUERY_HEADS + KEY_VALUE_HEADS + g)]
        grad_key = jnp.zeros((rows, HEAD_SIZE), F32)
        grad_value = jnp.zeros((rows, HEAD_SIZE), F32)
        for h in range(g * GROUP, (g + 1) * GROUP):
            query, grad = qkv[:, head(h)], grad_mixed[:, head(h)]
            probs = attention_probs(query, key, visible)
            grad_probs = nt(grad, value)
            grad_value = grad_value + tn(probs.astype(BF16), grad)
            row_dot = jnp.sum(probs * grad_probs, axis=-1, keepdims=True)
            grad_scores = (probs * (grad_probs - row_dot)).astype(BF16)
            grad_query = nn(grad_scores, key) * SCALE
            grad_key = grad_key + tn(grad_scores, query)
            grad_pre[:, head(h)] = (grad_query * cos - swapped(grad_query) * sin).astype(BF16)
        grad_key = grad_key * SCALE
        grad_pre[:, head(QUERY_HEADS + g)] = (
            grad_key * cos - swapped(grad_key) * sin
        ).astype(BF16)
        grad_pre[:, head(QUERY_HEADS + KEY_VALUE_HEADS + g)] = grad_value.astype(BF16)
    last = pltpu.make_async_copy(grad_pre, out_pre, out_sem.at[2])
    last.start()
    wait_all(stores + [last])


def back(
    ids, residual, h_two, grads, gains, router, cosine, sine, qkv, backs, weights, before, sizes
):
    ndp, nz = sizes["dp"], sizes["z"]
    places, parts = weights
    rows = residual.shape[0]
    data = [residual, *h_two, grads, qkv]
    made = [
        shape((rows, MODEL_WIDTH), F32),
        shape((rows, MODEL_WIDTH), BF16),
        shape((rows, QKV), BF16),
    ]
    room = lambda array: pltpu.VMEM(array.shape, array.dtype)
    return pl.pallas_call(
        functools.partial(
            back_kernel, ndp, nz, places, len(parts), len(backs), len(before)
        ),
        out_shape=(*made, shape((16, MODEL_WIDTH), F32)),
        in_specs=[SMEM]
        + [VMEM] * 4
        + [HBM] * (len(data) + len(backs) + len(parts) + len(before)),
        out_specs=(HBM, HBM, HBM, VMEM),
        scratch_shapes=[
            *(room(array) for array in data + backs),
            pltpu.VMEM((QW, MODEL_WIDTH), BF16),
            pltpu.VMEM((rows, QW), BF16),
            *(room(array) for array in made),
            pltpu.SemaphoreType.DMA((2 * ndp * nz,)),
            pltpu.SemaphoreType.DMA((len(data) + len(backs),)),
            pltpu.SemaphoreType.DMA((3,)),
        ],
        compiler_params=params(60),
        cost_estimate=cost(3 * rows * MODEL_WIDTH * QW, 16 * MIB, 12 * rows * rows),
        name="back",
    )(ids, gains, router, cosine, sine, *data, *backs, *parts, *before)


def tokens_back_kernel(ndp, nz, places, count, ids, tokens, gains, grad_pre, grad_resid, *refs):
    parts = refs[:count]
    grad_tokens, w, sem = refs[-3:]
    loads = load_rows(ids, ndp, nz, places, parts, w, sem)
    tok = tokens[...].astype(F32)
    scale = rms_scale(tok)
    normed = tok * scale
    for load in loads:
        load.wait()
    for t in range(MODEL_WIDTH // TILE):
        lane = slice(t * TILE, (t + 1) * TILE)
        grad_tokens[:, lane] = nt(grad_pre[...], w[lane, :QKV])
    grad_h = grad_tokens[...]
    grad_tokens[...] = grad_resid[...] + norm_back(normed, scale, grad_h * gains[0:1])


def tokens_back(ids, tokens, gains, grad_pre, grad_resid, weights, before, sizes):
    ndp, nz = sizes["dp"], sizes["z"]
    places, parts = weights
    rows = tokens.shape[0]
    return pl.pallas_call(
        functools.partial(tokens_back_kernel, ndp, nz, places, len(parts)),
        out_shape=shape((rows, MODEL_WIDTH), F32),
        in_specs=[SMEM] + [VMEM] * 4 + [HBM] * (len(parts) + len(before)),
        out_specs=VMEM,
        scratch_shapes=[
            pltpu.VMEM((MODEL_WIDTH, FIRST), BF16),
            pltpu.SemaphoreType.DMA((2 * ndp * nz,)),
        ],
        compiler_params=params(60),
        cost_estimate=cost(2 * rows * MODEL_WIDTH * QKV, 12 * MIB),
        name="tokens_back",
    )(ids, tokens, gains, grad_pre, grad_resid, *parts, *before)


def terms_kernel(ndp, nz, noted, unread, ids, *refs):
    refs = list(refs)
    take = lambda n: [refs.pop(0) for _ in range(n)]
    notes, given = take(2 if noted else 0), take(4)
    take(unread)
    count = 2 * ndp - 1
    outs, held, dests = take(count), take(4), take(count)
    note_rows, in_sem, out_sem = refs
    wait_all(start_all(list(zip(given, held)), in_sem))
    left = jnp.concatenate([held[0][...], held[1][...]], axis=1)
    right = jnp.concatenate([held[2][...], held[3][...]], axis=0)
    slot = MODEL_WIDTH // (2 * ndp)
    stores = []

    def put(lane, value):
        dests[0][:, lane] = value[:slot]
        for i in range(1, count):
            at = slot + (i - 1) * (slot // 2)
            dests[i][:, lane] = value[at : at + slot // 2].astype(BF16)
        pairs = [(dests[i].at[:, lane], outs[i].at[:, lane]) for i in range(count)]
        stores.extend(start_all(pairs, out_sem.at[len(stores) // count]))

    if noted:
        note = notes[0][...] + notes[1][...]
        block = jnp.concatenate([note, jnp.zeros((PAD - 16, note.shape[1]), F32)], axis=0)
        block = jnp.transpose(block)
    if noted == 1:
        note_rows[...] = block
        rows = MODEL_WIDTH // (2 * ndp * nz)
        taken = []
        for k in range(ndp):
            for z in range(nz):
                at = ((ids[0] ^ k) * nz + (ids[1] ^ z)) * 2 + ids[2]
                taken.append(note_rows[pl.ds(pl.multiple_of(at * rows, rows), rows), :])
        block = jnp.concatenate(taken, axis=0)
    if noted:
        put(slice(right.shape[1], right.shape[1] + PAD), block)
    for t in range(right.shape[1] // TILE):
        lane = slice(t * TILE, (t + 1) * TILE)
        put(lane, nn(left, right[:, lane]))
    wait_all(stores)


def weight_terms(ids, left, right, notes, before, sizes):
    ndp, nz = sizes["dp"], sizes["z"]
    slot = MODEL_WIDTH // (2 * ndp)
    columns = right[0].shape[1] + (PAD if notes else 0)
    noted = 0 if not notes else 1 if notes[0].shape[1] == MODEL_WIDTH else 2
    made = [shape((slot, columns), F32)] + [shape((slot // 2, columns), BF16)] * (2 * ndp - 2)
    room = lambda array: pltpu.VMEM(array.shape, array.dtype)
    arrays = [*left, *right]
    found = pl.pallas_call(
        functools.partial(terms_kernel, ndp, nz, noted, len(before)),
        out_shape=tuple(made),
        in_specs=[SMEM] + [VMEM] * len(notes) + [HBM] * (4 + len(before)),
        out_specs=(HBM,) * len(made),
        scratch_shapes=[
            *(room(array) for array in arrays + made),
            pltpu.VMEM((MODEL_WIDTH, PAD), F32),
            pltpu.SemaphoreType.DMA((4,)),
            pltpu.SemaphoreType.DMA((columns // TILE + 1, len(made))),
        ],
        compiler_params=params(60),
        cost_estimate=cost(2 * MODEL_WIDTH * left[0].shape[1] * columns, 5 * MIB),
        name="weight_terms",
    )(ids, *notes, *arrays, *before)
    return found[0], [tuple(found[i : i + 2]) for i in range(1, len(found), 2)]


def settle_kernel(count, *refs):
    own, got = refs[0], refs[1 : 1 + count]
    mats = refs[1 + count : 4 + count]
    outs, small = refs[-4:-1], refs[-1]
    total = own[...]
    for part in got:
        total = total + part[...].astype(F32)
    dot, at = jnp.zeros((total.shape[0], 1), F32), 0
    for mat, out in zip(mats, outs):
        width = mat.shape[1]
        part = total[:, at : at + width]
        out[...] = part
        dot = dot + jnp.sum(part * mat[...].astype(F32), axis=1, keepdims=True)
        at += width
    lane = lax.broadcasted_iota(jnp.int32, small.shape, 1)
    small[...] = jnp.where(lane == PAD - 1, dot, total[:, at:])


def settle(own, got, mats):
    rows = own.shape[0]
    return pl.pallas_call(
        functools.partial(settle_kernel, len(got)),
        out_shape=tuple(shape(mat.shape, F32) for mat in mats) + (shape((rows, PAD), F32),),
        in_specs=[VMEM] * (1 + len(got) + 3),
        out_specs=(VMEM,) * 4,
        compiler_params=params(60),
        name="settle",
    )(own, *got, *mats)


def rope_tables(rows):
    half = HEAD_SIZE // 2
    position = jnp.arange(rows).astype(F32)
    inverse = ROPE_BASE ** (-jnp.arange(half).astype(F32) / half)
    angles = position[:, None] * inverse[None, :]
    cosine, sine = jnp.cos(angles), jnp.sin(angles)
    return jnp.concatenate([cosine, cosine], axis=1), jnp.concatenate([-sine, sine], axis=1)


def per_device(
    sizes,
    tokens,
    lengths,
    routes,
    cotangent,
    gain_one,
    w_query,
    key_matrix,
    value_matrix,
    w_out,
    gain_two,
    w_router,
    w_gate,
    w_up,
    w_down,
):
    ndp = sizes["dp"]
    rows = tokens.shape[0]
    local, _, width = w_gate.shape
    me_dp = lax.axis_index("dp")
    length = lengths[0]
    ids = jnp.stack([me_dp, lax.axis_index("z"), lax.axis_index("core"), length]).astype(jnp.int32)
    live = (jnp.arange(rows) < length)[:, None]
    expert_ids = jnp.arange(EXPERTS, dtype=jnp.int32)

    extra = jnp.concatenate([gain_one[:, None], gain_two[:, None], w_router], axis=1)
    extra = jnp.pad(extra, ((0, 0), (0, PAD - extra.shape[1])))
    first = jnp.concatenate([w_query, key_matrix, value_matrix, extra], axis=1)
    named = jnp.any(routes[None, :, :] == expert_ids[:, None, None], axis=2).astype(BF16)
    named = jnp.pad(named, ((0, NOTE - EXPERTS), (0, MODEL_WIDTH - rows)))
    grad_low = jnp.where(live, cotangent, jnp.zeros_like(cotangent))
    grad_low = jnp.concatenate([grad_low, named], axis=0)
    grad_near = start_dp(grad_low, ndp)

    nz = sizes["z"]
    grad_far = pass_on(grad_low, grad_near, ndp)
    second_z = [w_out] + [exchange(w_out, "z", nz, k) for k in range(1, nz)]
    first = lax.all_gather(first, "z", axis=0)
    (first,) = after([first], [piece for *_, piece in grad_far[1:]] + second_z[1:])
    packed = after([pack(j, (w_gate, w_up, w_down)) for j in range(local)], [first])
    expert_mats = [lax.all_gather(p, ("z", "core"), axis=0, tiled=True) for p in packed]
    first_dp = pass_on(first, start_dp(first, ndp), ndp)
    second = stack_after(second_z, [piece for *_, piece in first_dp[1:]])
    second_dp = gather_direct(second, ndp)

    cosine, sine = rope_tables(rows)
    weights_in = gather_rows(first_dp, False, ids, sizes)
    qkv, mixed, h_one, gains, router = attend(ids, tokens, cosine, sine, weights_in, [], sizes)
    second_far = after([piece for *_, piece in second_dp[1:]], [mixed])
    second_dp = [(k, 0, piece) for k, piece in enumerate([second, *second_far])]
    weights_out = gather_rows(second_dp, True, ids, sizes)
    residual, *h_two = project(ids, tokens, mixed, gains, weights_out, sizes)
    hidden = gather_halves(h_two, ndp)
    turned = turn([mixed, h_one], [hidden[2][2]], ids, sizes)
    mixed, h_one = ([mine, exchange(other, "core", 2, 1)] for mine, other in turned)

    prev, gate_grads, sums = (), [], []
    for j in range(local):
        expert = jnp.stack([me_dp * local + j, me_dp, ids[2]]).astype(jnp.int32)
        last = j == local - 1
        found = run_expert(
            j,
            last,
            expert,
            router,
            hidden,
            grad_far,
            expert_mats[j],
            prev,
            gate_grads,
            ndp,
            w_gate.shape[1],
            [*mixed, *h_one],
        )
        if last:
            *prev, grad_gate, terms, other = found
            terms = terms.astype(F32) + exchange(other, "core", 2, 1).astype(F32)
            terms = terms.astype(BF16)
            sums.append(lax.psum_scatter(terms, "z", scatter_dimension=0, tiled=False))
        else:
            *prev, grad_gate, terms = found
            sums.append(lax.psum_scatter(terms, ("z", "core"), scatter_dimension=0, tiled=True))
        gate_grads.append(grad_gate)
    outs, *backs = prev
    pairs = [tuple(backs[2 * k : 2 * k + 2]) for k in range(ndp)]
    backs = [*pairs[0], *scatter_dp(pairs, ndp)]
    (sent,) = after([outs], backs[2:])
    outs = lax.all_to_all(sent, "dp", split_axis=0, concat_axis=0, tiled=True)
    grad_resid, grad_attn, grad_pre, notes = back(
        ids,
        residual,
        h_two,
        cotangent,
        gains,
        router,
        cosine,
        sine,
        qkv,
        backs,
        weights_out,
        [sent, terms],
        sizes,
    )
    if not by_blocks(sizes):
        notes = split_cores(notes, ids, sizes)
        notes = notes[0], exchange(notes[1], "core", 2, 1)
    else:
        notes = notes, exchange(notes, "core", 2, 1)
    grad_attn = grad_attn, exchange(grad_attn, "core", 2, 1)
    (sent_pre,) = after([grad_pre], sums[:-1])
    grad_pre = sent_pre, exchange(sent_pre, "core", 2, 1)
    out_terms = weight_terms(ids, mixed, grad_attn, (), grad_pre[1:], sizes)
    in_terms = weight_terms(ids, h_one, grad_pre, notes, [out_terms[0], outs], sizes)
    grad_tokens = tokens_back(
        ids, tokens, gains, grad_pre[0], grad_resid, weights_in, in_terms[:1], sizes
    )
    (outs,) = after([outs], in_terms[:1])
    block_out = (residual + jnp.sum(outs.astype(F32), axis=0)).astype(BF16)
    own, late = scatter_rows(*out_terms, sizes, in_terms[:1])
    grad_out = own + sum(part.astype(F32) for part in late)
    own, got = scatter_rows(*in_terms, sizes, [grad_tokens])
    *grad_in, small = settle(own, got, (w_query, key_matrix, value_matrix))
    expert_sums = finish_after(sums, late[:1])
    return (
        block_out,
        grad_tokens,
        small[:, PAD - 1] / gain_one.astype(F32),
        *grad_in,
        grad_out,
        small[:, 0],
        small[:, 8 : 8 + EXPERTS],
        *expert_sums,
    )


def solution(mesh):
    ndp, nf = mesh.shape["dp"], mesh.shape["fsdp"]
    sizes = {"dp": ndp, "z": nf // 2, "core": 2}
    split = Mesh(mesh.devices.reshape(ndp, nf // 2, 2), ("dp", "z", "core"))
    every = ("dp", "z", "core")
    rows = P(every, None)
    vector = P(every)
    expert = P("dp", ("z", "core"), None)

    def run(*args):
        return per_device(sizes, *args)

    return jax.shard_map(
        run,
        mesh=split,
        in_specs=(rows, vector, rows, rows, vector, rows, rows, rows, rows, vector, rows)
        + (expert,) * 3,
        out_specs=(rows, rows, vector, rows, rows, rows, rows, vector, rows) + (expert,) * 3,
        check_vma=False,
    )
```

```python
import functools

import jax
import jax.numpy as jnp
from jax import lax
from jax.experimental import pallas as pl
from jax.experimental.pallas import tpu as pltpu
from jax.sharding import Mesh
from jax.sharding import PartitionSpec as P

MODEL_WIDTH = 1536
QUERY_HEADS = 12
KEY_VALUE_HEADS = 2
HEAD_SIZE = 128
EXPERTS = 8
CAP = 160
GROUP = QUERY_HEADS // KEY_VALUE_HEADS
QW = QUERY_HEADS * HEAD_SIZE
KW = KEY_VALUE_HEADS * HEAD_SIZE
QKV = QW + 2 * KW
PAD = 128
FIRST = QKV + PAD
NOTE = 32
ROUTER = 16
EPS = 1e-06
ROPE_BASE = 1500000.0
NEG_FILL = -1e30
SCALE = HEAD_SIZE ** (-0.5)
F32 = jnp.float32
BF16 = jnp.bfloat16
TILE = 256
MIB = 1024 * 1024
HBM = pl.BlockSpec(memory_space=pltpu.HBM)
VMEM = pl.BlockSpec(memory_space=pltpu.VMEM)
SMEM = pl.BlockSpec(memory_space=pltpu.SMEM)


def nn(a, b):
    return lax.dot_general(a, b, (((1,), (0,)), ((), ())), preferred_element_type=F32)


def nt(a, b):
    return lax.dot_general(a, b, (((1,), (1,)), ((), ())), preferred_element_type=F32)


def tn(a, b):
    return lax.dot_general(a, b, (((0,), (0,)), ((), ())), preferred_element_type=F32)


def shape(dims, dtype):
    return jax.ShapeDtypeStruct(dims, dtype)


def params(mib):
    return pltpu.CompilerParams(vmem_limit_bytes=mib * MIB)


def cost(flops, data, special=0):
    return pl.CostEstimate(flops=flops, bytes_accessed=data, transcendentals=special)


def exchange(block, axis, size, step):
    return lax.ppermute(block, axis, [(i, i ^ step) for i in range(size)])


def start_dp(block, ndp):
    return [exchange(block, "dp", ndp, k) for k in ((1, 2) if ndp == 4 else range(1, ndp))]


def pass_on(block, near, ndp, before=()):
    if ndp != 4:
        return [(k, 0, piece) for k, piece in enumerate([block] + near)]
    side, up = after(near, before) if before else near
    half = block.shape[0] // 2
    return [
        (0, 0, block),
        (1, 0, side),
        (2, 0, up),
        (3, 0, exchange(side[:half], "dp", ndp, 2)),
        (3, half, exchange(up[half:], "dp", ndp, 1)),
    ]


def gather_direct(block, ndp):
    return [(k, 0, exchange(block, "dp", ndp, k) if k else block) for k in range(ndp)]


def gather_halves(halves, ndp):
    top, low = halves
    at = top.shape[0]
    if ndp != 4:
        return [
            (k, i * at, exchange(half, "dp", ndp, k) if k else half)
            for k in range(ndp)
            for i, half in enumerate(halves)
        ]
    side_top, up_low = exchange(top, "dp", ndp, 1), exchange(low, "dp", ndp, 2)
    side_low, up_top = exchange(low, "dp", ndp, 1), exchange(top, "dp", ndp, 2)
    return [
        (0, 0, top),
        (0, at, low),
        (1, 0, side_top),
        (2, at, up_low),
        (1, at, side_low),
        (2, 0, up_top),
        (3, 0, exchange(side_top, "dp", ndp, 2)),
        (3, at, exchange(up_low, "dp", ndp, 1)),
    ]


def scatter_dp(slots, ndp, before=(), seen=None):
    if ndp != 4:
        whole = [jnp.concatenate(slot, axis=0) for slot in slots[1:]]
        if seen is not None:
            seen.extend(whole)
        return [exchange(part, "dp", ndp, k + 1) for k, part in enumerate(whole)]
    past = [exchange(slots[3][0], "dp", ndp, 1), exchange(slots[3][1], "dp", ndp, 2)]
    if before:
        past = after(past, before)
    add = lambda a, b: (a.astype(F32) + b.astype(F32)).astype(BF16)
    side = jnp.concatenate([slots[1][0], add(slots[1][1], past[1])], axis=0)
    up = jnp.concatenate([add(slots[2][0], past[0]), slots[2][1]], axis=0)
    if seen is not None:
        seen.extend([side, up])
    return [exchange(side, "dp", ndp, 1), exchange(up, "dp", ndp, 2)]


def both_cores(pieces):
    return [
        (k, c, start, exchange(piece, "core", 2, 1) if c else piece)
        for k, start, piece in pieces
        for c in range(2)
    ]


def stack_kernel(count, *refs):
    for i in range(count):
        refs[-1][i] = refs[i][...]


def stack_after(parts, before):
    dims = (len(parts),) + parts[0].shape
    return pl.pallas_call(
        functools.partial(stack_kernel, len(parts)),
        out_shape=shape(dims, parts[0].dtype),
        in_specs=[VMEM] * len(parts) + [HBM] * len(before),
        out_specs=VMEM,
        compiler_params=params(60),
        cost_estimate=cost(0, 4 * dims[0] * dims[1] * dims[2]),
        name="stack",
    )(*parts, *before)


def pack_kernel(index, *refs):
    width = refs[0].shape[2]
    for i in range(3):
        refs[-1][:, i * width : (i + 1) * width] = refs[i][index]


def pack(index, mats):
    _, rows, width = mats[0].shape
    return pl.pallas_call(
        functools.partial(pack_kernel, index),
        out_shape=shape((rows, 3 * width), BF16),
        in_specs=[VMEM] * 3,
        out_specs=VMEM,
        compiler_params=params(60),
        name="pack",
    )(*mats)


def finish_kernel(count, *refs):
    outs = refs[-3:]
    width = outs[0].shape[2]
    for j in range(count):
        for i in range(3):
            outs[i][j] = refs[j][:, i * width : (i + 1) * width].astype(F32)


def finish_after(sums, before):
    rows, width = sums[0].shape[0], sums[0].shape[1] // 3
    return pl.pallas_call(
        functools.partial(finish_kernel, len(sums)),
        out_shape=(shape((len(sums), rows, width), F32),) * 3,
        in_specs=[VMEM] * len(sums) + [HBM] * len(before),
        out_specs=(VMEM,) * 3,
        compiler_params=params(60),
        name="finish",
    )(*sums, *before)


def after_kernel(*refs):
    pass


def after(arrays, before):
    return pl.pallas_call(
        after_kernel,
        out_shape=tuple(shape(a.shape, a.dtype) for a in arrays),
        in_specs=[HBM] * (len(arrays) + len(before)),
        out_specs=(HBM,) * len(arrays),
        input_output_aliases={i: i for i in range(len(arrays))},
        name="after",
    )(*arrays, *before)


def block_rows(sizes):
    return MODEL_WIDTH // (2 * sizes["dp"] * sizes["z"])


def by_blocks(sizes):
    return block_rows(sizes) % 16 == 0


def gather_rows(block, along_dp, ids, sizes):
    ndp, nz = sizes["dp"], sizes["z"]
    pieces = both_cores(along_dp)
    if by_blocks(sizes):
        places = tuple((k, c, start, piece.shape[0]) for k, c, start, piece in pieces)
        return places, [piece for *_, piece in pieces]
    columns = block.shape[-1]
    whole = jnp.zeros((ndp, nz, 2, block_rows(sizes), columns), BF16)
    for k, c, start, piece in pieces:
        order = ids[1] ^ jnp.arange(start, start + piece.shape[0])
        whole = whole.at[ids[0] ^ k, order, ids[2] ^ c].set(piece)
    return None, [whole.reshape(MODEL_WIDTH, columns)]


def split_cores(columns, ids, sizes):
    ndp, nz = sizes["dp"], sizes["z"]
    rows = columns.shape[0]
    blocks = columns.reshape(rows, ndp, nz, 2, block_rows(sizes))
    blocks = jnp.take(jnp.take(blocks, ids[0] ^ jnp.arange(ndp), 1), ids[1] ^ jnp.arange(nz), 2)
    halves = [lax.dynamic_index_in_dim(blocks, ids[2] ^ c, 3, keepdims=False) for c in range(2)]
    return [half.reshape(rows, MODEL_WIDTH // 2) for half in halves]


def turn_kernel(ndp, nz, count, ids, *refs):
    block = MODEL_WIDTH // (2 * ndp * nz)
    turned = refs[-1]
    for i in range(count):
        turned[...] = jnp.transpose(refs[i][...])
        for k in range(ndp):
            for z in range(nz):
                for c in range(2):
                    at = ((ids[0] ^ k) * nz + (ids[1] ^ z)) * 2 + (ids[2] ^ c)
                    place = pl.ds(pl.multiple_of(at * block, block), block)
                    dest = refs[-1 - 2 * count + 2 * i + c]
                    dest[(k * nz + z) * block : (k * nz + z + 1) * block] = turned[place, :]


def turn(arrays, before, ids, sizes):
    if not by_blocks(sizes):
        return [[half.T for half in split_cores(array, ids, sizes)] for array in arrays]
    rows = arrays[0].shape[0]
    halves = pl.pallas_call(
        functools.partial(turn_kernel, sizes["dp"], sizes["z"], len(arrays)),
        out_shape=(shape((MODEL_WIDTH // 2, rows), BF16),) * (2 * len(arrays)),
        in_specs=[SMEM] + [VMEM] * len(arrays) + [HBM] * len(before),
        out_specs=(VMEM,) * (2 * len(arrays)),
        scratch_shapes=[pltpu.VMEM((MODEL_WIDTH, rows), BF16)],
        compiler_params=params(60),
        name="turn",
    )(ids, *arrays, *before)
    return [halves[2 * i : 2 * i + 2] for i in range(len(arrays))]


def scatter_rows(own, slots, sizes, before=(), seen=None):
    ndp, nz = sizes["dp"], sizes["z"]
    total = own
    for part in scatter_dp([None, *slots], ndp, before, seen):
        total = total + part.astype(F32)
    rows = block_rows(sizes)
    blocks = [total[z * rows : (z + 1) * rows] for z in range(nz)]
    if nz != 4:
        return blocks[0], [exchange(blocks[z].astype(BF16), "z", nz, z) for z in range(1, nz)]
    near = exchange(jnp.concatenate([blocks[1], blocks[3]], axis=0).astype(BF16), "z", nz, 1)
    passed = (blocks[2] + near[rows:].astype(F32)).astype(BF16)
    return blocks[0], [near[:rows], exchange(passed, "z", nz, 2)]


def load_rows(ids, ndp, nz, places, parts, dest, sem):
    if places is None:
        loads = [pltpu.make_async_copy(parts[0], dest, sem.at[0])]
        loads[0].start()
        return loads
    rows = MODEL_WIDTH // (ndp * nz * 2)
    loads = []
    for (k, c, start, count), part in zip(places, parts):
        for z in range(count):
            block = ((ids[0] ^ k) * nz + (ids[1] ^ (start + z))) * 2 + (ids[2] ^ c)
            place = pl.ds(pl.multiple_of(block * rows, rows), rows)
            copy = pltpu.make_async_copy(part.at[z], dest.at[place, :], sem.at[len(loads)])
            loads.append(copy)
    for load in loads:
        load.start()
    return loads


def start_all(pairs, sem):
    copies = [pltpu.make_async_copy(a, b, sem.at[i]) for i, (a, b) in enumerate(pairs)]
    for copy in copies:
        copy.start()
    return copies


def wait_all(copies):
    for copy in copies:
        copy.wait()


def rms_scale(rows):
    return lax.rsqrt(jnp.mean(rows * rows, axis=-1, keepdims=True) + EPS)


def norm_back(normed, row_scale, grad):
    return row_scale * (grad - normed * jnp.mean(grad * normed, axis=-1, keepdims=True))


def swapped(vals):
    return pltpu.roll(vals, HEAD_SIZE // 2, 1)


def head(h):
    return slice(h * HEAD_SIZE, (h + 1) * HEAD_SIZE)


def seen(rows, length):
    q = lax.broadcasted_iota(jnp.int32, (rows, rows), 0)
    s = lax.broadcasted_iota(jnp.int32, (rows, rows), 1)
    return (s <= q) & (s < length)


def attention_probs(query, key, visible):
    scores = jnp.where(visible, nt(query, key) * SCALE, NEG_FILL)
    expon = jnp.exp(scores - jnp.max(scores, axis=-1, keepdims=True))
    return expon / jnp.sum(expon, axis=-1, keepdims=True)


def route_softmax(router_rows, hidden):
    logits = nt(router_rows, hidden)[:EXPERTS]
    expon = jnp.exp(logits - jnp.max(logits, axis=0, keepdims=True))
    return expon / jnp.sum(expon, axis=0, keepdims=True)


def attend_kernel(ndp, nz, places, count, ids, tokens, cosine, sine, *refs):
    parts = refs[:count]
    qkv, mixed, h_one, gains, router, w, sem = refs[-7:]
    rows = tokens.shape[0]
    loads = load_rows(ids, ndp, nz, places, parts, w, sem)
    tok = tokens[...].astype(F32)
    normed = tok * rms_scale(tok)
    for load in loads:
        load.wait()
    extra = jnp.transpose(w[:, QKV:].astype(F32))
    gains[...] = extra[:8]
    router[...] = extra[2 : 2 + ROUTER].astype(BF16)
    h_one[...] = (normed * extra[0:1]).astype(BF16)
    cos, sin = cosine[...], sine[...]
    for t in range(QKV // TILE):
        pre = nn(h_one[...], w[:, t * TILE : (t + 1) * TILE])
        for i in range(TILE // HEAD_SIZE):
            part = pre[:, head(i)]
            at = t * TILE + i * HEAD_SIZE
            if at < QW + KW:
                part = part * cos + swapped(part) * sin
            qkv[:, at : at + HEAD_SIZE] = part.astype(BF16)
    visible = seen(rows, ids[3])
    for h in range(QUERY_HEADS):
        g = h // GROUP
        probs = attention_probs(qkv[:, head(h)], qkv[:, head(QUERY_HEADS + g)], visible)
        values = qkv[:, head(QUERY_HEADS + KEY_VALUE_HEADS + g)]
        mixed[:, head(h)] = nn(probs.astype(BF16), values).astype(BF16)


def attend(ids, tokens, cosine, sine, weights, before, sizes):
    places, parts = weights
    ndp, nz = sizes["dp"], sizes["z"]
    rows = tokens.shape[0]
    return pl.pallas_call(
        functools.partial(attend_kernel, ndp, nz, places, len(parts)),
        out_shape=(
            shape((rows, QKV), BF16),
            shape((rows, QW), BF16),
            shape((rows, MODEL_WIDTH), BF16),
            shape((8, MODEL_WIDTH), F32),
            shape((ROUTER, MODEL_WIDTH), BF16),
        ),
        in_specs=[SMEM, VMEM, VMEM, VMEM] + [HBM] * (len(parts) + len(before)),
        out_specs=(VMEM,) * 5,
        scratch_shapes=[
            pltpu.VMEM((MODEL_WIDTH, FIRST), BF16),
            pltpu.SemaphoreType.DMA((2 * ndp * nz,)),
        ],
        compiler_params=params(60),
        cost_estimate=cost(2 * rows * MODEL_WIDTH * QKV, 10 * MIB, 12 * rows * rows),
        name="attend",
    )(ids, tokens, cosine, sine, *parts, *before)


def project_kernel(ndp, nz, places, ids, tokens, mixed, gains, *refs):
    *parts, residual, top, low, w, sem = refs
    loads = load_rows(ids, ndp, nz, places, parts, w, sem)
    for load in loads:
        load.wait()
    for t in range(MODEL_WIDTH // TILE):
        lane = slice(t * TILE, (t + 1) * TILE)
        residual[:, lane] = tokens[:, lane].astype(F32) + nn(mixed[...], w[:, lane])
    whole = residual[...]
    h_two = (whole * rms_scale(whole) * gains[1:2]).astype(BF16)
    half = top.shape[0]
    top[...], low[...] = h_two[:half], h_two[half:]


def project(ids, tokens, mixed, gains, weights, sizes):
    places, parts = weights
    ndp, nz = sizes["dp"], sizes["z"]
    rows = tokens.shape[0]
    return pl.pallas_call(
        functools.partial(project_kernel, ndp, nz, places),
        out_shape=(shape((rows, MODEL_WIDTH), F32),)
        + (shape((rows // 2, MODEL_WIDTH), BF16),) * 2,
        in_specs=[SMEM, VMEM, VMEM, VMEM] + [HBM] * len(parts),
        out_specs=(VMEM,) * 3,
        scratch_shapes=[
            pltpu.VMEM((QW, MODEL_WIDTH), BF16),
            pltpu.SemaphoreType.DMA((2 * ndp * nz,)),
        ],
        compiler_params=params(60),
        cost_estimate=cost(2 * rows * MODEL_WIDTH * QW, 8 * MIB),
        name="project",
    )(ids, tokens, mixed, gains, *parts)


def expert_kernel(ndp, rows, width, index, last, near, far, unread, *refs):
    it = iter(refs)
    take = lambda n: [next(it) for _ in range(n)]
    (expert_ref, router_ref) = take(2)
    prev_gates = take(index)
    hid_in, cot_in = take(len(near)), take(len(far))
    (w_in,) = take(1)
    prev_in = take(2) if index else []
    take(unread)
    (out_hbm,), back_hbm = take(1), take(2 * ndp if last else 1)
    gates_ref, terms_hbm = take(2)
    hid, cot, w, x, d, ge, inner, dg, du, pick, pick_t, slot_gate, slot_dot = take(13)
    (terms_buf,) = take(1)
    prev = take(2) if index else []
    in_sem, out_sem = take(2)
    depth = MODEL_WIDTH
    tiles = depth // TILE

    loads = {}

    def load(name, source, dest):
        copy = pltpu.make_async_copy(source, dest, in_sem.at[len(loads)])
        copy.start()
        loads[name] = copy

    for i, (k, start, count) in enumerate(near):
        load(("hid", i), hid_in[i], hid.at[k, pl.ds(start, count), :])
    for i, (k, start, count) in enumerate(far):
        load(("cot", i), cot_in[i], cot.at[k, pl.ds(start, count), :])
    load("w", w_in, w)
    for i in range(len(prev)):
        load(("prev", i), prev_in[i], prev[i])

    expert, me = expert_ref[0], expert_ref[1]
    which = lax.broadcasted_iota(jnp.int32, (EXPERTS, rows), 0) == expert
    earlier = (
        (
            lax.broadcasted_iota(jnp.int32, (rows, rows), 0)
            < lax.broadcasted_iota(jnp.int32, (rows, rows), 1)
        )
        .astype(F32)
        .astype(BF16)
    )
    slot = lax.broadcasted_iota(jnp.int32, (CAP, rows), 0).astype(F32)
    for s in range(ndp):
        for i, piece in enumerate(near):
            if piece[0] == s:
                loads["hid", i].wait()
        for i, piece in enumerate(far):
            if piece[0] == s:
                loads["cot", i].wait()
        hidden = hid[s]
        probs = route_softmax(router_ref[...], hidden)
        named = cot[s, rows : rows + NOTE, :rows]
        place = nn(named, earlier)[:EXPERTS]
        named = named[:EXPERTS].astype(F32)
        named_row = jnp.sum(jnp.where(which, named, 0.0), axis=0, keepdims=True)
        gate_row = jnp.sum(jnp.where(which, probs, 0.0), axis=0, keepdims=True)
        place_row = jnp.sum(jnp.where(which, place, 0.0), axis=0, keepdims=True)
        chosen = jnp.where((slot == place_row) & (named_row > 0.5), 1.0, 0.0)
        pick[s] = chosen.astype(BF16)
        pick_t[s] = jnp.transpose(chosen).astype(BF16)
        at = pl.ds(s * CAP, CAP)
        gate = jnp.sum(chosen * gate_row, axis=1, keepdims=True)
        slot_gate[at, :] = jnp.broadcast_to(gate, (CAP, 128))
        x[at, :] = nn(pick[s], hidden).astype(BF16)
        grads = nn(pick[s], cot[s, :rows])
        d[at, :] = grads.astype(BF16)
        ge[at, :] = (gate * grads).astype(BF16)
    loads["w"].wait()

    def hidden_units(t, carry):
        at = pl.multiple_of(t * TILE, TILE)
        gate_pre = nn(x[...], w[:, pl.ds(at, TILE)])
        up_pre = nn(x[...], w[:, pl.ds(width + at, TILE)])
        grad_inner = nn(ge[...], w[:, pl.ds(2 * width + at, TILE)])
        sig = 1.0 / (1.0 + jnp.exp(-gate_pre))
        act = gate_pre * sig
        inner[:, pl.ds(at, TILE)] = (act * up_pre).astype(BF16)
        dg[:, pl.ds(at, TILE)] = (
            grad_inner * up_pre * sig * (1.0 + gate_pre * (1.0 - sig))
        ).astype(BF16)
        du[:, pl.ds(at, TILE)] = (grad_inner * act).astype(BF16)
        return carry

    lax.fori_loop(0, width // TILE, hidden_units, 0)
    slot_dot[...] = jnp.zeros_like(slot_dot)
    for i in range(len(prev)):
        loads["prev", i].wait()

    noted = (rows + NOTE) // 2

    def stores(t):
        lane = pl.ds(pl.multiple_of(t * TILE, TILE), TILE)
        copies = [(terms_buf.at[lane, :], terms_hbm.at[lane, :])]
        if not last:
            body = pl.ds(0, rows)
            copies.append((hid.at[:, :, lane], out_hbm.at[:, :, lane]))
            copies.append((cot.at[:, body, lane], back_hbm[0].at[:, body, lane]))
        else:
            for k in range(ndp):
                copies.append((hid.at[k, :, lane], out_hbm.at[me ^ k, :, lane]))
            for i in range(2 * ndp):
                body = pl.ds(0, noted if i % 2 == 0 else rows - noted)
                taken = pl.ds(i % 2 * noted, noted if i % 2 == 0 else rows - noted)
                copies.append((cot.at[i // 2, taken, lane], back_hbm[i].at[body, lane]))
        return [
            pltpu.make_async_copy(source, dest, out_sem.at[i, t])
            for i, (source, dest) in enumerate(copies)
        ]

    def features(t, carry):
        lane = pl.ds(pl.multiple_of(t * TILE, TILE), TILE)
        result = nt(inner[...], w[lane, pl.ds(2 * width, width)]).astype(BF16).astype(F32)
        partial = jnp.sum(result * d[:, lane].astype(F32), axis=1, keepdims=True)
        slot_dot[...] += jnp.broadcast_to(partial, slot_dot.shape)
        gated = (slot_gate[:, :1] * result).astype(BF16)
        grad_in = (
            nt(dg[...], w[lane, pl.ds(0, width)]) + nt(du[...], w[lane, pl.ds(width, width)])
        ).astype(BF16)
        for s in range(ndp):
            part = slice(s * CAP, (s + 1) * CAP)
            sent = nn(pick_t[s], gated[part])
            back = nn(pick_t[s], grad_in[part])
            if prev:
                sent = sent + prev[0][s, :, lane].astype(F32)
                back = back + prev[1][s, :rows, lane].astype(F32)
            hid[s, :, lane] = sent.astype(BF16)
            cot[s, :rows, lane] = back.astype(BF16)
        x_t = jnp.transpose(x[:, lane])
        terms_buf[lane, pl.ds(0, width)] = nn(x_t, dg[...]).astype(BF16)
        terms_buf[lane, pl.ds(width, width)] = nn(x_t, du[...]).astype(BF16)
        ge_t = jnp.transpose(ge[:, lane])
        terms_buf[lane, pl.ds(2 * width, width)] = nn(ge_t, inner[...]).astype(BF16)
        for store in stores(t):
            store.start()
        return carry

    lax.fori_loop(0, tiles, features, 0)
    line = lax.broadcasted_iota(jnp.int32, (NOTE, 3 * rows), 0)
    notes = []
    for s in range(ndp):
        part = slice(s * CAP, (s + 1) * CAP)
        own = jnp.sum(pick[s].astype(F32) * slot_dot[part, :1], axis=0, keepdims=True)
        gates_ref[s] = own
        if not last:
            continue
        note = jnp.zeros((NOTE, 3 * rows), F32)
        for j, row in enumerate([p[s] for p in prev_gates] + [own]):
            high = row.astype(BF16).astype(F32)
            middle = (row - high).astype(BF16).astype(F32)
            low = row - high - middle
            at = expert - index + j
            note = jnp.where(line == at, jnp.concatenate([high, middle, low], axis=1), note)
        cot[s, rows : rows + NOTE, : 3 * rows] = note.astype(BF16)
        notes.append(
            pltpu.make_async_copy(
                cot.at[s, pl.ds(rows, NOTE), :],
                back_hbm[2 * s + 1].at[pl.ds(rows - noted, NOTE), :],
                out_sem.at[4 * ndp + 1, s],
            )
        )
        notes[-1].start()
    for t in range(tiles):
        for store in stores(t):
            store.wait()
    for note in notes:
        note.wait()


def run_expert(index, last, expert, router, hidden, grads, w_all, prev, prev_gates, ndp, before):
    rows = 2 * hidden[0][2].shape[0]
    near, far = (tuple((k, at, p.shape[0]) for k, at, p in group) for group in (hidden, grads))
    width = w_all.shape[1] // 3
    slots = ndp * CAP
    depth = MODEL_WIDTH
    tiles = depth // TILE
    scratch = [
        pltpu.VMEM((ndp, rows, depth), BF16),
        pltpu.VMEM((ndp, rows + NOTE, depth), BF16),
        pltpu.VMEM((depth, 3 * width), BF16),
        pltpu.VMEM((slots, depth), BF16),
        pltpu.VMEM((slots, depth), BF16),
        pltpu.VMEM((slots, depth), BF16),
        pltpu.VMEM((slots, width), BF16),
        pltpu.VMEM((slots, width), BF16),
        pltpu.VMEM((slots, width), BF16),
        pltpu.VMEM((ndp, CAP, rows), BF16),
        pltpu.VMEM((ndp, rows, CAP), BF16),
        pltpu.VMEM((slots, 128), F32),
        pltpu.VMEM((slots, 128), F32),
        pltpu.VMEM((depth, 3 * width), BF16),
    ]
    if index:
        scratch += [
            pltpu.VMEM((ndp, rows, depth), BF16),
            pltpu.VMEM((ndp, rows + NOTE, depth), BF16),
        ]
    scratch += [
        pltpu.SemaphoreType.DMA((len(near) + len(far) + 3,)),
        pltpu.SemaphoreType.DMA((4 * ndp + 2, max(tiles, ndp))),
    ]
    sent = [shape((ndp, rows, depth), BF16), shape((ndp, rows + NOTE, depth), BF16)]
    if last:
        sent = sent[:1] + [shape(((rows + NOTE) // 2, depth), BF16)] * (2 * ndp)
    flops = 2 * slots * depth * width * 9 + 8 * ndp * CAP * rows * depth
    return pl.pallas_call(
        functools.partial(
            expert_kernel, ndp, rows, width, index, last, near, far, len(before)
        ),
        out_shape=(
            *sent,
            shape((ndp, 1, rows), F32),
            shape((depth, 3 * width), BF16),
        ),
        in_specs=[SMEM, VMEM]
        + [VMEM] * len(prev_gates)
        + [HBM] * (len(near) + len(far) + 1 + len(prev) + len(before)),
        out_specs=(HBM,) * len(sent) + (VMEM, HBM),
        scratch_shapes=scratch,
        compiler_params=params(60),
        cost_estimate=cost(flops, 40 * MIB, slots * width),
        name="expert",
    )(
        expert,
        router,
        *prev_gates,
        *(piece for *_, piece in hidden),
        *(piece for *_, piece in grads),
        w_all,
        *prev,
        *before,
    )


def back_kernel(ndp, nz, places, count, given, unread, ids, gains, router, cosine, sine, *refs):
    refs = list(refs)
    take = lambda n: [refs.pop(0) for _ in range(n)]
    data, backs, parts = take(5), take(given), take(count)
    take(unread)
    out_resid, out_attn, out_pre, notes = take(4)
    residual, top, low, grads, qkv = held = take(5)
    got = take(given)
    w, grad_mixed, grad_resid, grad_attn, grad_pre, sem, data_sem, out_sem = refs
    rows = residual.shape[0]
    fetched = start_all(list(zip(backs + data[1:3] + data[:1] + data[3:], got + held[1:3] + held[:1] + held[3:])), data_sem)
    loads = load_rows(ids, ndp, nz, places, parts, w, sem)
    wait_all(fetched[:given])
    whole = jnp.concatenate([got[0][...], got[1][...]], axis=0).astype(F32)
    for part in got[2:]:
        whole = whole + part[...].astype(F32)
    grad_h = whole[:rows]
    note = whole[rows : rows + EXPERTS, : 3 * rows]
    grad_route = note[:, :rows] + note[:, rows : 2 * rows] + note[:, 2 * rows :]
    wait_all(fetched[given : given + 4])
    hidden = jnp.concatenate([top[...], low[...]], axis=0)
    probs = route_softmax(router[...], hidden)
    grad_logits = probs * (grad_route - jnp.sum(probs * grad_route, axis=0, keepdims=True))
    grad_logits = jnp.concatenate([grad_logits, jnp.zeros_like(grad_logits)], axis=0)
    grad_logits = grad_logits.astype(BF16)
    grad_h = grad_h + tn(grad_logits, router[...])
    res = residual[...]
    scale = rms_scale(res)
    normed = res * scale
    notes[0:8] = jnp.broadcast_to(
        jnp.sum(normed * grad_h, axis=0, keepdims=True), (8, MODEL_WIDTH)
    )
    notes[8:16] = nn(grad_logits, hidden)[:EXPERTS]
    live = lax.broadcasted_iota(jnp.int32, (rows, 1), 0) < ids[3]
    final = jnp.where(live, grads[...].astype(F32), 0.0)
    total = final + norm_back(normed, scale, grad_h * gains[1:2])
    grad_resid[...] = total
    grad_attn[...] = total.astype(BF16)
    stores = start_all([(grad_attn, out_attn), (grad_resid, out_resid)], out_sem)
    wait_all(loads)
    for t in range(QW // TILE):
        lane = slice(t * TILE, (t + 1) * TILE)
        grad_mixed[:, lane] = nt(grad_attn[...], w[lane, :]).astype(BF16)
    wait_all(fetched[given + 4 :])
    source = lax.broadcasted_iota(jnp.int32, (rows, rows), 0)
    visible = (source <= lax.broadcasted_iota(jnp.int32, (rows, rows), 1)) & (source < ids[3])
    cos, sin = cosine[...], sine[...]
    for g in range(KEY_VALUE_HEADS):
        key = qkv[:, head(QUERY_HEADS + g)]
        value = qkv[:, head(QUERY_HEADS + KEY_VALUE_HEADS + g)]
        grad_key = jnp.zeros((rows, HEAD_SIZE), F32)
        grad_value = jnp.zeros((rows, HEAD_SIZE), F32)
        for h in range(g * GROUP, (g + 1) * GROUP):
            query, grad = qkv[:, head(h)], grad_mixed[:, head(h)]
            scores = jnp.where(visible, nt(key, query) * SCALE, NEG_FILL)
            expon = jnp.exp(scores - jnp.max(scores, axis=0, keepdims=True))
            probs = expon / jnp.sum(expon, axis=0, keepdims=True)
            grad_probs = nt(value, grad)
            grad_value = grad_value + nn(probs.astype(BF16), grad)
            row_dot = jnp.sum(probs * grad_probs, axis=0, keepdims=True)
            grad_scores = (probs * (grad_probs - row_dot)).astype(BF16)
            grad_query = tn(grad_scores, key) * SCALE
            grad_key = grad_key + nn(grad_scores, query)
            grad_pre[:, head(h)] = (grad_query * cos - swapped(grad_query) * sin).astype(BF16)
        grad_key = grad_key * SCALE
        grad_pre[:, head(QUERY_HEADS + g)] = (
            grad_key * cos - swapped(grad_key) * sin
        ).astype(BF16)
        grad_pre[:, head(QUERY_HEADS + KEY_VALUE_HEADS + g)] = grad_value.astype(BF16)
    last = pltpu.make_async_copy(grad_pre, out_pre, out_sem.at[2])
    last.start()
    wait_all(stores + [last])


def back(
    ids, residual, h_two, grads, gains, router, cosine, sine, qkv, backs, weights, before, sizes
):
    ndp, nz = sizes["dp"], sizes["z"]
    places, parts = weights
    rows = residual.shape[0]
    data = [residual, *h_two, grads, qkv]
    made = [
        shape((rows, MODEL_WIDTH), F32),
        shape((rows, MODEL_WIDTH), BF16),
        shape((rows, QKV), BF16),
    ]
    room = lambda array: pltpu.VMEM(array.shape, array.dtype)
    return pl.pallas_call(
        functools.partial(
            back_kernel, ndp, nz, places, len(parts), len(backs), len(before)
        ),
        out_shape=(*made, shape((16, MODEL_WIDTH), F32)),
        in_specs=[SMEM]
        + [VMEM] * 4
        + [HBM] * (len(data) + len(backs) + len(parts) + len(before)),
        out_specs=(HBM, HBM, HBM, VMEM),
        scratch_shapes=[
            *(room(array) for array in data + backs),
            pltpu.VMEM((QW, MODEL_WIDTH), BF16),
            pltpu.VMEM((rows, QW), BF16),
            *(room(array) for array in made),
            pltpu.SemaphoreType.DMA((2 * ndp * nz,)),
            pltpu.SemaphoreType.DMA((len(data) + len(backs),)),
            pltpu.SemaphoreType.DMA((3,)),
        ],
        compiler_params=params(60),
        cost_estimate=cost(3 * rows * MODEL_WIDTH * QW, 16 * MIB, 12 * rows * rows),
        name="back",
    )(ids, gains, router, cosine, sine, *data, *backs, *parts, *before)


def tokens_back_kernel(ndp, nz, places, count, ids, tokens, gains, grad_pre, grad_resid, *refs):
    parts = refs[:count]
    grad_tokens, w, sem = refs[-3:]
    loads = load_rows(ids, ndp, nz, places, parts, w, sem)
    tok = tokens[...].astype(F32)
    scale = rms_scale(tok)
    normed = tok * scale
    for load in loads:
        load.wait()
    for t in range(MODEL_WIDTH // TILE):
        lane = slice(t * TILE, (t + 1) * TILE)
        grad_tokens[:, lane] = nt(grad_pre[...], w[lane, :QKV])
    grad_h = grad_tokens[...]
    grad_tokens[...] = grad_resid[...] + norm_back(normed, scale, grad_h * gains[0:1])


def tokens_back(ids, tokens, gains, grad_pre, grad_resid, weights, before, sizes):
    ndp, nz = sizes["dp"], sizes["z"]
    places, parts = weights
    rows = tokens.shape[0]
    return pl.pallas_call(
        functools.partial(tokens_back_kernel, ndp, nz, places, len(parts)),
        out_shape=shape((rows, MODEL_WIDTH), F32),
        in_specs=[SMEM] + [VMEM] * 4 + [HBM] * (len(parts) + len(before)),
        out_specs=VMEM,
        scratch_shapes=[
            pltpu.VMEM((MODEL_WIDTH, FIRST), BF16),
            pltpu.SemaphoreType.DMA((2 * ndp * nz,)),
        ],
        compiler_params=params(60),
        cost_estimate=cost(2 * rows * MODEL_WIDTH * QKV, 12 * MIB),
        name="tokens_back",
    )(ids, tokens, gains, grad_pre, grad_resid, *parts, *before)


def terms_kernel(ndp, nz, noted, unread, ids, *refs):
    refs = list(refs)
    take = lambda n: [refs.pop(0) for _ in range(n)]
    notes, given = take(2 if noted else 0), take(4)
    take(unread)
    count = 2 * ndp - 1
    outs, held, dests = take(count), take(4), take(count)
    note_rows, in_sem, out_sem = refs
    wait_all(start_all(list(zip(given, held)), in_sem))
    left = jnp.concatenate([held[0][...], held[1][...]], axis=1)
    right = jnp.concatenate([held[2][...], held[3][...]], axis=0)
    slot = MODEL_WIDTH // (2 * ndp)
    stores = []

    def put(lane, value):
        dests[0][:, lane] = value[:slot]
        for i in range(1, count):
            at = slot + (i - 1) * (slot // 2)
            dests[i][:, lane] = value[at : at + slot // 2].astype(BF16)
        pairs = [(dests[i].at[:, lane], outs[i].at[:, lane]) for i in range(count)]
        stores.extend(start_all(pairs, out_sem.at[len(stores) // count]))

    if noted:
        note = notes[0][...] + notes[1][...]
        block = jnp.concatenate([note, jnp.zeros((PAD - 16, note.shape[1]), F32)], axis=0)
        block = jnp.transpose(block)
    if noted == 1:
        note_rows[...] = block
        rows = MODEL_WIDTH // (2 * ndp * nz)
        taken = []
        for k in range(ndp):
            for z in range(nz):
                at = ((ids[0] ^ k) * nz + (ids[1] ^ z)) * 2 + ids[2]
                taken.append(note_rows[pl.ds(pl.multiple_of(at * rows, rows), rows), :])
        block = jnp.concatenate(taken, axis=0)
    if noted:
        put(slice(right.shape[1], right.shape[1] + PAD), block)
    for t in range(right.shape[1] // TILE):
        lane = slice(t * TILE, (t + 1) * TILE)
        put(lane, nn(left, right[:, lane]))
    wait_all(stores)


def weight_terms(ids, left, right, notes, before, sizes):
    ndp, nz = sizes["dp"], sizes["z"]
    slot = MODEL_WIDTH // (2 * ndp)
    columns = right[0].shape[1] + (PAD if notes else 0)
    noted = 0 if not notes else 1 if notes[0].shape[1] == MODEL_WIDTH else 2
    made = [shape((slot, columns), F32)] + [shape((slot // 2, columns), BF16)] * (2 * ndp - 2)
    room = lambda array: pltpu.VMEM(array.shape, array.dtype)
    arrays = [*left, *right]
    found = pl.pallas_call(
        functools.partial(terms_kernel, ndp, nz, noted, len(before)),
        out_shape=tuple(made),
        in_specs=[SMEM] + [VMEM] * len(notes) + [HBM] * (4 + len(before)),
        out_specs=(HBM,) * len(made),
        scratch_shapes=[
            *(room(array) for array in arrays + made),
            pltpu.VMEM((MODEL_WIDTH, PAD), F32),
            pltpu.SemaphoreType.DMA((4,)),
            pltpu.SemaphoreType.DMA((columns // TILE + 1, len(made))),
        ],
        compiler_params=params(60),
        cost_estimate=cost(2 * MODEL_WIDTH * left[0].shape[1] * columns, 5 * MIB),
        name="weight_terms",
    )(ids, *notes, *arrays, *before)
    return found[0], [tuple(found[i : i + 2]) for i in range(1, len(found), 2)]


def settle_kernel(count, *refs):
    own, got = refs[0], refs[1 : 1 + count]
    mats = refs[1 + count : 4 + count]
    outs, small = refs[-4:-1], refs[-1]
    total = own[...]
    for part in got:
        total = total + part[...].astype(F32)
    dot, at = jnp.zeros((total.shape[0], 1), F32), 0
    for mat, out in zip(mats, outs):
        width = mat.shape[1]
        part = total[:, at : at + width]
        out[...] = part
        dot = dot + jnp.sum(part * mat[...].astype(F32), axis=1, keepdims=True)
        at += width
    lane = lax.broadcasted_iota(jnp.int32, small.shape, 1)
    small[...] = jnp.where(lane == PAD - 1, dot, total[:, at:])


def settle(own, got, mats):
    rows = own.shape[0]
    return pl.pallas_call(
        functools.partial(settle_kernel, len(got)),
        out_shape=tuple(shape(mat.shape, F32) for mat in mats) + (shape((rows, PAD), F32),),
        in_specs=[VMEM] * (1 + len(got) + 3),
        out_specs=(VMEM,) * 4,
        compiler_params=params(60),
        name="settle",
    )(own, *got, *mats)


def rope_tables(rows):
    half = HEAD_SIZE // 2
    position = jnp.arange(rows).astype(F32)
    inverse = ROPE_BASE ** (-jnp.arange(half).astype(F32) / half)
    angles = position[:, None] * inverse[None, :]
    cosine, sine = jnp.cos(angles), jnp.sin(angles)
    return jnp.concatenate([cosine, cosine], axis=1), jnp.concatenate([-sine, sine], axis=1)


def per_device(
    sizes,
    tokens,
    lengths,
    routes,
    cotangent,
    gain_one,
    w_query,
    key_matrix,
    value_matrix,
    w_out,
    gain_two,
    w_router,
    w_gate,
    w_up,
    w_down,
):
    ndp = sizes["dp"]
    rows = tokens.shape[0]
    local, _, width = w_gate.shape
    me_dp = lax.axis_index("dp")
    length = lengths[0]
    ids = jnp.stack([me_dp, lax.axis_index("z"), lax.axis_index("core"), length]).astype(jnp.int32)
    live = (jnp.arange(rows) < length)[:, None]
    expert_ids = jnp.arange(EXPERTS, dtype=jnp.int32)

    extra = jnp.concatenate([gain_one[:, None], gain_two[:, None], w_router], axis=1)
    extra = jnp.pad(extra, ((0, 0), (0, PAD - extra.shape[1])))
    first = jnp.concatenate([w_query, key_matrix, value_matrix, extra], axis=1)
    named = jnp.any(routes[None, :, :] == expert_ids[:, None, None], axis=2).astype(BF16)
    named = jnp.pad(named, ((0, NOTE - EXPERTS), (0, MODEL_WIDTH - rows)))
    grad_low = jnp.where(live, cotangent, jnp.zeros_like(cotangent))
    grad_low = jnp.concatenate([grad_low, named], axis=0)
    grad_near = start_dp(grad_low, ndp)

    nz = sizes["z"]
    first_z = [first] + [exchange(first, "z", nz, k) for k in range(1, nz)]
    first_block = stack_after(first_z, grad_near)
    second_z = [w_out] + [exchange(w_out, "z", nz, k) for k in range(1, nz)]
    first_near = start_dp(first_block, ndp)
    first_dp = pass_on(first_block, first_near, ndp, second_z[1:])
    packed = after([pack(j, (w_gate, w_up, w_down)) for j in range(local)], first_z[1:] + grad_near)
    expert_mats = [lax.all_gather(p, ("z", "core"), axis=0, tiled=True) for p in packed]
    second_block = stack_after(second_z, [piece for *_, piece in first_dp[1:3]])
    second_dp = gather_direct(second_block, ndp)

    cosine, sine = rope_tables(rows)
    weights_in = gather_rows(first, first_dp, ids, sizes)
    qkv, mixed, h_one, gains, router = attend(ids, tokens, cosine, sine, weights_in, [], sizes)
    second_far = after([piece for *_, piece in second_dp[1:]], [mixed])
    second_dp = [(k, 0, piece) for k, piece in enumerate([second_block, *second_far])]
    grad_far = pass_on(grad_low, grad_near, ndp, second_far)
    weights_out = gather_rows(w_out, second_dp, ids, sizes)
    residual, *h_two = project(ids, tokens, mixed, gains, weights_out, sizes)
    hidden = gather_halves(h_two, ndp)
    turned = turn([mixed, h_one], [hidden[2][2]], ids, sizes)
    mixed, h_one = ([mine, exchange(other, "core", 2, 1)] for mine, other in turned)

    prev, gate_grads, sums = (), [], []
    for j in range(local):
        expert = jnp.stack([me_dp * local + j, me_dp]).astype(jnp.int32)
        *prev, grad_gate, terms = run_expert(
            j,
            j == local - 1,
            expert,
            router,
            hidden,
            grad_far,
            expert_mats[j],
            prev,
            gate_grads,
            ndp,
            [*mixed, *h_one],
        )
        gate_grads.append(grad_gate)
        sums.append(lax.psum_scatter(terms, ("z", "core"), scatter_dimension=0, tiled=True))
    outs, *backs = prev
    pairs = [tuple(backs[2 * k : 2 * k + 2]) for k in range(ndp)]
    backs = [*pairs[0], *scatter_dp(pairs, ndp)]
    (sent,) = after([outs], backs[2:])
    outs = lax.all_to_all(sent, "dp", split_axis=0, concat_axis=0, tiled=True)
    grad_resid, grad_attn, grad_pre, notes = back(
        ids,
        residual,
        h_two,
        cotangent,
        gains,
        router,
        cosine,
        sine,
        qkv,
        backs,
        weights_out,
        [sent],
        sizes,
    )
    if not by_blocks(sizes):
        notes = split_cores(notes, ids, sizes)
        notes = notes[0], exchange(notes[1], "core", 2, 1)
    else:
        notes = notes, exchange(notes, "core", 2, 1)
    grad_attn = grad_attn, exchange(grad_attn, "core", 2, 1)
    grad_pre = grad_pre, exchange(grad_pre, "core", 2, 1)
    out_terms = weight_terms(ids, mixed, grad_attn, (), grad_pre[1:], sizes)
    in_terms = weight_terms(ids, h_one, grad_pre, notes, sums[:-1] + [out_terms[0], outs], sizes)
    own, late = scatter_rows(*out_terms, sizes, in_terms[:1])
    grad_out = own + sum(part.astype(F32) for part in late)
    sending = []
    own, got = scatter_rows(*in_terms, sizes, seen=sending)
    grad_tokens = tokens_back(
        ids, tokens, gains, grad_pre[0], grad_resid, weights_in, sending, sizes
    )
    (outs,) = after([outs], sending)
    block_out = (residual + jnp.sum(outs.astype(F32), axis=0)).astype(BF16)
    *grad_in, small = settle(own, got, (w_query, key_matrix, value_matrix))
    expert_sums = finish_after(sums, late[:1])
    return (
        block_out,
        grad_tokens,
        small[:, PAD - 1] / gain_one.astype(F32),
        *grad_in,
        grad_out,
        small[:, 0],
        small[:, 8 : 8 + EXPERTS],
        *expert_sums,
    )


def solution(mesh):
    ndp, nf = mesh.shape["dp"], mesh.shape["fsdp"]
    sizes = {"dp": ndp, "z": nf // 2, "core": 2}
    split = Mesh(mesh.devices.reshape(ndp, nf // 2, 2), ("dp", "z", "core"))
    every = ("dp", "z", "core")
    rows = P(every, None)
    vector = P(every)
    expert = P("dp", ("z", "core"), None)

    def run(*args):
        return per_device(sizes, *args)

    return jax.shard_map(
        run,
        mesh=split,
        in_specs=(rows, vector, rows, rows, vector, rows, rows, rows, rows, vector, rows)
        + (expert,) * 3,
        out_specs=(rows, rows, vector, rows, rows, rows, rows, vector, rows) + (expert,) * 3,
        check_vma=False,
    )
```

```python
import functools

import jax
import jax.numpy as jnp
from jax import lax
from jax.experimental import pallas as pl
from jax.experimental.pallas import tpu as pltpu
from jax.sharding import Mesh
from jax.sharding import PartitionSpec as P

MODEL_WIDTH = 1536
QUERY_HEADS = 12
KEY_VALUE_HEADS = 2
HEAD_SIZE = 128
EXPERTS = 8
CAP = 160
GROUP = QUERY_HEADS // KEY_VALUE_HEADS
QW = QUERY_HEADS * HEAD_SIZE
KW = KEY_VALUE_HEADS * HEAD_SIZE
QKV = QW + 2 * KW
PAD = 128
FIRST = QKV + PAD
NOTE = 32
ROUTER = 16
EPS = 1e-06
ROPE_BASE = 1500000.0
NEG_FILL = -1e30
SCALE = HEAD_SIZE ** (-0.5)
F32 = jnp.float32
BF16 = jnp.bfloat16
TILE = 256
MIB = 1024 * 1024
HBM = pl.BlockSpec(memory_space=pltpu.HBM)
VMEM = pl.BlockSpec(memory_space=pltpu.VMEM)
SMEM = pl.BlockSpec(memory_space=pltpu.SMEM)


def nn(a, b):
    return lax.dot_general(a, b, (((1,), (0,)), ((), ())), preferred_element_type=F32)


def nt(a, b):
    return lax.dot_general(a, b, (((1,), (1,)), ((), ())), preferred_element_type=F32)


def tn(a, b):
    return lax.dot_general(a, b, (((0,), (0,)), ((), ())), preferred_element_type=F32)


def shape(dims, dtype):
    return jax.ShapeDtypeStruct(dims, dtype)


def params(mib):
    return pltpu.CompilerParams(vmem_limit_bytes=mib * MIB)


def cost(flops, data, special=0):
    return pl.CostEstimate(flops=flops, bytes_accessed=data, transcendentals=special)


def exchange(block, axis, size, step):
    return lax.ppermute(block, axis, [(i, i ^ step) for i in range(size)])


def start_dp(block, ndp):
    return [exchange(block, "dp", ndp, k) for k in ((1, 2) if ndp == 4 else range(1, ndp))]


def pass_on(block, near, ndp, before=()):
    if ndp != 4:
        return [(k, 0, piece) for k, piece in enumerate([block] + near)]
    side, up = after(near, before) if before else near
    half = block.shape[0] // 2
    return [
        (0, 0, block),
        (1, 0, side),
        (2, 0, up),
        (3, 0, exchange(side[:half], "dp", ndp, 2)),
        (3, half, exchange(up[half:], "dp", ndp, 1)),
    ]


def gather_direct(block, ndp):
    return [(k, 0, exchange(block, "dp", ndp, k) if k else block) for k in range(ndp)]


def gather_halves(halves, ndp):
    top, low = halves
    at = top.shape[0]
    if ndp != 4:
        return [
            (k, i * at, exchange(half, "dp", ndp, k) if k else half)
            for k in range(ndp)
            for i, half in enumerate(halves)
        ]
    side_top, up_low = exchange(top, "dp", ndp, 1), exchange(low, "dp", ndp, 2)
    side_low, up_top = exchange(low, "dp", ndp, 1), exchange(top, "dp", ndp, 2)
    return [
        (0, 0, top),
        (0, at, low),
        (1, 0, side_top),
        (2, at, up_low),
        (1, at, side_low),
        (2, 0, up_top),
        (3, 0, exchange(side_top, "dp", ndp, 2)),
        (3, at, exchange(up_low, "dp", ndp, 1)),
    ]


def start_sum(slots, ndp):
    if ndp != 4:
        return []
    return [exchange(slots[3][0], "dp", ndp, 1), exchange(slots[3][1], "dp", ndp, 2)]


def finish_sum(slots, past, ndp, before=(), seen=None):
    if ndp != 4:
        sent = [jnp.concatenate(slot, axis=0) for slot in slots[1:]]
    else:
        past = after(past, before) if before else past
        add = lambda a, b: (a.astype(F32) + b.astype(F32)).astype(BF16)
        sent = [
            jnp.concatenate([slots[1][0], add(slots[1][1], past[1])], axis=0),
            jnp.concatenate([add(slots[2][0], past[0]), slots[2][1]], axis=0),
        ]
    if seen is not None:
        seen.extend(sent)
    return [exchange(part, "dp", ndp, k + 1) for k, part in enumerate(sent)]


def both_cores(pieces):
    return [
        (k, c, start, exchange(piece, "core", 2, 1) if c else piece)
        for k, start, piece in pieces
        for c in range(2)
    ]


def stack_kernel(count, *refs):
    for i in range(count):
        refs[-1][i] = refs[i][...]


def stack_after(parts, before):
    dims = (len(parts),) + parts[0].shape
    return pl.pallas_call(
        functools.partial(stack_kernel, len(parts)),
        out_shape=shape(dims, parts[0].dtype),
        in_specs=[VMEM] * len(parts) + [HBM] * len(before),
        out_specs=VMEM,
        compiler_params=params(60),
        cost_estimate=cost(0, 4 * dims[0] * dims[1] * dims[2]),
        name="stack",
    )(*parts, *before)


def pack_kernel(index, *refs):
    width = refs[0].shape[2]
    for i in range(3):
        refs[-1][:, i * width : (i + 1) * width] = refs[i][index]


def pack(index, mats):
    _, rows, width = mats[0].shape
    return pl.pallas_call(
        functools.partial(pack_kernel, index),
        out_shape=shape((rows, 3 * width), BF16),
        in_specs=[VMEM] * 3,
        out_specs=VMEM,
        compiler_params=params(60),
        name="pack",
    )(*mats)


def finish_kernel(count, *refs):
    outs = refs[-3:]
    width = outs[0].shape[2]
    for j in range(count):
        for i in range(3):
            outs[i][j] = refs[j][:, i * width : (i + 1) * width].astype(F32)


def finish_after(sums, before):
    rows, width = sums[0].shape[0], sums[0].shape[1] // 3
    return pl.pallas_call(
        functools.partial(finish_kernel, len(sums)),
        out_shape=(shape((len(sums), rows, width), F32),) * 3,
        in_specs=[VMEM] * len(sums) + [HBM] * len(before),
        out_specs=(VMEM,) * 3,
        compiler_params=params(60),
        name="finish",
    )(*sums, *before)


def after_kernel(*refs):
    pass


def after(arrays, before):
    return pl.pallas_call(
        after_kernel,
        out_shape=tuple(shape(a.shape, a.dtype) for a in arrays),
        in_specs=[HBM] * (len(arrays) + len(before)),
        out_specs=(HBM,) * len(arrays),
        input_output_aliases={i: i for i in range(len(arrays))},
        name="after",
    )(*arrays, *before)


def block_rows(sizes):
    return MODEL_WIDTH // (2 * sizes["dp"] * sizes["z"])


def by_blocks(sizes):
    return block_rows(sizes) % 16 == 0


def gather_rows(block, along_dp, ids, sizes):
    ndp, nz = sizes["dp"], sizes["z"]
    pieces = both_cores(along_dp)
    if by_blocks(sizes):
        places = tuple((k, c, start, piece.shape[0]) for k, c, start, piece in pieces)
        return places, [piece for *_, piece in pieces]
    columns = block.shape[-1]
    whole = jnp.zeros((ndp, nz, 2, block_rows(sizes), columns), BF16)
    for k, c, start, piece in pieces:
        order = ids[1] ^ jnp.arange(start, start + piece.shape[0])
        whole = whole.at[ids[0] ^ k, order, ids[2] ^ c].set(piece)
    return None, [whole.reshape(MODEL_WIDTH, columns)]


def split_cores(columns, ids, sizes):
    ndp, nz = sizes["dp"], sizes["z"]
    rows = columns.shape[0]
    blocks = columns.reshape(rows, ndp, nz, 2, block_rows(sizes))
    blocks = jnp.take(jnp.take(blocks, ids[0] ^ jnp.arange(ndp), 1), ids[1] ^ jnp.arange(nz), 2)
    halves = [lax.dynamic_index_in_dim(blocks, ids[2] ^ c, 3, keepdims=False) for c in range(2)]
    return [half.reshape(rows, MODEL_WIDTH // 2) for half in halves]


def turn_kernel(ndp, nz, count, ids, *refs):
    block = MODEL_WIDTH // (2 * ndp * nz)
    turned = refs[-1]
    for i in range(count):
        turned[...] = jnp.transpose(refs[i][...])
        for k in range(ndp):
            for z in range(nz):
                for c in range(2):
                    at = ((ids[0] ^ k) * nz + (ids[1] ^ z)) * 2 + (ids[2] ^ c)
                    place = pl.ds(pl.multiple_of(at * block, block), block)
                    dest = refs[-1 - 2 * count + 2 * i + c]
                    dest[(k * nz + z) * block : (k * nz + z + 1) * block] = turned[place, :]


def turn(arrays, before, ids, sizes):
    if not by_blocks(sizes):
        return [[half.T for half in split_cores(array, ids, sizes)] for array in arrays]
    rows = arrays[0].shape[0]
    halves = pl.pallas_call(
        functools.partial(turn_kernel, sizes["dp"], sizes["z"], len(arrays)),
        out_shape=(shape((MODEL_WIDTH // 2, rows), BF16),) * (2 * len(arrays)),
        in_specs=[SMEM] + [VMEM] * len(arrays) + [HBM] * len(before),
        out_specs=(VMEM,) * (2 * len(arrays)),
        scratch_shapes=[pltpu.VMEM((MODEL_WIDTH, rows), BF16)],
        compiler_params=params(60),
        name="turn",
    )(ids, *arrays, *before)
    return [halves[2 * i : 2 * i + 2] for i in range(len(arrays))]


def scatter_rows(own, slots, sizes, before=(), seen=None):
    ndp, nz = sizes["dp"], sizes["z"]
    slots = [None, *slots]
    total, parts = own, finish_sum(slots, start_sum(slots, ndp), ndp, before, seen)
    for part in parts:
        total = total + part.astype(F32)
    rows = block_rows(sizes)
    blocks = [total[z * rows : (z + 1) * rows] for z in range(nz)]
    if nz != 4:
        sent = [block.astype(BF16) for block in blocks[1:]]
        got = [exchange(block, "z", nz, z + 1) for z, block in enumerate(sent)]
        return blocks[0], got, parts, sent[-1]
    near = exchange(jnp.concatenate([blocks[1], blocks[3]], axis=0).astype(BF16), "z", nz, 1)
    passed = (blocks[2] + near[rows:].astype(F32)).astype(BF16)
    return blocks[0], [near[:rows], exchange(passed, "z", nz, 2)], parts, passed


def load_rows(ids, ndp, nz, places, parts, dest, sem):
    if places is None:
        loads = [pltpu.make_async_copy(parts[0], dest, sem.at[0])]
        loads[0].start()
        return loads
    rows = MODEL_WIDTH // (ndp * nz * 2)
    loads = []
    for (k, c, start, count), part in zip(places, parts):
        for z in range(count):
            block = ((ids[0] ^ k) * nz + (ids[1] ^ (start + z))) * 2 + (ids[2] ^ c)
            place = pl.ds(pl.multiple_of(block * rows, rows), rows)
            copy = pltpu.make_async_copy(part.at[z], dest.at[place, :], sem.at[len(loads)])
            loads.append(copy)
    for load in loads:
        load.start()
    return loads


def start_all(pairs, sem):
    copies = [pltpu.make_async_copy(a, b, sem.at[i]) for i, (a, b) in enumerate(pairs)]
    for copy in copies:
        copy.start()
    return copies


def wait_all(copies):
    for copy in copies:
        copy.wait()


def rms_scale(rows):
    return lax.rsqrt(jnp.mean(rows * rows, axis=-1, keepdims=True) + EPS)


def norm_back(normed, row_scale, grad):
    return row_scale * (grad - normed * jnp.mean(grad * normed, axis=-1, keepdims=True))


def swapped(vals):
    return pltpu.roll(vals, HEAD_SIZE // 2, 1)


def head(h):
    return slice(h * HEAD_SIZE, (h + 1) * HEAD_SIZE)


def seen(rows, length):
    q = lax.broadcasted_iota(jnp.int32, (rows, rows), 0)
    s = lax.broadcasted_iota(jnp.int32, (rows, rows), 1)
    return (s <= q) & (s < length)


def attention_probs(query, key, visible):
    scores = jnp.where(visible, nt(query, key) * SCALE, NEG_FILL)
    expon = jnp.exp(scores - jnp.max(scores, axis=-1, keepdims=True))
    return expon / jnp.sum(expon, axis=-1, keepdims=True)


def route_softmax(router_rows, hidden):
    logits = nt(router_rows, hidden)[:EXPERTS]
    expon = jnp.exp(logits - jnp.max(logits, axis=0, keepdims=True))
    return expon / jnp.sum(expon, axis=0, keepdims=True)


def attend_kernel(ndp, nz, places, count, ids, tokens, cosine, sine, *refs):
    parts = refs[:count]
    qkv, mixed, h_one, gains, router, w, sem = refs[-7:]
    rows = tokens.shape[0]
    loads = load_rows(ids, ndp, nz, places, parts, w, sem)
    tok = tokens[...].astype(F32)
    normed = tok * rms_scale(tok)
    for load in loads:
        load.wait()
    extra = jnp.transpose(w[:, QKV:].astype(F32))
    gains[...] = extra[:8]
    router[...] = extra[2 : 2 + ROUTER].astype(BF16)
    h_one[...] = (normed * extra[0:1]).astype(BF16)
    cos, sin = cosine[...], sine[...]
    for t in range(QKV // TILE):
        pre = nn(h_one[...], w[:, t * TILE : (t + 1) * TILE])
        for i in range(TILE // HEAD_SIZE):
            part = pre[:, head(i)]
            at = t * TILE + i * HEAD_SIZE
            if at < QW + KW:
                part = part * cos + swapped(part) * sin
            qkv[:, at : at + HEAD_SIZE] = part.astype(BF16)
    visible = seen(rows, ids[3])
    for h in range(QUERY_HEADS):
        g = h // GROUP
        probs = attention_probs(qkv[:, head(h)], qkv[:, head(QUERY_HEADS + g)], visible)
        values = qkv[:, head(QUERY_HEADS + KEY_VALUE_HEADS + g)]
        mixed[:, head(h)] = nn(probs.astype(BF16), values).astype(BF16)


def attend(ids, tokens, cosine, sine, weights, before, sizes):
    places, parts = weights
    ndp, nz = sizes["dp"], sizes["z"]
    rows = tokens.shape[0]
    return pl.pallas_call(
        functools.partial(attend_kernel, ndp, nz, places, len(parts)),
        out_shape=(
            shape((rows, QKV), BF16),
            shape((rows, QW), BF16),
            shape((rows, MODEL_WIDTH), BF16),
            shape((8, MODEL_WIDTH), F32),
            shape((ROUTER, MODEL_WIDTH), BF16),
        ),
        in_specs=[SMEM, VMEM, VMEM, VMEM] + [HBM] * (len(parts) + len(before)),
        out_specs=(VMEM,) * 5,
        scratch_shapes=[
            pltpu.VMEM((MODEL_WIDTH, FIRST), BF16),
            pltpu.SemaphoreType.DMA((2 * ndp * nz,)),
        ],
        compiler_params=params(60),
        cost_estimate=cost(2 * rows * MODEL_WIDTH * QKV, 10 * MIB, 12 * rows * rows),
        name="attend",
    )(ids, tokens, cosine, sine, *parts, *before)


def project_kernel(ndp, nz, places, ids, tokens, mixed, gains, *refs):
    *parts, residual, top, low, w, sem = refs
    loads = load_rows(ids, ndp, nz, places, parts, w, sem)
    for load in loads:
        load.wait()
    for t in range(MODEL_WIDTH // TILE):
        lane = slice(t * TILE, (t + 1) * TILE)
        residual[:, lane] = tokens[:, lane].astype(F32) + nn(mixed[...], w[:, lane])
    whole = residual[...]
    h_two = (whole * rms_scale(whole) * gains[1:2]).astype(BF16)
    half = top.shape[0]
    top[...], low[...] = h_two[:half], h_two[half:]


def project(ids, tokens, mixed, gains, weights, sizes):
    places, parts = weights
    ndp, nz = sizes["dp"], sizes["z"]
    rows = tokens.shape[0]
    return pl.pallas_call(
        functools.partial(project_kernel, ndp, nz, places),
        out_shape=(shape((rows, MODEL_WIDTH), F32),)
        + (shape((rows // 2, MODEL_WIDTH), BF16),) * 2,
        in_specs=[SMEM, VMEM, VMEM, VMEM] + [HBM] * len(parts),
        out_specs=(VMEM,) * 3,
        scratch_shapes=[
            pltpu.VMEM((QW, MODEL_WIDTH), BF16),
            pltpu.SemaphoreType.DMA((2 * ndp * nz,)),
        ],
        compiler_params=params(60),
        cost_estimate=cost(2 * rows * MODEL_WIDTH * QW, 8 * MIB),
        name="project",
    )(ids, tokens, mixed, gains, *parts)


def expert_kernel(ndp, rows, width, index, last, near, far, unread, *refs):
    it = iter(refs)
    take = lambda n: [next(it) for _ in range(n)]
    (expert_ref, router_ref) = take(2)
    prev_gates = take(index)
    hid_in, cot_in = take(len(near)), take(len(far))
    (w_in,) = take(1)
    prev_in = take(2) if index else []
    take(unread)
    out_hbm, back_hbm = take(2 * ndp - 1 if last else 1), take(2 * ndp if last else 1)
    gates_ref, terms_hbm = take(2)
    hid, cot, w, x, d, ge, inner, dg, du, pick, pick_t, slot_gate, slot_dot = take(13)
    (terms_buf,) = take(1)
    prev = take(2) if index else []
    in_sem, out_sem = take(2)
    depth = MODEL_WIDTH
    tiles = depth // TILE

    loads = {}

    def load(name, source, dest):
        copy = pltpu.make_async_copy(source, dest, in_sem.at[len(loads)])
        copy.start()
        loads[name] = copy

    for i, (k, start, count) in enumerate(near):
        load(("hid", i), hid_in[i], hid.at[k, pl.ds(start, count), :])
    for i, (k, start, count) in enumerate(far):
        load(("cot", i), cot_in[i], cot.at[k, pl.ds(start, count), :])
    load("w", w_in, w)
    for i in range(len(prev)):
        load(("prev", i), prev_in[i], prev[i])

    expert = expert_ref[0]
    which = lax.broadcasted_iota(jnp.int32, (EXPERTS, rows), 0) == expert
    earlier = (
        (
            lax.broadcasted_iota(jnp.int32, (rows, rows), 0)
            < lax.broadcasted_iota(jnp.int32, (rows, rows), 1)
        )
        .astype(F32)
        .astype(BF16)
    )
    slot = lax.broadcasted_iota(jnp.int32, (CAP, rows), 0).astype(F32)
    for s in range(ndp):
        for i, piece in enumerate(near):
            if piece[0] == s:
                loads["hid", i].wait()
        for i, piece in enumerate(far):
            if piece[0] == s:
                loads["cot", i].wait()
        hidden = hid[s]
        probs = route_softmax(router_ref[...], hidden)
        named = cot[s, rows : rows + NOTE, :rows]
        place = nn(named, earlier)[:EXPERTS]
        named = named[:EXPERTS].astype(F32)
        named_row = jnp.sum(jnp.where(which, named, 0.0), axis=0, keepdims=True)
        gate_row = jnp.sum(jnp.where(which, probs, 0.0), axis=0, keepdims=True)
        place_row = jnp.sum(jnp.where(which, place, 0.0), axis=0, keepdims=True)
        chosen = jnp.where((slot == place_row) & (named_row > 0.5), 1.0, 0.0)
        pick[s] = chosen.astype(BF16)
        pick_t[s] = jnp.transpose(chosen).astype(BF16)
        at = pl.ds(s * CAP, CAP)
        gate = jnp.sum(chosen * gate_row, axis=1, keepdims=True)
        slot_gate[at, :] = jnp.broadcast_to(gate, (CAP, 128))
        x[at, :] = nn(pick[s], hidden).astype(BF16)
        grads = nn(pick[s], cot[s, :rows])
        d[at, :] = grads.astype(BF16)
        ge[at, :] = (gate * grads).astype(BF16)
    loads["w"].wait()

    def hidden_units(t, carry):
        at = pl.multiple_of(t * TILE, TILE)
        gate_pre = nn(x[...], w[:, pl.ds(at, TILE)])
        up_pre = nn(x[...], w[:, pl.ds(width + at, TILE)])
        grad_inner = nn(ge[...], w[:, pl.ds(2 * width + at, TILE)])
        sig = 1.0 / (1.0 + jnp.exp(-gate_pre))
        act = gate_pre * sig
        inner[:, pl.ds(at, TILE)] = (act * up_pre).astype(BF16)
        dg[:, pl.ds(at, TILE)] = (
            grad_inner * up_pre * sig * (1.0 + gate_pre * (1.0 - sig))
        ).astype(BF16)
        du[:, pl.ds(at, TILE)] = (grad_inner * act).astype(BF16)
        return carry

    lax.fori_loop(0, width // TILE, hidden_units, 0)
    slot_dot[...] = jnp.zeros_like(slot_dot)
    for i in range(len(prev)):
        loads["prev", i].wait()

    noted = (rows + NOTE) // 2

    def stores(t):
        lane = pl.ds(pl.multiple_of(t * TILE, TILE), TILE)
        copies = [(terms_buf.at[lane, :], terms_hbm.at[lane, :])]
        if not last:
            body = pl.ds(0, rows)
            copies.append((hid.at[:, :, lane], out_hbm[0].at[:, :, lane]))
            copies.append((cot.at[:, body, lane], back_hbm[0].at[:, body, lane]))
        else:
            copies.append((hid.at[0, :, lane], out_hbm[0].at[:, lane]))
            for i in range(2, 2 * ndp):
                first = pl.ds(i % 2 * (rows // 2), rows // 2)
                copies.append((hid.at[i // 2, first, lane], out_hbm[i - 1].at[:, lane]))
            for i in range(2 * ndp):
                body = pl.ds(0, noted if i % 2 == 0 else rows - noted)
                taken = pl.ds(i % 2 * noted, noted if i % 2 == 0 else rows - noted)
                copies.append((cot.at[i // 2, taken, lane], back_hbm[i].at[body, lane]))
        return [
            pltpu.make_async_copy(source, dest, out_sem.at[i, t])
            for i, (source, dest) in enumerate(copies)
        ]

    def features(t, carry):
        lane = pl.ds(pl.multiple_of(t * TILE, TILE), TILE)
        result = nt(inner[...], w[lane, pl.ds(2 * width, width)]).astype(BF16).astype(F32)
        partial = jnp.sum(result * d[:, lane].astype(F32), axis=1, keepdims=True)
        slot_dot[...] += jnp.broadcast_to(partial, slot_dot.shape)
        gated = (slot_gate[:, :1] * result).astype(BF16)
        grad_in = (
            nt(dg[...], w[lane, pl.ds(0, width)]) + nt(du[...], w[lane, pl.ds(width, width)])
        ).astype(BF16)
        for s in range(ndp):
            part = slice(s * CAP, (s + 1) * CAP)
            sent = nn(pick_t[s], gated[part])
            back = nn(pick_t[s], grad_in[part])
            if prev:
                sent = sent + prev[0][s, :, lane].astype(F32)
                back = back + prev[1][s, :rows, lane].astype(F32)
            hid[s, :, lane] = sent.astype(BF16)
            cot[s, :rows, lane] = back.astype(BF16)
        x_t = jnp.transpose(x[:, lane])
        terms_buf[lane, pl.ds(0, width)] = nn(x_t, dg[...]).astype(BF16)
        terms_buf[lane, pl.ds(width, width)] = nn(x_t, du[...]).astype(BF16)
        ge_t = jnp.transpose(ge[:, lane])
        terms_buf[lane, pl.ds(2 * width, width)] = nn(ge_t, inner[...]).astype(BF16)
        for store in stores(t):
            store.start()
        return carry

    lax.fori_loop(0, tiles, features, 0)
    line = lax.broadcasted_iota(jnp.int32, (NOTE, 3 * rows), 0)
    notes = []
    for s in range(ndp):
        part = slice(s * CAP, (s + 1) * CAP)
        own = jnp.sum(pick[s].astype(F32) * slot_dot[part, :1], axis=0, keepdims=True)
        gates_ref[s] = own
        if not last:
            continue
        note = jnp.zeros((NOTE, 3 * rows), F32)
        for j, row in enumerate([p[s] for p in prev_gates] + [own]):
            high = row.astype(BF16).astype(F32)
            middle = (row - high).astype(BF16).astype(F32)
            low = row - high - middle
            at = expert - index + j
            note = jnp.where(line == at, jnp.concatenate([high, middle, low], axis=1), note)
        cot[s, rows : rows + NOTE, : 3 * rows] = note.astype(BF16)
        notes.append(
            pltpu.make_async_copy(
                cot.at[s, pl.ds(rows, NOTE), :],
                back_hbm[2 * s + 1].at[pl.ds(rows - noted, NOTE), :],
                out_sem.at[4 * ndp + 1, s],
            )
        )
        notes[-1].start()
    for t in range(tiles):
        for store in stores(t):
            store.wait()
    for note in notes:
        note.wait()


def run_expert(index, last, expert, router, hidden, grads, w_all, prev, prev_gates, ndp, before):
    rows = 2 * hidden[0][2].shape[0]
    near, far = (tuple((k, at, p.shape[0]) for k, at, p in group) for group in (hidden, grads))
    width = w_all.shape[1] // 3
    slots = ndp * CAP
    depth = MODEL_WIDTH
    tiles = depth // TILE
    scratch = [
        pltpu.VMEM((ndp, rows, depth), BF16),
        pltpu.VMEM((ndp, rows + NOTE, depth), BF16),
        pltpu.VMEM((depth, 3 * width), BF16),
        pltpu.VMEM((slots, depth), BF16),
        pltpu.VMEM((slots, depth), BF16),
        pltpu.VMEM((slots, depth), BF16),
        pltpu.VMEM((slots, width), BF16),
        pltpu.VMEM((slots, width), BF16),
        pltpu.VMEM((slots, width), BF16),
        pltpu.VMEM((ndp, CAP, rows), BF16),
        pltpu.VMEM((ndp, rows, CAP), BF16),
        pltpu.VMEM((slots, 128), F32),
        pltpu.VMEM((slots, 128), F32),
        pltpu.VMEM((depth, 3 * width), BF16),
    ]
    if index:
        scratch += [
            pltpu.VMEM((ndp, rows, depth), BF16),
            pltpu.VMEM((ndp, rows + NOTE, depth), BF16),
        ]
    scratch += [
        pltpu.SemaphoreType.DMA((len(near) + len(far) + 3,)),
        pltpu.SemaphoreType.DMA((4 * ndp + 2, max(tiles, ndp))),
    ]
    sent = [shape((ndp, rows, depth), BF16), shape((ndp, rows + NOTE, depth), BF16)]
    if last:
        sent = [shape((rows, depth), BF16)]
        sent += [shape((rows // 2, depth), BF16)] * (2 * ndp - 2)
        sent += [shape(((rows + NOTE) // 2, depth), BF16)] * (2 * ndp)
    flops = 2 * slots * depth * width * 9 + 8 * ndp * CAP * rows * depth
    return pl.pallas_call(
        functools.partial(
            expert_kernel, ndp, rows, width, index, last, near, far, len(before)
        ),
        out_shape=(
            *sent,
            shape((ndp, 1, rows), F32),
            shape((depth, 3 * width), BF16),
        ),
        in_specs=[SMEM, VMEM]
        + [VMEM] * len(prev_gates)
        + [HBM] * (len(near) + len(far) + 1 + len(prev) + len(before)),
        out_specs=(HBM,) * len(sent) + (VMEM, HBM),
        scratch_shapes=scratch,
        compiler_params=params(60),
        cost_estimate=cost(flops, 40 * MIB, slots * width),
        name="expert",
    )(
        expert,
        router,
        *prev_gates,
        *(piece for *_, piece in hidden),
        *(piece for *_, piece in grads),
        w_all,
        *prev,
        *before,
    )


def back_kernel(ndp, nz, places, count, given, unread, ids, gains, router, cosine, sine, *refs):
    refs = list(refs)
    take = lambda n: [refs.pop(0) for _ in range(n)]
    data, backs, parts = take(5), take(given), take(count)
    take(unread)
    out_resid, out_attn, out_pre, notes = take(4)
    residual, top, low, grads, qkv = held = take(5)
    got = take(given)
    w, grad_mixed, grad_resid, grad_attn, grad_pre, sem, data_sem, out_sem = refs
    rows = residual.shape[0]
    fetched = start_all(list(zip(backs + data[1:3] + data[:1] + data[3:], got + held[1:3] + held[:1] + held[3:])), data_sem)
    loads = load_rows(ids, ndp, nz, places, parts, w, sem)
    wait_all(fetched[:given])
    whole = jnp.concatenate([got[0][...], got[1][...]], axis=0).astype(F32)
    for part in got[2:]:
        whole = whole + part[...].astype(F32)
    grad_h = whole[:rows]
    note = whole[rows : rows + EXPERTS, : 3 * rows]
    grad_route = note[:, :rows] + note[:, rows : 2 * rows] + note[:, 2 * rows :]
    wait_all(fetched[given : given + 4])
    hidden = jnp.concatenate([top[...], low[...]], axis=0)
    probs = route_softmax(router[...], hidden)
    grad_logits = probs * (grad_route - jnp.sum(probs * grad_route, axis=0, keepdims=True))
    grad_logits = jnp.concatenate([grad_logits, jnp.zeros_like(grad_logits)], axis=0)
    grad_logits = grad_logits.astype(BF16)
    grad_h = grad_h + tn(grad_logits, router[...])
    res = residual[...]
    scale = rms_scale(res)
    normed = res * scale
    notes[0:8] = jnp.broadcast_to(
        jnp.sum(normed * grad_h, axis=0, keepdims=True), (8, MODEL_WIDTH)
    )
    notes[8:16] = nn(grad_logits, hidden)[:EXPERTS]
    live = lax.broadcasted_iota(jnp.int32, (rows, 1), 0) < ids[3]
    final = jnp.where(live, grads[...].astype(F32), 0.0)
    total = final + norm_back(normed, scale, grad_h * gains[1:2])
    grad_resid[...] = total
    grad_attn[...] = total.astype(BF16)
    stores = start_all([(grad_attn, out_attn), (grad_resid, out_resid)], out_sem)
    wait_all(loads)
    for t in range(QW // TILE):
        lane = slice(t * TILE, (t + 1) * TILE)
        grad_mixed[:, lane] = nt(grad_attn[...], w[lane, :]).astype(BF16)
    wait_all(fetched[given + 4 :])
    source = lax.broadcasted_iota(jnp.int32, (rows, rows), 0)
    visible = (source <= lax.broadcasted_iota(jnp.int32, (rows, rows), 1)) & (source < ids[3])
    cos, sin = cosine[...], sine[...]
    for g in range(KEY_VALUE_HEADS):
        key = qkv[:, head(QUERY_HEADS + g)]
        value = qkv[:, head(QUERY_HEADS + KEY_VALUE_HEADS + g)]
        grad_key = jnp.zeros((rows, HEAD_SIZE), F32)
        grad_value = jnp.zeros((rows, HEAD_SIZE), F32)
        for h in range(g * GROUP, (g + 1) * GROUP):
            query, grad = qkv[:, head(h)], grad_mixed[:, head(h)]
            scores = jnp.where(visible, nt(key, query) * SCALE, NEG_FILL)
            expon = jnp.exp(scores - jnp.max(scores, axis=0, keepdims=True))
            probs = expon / jnp.sum(expon, axis=0, keepdims=True)
            grad_probs = nt(value, grad)
            grad_value = grad_value + nn(probs.astype(BF16), grad)
            row_dot = jnp.sum(probs * grad_probs, axis=0, keepdims=True)
            grad_scores = (probs * (grad_probs - row_dot)).astype(BF16)
            grad_query = tn(grad_scores, key) * SCALE
            grad_key = grad_key + nn(grad_scores, query)
            grad_pre[:, head(h)] = (grad_query * cos - swapped(grad_query) * sin).astype(BF16)
        grad_key = grad_key * SCALE
        grad_pre[:, head(QUERY_HEADS + g)] = (
            grad_key * cos - swapped(grad_key) * sin
        ).astype(BF16)
        grad_pre[:, head(QUERY_HEADS + KEY_VALUE_HEADS + g)] = grad_value.astype(BF16)
    last = pltpu.make_async_copy(grad_pre, out_pre, out_sem.at[2])
    last.start()
    wait_all(stores + [last])


def back(
    ids, residual, h_two, grads, gains, router, cosine, sine, qkv, backs, weights, before, sizes
):
    ndp, nz = sizes["dp"], sizes["z"]
    places, parts = weights
    rows = residual.shape[0]
    data = [residual, *h_two, grads, qkv]
    made = [
        shape((rows, MODEL_WIDTH), F32),
        shape((rows, MODEL_WIDTH), BF16),
        shape((rows, QKV), BF16),
    ]
    room = lambda array: pltpu.VMEM(array.shape, array.dtype)
    return pl.pallas_call(
        functools.partial(
            back_kernel, ndp, nz, places, len(parts), len(backs), len(before)
        ),
        out_shape=(*made, shape((16, MODEL_WIDTH), F32)),
        in_specs=[SMEM]
        + [VMEM] * 4
        + [HBM] * (len(data) + len(backs) + len(parts) + len(before)),
        out_specs=(HBM, HBM, HBM, VMEM),
        scratch_shapes=[
            *(room(array) for array in data + backs),
            pltpu.VMEM((QW, MODEL_WIDTH), BF16),
            pltpu.VMEM((rows, QW), BF16),
            *(room(array) for array in made),
            pltpu.SemaphoreType.DMA((2 * ndp * nz,)),
            pltpu.SemaphoreType.DMA((len(data) + len(backs),)),
            pltpu.SemaphoreType.DMA((3,)),
        ],
        compiler_params=params(60),
        cost_estimate=cost(3 * rows * MODEL_WIDTH * QW, 16 * MIB, 12 * rows * rows),
        name="back",
    )(ids, gains, router, cosine, sine, *data, *backs, *parts, *before)


def tokens_back_kernel(ndp, nz, places, count, ids, tokens, gains, grad_pre, grad_resid, *refs):
    parts = refs[:count]
    grad_tokens, w, sem = refs[-3:]
    loads = load_rows(ids, ndp, nz, places, parts, w, sem)
    tok = tokens[...].astype(F32)
    scale = rms_scale(tok)
    normed = tok * scale
    for load in loads:
        load.wait()
    for t in range(MODEL_WIDTH // TILE):
        lane = slice(t * TILE, (t + 1) * TILE)
        grad_tokens[:, lane] = nt(grad_pre[...], w[lane, :QKV])
    grad_h = grad_tokens[...]
    grad_tokens[...] = grad_resid[...] + norm_back(normed, scale, grad_h * gains[0:1])


def tokens_back(ids, tokens, gains, grad_pre, grad_resid, weights, before, sizes):
    ndp, nz = sizes["dp"], sizes["z"]
    places, parts = weights
    rows = tokens.shape[0]
    return pl.pallas_call(
        functools.partial(tokens_back_kernel, ndp, nz, places, len(parts)),
        out_shape=shape((rows, MODEL_WIDTH), F32),
        in_specs=[SMEM] + [VMEM] * 4 + [HBM] * (len(parts) + len(before)),
        out_specs=VMEM,
        scratch_shapes=[
            pltpu.VMEM((MODEL_WIDTH, FIRST), BF16),
            pltpu.SemaphoreType.DMA((2 * ndp * nz,)),
        ],
        compiler_params=params(60),
        cost_estimate=cost(2 * rows * MODEL_WIDTH * QKV, 12 * MIB),
        name="tokens_back",
    )(ids, tokens, gains, grad_pre, grad_resid, *parts, *before)


def terms_kernel(ndp, nz, noted, unread, ids, *refs):
    refs = list(refs)
    take = lambda n: [refs.pop(0) for _ in range(n)]
    notes, given = take(2 if noted else 0), take(4)
    take(unread)
    count = 2 * ndp - 1
    outs, held, dests = take(count), take(4), take(count)
    note_rows, in_sem, out_sem = refs
    wait_all(start_all(list(zip(given, held)), in_sem))
    left = jnp.concatenate([held[0][...], held[1][...]], axis=1)
    right = jnp.concatenate([held[2][...], held[3][...]], axis=0)
    slot = MODEL_WIDTH // (2 * ndp)
    stores = []

    def put(lane, value):
        dests[0][:, lane] = value[:slot]
        for i in range(1, count):
            at = slot + (i - 1) * (slot // 2)
            dests[i][:, lane] = value[at : at + slot // 2].astype(BF16)
        pairs = [(dests[i].at[:, lane], outs[i].at[:, lane]) for i in range(count)]
        stores.extend(start_all(pairs, out_sem.at[len(stores) // count]))

    if noted:
        note = notes[0][...] + notes[1][...]
        block = jnp.concatenate([note, jnp.zeros((PAD - 16, note.shape[1]), F32)], axis=0)
        block = jnp.transpose(block)
    if noted == 1:
        note_rows[...] = block
        rows = MODEL_WIDTH // (2 * ndp * nz)
        taken = []
        for k in range(ndp):
            for z in range(nz):
                at = ((ids[0] ^ k) * nz + (ids[1] ^ z)) * 2 + ids[2]
                taken.append(note_rows[pl.ds(pl.multiple_of(at * rows, rows), rows), :])
        block = jnp.concatenate(taken, axis=0)
    if noted:
        put(slice(right.shape[1], right.shape[1] + PAD), block)
    for t in range(right.shape[1] // TILE):
        lane = slice(t * TILE, (t + 1) * TILE)
        put(lane, nn(left, right[:, lane]))
    wait_all(stores)


def weight_terms(ids, left, right, notes, before, sizes):
    ndp, nz = sizes["dp"], sizes["z"]
    slot = MODEL_WIDTH // (2 * ndp)
    columns = right[0].shape[1] + (PAD if notes else 0)
    noted = 0 if not notes else 1 if notes[0].shape[1] == MODEL_WIDTH else 2
    made = [shape((slot, columns), F32)] + [shape((slot // 2, columns), BF16)] * (2 * ndp - 2)
    room = lambda array: pltpu.VMEM(array.shape, array.dtype)
    arrays = [*left, *right]
    found = pl.pallas_call(
        functools.partial(terms_kernel, ndp, nz, noted, len(before)),
        out_shape=tuple(made),
        in_specs=[SMEM] + [VMEM] * len(notes) + [HBM] * (4 + len(before)),
        out_specs=(HBM,) * len(made),
        scratch_shapes=[
            *(room(array) for array in arrays + made),
            pltpu.VMEM((MODEL_WIDTH, PAD), F32),
            pltpu.SemaphoreType.DMA((4,)),
            pltpu.SemaphoreType.DMA((columns // TILE + 1, len(made))),
        ],
        compiler_params=params(60),
        cost_estimate=cost(2 * MODEL_WIDTH * left[0].shape[1] * columns, 5 * MIB),
        name="weight_terms",
    )(ids, *notes, *arrays, *before)
    return found[0], [tuple(found[i : i + 2]) for i in range(1, len(found), 2)]


def settle_kernel(count, *refs):
    own, got = refs[0], refs[1 : 1 + count]
    mats = refs[1 + count : 4 + count]
    outs, small = refs[-4:-1], refs[-1]
    total = own[...]
    for part in got:
        total = total + part[...].astype(F32)
    dot, at = jnp.zeros((total.shape[0], 1), F32), 0
    for mat, out in zip(mats, outs):
        width = mat.shape[1]
        part = total[:, at : at + width]
        out[...] = part
        dot = dot + jnp.sum(part * mat[...].astype(F32), axis=1, keepdims=True)
        at += width
    lane = lax.broadcasted_iota(jnp.int32, small.shape, 1)
    small[...] = jnp.where(lane == PAD - 1, dot, total[:, at:])


def settle(own, got, mats):
    rows = own.shape[0]
    return pl.pallas_call(
        functools.partial(settle_kernel, len(got)),
        out_shape=tuple(shape(mat.shape, F32) for mat in mats) + (shape((rows, PAD), F32),),
        in_specs=[VMEM] * (1 + len(got) + 3),
        out_specs=(VMEM,) * 4,
        compiler_params=params(60),
        name="settle",
    )(own, *got, *mats)


def rope_tables(rows):
    half = HEAD_SIZE // 2
    position = jnp.arange(rows).astype(F32)
    inverse = ROPE_BASE ** (-jnp.arange(half).astype(F32) / half)
    angles = position[:, None] * inverse[None, :]
    cosine, sine = jnp.cos(angles), jnp.sin(angles)
    return jnp.concatenate([cosine, cosine], axis=1), jnp.concatenate([-sine, sine], axis=1)


def per_device(
    sizes,
    tokens,
    lengths,
    routes,
    cotangent,
    gain_one,
    w_query,
    key_matrix,
    value_matrix,
    w_out,
    gain_two,
    w_router,
    w_gate,
    w_up,
    w_down,
):
    ndp = sizes["dp"]
    rows = tokens.shape[0]
    local, _, width = w_gate.shape
    me_dp = lax.axis_index("dp")
    length = lengths[0]
    ids = jnp.stack([me_dp, lax.axis_index("z"), lax.axis_index("core"), length]).astype(jnp.int32)
    live = (jnp.arange(rows) < length)[:, None]
    expert_ids = jnp.arange(EXPERTS, dtype=jnp.int32)

    extra = jnp.concatenate([gain_one[:, None], gain_two[:, None], w_router], axis=1)
    extra = jnp.pad(extra, ((0, 0), (0, PAD - extra.shape[1])))
    first = jnp.concatenate([w_query, key_matrix, value_matrix, extra], axis=1)
    named = jnp.any(routes[None, :, :] == expert_ids[:, None, None], axis=2).astype(BF16)
    named = jnp.pad(named, ((0, NOTE - EXPERTS), (0, MODEL_WIDTH - rows)))
    grad_low = jnp.where(live, cotangent, jnp.zeros_like(cotangent))
    grad_low = jnp.concatenate([grad_low, named], axis=0)
    grad_near = start_dp(grad_low, ndp)

    nz = sizes["z"]
    first_z = [first] + [exchange(first, "z", nz, k) for k in range(1, nz)]
    first_block = stack_after(first_z, grad_near)
    second_z = [w_out] + [exchange(w_out, "z", nz, k) for k in range(1, nz)]
    first_near = start_dp(first_block, ndp)
    first_dp = pass_on(first_block, first_near, ndp, second_z[1:])
    packed = after([pack(j, (w_gate, w_up, w_down)) for j in range(local)], first_z[1:] + grad_near)
    expert_mats = [lax.all_gather(p, ("z", "core"), axis=0, tiled=True) for p in packed]
    second_block = stack_after(second_z, [piece for *_, piece in first_dp[1:3]])
    second_dp = gather_direct(second_block, ndp)

    cosine, sine = rope_tables(rows)
    weights_in = gather_rows(first, first_dp, ids, sizes)
    qkv, mixed, h_one, gains, router = attend(ids, tokens, cosine, sine, weights_in, [], sizes)
    second_far = after([piece for *_, piece in second_dp[1:]], [mixed])
    second_dp = [(k, 0, piece) for k, piece in enumerate([second_block, *second_far])]
    grad_far = pass_on(grad_low, grad_near, ndp, second_far)
    weights_out = gather_rows(w_out, second_dp, ids, sizes)
    residual, *h_two = project(ids, tokens, mixed, gains, weights_out, sizes)
    hidden = gather_halves(h_two, ndp)
    turned = turn([mixed, h_one], [hidden[2][2]], ids, sizes)
    mixed, h_one = ([mine, exchange(other, "core", 2, 1)] for mine, other in turned)

    prev, gate_grads, sums = (), [], []
    for j in range(local):
        expert = (me_dp * local + j).astype(jnp.int32).reshape(1)
        *prev, grad_gate, terms = run_expert(
            j,
            j == local - 1,
            expert,
            router,
            hidden,
            grad_far,
            expert_mats[j],
            prev,
            gate_grads,
            ndp,
            [*mixed, *h_one],
        )
        gate_grads.append(grad_gate)
        sums.append(lax.psum_scatter(terms, ("z", "core"), scatter_dimension=0, tiled=True))
    count = 2 * ndp - 1
    outs, backs = prev[:count], prev[count:]
    pairs = [tuple(backs[2 * k : 2 * k + 2]) for k in range(ndp)]
    backs = [*pairs[0], *finish_sum(pairs, start_sum(pairs, ndp), ndp)]
    out_slots = [None] + [tuple(outs[i : i + 2]) for i in range(1, count, 2)]
    out_past = start_sum(out_slots, ndp)

    grad_resid, grad_attn, grad_pre, notes = back(
        ids,
        residual,
        h_two,
        cotangent,
        gains,
        router,
        cosine,
        sine,
        qkv,
        backs,
        weights_out,
        [],
        sizes,
    )
    if not by_blocks(sizes):
        notes = split_cores(notes, ids, sizes)
        notes = notes[0], exchange(notes[1], "core", 2, 1)
    else:
        notes = notes, exchange(notes, "core", 2, 1)
    grad_attn = grad_attn, exchange(grad_attn, "core", 2, 1)
    grad_pre = grad_pre, exchange(grad_pre, "core", 2, 1)
    out_terms = weight_terms(ids, mixed, grad_attn, (), grad_pre[1:], sizes)
    in_terms = weight_terms(ids, h_one, grad_pre, notes, sums[:-1] + [out_terms[0]] + out_past, sizes)
    own, late, _, _ = scatter_rows(*out_terms, sizes, in_terms[:1])
    grad_out = own + sum(part.astype(F32) for part in late)
    sending = []
    own, got, arrived, leaving = scatter_rows(*in_terms, sizes, seen=sending)
    grad_tokens = tokens_back(
        ids, tokens, gains, grad_pre[0], grad_resid, weights_in, sending, sizes
    )
    block = residual + outs[0].astype(F32)
    for part in finish_sum(out_slots, out_past, ndp, arrived):
        block = block + part.astype(F32)
    block_out = block.astype(BF16)
    *grad_in, small = settle(own, got, (w_query, key_matrix, value_matrix))
    expert_sums = finish_after(sums, [leaving])
    return (
        block_out,
        grad_tokens,
        small[:, PAD - 1] / gain_one.astype(F32),
        *grad_in,
        grad_out,
        small[:, 0],
        small[:, 8 : 8 + EXPERTS],
        *expert_sums,
    )


def solution(mesh):
    ndp, nf = mesh.shape["dp"], mesh.shape["fsdp"]
    sizes = {"dp": ndp, "z": nf // 2, "core": 2}
    split = Mesh(mesh.devices.reshape(ndp, nf // 2, 2), ("dp", "z", "core"))
    every = ("dp", "z", "core")
    rows = P(every, None)
    vector = P(every)
    expert = P("dp", ("z", "core"), None)

    def run(*args):
        return per_device(sizes, *args)

    return jax.shard_map(
        run,
        mesh=split,
        in_specs=(rows, vector, rows, rows, vector, rows, rows, rows, rows, vector, rows)
        + (expert,) * 3,
        out_specs=(rows, rows, vector, rows, rows, rows, rows, vector, rows) + (expert,) * 3,
        check_vma=False,
    )
```

```python
import functools

import jax
import jax.numpy as jnp
from jax import lax
from jax.experimental import pallas as pl
from jax.experimental.pallas import tpu as pltpu
from jax.sharding import Mesh
from jax.sharding import PartitionSpec as P

MODEL_WIDTH = 1536
QUERY_HEADS = 12
KEY_VALUE_HEADS = 2
HEAD_SIZE = 128
EXPERTS = 8
CAP = 160
GROUP = QUERY_HEADS // KEY_VALUE_HEADS
QW = QUERY_HEADS * HEAD_SIZE
KW = KEY_VALUE_HEADS * HEAD_SIZE
QKV = QW + 2 * KW
PAD = 128
FIRST = QKV + PAD
NOTE = 32
ROUTER = 16
EPS = 1e-06
ROPE_BASE = 1500000.0
NEG_FILL = -1e30
SCALE = HEAD_SIZE ** (-0.5)
F32 = jnp.float32
BF16 = jnp.bfloat16
TILE = 256
MIB = 1024 * 1024
HBM = pl.BlockSpec(memory_space=pltpu.HBM)
VMEM = pl.BlockSpec(memory_space=pltpu.VMEM)
SMEM = pl.BlockSpec(memory_space=pltpu.SMEM)


def nn(a, b):
    return lax.dot_general(a, b, (((1,), (0,)), ((), ())), preferred_element_type=F32)


def nt(a, b):
    return lax.dot_general(a, b, (((1,), (1,)), ((), ())), preferred_element_type=F32)


def tn(a, b):
    return lax.dot_general(a, b, (((0,), (0,)), ((), ())), preferred_element_type=F32)


def shape(dims, dtype):
    return jax.ShapeDtypeStruct(dims, dtype)


def params(mib):
    return pltpu.CompilerParams(vmem_limit_bytes=mib * MIB)


def cost(flops, data, special=0):
    return pl.CostEstimate(flops=flops, bytes_accessed=data, transcendentals=special)


def exchange(block, axis, size, step):
    return lax.ppermute(block, axis, [(i, i ^ step) for i in range(size)])


def start_dp(block, ndp):
    return [exchange(block, "dp", ndp, k) for k in ((1, 2) if ndp == 4 else range(1, ndp))]


def pass_on(block, near, ndp, before=()):
    if ndp != 4:
        return [(k, 0, piece) for k, piece in enumerate([block] + near)]
    side, up = after(near, before) if before else near
    half = block.shape[0] // 2
    return [
        (0, 0, block),
        (1, 0, side),
        (2, 0, up),
        (3, 0, exchange(side[:half], "dp", ndp, 2)),
        (3, half, exchange(up[half:], "dp", ndp, 1)),
    ]


def gather_direct(block, ndp):
    return [(k, 0, exchange(block, "dp", ndp, k) if k else block) for k in range(ndp)]


def gather_halves(halves, ndp):
    top, low = halves
    at = top.shape[0]
    if ndp != 4:
        return [
            (k, i * at, exchange(half, "dp", ndp, k) if k else half)
            for k in range(ndp)
            for i, half in enumerate(halves)
        ]
    side_top, up_low = exchange(top, "dp", ndp, 1), exchange(low, "dp", ndp, 2)
    side_low, up_top = exchange(low, "dp", ndp, 1), exchange(top, "dp", ndp, 2)
    return [
        (0, 0, top),
        (0, at, low),
        (1, 0, side_top),
        (2, at, up_low),
        (1, at, side_low),
        (2, 0, up_top),
        (3, 0, exchange(side_top, "dp", ndp, 2)),
        (3, at, exchange(up_low, "dp", ndp, 1)),
    ]


def start_sum(slots, ndp):
    if ndp != 4:
        return []
    return [exchange(slots[3][0], "dp", ndp, 1), exchange(slots[3][1], "dp", ndp, 2)]


def finish_sum(slots, past, ndp, before=(), seen=None):
    if ndp != 4:
        sent = [jnp.concatenate(slot, axis=0) for slot in slots[1:]]
    else:
        past = after(past, before) if before else past
        add = lambda a, b: (a.astype(F32) + b.astype(F32)).astype(BF16)
        sent = [
            jnp.concatenate([slots[1][0], add(slots[1][1], past[1])], axis=0),
            jnp.concatenate([add(slots[2][0], past[0]), slots[2][1]], axis=0),
        ]
    if seen is not None:
        seen.extend(sent)
    return [exchange(part, "dp", ndp, k + 1) for k, part in enumerate(sent)]


def both_cores(pieces):
    return [
        (k, c, start, exchange(piece, "core", 2, 1) if c else piece)
        for k, start, piece in pieces
        for c in range(2)
    ]


def stack_kernel(count, *refs):
    for i in range(count):
        refs[-1][i] = refs[i][...]


def stack_after(parts, before):
    dims = (len(parts),) + parts[0].shape
    return pl.pallas_call(
        functools.partial(stack_kernel, len(parts)),
        out_shape=shape(dims, parts[0].dtype),
        in_specs=[VMEM] * len(parts) + [HBM] * len(before),
        out_specs=VMEM,
        compiler_params=params(60),
        cost_estimate=cost(0, 4 * dims[0] * dims[1] * dims[2]),
        name="stack",
    )(*parts, *before)


def pack_kernel(index, *refs):
    width = refs[0].shape[2]
    for i in range(3):
        refs[-1][:, i * width : (i + 1) * width] = refs[i][index]


def pack(index, mats):
    _, rows, width = mats[0].shape
    return pl.pallas_call(
        functools.partial(pack_kernel, index),
        out_shape=shape((rows, 3 * width), BF16),
        in_specs=[VMEM] * 3,
        out_specs=VMEM,
        compiler_params=params(60),
        name="pack",
    )(*mats)


def finish_kernel(count, *refs):
    outs = refs[-3:]
    width = outs[0].shape[2]
    for j in range(count):
        for i in range(3):
            outs[i][j] = refs[j][:, i * width : (i + 1) * width].astype(F32)


def finish_after(sums, before):
    rows, width = sums[0].shape[0], sums[0].shape[1] // 3
    return pl.pallas_call(
        functools.partial(finish_kernel, len(sums)),
        out_shape=(shape((len(sums), rows, width), F32),) * 3,
        in_specs=[VMEM] * len(sums) + [HBM] * len(before),
        out_specs=(VMEM,) * 3,
        compiler_params=params(60),
        name="finish",
    )(*sums, *before)


def after_kernel(*refs):
    pass


def after(arrays, before):
    return pl.pallas_call(
        after_kernel,
        out_shape=tuple(shape(a.shape, a.dtype) for a in arrays),
        in_specs=[HBM] * (len(arrays) + len(before)),
        out_specs=(HBM,) * len(arrays),
        input_output_aliases={i: i for i in range(len(arrays))},
        name="after",
    )(*arrays, *before)


def block_rows(sizes):
    return MODEL_WIDTH // (2 * sizes["dp"] * sizes["z"])


def by_blocks(sizes):
    return block_rows(sizes) % 16 == 0


def gather_rows(block, along_dp, ids, sizes):
    ndp, nz = sizes["dp"], sizes["z"]
    pieces = both_cores(along_dp)
    if by_blocks(sizes):
        places = tuple((k, c, start, piece.shape[0]) for k, c, start, piece in pieces)
        return places, [piece for *_, piece in pieces]
    columns = block.shape[-1]
    whole = jnp.zeros((ndp, nz, 2, block_rows(sizes), columns), BF16)
    for k, c, start, piece in pieces:
        order = ids[1] ^ jnp.arange(start, start + piece.shape[0])
        whole = whole.at[ids[0] ^ k, order, ids[2] ^ c].set(piece)
    return None, [whole.reshape(MODEL_WIDTH, columns)]


def split_cores(columns, ids, sizes):
    ndp, nz = sizes["dp"], sizes["z"]
    rows = columns.shape[0]
    blocks = columns.reshape(rows, ndp, nz, 2, block_rows(sizes))
    blocks = jnp.take(jnp.take(blocks, ids[0] ^ jnp.arange(ndp), 1), ids[1] ^ jnp.arange(nz), 2)
    halves = [lax.dynamic_index_in_dim(blocks, ids[2] ^ c, 3, keepdims=False) for c in range(2)]
    return [half.reshape(rows, MODEL_WIDTH // 2) for half in halves]


def turn_kernel(ndp, nz, count, ids, *refs):
    block = MODEL_WIDTH // (2 * ndp * nz)
    turned = refs[-1]
    for i in range(count):
        turned[...] = jnp.transpose(refs[i][...])
        for k in range(ndp):
            for z in range(nz):
                for c in range(2):
                    at = ((ids[0] ^ k) * nz + (ids[1] ^ z)) * 2 + (ids[2] ^ c)
                    place = pl.ds(pl.multiple_of(at * block, block), block)
                    dest = refs[-1 - 2 * count + 2 * i + c]
                    dest[(k * nz + z) * block : (k * nz + z + 1) * block] = turned[place, :]


def turn(arrays, before, ids, sizes):
    if not by_blocks(sizes):
        return [[half.T for half in split_cores(array, ids, sizes)] for array in arrays]
    rows = arrays[0].shape[0]
    halves = pl.pallas_call(
        functools.partial(turn_kernel, sizes["dp"], sizes["z"], len(arrays)),
        out_shape=(shape((MODEL_WIDTH // 2, rows), BF16),) * (2 * len(arrays)),
        in_specs=[SMEM] + [VMEM] * len(arrays) + [HBM] * len(before),
        out_specs=(VMEM,) * (2 * len(arrays)),
        scratch_shapes=[pltpu.VMEM((MODEL_WIDTH, rows), BF16)],
        compiler_params=params(60),
        name="turn",
    )(ids, *arrays, *before)
    return [halves[2 * i : 2 * i + 2] for i in range(len(arrays))]


def scatter_rows(own, slots, sizes, before=(), seen=None, relay=False):
    ndp, nz = sizes["dp"], sizes["z"]
    slots = [None, *slots]
    total, parts = own, finish_sum(slots, start_sum(slots, ndp), ndp, before, seen)
    for part in parts:
        total = total + part.astype(F32)
    rows = block_rows(sizes)
    blocks = [total[z * rows : (z + 1) * rows] for z in range(nz)]
    if relay and nz == 4:
        near = exchange(jnp.concatenate([blocks[1], blocks[3]], axis=0).astype(BF16), "z", nz, 1)
        sent = [(blocks[2] + near[rows:].astype(F32)).astype(BF16)]
        return blocks[0], [near[:rows], exchange(sent[0], "z", nz, 2)], parts, sent[0]
    sent = [block.astype(BF16) for block in blocks[1:]]
    got = [exchange(block, "z", nz, z + 1) for z, block in enumerate(sent)]
    return blocks[0], got, parts, sent[-1]


def load_rows(ids, ndp, nz, places, parts, dest, sem):
    if places is None:
        loads = [pltpu.make_async_copy(parts[0], dest, sem.at[0])]
        loads[0].start()
        return loads
    rows = MODEL_WIDTH // (ndp * nz * 2)
    loads = []
    for (k, c, start, count), part in zip(places, parts):
        for z in range(count):
            block = ((ids[0] ^ k) * nz + (ids[1] ^ (start + z))) * 2 + (ids[2] ^ c)
            place = pl.ds(pl.multiple_of(block * rows, rows), rows)
            copy = pltpu.make_async_copy(part.at[z], dest.at[place, :], sem.at[len(loads)])
            loads.append(copy)
    for load in loads:
        load.start()
    return loads


def start_all(pairs, sem):
    copies = [pltpu.make_async_copy(a, b, sem.at[i]) for i, (a, b) in enumerate(pairs)]
    for copy in copies:
        copy.start()
    return copies


def wait_all(copies):
    for copy in copies:
        copy.wait()


def rms_scale(rows):
    return lax.rsqrt(jnp.mean(rows * rows, axis=-1, keepdims=True) + EPS)


def norm_back(normed, row_scale, grad):
    return row_scale * (grad - normed * jnp.mean(grad * normed, axis=-1, keepdims=True))


def swapped(vals):
    return pltpu.roll(vals, HEAD_SIZE // 2, 1)


def head(h):
    return slice(h * HEAD_SIZE, (h + 1) * HEAD_SIZE)


def seen(rows, length):
    q = lax.broadcasted_iota(jnp.int32, (rows, rows), 0)
    s = lax.broadcasted_iota(jnp.int32, (rows, rows), 1)
    return (s <= q) & (s < length)


def attention_probs(query, key, visible):
    scores = jnp.where(visible, nt(query, key) * SCALE, NEG_FILL)
    expon = jnp.exp(scores - jnp.max(scores, axis=-1, keepdims=True))
    return expon / jnp.sum(expon, axis=-1, keepdims=True)


def route_softmax(router_rows, hidden):
    logits = nt(router_rows, hidden)[:EXPERTS]
    expon = jnp.exp(logits - jnp.max(logits, axis=0, keepdims=True))
    return expon / jnp.sum(expon, axis=0, keepdims=True)


def attend_kernel(ndp, nz, places, count, ids, tokens, cosine, sine, *refs):
    parts = refs[:count]
    qkv, mixed, h_one, gains, router, w, sem = refs[-7:]
    rows = tokens.shape[0]
    loads = load_rows(ids, ndp, nz, places, parts, w, sem)
    tok = tokens[...].astype(F32)
    normed = tok * rms_scale(tok)
    for load in loads:
        load.wait()
    extra = jnp.transpose(w[:, QKV:].astype(F32))
    gains[...] = extra[:8]
    router[...] = extra[2 : 2 + ROUTER].astype(BF16)
    h_one[...] = (normed * extra[0:1]).astype(BF16)
    cos, sin = cosine[...], sine[...]
    for t in range(QKV // TILE):
        pre = nn(h_one[...], w[:, t * TILE : (t + 1) * TILE])
        for i in range(TILE // HEAD_SIZE):
            part = pre[:, head(i)]
            at = t * TILE + i * HEAD_SIZE
            if at < QW + KW:
                part = part * cos + swapped(part) * sin
            qkv[:, at : at + HEAD_SIZE] = part.astype(BF16)
    visible = seen(rows, ids[3])
    for h in range(QUERY_HEADS):
        g = h // GROUP
        probs = attention_probs(qkv[:, head(h)], qkv[:, head(QUERY_HEADS + g)], visible)
        values = qkv[:, head(QUERY_HEADS + KEY_VALUE_HEADS + g)]
        mixed[:, head(h)] = nn(probs.astype(BF16), values).astype(BF16)


def attend(ids, tokens, cosine, sine, weights, before, sizes):
    places, parts = weights
    ndp, nz = sizes["dp"], sizes["z"]
    rows = tokens.shape[0]
    return pl.pallas_call(
        functools.partial(attend_kernel, ndp, nz, places, len(parts)),
        out_shape=(
            shape((rows, QKV), BF16),
            shape((rows, QW), BF16),
            shape((rows, MODEL_WIDTH), BF16),
            shape((8, MODEL_WIDTH), F32),
            shape((ROUTER, MODEL_WIDTH), BF16),
        ),
        in_specs=[SMEM, VMEM, VMEM, VMEM] + [HBM] * (len(parts) + len(before)),
        out_specs=(VMEM,) * 5,
        scratch_shapes=[
            pltpu.VMEM((MODEL_WIDTH, FIRST), BF16),
            pltpu.SemaphoreType.DMA((2 * ndp * nz,)),
        ],
        compiler_params=params(60),
        cost_estimate=cost(2 * rows * MODEL_WIDTH * QKV, 10 * MIB, 12 * rows * rows),
        name="attend",
    )(ids, tokens, cosine, sine, *parts, *before)


def project_kernel(ndp, nz, places, ids, tokens, mixed, gains, *refs):
    *parts, residual, top, low, w, sem = refs
    loads = load_rows(ids, ndp, nz, places, parts, w, sem)
    for load in loads:
        load.wait()
    for t in range(MODEL_WIDTH // TILE):
        lane = slice(t * TILE, (t + 1) * TILE)
        residual[:, lane] = tokens[:, lane].astype(F32) + nn(mixed[...], w[:, lane])
    whole = residual[...]
    h_two = (whole * rms_scale(whole) * gains[1:2]).astype(BF16)
    half = top.shape[0]
    top[...], low[...] = h_two[:half], h_two[half:]


def project(ids, tokens, mixed, gains, weights, sizes):
    places, parts = weights
    ndp, nz = sizes["dp"], sizes["z"]
    rows = tokens.shape[0]
    return pl.pallas_call(
        functools.partial(project_kernel, ndp, nz, places),
        out_shape=(shape((rows, MODEL_WIDTH), F32),)
        + (shape((rows // 2, MODEL_WIDTH), BF16),) * 2,
        in_specs=[SMEM, VMEM, VMEM, VMEM] + [HBM] * len(parts),
        out_specs=(VMEM,) * 3,
        scratch_shapes=[
            pltpu.VMEM((QW, MODEL_WIDTH), BF16),
            pltpu.SemaphoreType.DMA((2 * ndp * nz,)),
        ],
        compiler_params=params(60),
        cost_estimate=cost(2 * rows * MODEL_WIDTH * QW, 8 * MIB),
        name="project",
    )(ids, tokens, mixed, gains, *parts)


def expert_kernel(ndp, rows, width, index, last, near, far, unread, *refs):
    it = iter(refs)
    take = lambda n: [next(it) for _ in range(n)]
    (expert_ref, router_ref) = take(2)
    prev_gates = take(index)
    hid_in, cot_in = take(len(near)), take(len(far))
    (w_in,) = take(1)
    prev_in = take(2) if index else []
    take(unread)
    out_hbm, back_hbm = take(2 * ndp - 1 if last else 1), take(2 * ndp if last else 1)
    gates_ref, terms_hbm = take(2)
    hid, cot, w, x, d, ge, inner, dg, du, pick, pick_t, slot_gate, slot_dot = take(13)
    (terms_buf,) = take(1)
    prev = take(2) if index else []
    in_sem, out_sem = take(2)
    depth = MODEL_WIDTH
    tiles = depth // TILE

    loads = {}

    def load(name, source, dest):
        copy = pltpu.make_async_copy(source, dest, in_sem.at[len(loads)])
        copy.start()
        loads[name] = copy

    for i, (k, start, count) in enumerate(near):
        load(("hid", i), hid_in[i], hid.at[k, pl.ds(start, count), :])
    for i, (k, start, count) in enumerate(far):
        load(("cot", i), cot_in[i], cot.at[k, pl.ds(start, count), :])
    load("w", w_in, w)
    for i in range(len(prev)):
        load(("prev", i), prev_in[i], prev[i])

    expert = expert_ref[0]
    which = lax.broadcasted_iota(jnp.int32, (EXPERTS, rows), 0) == expert
    earlier = (
        (
            lax.broadcasted_iota(jnp.int32, (rows, rows), 0)
            < lax.broadcasted_iota(jnp.int32, (rows, rows), 1)
        )
        .astype(F32)
        .astype(BF16)
    )
    slot = lax.broadcasted_iota(jnp.int32, (CAP, rows), 0).astype(F32)
    for s in range(ndp):
        for i, piece in enumerate(near):
            if piece[0] == s:
                loads["hid", i].wait()
        for i, piece in enumerate(far):
            if piece[0] == s:
                loads["cot", i].wait()
        hidden = hid[s]
        probs = route_softmax(router_ref[...], hidden)
        named = cot[s, rows : rows + NOTE, :rows]
        place = nn(named, earlier)[:EXPERTS]
        named = named[:EXPERTS].astype(F32)
        named_row = jnp.sum(jnp.where(which, named, 0.0), axis=0, keepdims=True)
        gate_row = jnp.sum(jnp.where(which, probs, 0.0), axis=0, keepdims=True)
        place_row = jnp.sum(jnp.where(which, place, 0.0), axis=0, keepdims=True)
        chosen = jnp.where((slot == place_row) & (named_row > 0.5), 1.0, 0.0)
        pick[s] = chosen.astype(BF16)
        pick_t[s] = jnp.transpose(chosen).astype(BF16)
        at = pl.ds(s * CAP, CAP)
        gate = jnp.sum(chosen * gate_row, axis=1, keepdims=True)
        slot_gate[at, :] = jnp.broadcast_to(gate, (CAP, 128))
        x[at, :] = nn(pick[s], hidden).astype(BF16)
        grads = nn(pick[s], cot[s, :rows])
        d[at, :] = grads.astype(BF16)
        ge[at, :] = (gate * grads).astype(BF16)
    loads["w"].wait()

    def hidden_units(t, carry):
        at = pl.multiple_of(t * TILE, TILE)
        gate_pre = nn(x[...], w[:, pl.ds(at, TILE)])
        up_pre = nn(x[...], w[:, pl.ds(width + at, TILE)])
        grad_inner = nn(ge[...], w[:, pl.ds(2 * width + at, TILE)])
        sig = 1.0 / (1.0 + jnp.exp(-gate_pre))
        act = gate_pre * sig
        inner[:, pl.ds(at, TILE)] = (act * up_pre).astype(BF16)
        dg[:, pl.ds(at, TILE)] = (
            grad_inner * up_pre * sig * (1.0 + gate_pre * (1.0 - sig))
        ).astype(BF16)
        du[:, pl.ds(at, TILE)] = (grad_inner * act).astype(BF16)
        return carry

    lax.fori_loop(0, width // TILE, hidden_units, 0)
    slot_dot[...] = jnp.zeros_like(slot_dot)
    for i in range(len(prev)):
        loads["prev", i].wait()

    noted = (rows + NOTE) // 2

    def stores(t):
        lane = pl.ds(pl.multiple_of(t * TILE, TILE), TILE)
        copies = [(terms_buf.at[lane, :], terms_hbm.at[lane, :])]
        if not last:
            body = pl.ds(0, rows)
            copies.append((hid.at[:, :, lane], out_hbm[0].at[:, :, lane]))
            copies.append((cot.at[:, body, lane], back_hbm[0].at[:, body, lane]))
        else:
            copies.append((hid.at[0, :, lane], out_hbm[0].at[:, lane]))
            for i in range(2, 2 * ndp):
                first = pl.ds(i % 2 * (rows // 2), rows // 2)
                copies.append((hid.at[i // 2, first, lane], out_hbm[i - 1].at[:, lane]))
            for i in range(2 * ndp):
                body = pl.ds(0, noted if i % 2 == 0 else rows - noted)
                taken = pl.ds(i % 2 * noted, noted if i % 2 == 0 else rows - noted)
                copies.append((cot.at[i // 2, taken, lane], back_hbm[i].at[body, lane]))
        return [
            pltpu.make_async_copy(source, dest, out_sem.at[i, t])
            for i, (source, dest) in enumerate(copies)
        ]

    def features(t, carry):
        lane = pl.ds(pl.multiple_of(t * TILE, TILE), TILE)
        result = nt(inner[...], w[lane, pl.ds(2 * width, width)]).astype(BF16).astype(F32)
        partial = jnp.sum(result * d[:, lane].astype(F32), axis=1, keepdims=True)
        slot_dot[...] += jnp.broadcast_to(partial, slot_dot.shape)
        gated = (slot_gate[:, :1] * result).astype(BF16)
        grad_in = (
            nt(dg[...], w[lane, pl.ds(0, width)]) + nt(du[...], w[lane, pl.ds(width, width)])
        ).astype(BF16)
        for s in range(ndp):
            part = slice(s * CAP, (s + 1) * CAP)
            sent = nn(pick_t[s], gated[part])
            back = nn(pick_t[s], grad_in[part])
            if prev:
                sent = sent + prev[0][s, :, lane].astype(F32)
                back = back + prev[1][s, :rows, lane].astype(F32)
            hid[s, :, lane] = sent.astype(BF16)
            cot[s, :rows, lane] = back.astype(BF16)
        x_t = jnp.transpose(x[:, lane])
        terms_buf[lane, pl.ds(0, width)] = nn(x_t, dg[...]).astype(BF16)
        terms_buf[lane, pl.ds(width, width)] = nn(x_t, du[...]).astype(BF16)
        ge_t = jnp.transpose(ge[:, lane])
        terms_buf[lane, pl.ds(2 * width, width)] = nn(ge_t, inner[...]).astype(BF16)
        for store in stores(t):
            store.start()
        return carry

    lax.fori_loop(0, tiles, features, 0)
    line = lax.broadcasted_iota(jnp.int32, (NOTE, 3 * rows), 0)
    notes = []
    for s in range(ndp):
        part = slice(s * CAP, (s + 1) * CAP)
        own = jnp.sum(pick[s].astype(F32) * slot_dot[part, :1], axis=0, keepdims=True)
        gates_ref[s] = own
        if not last:
            continue
        note = jnp.zeros((NOTE, 3 * rows), F32)
        for j, row in enumerate([p[s] for p in prev_gates] + [own]):
            high = row.astype(BF16).astype(F32)
            middle = (row - high).astype(BF16).astype(F32)
            low = row - high - middle
            at = expert - index + j
            note = jnp.where(line == at, jnp.concatenate([high, middle, low], axis=1), note)
        cot[s, rows : rows + NOTE, : 3 * rows] = note.astype(BF16)
        notes.append(
            pltpu.make_async_copy(
                cot.at[s, pl.ds(rows, NOTE), :],
                back_hbm[2 * s + 1].at[pl.ds(rows - noted, NOTE), :],
                out_sem.at[4 * ndp + 1, s],
            )
        )
        notes[-1].start()
    for t in range(tiles):
        for store in stores(t):
            store.wait()
    for note in notes:
        note.wait()


def run_expert(index, last, expert, router, hidden, grads, w_all, prev, prev_gates, ndp, before):
    rows = 2 * hidden[0][2].shape[0]
    near, far = (tuple((k, at, p.shape[0]) for k, at, p in group) for group in (hidden, grads))
    width = w_all.shape[1] // 3
    slots = ndp * CAP
    depth = MODEL_WIDTH
    tiles = depth // TILE
    scratch = [
        pltpu.VMEM((ndp, rows, depth), BF16),
        pltpu.VMEM((ndp, rows + NOTE, depth), BF16),
        pltpu.VMEM((depth, 3 * width), BF16),
        pltpu.VMEM((slots, depth), BF16),
        pltpu.VMEM((slots, depth), BF16),
        pltpu.VMEM((slots, depth), BF16),
        pltpu.VMEM((slots, width), BF16),
        pltpu.VMEM((slots, width), BF16),
        pltpu.VMEM((slots, width), BF16),
        pltpu.VMEM((ndp, CAP, rows), BF16),
        pltpu.VMEM((ndp, rows, CAP), BF16),
        pltpu.VMEM((slots, 128), F32),
        pltpu.VMEM((slots, 128), F32),
        pltpu.VMEM((depth, 3 * width), BF16),
    ]
    if index:
        scratch += [
            pltpu.VMEM((ndp, rows, depth), BF16),
            pltpu.VMEM((ndp, rows + NOTE, depth), BF16),
        ]
    scratch += [
        pltpu.SemaphoreType.DMA((len(near) + len(far) + 3,)),
        pltpu.SemaphoreType.DMA((4 * ndp + 2, max(tiles, ndp))),
    ]
    sent = [shape((ndp, rows, depth), BF16), shape((ndp, rows + NOTE, depth), BF16)]
    if last:
        sent = [shape((rows, depth), BF16)]
        sent += [shape((rows // 2, depth), BF16)] * (2 * ndp - 2)
        sent += [shape(((rows + NOTE) // 2, depth), BF16)] * (2 * ndp)
    flops = 2 * slots * depth * width * 9 + 8 * ndp * CAP * rows * depth
    return pl.pallas_call(
        functools.partial(
            expert_kernel, ndp, rows, width, index, last, near, far, len(before)
        ),
        out_shape=(
            *sent,
            shape((ndp, 1, rows), F32),
            shape((depth, 3 * width), BF16),
        ),
        in_specs=[SMEM, VMEM]
        + [VMEM] * len(prev_gates)
        + [HBM] * (len(near) + len(far) + 1 + len(prev) + len(before)),
        out_specs=(HBM,) * len(sent) + (VMEM, HBM),
        scratch_shapes=scratch,
        compiler_params=params(60),
        cost_estimate=cost(flops, 40 * MIB, slots * width),
        name="expert",
    )(
        expert,
        router,
        *prev_gates,
        *(piece for *_, piece in hidden),
        *(piece for *_, piece in grads),
        w_all,
        *prev,
        *before,
    )


def back_kernel(ndp, nz, places, count, given, unread, ids, gains, router, cosine, sine, *refs):
    refs = list(refs)
    take = lambda n: [refs.pop(0) for _ in range(n)]
    data, backs, parts = take(5), take(given), take(count)
    take(unread)
    out_resid, out_attn, out_pre, notes = take(4)
    residual, top, low, grads, qkv = held = take(5)
    got = take(given)
    w, grad_mixed, grad_resid, grad_attn, grad_pre, sem, data_sem, out_sem = refs
    rows = residual.shape[0]
    fetched = start_all(list(zip(backs + data[1:3] + data[:1] + data[3:], got + held[1:3] + held[:1] + held[3:])), data_sem)
    loads = load_rows(ids, ndp, nz, places, parts, w, sem)
    wait_all(fetched[:given])
    whole = jnp.concatenate([got[0][...], got[1][...]], axis=0).astype(F32)
    for part in got[2:]:
        whole = whole + part[...].astype(F32)
    grad_h = whole[:rows]
    note = whole[rows : rows + EXPERTS, : 3 * rows]
    grad_route = note[:, :rows] + note[:, rows : 2 * rows] + note[:, 2 * rows :]
    wait_all(fetched[given : given + 4])
    hidden = jnp.concatenate([top[...], low[...]], axis=0)
    probs = route_softmax(router[...], hidden)
    grad_logits = probs * (grad_route - jnp.sum(probs * grad_route, axis=0, keepdims=True))
    grad_logits = jnp.concatenate([grad_logits, jnp.zeros_like(grad_logits)], axis=0)
    grad_logits = grad_logits.astype(BF16)
    grad_h = grad_h + tn(grad_logits, router[...])
    res = residual[...]
    scale = rms_scale(res)
    normed = res * scale
    notes[0:8] = jnp.broadcast_to(
        jnp.sum(normed * grad_h, axis=0, keepdims=True), (8, MODEL_WIDTH)
    )
    notes[8:16] = nn(grad_logits, hidden)[:EXPERTS]
    live = lax.broadcasted_iota(jnp.int32, (rows, 1), 0) < ids[3]
    final = jnp.where(live, grads[...].astype(F32), 0.0)
    total = final + norm_back(normed, scale, grad_h * gains[1:2])
    grad_resid[...] = total
    grad_attn[...] = total.astype(BF16)
    stores = start_all([(grad_attn, out_attn), (grad_resid, out_resid)], out_sem)
    wait_all(loads)
    for t in range(QW // TILE):
        lane = slice(t * TILE, (t + 1) * TILE)
        grad_mixed[:, lane] = nt(grad_attn[...], w[lane, :]).astype(BF16)
    wait_all(fetched[given + 4 :])
    source = lax.broadcasted_iota(jnp.int32, (rows, rows), 0)
    visible = (source <= lax.broadcasted_iota(jnp.int32, (rows, rows), 1)) & (source < ids[3])
    cos, sin = cosine[...], sine[...]
    for g in range(KEY_VALUE_HEADS):
        key = qkv[:, head(QUERY_HEADS + g)]
        value = qkv[:, head(QUERY_HEADS + KEY_VALUE_HEADS + g)]
        grad_key = jnp.zeros((rows, HEAD_SIZE), F32)
        grad_value = jnp.zeros((rows, HEAD_SIZE), F32)
        for h in range(g * GROUP, (g + 1) * GROUP):
            query, grad = qkv[:, head(h)], grad_mixed[:, head(h)]
            scores = jnp.where(visible, nt(key, query) * SCALE, NEG_FILL)
            expon = jnp.exp(scores - jnp.max(scores, axis=0, keepdims=True))
            probs = expon / jnp.sum(expon, axis=0, keepdims=True)
            grad_probs = nt(value, grad)
            grad_value = grad_value + nn(probs.astype(BF16), grad)
            row_dot = jnp.sum(probs * grad_probs, axis=0, keepdims=True)
            grad_scores = (probs * (grad_probs - row_dot)).astype(BF16)
            grad_query = tn(grad_scores, key) * SCALE
            grad_key = grad_key + nn(grad_scores, query)
            grad_pre[:, head(h)] = (grad_query * cos - swapped(grad_query) * sin).astype(BF16)
        grad_key = grad_key * SCALE
        grad_pre[:, head(QUERY_HEADS + g)] = (
            grad_key * cos - swapped(grad_key) * sin
        ).astype(BF16)
        grad_pre[:, head(QUERY_HEADS + KEY_VALUE_HEADS + g)] = grad_value.astype(BF16)
    last = pltpu.make_async_copy(grad_pre, out_pre, out_sem.at[2])
    last.start()
    wait_all(stores + [last])


def back(
    ids, residual, h_two, grads, gains, router, cosine, sine, qkv, backs, weights, before, sizes
):
    ndp, nz = sizes["dp"], sizes["z"]
    places, parts = weights
    rows = residual.shape[0]
    data = [residual, *h_two, grads, qkv]
    made = [
        shape((rows, MODEL_WIDTH), F32),
        shape((rows, MODEL_WIDTH), BF16),
        shape((rows, QKV), BF16),
    ]
    room = lambda array: pltpu.VMEM(array.shape, array.dtype)
    return pl.pallas_call(
        functools.partial(
            back_kernel, ndp, nz, places, len(parts), len(backs), len(before)
        ),
        out_shape=(*made, shape((16, MODEL_WIDTH), F32)),
        in_specs=[SMEM]
        + [VMEM] * 4
        + [HBM] * (len(data) + len(backs) + len(parts) + len(before)),
        out_specs=(HBM, HBM, HBM, VMEM),
        scratch_shapes=[
            *(room(array) for array in data + backs),
            pltpu.VMEM((QW, MODEL_WIDTH), BF16),
            pltpu.VMEM((rows, QW), BF16),
            *(room(array) for array in made),
            pltpu.SemaphoreType.DMA((2 * ndp * nz,)),
            pltpu.SemaphoreType.DMA((len(data) + len(backs),)),
            pltpu.SemaphoreType.DMA((3,)),
        ],
        compiler_params=params(60),
        cost_estimate=cost(3 * rows * MODEL_WIDTH * QW, 16 * MIB, 12 * rows * rows),
        name="back",
    )(ids, gains, router, cosine, sine, *data, *backs, *parts, *before)


def tokens_back_kernel(ndp, nz, places, count, ids, tokens, gains, grad_pre, grad_resid, *refs):
    parts = refs[:count]
    grad_tokens, w, sem = refs[-3:]
    loads = load_rows(ids, ndp, nz, places, parts, w, sem)
    tok = tokens[...].astype(F32)
    scale = rms_scale(tok)
    normed = tok * scale
    for load in loads:
        load.wait()
    for t in range(MODEL_WIDTH // TILE):
        lane = slice(t * TILE, (t + 1) * TILE)
        grad_tokens[:, lane] = nt(grad_pre[...], w[lane, :QKV])
    grad_h = grad_tokens[...]
    grad_tokens[...] = grad_resid[...] + norm_back(normed, scale, grad_h * gains[0:1])


def tokens_back(ids, tokens, gains, grad_pre, grad_resid, weights, before, sizes):
    ndp, nz = sizes["dp"], sizes["z"]
    places, parts = weights
    rows = tokens.shape[0]
    return pl.pallas_call(
        functools.partial(tokens_back_kernel, ndp, nz, places, len(parts)),
        out_shape=shape((rows, MODEL_WIDTH), F32),
        in_specs=[SMEM] + [VMEM] * 4 + [HBM] * (len(parts) + len(before)),
        out_specs=VMEM,
        scratch_shapes=[
            pltpu.VMEM((MODEL_WIDTH, FIRST), BF16),
            pltpu.SemaphoreType.DMA((2 * ndp * nz,)),
        ],
        compiler_params=params(60),
        cost_estimate=cost(2 * rows * MODEL_WIDTH * QKV, 12 * MIB),
        name="tokens_back",
    )(ids, tokens, gains, grad_pre, grad_resid, *parts, *before)


def terms_kernel(ndp, nz, noted, unread, ids, *refs):
    refs = list(refs)
    take = lambda n: [refs.pop(0) for _ in range(n)]
    notes, given = take(2 if noted else 0), take(4)
    take(unread)
    count = 2 * ndp - 1
    outs, held, dests = take(count), take(4), take(count)
    note_rows, in_sem, out_sem = refs
    wait_all(start_all(list(zip(given, held)), in_sem))
    left = jnp.concatenate([held[0][...], held[1][...]], axis=1)
    right = jnp.concatenate([held[2][...], held[3][...]], axis=0)
    slot = MODEL_WIDTH // (2 * ndp)
    stores = []

    def put(lane, value):
        dests[0][:, lane] = value[:slot]
        for i in range(1, count):
            at = slot + (i - 1) * (slot // 2)
            dests[i][:, lane] = value[at : at + slot // 2].astype(BF16)
        pairs = [(dests[i].at[:, lane], outs[i].at[:, lane]) for i in range(count)]
        stores.extend(start_all(pairs, out_sem.at[len(stores) // count]))

    if noted:
        note = notes[0][...] + notes[1][...]
        block = jnp.concatenate([note, jnp.zeros((PAD - 16, note.shape[1]), F32)], axis=0)
        block = jnp.transpose(block)
    if noted == 1:
        note_rows[...] = block
        rows = MODEL_WIDTH // (2 * ndp * nz)
        taken = []
        for k in range(ndp):
            for z in range(nz):
                at = ((ids[0] ^ k) * nz + (ids[1] ^ z)) * 2 + ids[2]
                taken.append(note_rows[pl.ds(pl.multiple_of(at * rows, rows), rows), :])
        block = jnp.concatenate(taken, axis=0)
    if noted:
        put(slice(right.shape[1], right.shape[1] + PAD), block)
    for t in range(right.shape[1] // TILE):
        lane = slice(t * TILE, (t + 1) * TILE)
        put(lane, nn(left, right[:, lane]))
    wait_all(stores)


def weight_terms(ids, left, right, notes, before, sizes):
    ndp, nz = sizes["dp"], sizes["z"]
    slot = MODEL_WIDTH // (2 * ndp)
    columns = right[0].shape[1] + (PAD if notes else 0)
    noted = 0 if not notes else 1 if notes[0].shape[1] == MODEL_WIDTH else 2
    made = [shape((slot, columns), F32)] + [shape((slot // 2, columns), BF16)] * (2 * ndp - 2)
    room = lambda array: pltpu.VMEM(array.shape, array.dtype)
    arrays = [*left, *right]
    found = pl.pallas_call(
        functools.partial(terms_kernel, ndp, nz, noted, len(before)),
        out_shape=tuple(made),
        in_specs=[SMEM] + [VMEM] * len(notes) + [HBM] * (4 + len(before)),
        out_specs=(HBM,) * len(made),
        scratch_shapes=[
            *(room(array) for array in arrays + made),
            pltpu.VMEM((MODEL_WIDTH, PAD), F32),
            pltpu.SemaphoreType.DMA((4,)),
            pltpu.SemaphoreType.DMA((columns // TILE + 1, len(made))),
        ],
        compiler_params=params(60),
        cost_estimate=cost(2 * MODEL_WIDTH * left[0].shape[1] * columns, 5 * MIB),
        name="weight_terms",
    )(ids, *notes, *arrays, *before)
    return found[0], [tuple(found[i : i + 2]) for i in range(1, len(found), 2)]


def settle_kernel(count, *refs):
    own, got = refs[0], refs[1 : 1 + count]
    mats = refs[1 + count : 4 + count]
    gain = refs[4 + count]
    outs, gains, router = refs[-5:-2], refs[-2], refs[-1]
    total = own[...]
    for part in got:
        total = total + part[...].astype(F32)
    dot, at = jnp.zeros((total.shape[0], 1), F32), 0
    for mat, out in zip(mats, outs):
        width = mat.shape[1]
        part = total[:, at : at + width]
        out[...] = part
        dot = dot + jnp.sum(part * mat[...].astype(F32), axis=1, keepdims=True)
        at += width
    small = total[:, at:]
    router[...] = small[:, 8 : 8 + EXPERTS]
    lane = lax.broadcasted_iota(jnp.int32, small.shape, 1)
    turned = jnp.transpose(jnp.where(lane == 1, dot, small))
    gains[0:1] = turned[1:2] / gain[...]
    gains[1:2] = turned[0:1]


def settle(own, got, mats, gain, before):
    rows = own.shape[0]
    return pl.pallas_call(
        functools.partial(settle_kernel, len(got)),
        out_shape=tuple(shape(mat.shape, F32) for mat in mats)
        + (shape((2, rows), F32), shape((rows, EXPERTS), F32)),
        in_specs=[VMEM] * (1 + len(got) + 4) + [HBM] * len(before),
        out_specs=(VMEM,) * 5,
        compiler_params=params(60),
        name="settle",
    )(own, *got, *mats, gain, *before)


def rope_tables(rows):
    half = HEAD_SIZE // 2
    position = jnp.arange(rows).astype(F32)
    inverse = ROPE_BASE ** (-jnp.arange(half).astype(F32) / half)
    angles = position[:, None] * inverse[None, :]
    cosine, sine = jnp.cos(angles), jnp.sin(angles)
    return jnp.concatenate([cosine, cosine], axis=1), jnp.concatenate([-sine, sine], axis=1)


def per_device(
    sizes,
    tokens,
    lengths,
    routes,
    cotangent,
    gain_one,
    w_query,
    key_matrix,
    value_matrix,
    w_out,
    gain_two,
    w_router,
    w_gate,
    w_up,
    w_down,
):
    ndp = sizes["dp"]
    rows = tokens.shape[0]
    local, _, width = w_gate.shape
    me_dp = lax.axis_index("dp")
    length = lengths[0]
    ids = jnp.stack([me_dp, lax.axis_index("z"), lax.axis_index("core"), length]).astype(jnp.int32)
    live = (jnp.arange(rows) < length)[:, None]
    expert_ids = jnp.arange(EXPERTS, dtype=jnp.int32)

    extra = jnp.concatenate([gain_one[:, None], gain_two[:, None], w_router], axis=1)
    extra = jnp.pad(extra, ((0, 0), (0, PAD - extra.shape[1])))
    first = jnp.concatenate([w_query, key_matrix, value_matrix, extra], axis=1)
    named = jnp.any(routes[None, :, :] == expert_ids[:, None, None], axis=2).astype(BF16)
    named = jnp.pad(named, ((0, NOTE - EXPERTS), (0, MODEL_WIDTH - rows)))
    grad_low = jnp.where(live, cotangent, jnp.zeros_like(cotangent))
    grad_low = jnp.concatenate([grad_low, named], axis=0)

    nz = sizes["z"]
    first_z = [first] + [exchange(first, "z", nz, k) for k in range(1, nz)]
    second_z = [w_out] + [exchange(w_out, "z", nz, k) for k in range(1, nz)]
    first_block = stack_after(first_z, [])
    first_near = start_dp(first_block, ndp)
    (grad_low,) = after([grad_low], first_near)
    grad_near = start_dp(grad_low, ndp)
    first_dp = pass_on(first_block, first_near, ndp, second_z[1:])
    packed = after([pack(j, (w_gate, w_up, w_down)) for j in range(local)], first_z[1:])
    expert_mats = [lax.all_gather(p, ("z", "core"), axis=0, tiled=True) for p in packed]
    second_block = stack_after(second_z, [piece for *_, piece in first_dp[1:3]])
    second_dp = gather_direct(second_block, ndp)

    cosine, sine = rope_tables(rows)
    weights_in = gather_rows(first, first_dp, ids, sizes)
    qkv, mixed, h_one, gains, router = attend(ids, tokens, cosine, sine, weights_in, [], sizes)
    second_far = after([piece for *_, piece in second_dp[1:]], [mixed])
    second_dp = [(k, 0, piece) for k, piece in enumerate([second_block, *second_far])]
    grad_far = pass_on(grad_low, grad_near, ndp)
    weights_out = gather_rows(w_out, second_dp, ids, sizes)
    residual, *h_two = project(ids, tokens, mixed, gains, weights_out, sizes)
    hidden = gather_halves(h_two, ndp)
    turned = turn([mixed, h_one], [hidden[2][2]], ids, sizes)
    mixed, h_one = ([mine, exchange(other, "core", 2, 1)] for mine, other in turned)

    prev, gate_grads, sums = (), [], []
    for j in range(local):
        expert = (me_dp * local + j).astype(jnp.int32).reshape(1)
        *prev, grad_gate, terms = run_expert(
            j,
            j == local - 1,
            expert,
            router,
            hidden,
            grad_far,
            expert_mats[j],
            prev,
            gate_grads,
            ndp,
            [*mixed, *h_one],
        )
        gate_grads.append(grad_gate)
        sums.append(lax.psum_scatter(terms, ("z", "core"), scatter_dimension=0, tiled=True))
    count = 2 * ndp - 1
    outs, backs = prev[:count], prev[count:]
    pairs = [tuple(backs[2 * k : 2 * k + 2]) for k in range(ndp)]
    backs = [*pairs[0], *finish_sum(pairs, start_sum(pairs, ndp), ndp)]
    out_slots = [None] + [tuple(outs[i : i + 2]) for i in range(1, count, 2)]
    out_past = start_sum(out_slots, ndp)

    grad_resid, grad_attn, grad_pre, notes = back(
        ids,
        residual,
        h_two,
        cotangent,
        gains,
        router,
        cosine,
        sine,
        qkv,
        backs,
        weights_out,
        [],
        sizes,
    )
    if not by_blocks(sizes):
        notes = split_cores(notes, ids, sizes)
        notes = notes[0], exchange(notes[1], "core", 2, 1)
    else:
        notes = notes, exchange(notes, "core", 2, 1)
    grad_attn = grad_attn, exchange(grad_attn, "core", 2, 1)
    grad_pre = grad_pre, exchange(grad_pre, "core", 2, 1)
    out_terms = weight_terms(ids, mixed, grad_attn, (), grad_pre[1:], sizes)
    in_terms = weight_terms(
        ids, h_one, grad_pre, notes, sums[:-1] + [out_terms[0]] + out_past, sizes
    )
    own_out, late, _, _ = scatter_rows(*out_terms, sizes, in_terms[:1], relay=True)
    sending = []
    own, got, arrived, leaving = scatter_rows(*in_terms, sizes, seen=sending, relay=True)
    grad_tokens = tokens_back(
        ids, tokens, gains, grad_pre[0], grad_resid, weights_in, sending, sizes
    )
    block = residual + outs[0].astype(F32)
    for part in finish_sum(out_slots, out_past, ndp, arrived):
        block = block + part.astype(F32)
    block_out = block.astype(BF16)
    gain = gain_one.astype(F32)[None]
    *grad_in, grad_gains, grad_router = settle(
        own, got, (w_query, key_matrix, value_matrix), gain, [block_out]
    )
    expert_sums = finish_after(sums, [leaving])
    grad_out = own_out + sum(part.astype(F32) for part in late)
    return (
        block_out,
        grad_tokens,
        grad_gains[0],
        *grad_in,
        grad_out,
        grad_gains[1],
        grad_router,
        *expert_sums,
    )


def solution(mesh):
    ndp, nf = mesh.shape["dp"], mesh.shape["fsdp"]
    sizes = {"dp": ndp, "z": nf // 2, "core": 2}
    split = Mesh(mesh.devices.reshape(ndp, nf // 2, 2), ("dp", "z", "core"))
    every = ("dp", "z", "core")
    rows = P(every, None)
    vector = P(every)
    expert = P("dp", ("z", "core"), None)

    def run(*args):
        return per_device(sizes, *args)

    return jax.shard_map(
        run,
        mesh=split,
        in_specs=(rows, vector, rows, rows, vector, rows, rows, rows, rows, vector, rows)
        + (expert,) * 3,
        out_specs=(rows, rows, vector, rows, rows, rows, rows, vector, rows) + (expert,) * 3,
        check_vma=False,
    )
```

```python
import functools

import jax
import jax.numpy as jnp
from jax import lax
from jax.experimental import pallas as pl
from jax.experimental.pallas import tpu as pltpu
from jax.sharding import Mesh
from jax.sharding import PartitionSpec as P

MODEL_WIDTH = 1536
QUERY_HEADS = 12
KEY_VALUE_HEADS = 2
HEAD_SIZE = 128
EXPERTS = 8
CAP = 160
GROUP = QUERY_HEADS // KEY_VALUE_HEADS
QW = QUERY_HEADS * HEAD_SIZE
KW = KEY_VALUE_HEADS * HEAD_SIZE
QKV = QW + 2 * KW
PAD = 128
FIRST = QKV + PAD
NOTE = 32
ROUTER = 16
EPS = 1e-06
ROPE_BASE = 1500000.0
NEG_FILL = -1e30
SCALE = HEAD_SIZE ** (-0.5)
F32 = jnp.float32
BF16 = jnp.bfloat16
TILE = 256
MIB = 1024 * 1024
HBM = pl.BlockSpec(memory_space=pltpu.HBM)
VMEM = pl.BlockSpec(memory_space=pltpu.VMEM)
SMEM = pl.BlockSpec(memory_space=pltpu.SMEM)


def nn(a, b):
    return lax.dot_general(a, b, (((1,), (0,)), ((), ())), preferred_element_type=F32)


def nt(a, b):
    return lax.dot_general(a, b, (((1,), (1,)), ((), ())), preferred_element_type=F32)


def tn(a, b):
    return lax.dot_general(a, b, (((0,), (0,)), ((), ())), preferred_element_type=F32)


def shape(dims, dtype):
    return jax.ShapeDtypeStruct(dims, dtype)


def params(mib):
    return pltpu.CompilerParams(vmem_limit_bytes=mib * MIB)


def cost(flops, data, special=0):
    return pl.CostEstimate(flops=flops, bytes_accessed=data, transcendentals=special)


def exchange(block, axis, size, step):
    return lax.ppermute(block, axis, [(i, i ^ step) for i in range(size)])


def start_dp(block, ndp):
    return [exchange(block, "dp", ndp, k) for k in ((1, 2) if ndp == 4 else range(1, ndp))]


def pass_on(block, near, ndp, before=()):
    if ndp != 4:
        return [(k, 0, piece) for k, piece in enumerate([block] + near)]
    side, up = after(near, before) if before else near
    half = block.shape[0] // 2
    return [
        (0, 0, block),
        (1, 0, side),
        (2, 0, up),
        (3, 0, exchange(side[:half], "dp", ndp, 2)),
        (3, half, exchange(up[half:], "dp", ndp, 1)),
    ]


def gather_direct(block, ndp):
    return [(k, 0, exchange(block, "dp", ndp, k) if k else block) for k in range(ndp)]


def gather_halves(halves, ndp):
    top, low = halves
    at = top.shape[0]
    if ndp != 4:
        return [
            (k, i * at, exchange(half, "dp", ndp, k) if k else half)
            for k in range(ndp)
            for i, half in enumerate(halves)
        ]
    side_top, up_low = exchange(top, "dp", ndp, 1), exchange(low, "dp", ndp, 2)
    side_low, up_top = exchange(low, "dp", ndp, 1), exchange(top, "dp", ndp, 2)
    return [
        (0, 0, top),
        (0, at, low),
        (1, 0, side_top),
        (2, at, up_low),
        (1, at, side_low),
        (2, 0, up_top),
        (3, 0, exchange(side_top, "dp", ndp, 2)),
        (3, at, exchange(up_low, "dp", ndp, 1)),
    ]


def start_sum(slots, ndp):
    if ndp != 4:
        return []
    return [exchange(slots[3][0], "dp", ndp, 1), exchange(slots[3][1], "dp", ndp, 2)]


def finish_sum(slots, past, ndp, before=(), seen=None):
    if ndp != 4:
        sent = [jnp.concatenate(slot, axis=0) for slot in slots[1:]]
    else:
        past = after(past, before) if before else past
        add = lambda a, b: (a.astype(F32) + b.astype(F32)).astype(BF16)
        sent = [
            jnp.concatenate([slots[1][0], add(slots[1][1], past[1])], axis=0),
            jnp.concatenate([add(slots[2][0], past[0]), slots[2][1]], axis=0),
        ]
    if seen is not None:
        seen.extend(sent)
    return [exchange(part, "dp", ndp, k + 1) for k, part in enumerate(sent)]


def both_cores(pieces):
    return [
        (k, c, start, exchange(piece, "core", 2, 1) if c else piece)
        for k, start, piece in pieces
        for c in range(2)
    ]


def stack_kernel(count, *refs):
    for i in range(count):
        refs[-1][i] = refs[i][...]


def stack_after(parts, before):
    dims = (len(parts),) + parts[0].shape
    return pl.pallas_call(
        functools.partial(stack_kernel, len(parts)),
        out_shape=shape(dims, parts[0].dtype),
        in_specs=[VMEM] * len(parts) + [HBM] * len(before),
        out_specs=VMEM,
        compiler_params=params(60),
        cost_estimate=cost(0, 4 * dims[0] * dims[1] * dims[2]),
        name="stack",
    )(*parts, *before)


def pack_kernel(index, *refs):
    width = refs[0].shape[2]
    for i in range(3):
        refs[-1][:, i * width : (i + 1) * width] = refs[i][index]


def pack(index, mats):
    _, rows, width = mats[0].shape
    return pl.pallas_call(
        functools.partial(pack_kernel, index),
        out_shape=shape((rows, 3 * width), BF16),
        in_specs=[VMEM] * 3,
        out_specs=VMEM,
        compiler_params=params(60),
        name="pack",
    )(*mats)


def finish_kernel(count, *refs):
    outs = refs[-3:]
    width = outs[0].shape[2]
    for j in range(count):
        for i in range(3):
            outs[i][j] = refs[j][:, i * width : (i + 1) * width].astype(F32)


def finish_after(sums, before):
    rows, width = sums[0].shape[0], sums[0].shape[1] // 3
    return pl.pallas_call(
        functools.partial(finish_kernel, len(sums)),
        out_shape=(shape((len(sums), rows, width), F32),) * 3,
        in_specs=[VMEM] * len(sums) + [HBM] * len(before),
        out_specs=(VMEM,) * 3,
        compiler_params=params(60),
        name="finish",
    )(*sums, *before)


def after_kernel(*refs):
    pass


def after(arrays, before):
    return pl.pallas_call(
        after_kernel,
        out_shape=tuple(shape(a.shape, a.dtype) for a in arrays),
        in_specs=[HBM] * (len(arrays) + len(before)),
        out_specs=(HBM,) * len(arrays),
        input_output_aliases={i: i for i in range(len(arrays))},
        name="after",
    )(*arrays, *before)


def block_rows(sizes):
    return MODEL_WIDTH // (2 * sizes["dp"] * sizes["z"])


def by_blocks(sizes):
    return block_rows(sizes) % 16 == 0


def gather_rows(block, along_dp, ids, sizes):
    ndp, nz = sizes["dp"], sizes["z"]
    pieces = both_cores(along_dp)
    if by_blocks(sizes):
        places = tuple((k, c, start, piece.shape[0]) for k, c, start, piece in pieces)
        return places, [piece for *_, piece in pieces]
    columns = block.shape[-1]
    whole = jnp.zeros((ndp, nz, 2, block_rows(sizes), columns), BF16)
    for k, c, start, piece in pieces:
        order = ids[1] ^ jnp.arange(start, start + piece.shape[0])
        whole = whole.at[ids[0] ^ k, order, ids[2] ^ c].set(piece)
    return None, [whole.reshape(MODEL_WIDTH, columns)]


def split_cores(columns, ids, sizes):
    ndp, nz = sizes["dp"], sizes["z"]
    rows = columns.shape[0]
    blocks = columns.reshape(rows, ndp, nz, 2, block_rows(sizes))
    blocks = jnp.take(jnp.take(blocks, ids[0] ^ jnp.arange(ndp), 1), ids[1] ^ jnp.arange(nz), 2)
    halves = [lax.dynamic_index_in_dim(blocks, ids[2] ^ c, 3, keepdims=False) for c in range(2)]
    return [half.reshape(rows, MODEL_WIDTH // 2) for half in halves]


def turn_kernel(ndp, nz, count, ids, *refs):
    block = MODEL_WIDTH // (2 * ndp * nz)
    turned = refs[-1]
    for i in range(count):
        turned[...] = jnp.transpose(refs[i][...])
        for k in range(ndp):
            for z in range(nz):
                for c in range(2):
                    at = ((ids[0] ^ k) * nz + (ids[1] ^ z)) * 2 + (ids[2] ^ c)
                    place = pl.ds(pl.multiple_of(at * block, block), block)
                    dest = refs[-1 - 2 * count + 2 * i + c]
                    dest[(k * nz + z) * block : (k * nz + z + 1) * block] = turned[place, :]


def turn(arrays, before, ids, sizes):
    if not by_blocks(sizes):
        return [[half.T for half in split_cores(array, ids, sizes)] for array in arrays]
    rows = arrays[0].shape[0]
    halves = pl.pallas_call(
        functools.partial(turn_kernel, sizes["dp"], sizes["z"], len(arrays)),
        out_shape=(shape((MODEL_WIDTH // 2, rows), BF16),) * (2 * len(arrays)),
        in_specs=[SMEM] + [VMEM] * len(arrays) + [HBM] * len(before),
        out_specs=(VMEM,) * (2 * len(arrays)),
        scratch_shapes=[pltpu.VMEM((MODEL_WIDTH, rows), BF16)],
        compiler_params=params(60),
        name="turn",
    )(ids, *arrays, *before)
    return [halves[2 * i : 2 * i + 2] for i in range(len(arrays))]


def scatter_rows(own, slots, sizes, before=(), seen=None):
    ndp, nz = sizes["dp"], sizes["z"]
    slots = [None, *slots]
    total, parts = own, finish_sum(slots, start_sum(slots, ndp), ndp, before, seen)
    for part in parts:
        total = total + part.astype(F32)
    rows = block_rows(sizes)
    blocks = [total[z * rows : (z + 1) * rows] for z in range(nz)]
    sent = [block.astype(BF16) for block in blocks[1:]]
    got = [exchange(block, "z", nz, z + 1) for z, block in enumerate(sent)]
    return blocks[0], got, parts, sent[-1]


def load_rows(ids, ndp, nz, places, parts, dest, sem):
    if places is None:
        loads = [pltpu.make_async_copy(parts[0], dest, sem.at[0])]
        loads[0].start()
        return loads
    rows = MODEL_WIDTH // (ndp * nz * 2)
    loads = []
    for (k, c, start, count), part in zip(places, parts):
        for z in range(count):
            block = ((ids[0] ^ k) * nz + (ids[1] ^ (start + z))) * 2 + (ids[2] ^ c)
            place = pl.ds(pl.multiple_of(block * rows, rows), rows)
            copy = pltpu.make_async_copy(part.at[z], dest.at[place, :], sem.at[len(loads)])
            loads.append(copy)
    for load in loads:
        load.start()
    return loads


def start_all(pairs, sem):
    copies = [pltpu.make_async_copy(a, b, sem.at[i]) for i, (a, b) in enumerate(pairs)]
    for copy in copies:
        copy.start()
    return copies


def wait_all(copies):
    for copy in copies:
        copy.wait()


def rms_scale(rows):
    return lax.rsqrt(jnp.mean(rows * rows, axis=-1, keepdims=True) + EPS)


def norm_back(normed, row_scale, grad):
    return row_scale * (grad - normed * jnp.mean(grad * normed, axis=-1, keepdims=True))


def swapped(vals):
    return pltpu.roll(vals, HEAD_SIZE // 2, 1)


def head(h):
    return slice(h * HEAD_SIZE, (h + 1) * HEAD_SIZE)


def seen(rows, length):
    q = lax.broadcasted_iota(jnp.int32, (rows, rows), 0)
    s = lax.broadcasted_iota(jnp.int32, (rows, rows), 1)
    return (s <= q) & (s < length)


def attention_probs(query, key, visible):
    scores = jnp.where(visible, nt(query, key) * SCALE, NEG_FILL)
    expon = jnp.exp(scores - jnp.max(scores, axis=-1, keepdims=True))
    return expon / jnp.sum(expon, axis=-1, keepdims=True)


def route_softmax(router_rows, hidden):
    logits = nt(router_rows, hidden)[:EXPERTS]
    expon = jnp.exp(logits - jnp.max(logits, axis=0, keepdims=True))
    return expon / jnp.sum(expon, axis=0, keepdims=True)


def attend_kernel(ndp, nz, places, count, ids, tokens, cosine, sine, *refs):
    parts = refs[:count]
    qkv, mixed, h_one, gains, router, w, sem = refs[-7:]
    rows = tokens.shape[0]
    loads = load_rows(ids, ndp, nz, places, parts, w, sem)
    tok = tokens[...].astype(F32)
    normed = tok * rms_scale(tok)
    for load in loads:
        load.wait()
    extra = jnp.transpose(w[:, QKV:].astype(F32))
    gains[...] = extra[:8]
    router[...] = extra[2 : 2 + ROUTER].astype(BF16)
    h_one[...] = (normed * extra[0:1]).astype(BF16)
    cos, sin = cosine[...], sine[...]
    for t in range(QKV // TILE):
        pre = nn(h_one[...], w[:, t * TILE : (t + 1) * TILE])
        for i in range(TILE // HEAD_SIZE):
            part = pre[:, head(i)]
            at = t * TILE + i * HEAD_SIZE
            if at < QW + KW:
                part = part * cos + swapped(part) * sin
            qkv[:, at : at + HEAD_SIZE] = part.astype(BF16)
    visible = seen(rows, ids[3])
    for h in range(QUERY_HEADS):
        g = h // GROUP
        probs = attention_probs(qkv[:, head(h)], qkv[:, head(QUERY_HEADS + g)], visible)
        values = qkv[:, head(QUERY_HEADS + KEY_VALUE_HEADS + g)]
        mixed[:, head(h)] = nn(probs.astype(BF16), values).astype(BF16)


def attend(ids, tokens, cosine, sine, weights, before, sizes):
    places, parts = weights
    ndp, nz = sizes["dp"], sizes["z"]
    rows = tokens.shape[0]
    return pl.pallas_call(
        functools.partial(attend_kernel, ndp, nz, places, len(parts)),
        out_shape=(
            shape((rows, QKV), BF16),
            shape((rows, QW), BF16),
            shape((rows, MODEL_WIDTH), BF16),
            shape((8, MODEL_WIDTH), F32),
            shape((ROUTER, MODEL_WIDTH), BF16),
        ),
        in_specs=[SMEM, VMEM, VMEM, VMEM] + [HBM] * (len(parts) + len(before)),
        out_specs=(VMEM,) * 5,
        scratch_shapes=[
            pltpu.VMEM((MODEL_WIDTH, FIRST), BF16),
            pltpu.SemaphoreType.DMA((2 * ndp * nz,)),
        ],
        compiler_params=params(60),
        cost_estimate=cost(2 * rows * MODEL_WIDTH * QKV, 10 * MIB, 12 * rows * rows),
        name="attend",
    )(ids, tokens, cosine, sine, *parts, *before)


def project_kernel(ndp, nz, places, ids, tokens, mixed, gains, *refs):
    *parts, residual, top, low, w, sem = refs
    loads = load_rows(ids, ndp, nz, places, parts, w, sem)
    for load in loads:
        load.wait()
    for t in range(MODEL_WIDTH // TILE):
        lane = slice(t * TILE, (t + 1) * TILE)
        residual[:, lane] = tokens[:, lane].astype(F32) + nn(mixed[...], w[:, lane])
    whole = residual[...]
    h_two = (whole * rms_scale(whole) * gains[1:2]).astype(BF16)
    half = top.shape[0]
    top[...], low[...] = h_two[:half], h_two[half:]


def project(ids, tokens, mixed, gains, weights, sizes):
    places, parts = weights
    ndp, nz = sizes["dp"], sizes["z"]
    rows = tokens.shape[0]
    return pl.pallas_call(
        functools.partial(project_kernel, ndp, nz, places),
        out_shape=(shape((rows, MODEL_WIDTH), F32),)
        + (shape((rows // 2, MODEL_WIDTH), BF16),) * 2,
        in_specs=[SMEM, VMEM, VMEM, VMEM] + [HBM] * len(parts),
        out_specs=(VMEM,) * 3,
        scratch_shapes=[
            pltpu.VMEM((QW, MODEL_WIDTH), BF16),
            pltpu.SemaphoreType.DMA((2 * ndp * nz,)),
        ],
        compiler_params=params(60),
        cost_estimate=cost(2 * rows * MODEL_WIDTH * QW, 8 * MIB),
        name="project",
    )(ids, tokens, mixed, gains, *parts)


def expert_kernel(ndp, rows, width, index, last, near, far, unread, *refs):
    it = iter(refs)
    take = lambda n: [next(it) for _ in range(n)]
    (expert_ref, router_ref) = take(2)
    prev_gates = take(index)
    hid_in, cot_in = take(len(near)), take(len(far))
    (w_in,) = take(1)
    prev_in = take(2) if index else []
    take(unread)
    out_hbm, back_hbm = take(2 * ndp - 1 if last else 1), take(2 * ndp if last else 1)
    gates_ref, terms_hbm = take(2)
    hid, cot, w, x, d, ge, inner, dg, du, pick, pick_t, slot_gate, slot_dot = take(13)
    (terms_buf,) = take(1)
    prev = take(2) if index else []
    in_sem, out_sem = take(2)
    depth = MODEL_WIDTH
    tiles = depth // TILE

    loads = {}

    def load(name, source, dest):
        copy = pltpu.make_async_copy(source, dest, in_sem.at[len(loads)])
        copy.start()
        loads[name] = copy

    for i, (k, start, count) in enumerate(near):
        load(("hid", i), hid_in[i], hid.at[k, pl.ds(start, count), :])
    for i, (k, start, count) in enumerate(far):
        load(("cot", i), cot_in[i], cot.at[k, pl.ds(start, count), :])
    load("w", w_in, w)
    for i in range(len(prev)):
        load(("prev", i), prev_in[i], prev[i])

    expert = expert_ref[0]
    which = lax.broadcasted_iota(jnp.int32, (EXPERTS, rows), 0) == expert
    earlier = (
        (
            lax.broadcasted_iota(jnp.int32, (rows, rows), 0)
            < lax.broadcasted_iota(jnp.int32, (rows, rows), 1)
        )
        .astype(F32)
        .astype(BF16)
    )
    slot = lax.broadcasted_iota(jnp.int32, (CAP, rows), 0).astype(F32)
    for s in range(ndp):
        for i, piece in enumerate(near):
            if piece[0] == s:
                loads["hid", i].wait()
        for i, piece in enumerate(far):
            if piece[0] == s:
                loads["cot", i].wait()
        hidden = hid[s]
        probs = route_softmax(router_ref[...], hidden)
        named = cot[s, rows : rows + NOTE, :rows]
        place = nn(named, earlier)[:EXPERTS]
        named = named[:EXPERTS].astype(F32)
        named_row = jnp.sum(jnp.where(which, named, 0.0), axis=0, keepdims=True)
        gate_row = jnp.sum(jnp.where(which, probs, 0.0), axis=0, keepdims=True)
        place_row = jnp.sum(jnp.where(which, place, 0.0), axis=0, keepdims=True)
        chosen = jnp.where((slot == place_row) & (named_row > 0.5), 1.0, 0.0)
        pick[s] = chosen.astype(BF16)
        pick_t[s] = jnp.transpose(chosen).astype(BF16)
        at = pl.ds(s * CAP, CAP)
        gate = jnp.sum(chosen * gate_row, axis=1, keepdims=True)
        slot_gate[at, :] = jnp.broadcast_to(gate, (CAP, 128))
        x[at, :] = nn(pick[s], hidden).astype(BF16)
        grads = nn(pick[s], cot[s, :rows])
        d[at, :] = grads.astype(BF16)
        ge[at, :] = (gate * grads).astype(BF16)
    loads["w"].wait()

    def hidden_units(t, carry):
        at = pl.multiple_of(t * TILE, TILE)
        gate_pre = nn(x[...], w[:, pl.ds(at, TILE)])
        up_pre = nn(x[...], w[:, pl.ds(width + at, TILE)])
        grad_inner = nn(ge[...], w[:, pl.ds(2 * width + at, TILE)])
        sig = 1.0 / (1.0 + jnp.exp(-gate_pre))
        act = gate_pre * sig
        inner[:, pl.ds(at, TILE)] = (act * up_pre).astype(BF16)
        dg[:, pl.ds(at, TILE)] = (
            grad_inner * up_pre * sig * (1.0 + gate_pre * (1.0 - sig))
        ).astype(BF16)
        du[:, pl.ds(at, TILE)] = (grad_inner * act).astype(BF16)
        return carry

    lax.fori_loop(0, width // TILE, hidden_units, 0)
    slot_dot[...] = jnp.zeros_like(slot_dot)
    for i in range(len(prev)):
        loads["prev", i].wait()

    noted = (rows + NOTE) // 2

    def stores(t):
        lane = pl.ds(pl.multiple_of(t * TILE, TILE), TILE)
        copies = [(terms_buf.at[lane, :], terms_hbm.at[lane, :])]
        if not last:
            body = pl.ds(0, rows)
            copies.append((hid.at[:, :, lane], out_hbm[0].at[:, :, lane]))
            copies.append((cot.at[:, body, lane], back_hbm[0].at[:, body, lane]))
        else:
            copies.append((hid.at[0, :, lane], out_hbm[0].at[:, lane]))
            for i in range(2, 2 * ndp):
                first = pl.ds(i % 2 * (rows // 2), rows // 2)
                copies.append((hid.at[i // 2, first, lane], out_hbm[i - 1].at[:, lane]))
            for i in range(2 * ndp):
                body = pl.ds(0, noted if i % 2 == 0 else rows - noted)
                taken = pl.ds(i % 2 * noted, noted if i % 2 == 0 else rows - noted)
                copies.append((cot.at[i // 2, taken, lane], back_hbm[i].at[body, lane]))
        return [
            pltpu.make_async_copy(source, dest, out_sem.at[i, t])
            for i, (source, dest) in enumerate(copies)
        ]

    def features(t, carry):
        lane = pl.ds(pl.multiple_of(t * TILE, TILE), TILE)
        result = nt(inner[...], w[lane, pl.ds(2 * width, width)]).astype(BF16).astype(F32)
        partial = jnp.sum(result * d[:, lane].astype(F32), axis=1, keepdims=True)
        slot_dot[...] += jnp.broadcast_to(partial, slot_dot.shape)
        gated = (slot_gate[:, :1] * result).astype(BF16)
        grad_in = (
            nt(dg[...], w[lane, pl.ds(0, width)]) + nt(du[...], w[lane, pl.ds(width, width)])
        ).astype(BF16)
        for s in range(ndp):
            part = slice(s * CAP, (s + 1) * CAP)
            sent = nn(pick_t[s], gated[part])
            back = nn(pick_t[s], grad_in[part])
            if prev:
                sent = sent + prev[0][s, :, lane].astype(F32)
                back = back + prev[1][s, :rows, lane].astype(F32)
            hid[s, :, lane] = sent.astype(BF16)
            cot[s, :rows, lane] = back.astype(BF16)
        x_t = jnp.transpose(x[:, lane])
        terms_buf[lane, pl.ds(0, width)] = nn(x_t, dg[...]).astype(BF16)
        terms_buf[lane, pl.ds(width, width)] = nn(x_t, du[...]).astype(BF16)
        ge_t = jnp.transpose(ge[:, lane])
        terms_buf[lane, pl.ds(2 * width, width)] = nn(ge_t, inner[...]).astype(BF16)
        for store in stores(t):
            store.start()
        return carry

    lax.fori_loop(0, tiles, features, 0)
    line = lax.broadcasted_iota(jnp.int32, (NOTE, 3 * rows), 0)
    notes = []
    for s in range(ndp):
        part = slice(s * CAP, (s + 1) * CAP)
        own = jnp.sum(pick[s].astype(F32) * slot_dot[part, :1], axis=0, keepdims=True)
        gates_ref[s] = own
        if not last:
            continue
        note = jnp.zeros((NOTE, 3 * rows), F32)
        for j, row in enumerate([p[s] for p in prev_gates] + [own]):
            high = row.astype(BF16).astype(F32)
            middle = (row - high).astype(BF16).astype(F32)
            low = row - high - middle
            at = expert - index + j
            note = jnp.where(line == at, jnp.concatenate([high, middle, low], axis=1), note)
        cot[s, rows : rows + NOTE, : 3 * rows] = note.astype(BF16)
        notes.append(
            pltpu.make_async_copy(
                cot.at[s, pl.ds(rows, NOTE), :],
                back_hbm[2 * s + 1].at[pl.ds(rows - noted, NOTE), :],
                out_sem.at[4 * ndp + 1, s],
            )
        )
        notes[-1].start()
    for t in range(tiles):
        for store in stores(t):
            store.wait()
    for note in notes:
        note.wait()


def run_expert(index, last, expert, router, hidden, grads, w_all, prev, prev_gates, ndp, before):
    rows = 2 * hidden[0][2].shape[0]
    near, far = (tuple((k, at, p.shape[0]) for k, at, p in group) for group in (hidden, grads))
    width = w_all.shape[1] // 3
    slots = ndp * CAP
    depth = MODEL_WIDTH
    tiles = depth // TILE
    scratch = [
        pltpu.VMEM((ndp, rows, depth), BF16),
        pltpu.VMEM((ndp, rows + NOTE, depth), BF16),
        pltpu.VMEM((depth, 3 * width), BF16),
        pltpu.VMEM((slots, depth), BF16),
        pltpu.VMEM((slots, depth), BF16),
        pltpu.VMEM((slots, depth), BF16),
        pltpu.VMEM((slots, width), BF16),
        pltpu.VMEM((slots, width), BF16),
        pltpu.VMEM((slots, width), BF16),
        pltpu.VMEM((ndp, CAP, rows), BF16),
        pltpu.VMEM((ndp, rows, CAP), BF16),
        pltpu.VMEM((slots, 128), F32),
        pltpu.VMEM((slots, 128), F32),
        pltpu.VMEM((depth, 3 * width), BF16),
    ]
    if index:
        scratch += [
            pltpu.VMEM((ndp, rows, depth), BF16),
            pltpu.VMEM((ndp, rows + NOTE, depth), BF16),
        ]
    scratch += [
        pltpu.SemaphoreType.DMA((len(near) + len(far) + 3,)),
        pltpu.SemaphoreType.DMA((4 * ndp + 2, max(tiles, ndp))),
    ]
    sent = [shape((ndp, rows, depth), BF16), shape((ndp, rows + NOTE, depth), BF16)]
    if last:
        sent = [shape((rows, depth), BF16)]
        sent += [shape((rows // 2, depth), BF16)] * (2 * ndp - 2)
        sent += [shape(((rows + NOTE) // 2, depth), BF16)] * (2 * ndp)
    flops = 2 * slots * depth * width * 9 + 8 * ndp * CAP * rows * depth
    return pl.pallas_call(
        functools.partial(
            expert_kernel, ndp, rows, width, index, last, near, far, len(before)
        ),
        out_shape=(
            *sent,
            shape((ndp, 1, rows), F32),
            shape((depth, 3 * width), BF16),
        ),
        in_specs=[SMEM, VMEM]
        + [VMEM] * len(prev_gates)
        + [HBM] * (len(near) + len(far) + 1 + len(prev) + len(before)),
        out_specs=(HBM,) * len(sent) + (VMEM, HBM),
        scratch_shapes=scratch,
        compiler_params=params(60),
        cost_estimate=cost(flops, 40 * MIB, slots * width),
        name="expert",
    )(
        expert,
        router,
        *prev_gates,
        *(piece for *_, piece in hidden),
        *(piece for *_, piece in grads),
        w_all,
        *prev,
        *before,
    )


def back_kernel(ndp, nz, places, count, given, unread, ids, gains, router, cosine, sine, *refs):
    refs = list(refs)
    take = lambda n: [refs.pop(0) for _ in range(n)]
    data, backs, parts = take(5), take(given), take(count)
    take(unread)
    out_resid, out_attn, out_pre, notes = take(4)
    residual, top, low, grads, qkv = held = take(5)
    got = take(given)
    w, grad_mixed, grad_resid, grad_attn, grad_pre, sem, data_sem, out_sem = refs
    rows = residual.shape[0]
    fetched = start_all(list(zip(backs + data[1:3] + data[:1] + data[3:], got + held[1:3] + held[:1] + held[3:])), data_sem)
    loads = load_rows(ids, ndp, nz, places, parts, w, sem)
    wait_all(fetched[:given])
    whole = jnp.concatenate([got[0][...], got[1][...]], axis=0).astype(F32)
    for part in got[2:]:
        whole = whole + part[...].astype(F32)
    grad_h = whole[:rows]
    note = whole[rows : rows + EXPERTS, : 3 * rows]
    grad_route = note[:, :rows] + note[:, rows : 2 * rows] + note[:, 2 * rows :]
    wait_all(fetched[given : given + 4])
    hidden = jnp.concatenate([top[...], low[...]], axis=0)
    probs = route_softmax(router[...], hidden)
    grad_logits = probs * (grad_route - jnp.sum(probs * grad_route, axis=0, keepdims=True))
    grad_logits = jnp.concatenate([grad_logits, jnp.zeros_like(grad_logits)], axis=0)
    grad_logits = grad_logits.astype(BF16)
    grad_h = grad_h + tn(grad_logits, router[...])
    res = residual[...]
    scale = rms_scale(res)
    normed = res * scale
    notes[0:8] = jnp.broadcast_to(
        jnp.sum(normed * grad_h, axis=0, keepdims=True), (8, MODEL_WIDTH)
    )
    notes[8:16] = nn(grad_logits, hidden)[:EXPERTS]
    live = lax.broadcasted_iota(jnp.int32, (rows, 1), 0) < ids[3]
    final = jnp.where(live, grads[...].astype(F32), 0.0)
    total = final + norm_back(normed, scale, grad_h * gains[1:2])
    grad_resid[...] = total
    grad_attn[...] = total.astype(BF16)
    stores = start_all([(grad_attn, out_attn), (grad_resid, out_resid)], out_sem)
    wait_all(loads)
    for t in range(QW // TILE):
        lane = slice(t * TILE, (t + 1) * TILE)
        grad_mixed[:, lane] = nt(grad_attn[...], w[lane, :]).astype(BF16)
    wait_all(fetched[given + 4 :])
    source = lax.broadcasted_iota(jnp.int32, (rows, rows), 0)
    visible = (source <= lax.broadcasted_iota(jnp.int32, (rows, rows), 1)) & (source < ids[3])
    cos, sin = cosine[...], sine[...]
    for g in range(KEY_VALUE_HEADS):
        key = qkv[:, head(QUERY_HEADS + g)]
        value = qkv[:, head(QUERY_HEADS + KEY_VALUE_HEADS + g)]
        grad_key = jnp.zeros((rows, HEAD_SIZE), F32)
        grad_value = jnp.zeros((rows, HEAD_SIZE), F32)
        for h in range(g * GROUP, (g + 1) * GROUP):
            query, grad = qkv[:, head(h)], grad_mixed[:, head(h)]
            scores = jnp.where(visible, nt(key, query) * SCALE, NEG_FILL)
            expon = jnp.exp(scores - jnp.max(scores, axis=0, keepdims=True))
            probs = expon / jnp.sum(expon, axis=0, keepdims=True)
            grad_probs = nt(value, grad)
            grad_value = grad_value + nn(probs.astype(BF16), grad)
            row_dot = jnp.sum(probs * grad_probs, axis=0, keepdims=True)
            grad_scores = (probs * (grad_probs - row_dot)).astype(BF16)
            grad_query = tn(grad_scores, key) * SCALE
            grad_key = grad_key + nn(grad_scores, query)
            grad_pre[:, head(h)] = (grad_query * cos - swapped(grad_query) * sin).astype(BF16)
        grad_key = grad_key * SCALE
        grad_pre[:, head(QUERY_HEADS + g)] = (
            grad_key * cos - swapped(grad_key) * sin
        ).astype(BF16)
        grad_pre[:, head(QUERY_HEADS + KEY_VALUE_HEADS + g)] = grad_value.astype(BF16)
    last = pltpu.make_async_copy(grad_pre, out_pre, out_sem.at[2])
    last.start()
    wait_all(stores + [last])


def back(
    ids, residual, h_two, grads, gains, router, cosine, sine, qkv, backs, weights, before, sizes
):
    ndp, nz = sizes["dp"], sizes["z"]
    places, parts = weights
    rows = residual.shape[0]
    data = [residual, *h_two, grads, qkv]
    made = [
        shape((rows, MODEL_WIDTH), F32),
        shape((rows, MODEL_WIDTH), BF16),
        shape((rows, QKV), BF16),
    ]
    room = lambda array: pltpu.VMEM(array.shape, array.dtype)
    return pl.pallas_call(
        functools.partial(
            back_kernel, ndp, nz, places, len(parts), len(backs), len(before)
        ),
        out_shape=(*made, shape((16, MODEL_WIDTH), F32)),
        in_specs=[SMEM]
        + [VMEM] * 4
        + [HBM] * (len(data) + len(backs) + len(parts) + len(before)),
        out_specs=(HBM, HBM, HBM, VMEM),
        scratch_shapes=[
            *(room(array) for array in data + backs),
            pltpu.VMEM((QW, MODEL_WIDTH), BF16),
            pltpu.VMEM((rows, QW), BF16),
            *(room(array) for array in made),
            pltpu.SemaphoreType.DMA((2 * ndp * nz,)),
            pltpu.SemaphoreType.DMA((len(data) + len(backs),)),
            pltpu.SemaphoreType.DMA((3,)),
        ],
        compiler_params=params(60),
        cost_estimate=cost(3 * rows * MODEL_WIDTH * QW, 16 * MIB, 12 * rows * rows),
        name="back",
    )(ids, gains, router, cosine, sine, *data, *backs, *parts, *before)


def tokens_back_kernel(ndp, nz, places, count, ids, tokens, gains, grad_pre, grad_resid, *refs):
    parts = refs[:count]
    grad_tokens, w, sem = refs[-3:]
    loads = load_rows(ids, ndp, nz, places, parts, w, sem)
    tok = tokens[...].astype(F32)
    scale = rms_scale(tok)
    normed = tok * scale
    for load in loads:
        load.wait()
    for t in range(MODEL_WIDTH // TILE):
        lane = slice(t * TILE, (t + 1) * TILE)
        grad_tokens[:, lane] = nt(grad_pre[...], w[lane, :QKV])
    grad_h = grad_tokens[...]
    grad_tokens[...] = grad_resid[...] + norm_back(normed, scale, grad_h * gains[0:1])


def tokens_back(ids, tokens, gains, grad_pre, grad_resid, weights, before, sizes):
    ndp, nz = sizes["dp"], sizes["z"]
    places, parts = weights
    rows = tokens.shape[0]
    return pl.pallas_call(
        functools.partial(tokens_back_kernel, ndp, nz, places, len(parts)),
        out_shape=shape((rows, MODEL_WIDTH), F32),
        in_specs=[SMEM] + [VMEM] * 4 + [HBM] * (len(parts) + len(before)),
        out_specs=VMEM,
        scratch_shapes=[
            pltpu.VMEM((MODEL_WIDTH, FIRST), BF16),
            pltpu.SemaphoreType.DMA((2 * ndp * nz,)),
        ],
        compiler_params=params(60),
        cost_estimate=cost(2 * rows * MODEL_WIDTH * QKV, 12 * MIB),
        name="tokens_back",
    )(ids, tokens, gains, grad_pre, grad_resid, *parts, *before)


def terms_kernel(ndp, nz, noted, unread, ids, *refs):
    refs = list(refs)
    take = lambda n: [refs.pop(0) for _ in range(n)]
    notes, given = take(2 if noted else 0), take(4)
    take(unread)
    count = 2 * ndp - 1
    outs, held, dests = take(count), take(4), take(count)
    note_rows, in_sem, out_sem = refs
    wait_all(start_all(list(zip(given, held)), in_sem))
    left = jnp.concatenate([held[0][...], held[1][...]], axis=1)
    right = jnp.concatenate([held[2][...], held[3][...]], axis=0)
    slot = MODEL_WIDTH // (2 * ndp)
    stores = []

    def put(lane, value):
        dests[0][:, lane] = value[:slot]
        for i in range(1, count):
            at = slot + (i - 1) * (slot // 2)
            dests[i][:, lane] = value[at : at + slot // 2].astype(BF16)
        pairs = [(dests[i].at[:, lane], outs[i].at[:, lane]) for i in range(count)]
        stores.extend(start_all(pairs, out_sem.at[len(stores) // count]))

    if noted:
        note = notes[0][...] + notes[1][...]
        block = jnp.concatenate([note, jnp.zeros((PAD - 16, note.shape[1]), F32)], axis=0)
        block = jnp.transpose(block)
    if noted == 1:
        note_rows[...] = block
        rows = MODEL_WIDTH // (2 * ndp * nz)
        taken = []
        for k in range(ndp):
            for z in range(nz):
                at = ((ids[0] ^ k) * nz + (ids[1] ^ z)) * 2 + ids[2]
                taken.append(note_rows[pl.ds(pl.multiple_of(at * rows, rows), rows), :])
        block = jnp.concatenate(taken, axis=0)
    if noted:
        put(slice(right.shape[1], right.shape[1] + PAD), block)
    for t in range(right.shape[1] // TILE):
        lane = slice(t * TILE, (t + 1) * TILE)
        put(lane, nn(left, right[:, lane]))
    wait_all(stores)


def weight_terms(ids, left, right, notes, before, sizes):
    ndp, nz = sizes["dp"], sizes["z"]
    slot = MODEL_WIDTH // (2 * ndp)
    columns = right[0].shape[1] + (PAD if notes else 0)
    noted = 0 if not notes else 1 if notes[0].shape[1] == MODEL_WIDTH else 2
    made = [shape((slot, columns), F32)] + [shape((slot // 2, columns), BF16)] * (2 * ndp - 2)
    room = lambda array: pltpu.VMEM(array.shape, array.dtype)
    arrays = [*left, *right]
    found = pl.pallas_call(
        functools.partial(terms_kernel, ndp, nz, noted, len(before)),
        out_shape=tuple(made),
        in_specs=[SMEM] + [VMEM] * len(notes) + [HBM] * (4 + len(before)),
        out_specs=(HBM,) * len(made),
        scratch_shapes=[
            *(room(array) for array in arrays + made),
            pltpu.VMEM((MODEL_WIDTH, PAD), F32),
            pltpu.SemaphoreType.DMA((4,)),
            pltpu.SemaphoreType.DMA((columns // TILE + 1, len(made))),
        ],
        compiler_params=params(60),
        cost_estimate=cost(2 * MODEL_WIDTH * left[0].shape[1] * columns, 5 * MIB),
        name="weight_terms",
    )(ids, *notes, *arrays, *before)
    return found[0], [tuple(found[i : i + 2]) for i in range(1, len(found), 2)]


def settle_kernel(count, *refs):
    own, got = refs[0], refs[1 : 1 + count]
    mats = refs[1 + count : 4 + count]
    gain = refs[4 + count]
    outs, gains, router = refs[-5:-2], refs[-2], refs[-1]
    total = own[...]
    for part in got:
        total = total + part[...].astype(F32)
    dot, at = jnp.zeros((total.shape[0], 1), F32), 0
    for mat, out in zip(mats, outs):
        width = mat.shape[1]
        part = total[:, at : at + width]
        out[...] = part
        dot = dot + jnp.sum(part * mat[...].astype(F32), axis=1, keepdims=True)
        at += width
    small = total[:, at:]
    router[...] = small[:, 8 : 8 + EXPERTS]
    lane = lax.broadcasted_iota(jnp.int32, small.shape, 1)
    turned = jnp.transpose(jnp.where(lane == 1, dot, small))
    gains[0:1] = turned[1:2] / gain[...]
    gains[1:2] = turned[0:1]


def settle(own, got, mats, gain, before):
    rows = own.shape[0]
    return pl.pallas_call(
        functools.partial(settle_kernel, len(got)),
        out_shape=tuple(shape(mat.shape, F32) for mat in mats)
        + (shape((2, rows), F32), shape((rows, EXPERTS), F32)),
        in_specs=[VMEM] * (1 + len(got) + 4) + [HBM] * len(before),
        out_specs=(VMEM,) * 5,
        compiler_params=params(60),
        name="settle",
    )(own, *got, *mats, gain, *before)


def rope_tables(rows):
    half = HEAD_SIZE // 2
    position = jnp.arange(rows).astype(F32)
    inverse = ROPE_BASE ** (-jnp.arange(half).astype(F32) / half)
    angles = position[:, None] * inverse[None, :]
    cosine, sine = jnp.cos(angles), jnp.sin(angles)
    return jnp.concatenate([cosine, cosine], axis=1), jnp.concatenate([-sine, sine], axis=1)


def per_device(
    sizes,
    tokens,
    lengths,
    routes,
    cotangent,
    gain_one,
    w_query,
    key_matrix,
    value_matrix,
    w_out,
    gain_two,
    w_router,
    w_gate,
    w_up,
    w_down,
):
    ndp = sizes["dp"]
    rows = tokens.shape[0]
    local, _, width = w_gate.shape
    me_dp = lax.axis_index("dp")
    length = lengths[0]
    ids = jnp.stack([me_dp, lax.axis_index("z"), lax.axis_index("core"), length]).astype(jnp.int32)
    live = (jnp.arange(rows) < length)[:, None]
    expert_ids = jnp.arange(EXPERTS, dtype=jnp.int32)

    extra = jnp.concatenate([gain_one[:, None], gain_two[:, None], w_router], axis=1)
    extra = jnp.pad(extra, ((0, 0), (0, PAD - extra.shape[1])))
    first = jnp.concatenate([w_query, key_matrix, value_matrix, extra], axis=1)
    named = jnp.any(routes[None, :, :] == expert_ids[:, None, None], axis=2).astype(BF16)
    named = jnp.pad(named, ((0, NOTE - EXPERTS), (0, MODEL_WIDTH - rows)))
    grad_low = jnp.where(live, cotangent, jnp.zeros_like(cotangent))
    grad_low = jnp.concatenate([grad_low, named], axis=0)
    grad_near = start_dp(grad_low, ndp)

    nz = sizes["z"]
    first_z = [first] + [exchange(first, "z", nz, k) for k in range(1, nz)]
    first_block = stack_after(first_z, grad_near)
    second_z = [w_out] + [exchange(w_out, "z", nz, k) for k in range(1, nz)]
    first_near = start_dp(first_block, ndp)
    first_dp = pass_on(first_block, first_near, ndp, second_z[1:])
    packed = after([pack(j, (w_gate, w_up, w_down)) for j in range(local)], first_z[1:] + grad_near)
    expert_mats = [lax.all_gather(p, ("z", "core"), axis=0, tiled=True) for p in packed]
    second_block = stack_after(second_z, [piece for *_, piece in first_dp[1:3]])
    second_dp = gather_direct(second_block, ndp)

    cosine, sine = rope_tables(rows)
    weights_in = gather_rows(first, first_dp, ids, sizes)
    qkv, mixed, h_one, gains, router = attend(ids, tokens, cosine, sine, weights_in, [], sizes)
    second_far = after([piece for *_, piece in second_dp[1:]], [mixed])
    second_dp = [(k, 0, piece) for k, piece in enumerate([second_block, *second_far])]
    grad_far = pass_on(grad_low, grad_near, ndp, second_far)
    weights_out = gather_rows(w_out, second_dp, ids, sizes)
    residual, *h_two = project(ids, tokens, mixed, gains, weights_out, sizes)
    hidden = gather_halves(h_two, ndp)
    turned = turn([mixed, h_one], [hidden[2][2]], ids, sizes)
    mixed, h_one = ([mine, exchange(other, "core", 2, 1)] for mine, other in turned)

    prev, gate_grads, sums = (), [], []
    for j in range(local):
        expert = (me_dp * local + j).astype(jnp.int32).reshape(1)
        *prev, grad_gate, terms = run_expert(
            j,
            j == local - 1,
            expert,
            router,
            hidden,
            grad_far,
            expert_mats[j],
            prev,
            gate_grads,
            ndp,
            [*mixed, *h_one],
        )
        gate_grads.append(grad_gate)
        sums.append(lax.psum_scatter(terms, ("z", "core"), scatter_dimension=0, tiled=True))
    count = 2 * ndp - 1
    outs, backs = prev[:count], prev[count:]
    pairs = [tuple(backs[2 * k : 2 * k + 2]) for k in range(ndp)]
    backs = [*pairs[0], *finish_sum(pairs, start_sum(pairs, ndp), ndp)]
    out_slots = [None] + [tuple(outs[i : i + 2]) for i in range(1, count, 2)]
    out_past = start_sum(out_slots, ndp)

    grad_resid, grad_attn, grad_pre, notes = back(
        ids,
        residual,
        h_two,
        cotangent,
        gains,
        router,
        cosine,
        sine,
        qkv,
        backs,
        weights_out,
        [],
        sizes,
    )
    if not by_blocks(sizes):
        notes = split_cores(notes, ids, sizes)
        notes = notes[0], exchange(notes[1], "core", 2, 1)
    else:
        notes = notes, exchange(notes, "core", 2, 1)
    grad_attn = grad_attn, exchange(grad_attn, "core", 2, 1)
    grad_pre = grad_pre, exchange(grad_pre, "core", 2, 1)
    out_terms = weight_terms(ids, mixed, grad_attn, (), grad_pre[1:], sizes)
    in_terms = weight_terms(
        ids, h_one, grad_pre, notes, sums[:-1] + [out_terms[0]] + out_past, sizes
    )
    own_out, late, _, _ = scatter_rows(*out_terms, sizes, in_terms[:1])
    sending = []
    own, got, arrived, leaving = scatter_rows(*in_terms, sizes, seen=sending)
    grad_tokens = tokens_back(
        ids, tokens, gains, grad_pre[0], grad_resid, weights_in, sending, sizes
    )
    block = residual + outs[0].astype(F32)
    for part in finish_sum(out_slots, out_past, ndp, arrived):
        block = block + part.astype(F32)
    block_out = block.astype(BF16)
    gain = gain_one.astype(F32)[None]
    *grad_in, grad_gains, grad_router = settle(
        own, got, (w_query, key_matrix, value_matrix), gain, [block_out]
    )
    expert_sums = finish_after(sums, [leaving])
    grad_out = own_out + sum(part.astype(F32) for part in late)
    return (
        block_out,
        grad_tokens,
        grad_gains[0],
        *grad_in,
        grad_out,
        grad_gains[1],
        grad_router,
        *expert_sums,
    )


def solution(mesh):
    ndp, nf = mesh.shape["dp"], mesh.shape["fsdp"]
    sizes = {"dp": ndp, "z": nf // 2, "core": 2}
    split = Mesh(mesh.devices.reshape(ndp, nf // 2, 2), ("dp", "z", "core"))
    every = ("dp", "z", "core")
    rows = P(every, None)
    vector = P(every)
    expert = P("dp", ("z", "core"), None)

    def run(*args):
        return per_device(sizes, *args)

    return jax.shard_map(
        run,
        mesh=split,
        in_specs=(rows, vector, rows, rows, vector, rows, rows, rows, rows, vector, rows)
        + (expert,) * 3,
        out_specs=(rows, rows, vector, rows, rows, rows, rows, vector, rows) + (expert,) * 3,
        check_vma=False,
    )
```

```python
import functools

import jax
import jax.numpy as jnp
from jax import lax
from jax.experimental import pallas as pl
from jax.experimental.pallas import tpu as pltpu
from jax.sharding import Mesh
from jax.sharding import PartitionSpec as P

MODEL_WIDTH = 1536
QUERY_HEADS = 12
KEY_VALUE_HEADS = 2
HEAD_SIZE = 128
EXPERTS = 8
CAP = 160
GROUP = QUERY_HEADS // KEY_VALUE_HEADS
QW = QUERY_HEADS * HEAD_SIZE
KW = KEY_VALUE_HEADS * HEAD_SIZE
QKV = QW + 2 * KW
PAD = 128
FIRST = QKV + PAD
NOTE = 32
ROUTER = 16
EPS = 1e-06
ROPE_BASE = 1500000.0
NEG_FILL = -1e30
SCALE = HEAD_SIZE ** (-0.5)
F32 = jnp.float32
BF16 = jnp.bfloat16
TILE = 256
MIB = 1024 * 1024
HBM = pl.BlockSpec(memory_space=pltpu.HBM)
VMEM = pl.BlockSpec(memory_space=pltpu.VMEM)
SMEM = pl.BlockSpec(memory_space=pltpu.SMEM)


def nn(a, b):
    return lax.dot_general(a, b, (((1,), (0,)), ((), ())), preferred_element_type=F32)


def nt(a, b):
    return lax.dot_general(a, b, (((1,), (1,)), ((), ())), preferred_element_type=F32)


def tn(a, b):
    return lax.dot_general(a, b, (((0,), (0,)), ((), ())), preferred_element_type=F32)


def shape(dims, dtype):
    return jax.ShapeDtypeStruct(dims, dtype)


def params(mib):
    return pltpu.CompilerParams(vmem_limit_bytes=mib * MIB)


def cost(flops, data, special=0):
    return pl.CostEstimate(flops=flops, bytes_accessed=data, transcendentals=special)


def exchange(block, axis, size, step):
    return lax.ppermute(block, axis, [(i, i ^ step) for i in range(size)])


def start_dp(block, ndp):
    return [exchange(block, "dp", ndp, k) for k in ((1, 2) if ndp == 4 else range(1, ndp))]


def pass_on(block, near, ndp, before=()):
    if ndp != 4:
        return [(k, 0, piece) for k, piece in enumerate([block] + near)]
    side, up = after(near, before) if before else near
    half = block.shape[0] // 2
    return [
        (0, 0, block),
        (1, 0, side),
        (2, 0, up),
        (3, 0, exchange(side[:half], "dp", ndp, 2)),
        (3, half, exchange(up[half:], "dp", ndp, 1)),
    ]


def gather_direct(block, ndp):
    return [(k, 0, exchange(block, "dp", ndp, k) if k else block) for k in range(ndp)]


def gather_halves(halves, ndp):
    top, low = halves
    at = top.shape[0]
    if ndp != 4:
        return [
            (k, i * at, exchange(half, "dp", ndp, k) if k else half)
            for k in range(ndp)
            for i, half in enumerate(halves)
        ]
    side_top, up_low = exchange(top, "dp", ndp, 1), exchange(low, "dp", ndp, 2)
    side_low, up_top = exchange(low, "dp", ndp, 1), exchange(top, "dp", ndp, 2)
    return [
        (0, 0, top),
        (0, at, low),
        (1, 0, side_top),
        (2, at, up_low),
        (1, at, side_low),
        (2, 0, up_top),
        (3, 0, exchange(side_top, "dp", ndp, 2)),
        (3, at, exchange(up_low, "dp", ndp, 1)),
    ]


def start_sum(slots, ndp):
    if ndp != 4:
        return []
    return [exchange(slots[3][0], "dp", ndp, 1), exchange(slots[3][1], "dp", ndp, 2)]


def finish_sum(slots, past, ndp, before=()):
    if ndp != 4:
        sent = [jnp.concatenate(slot, axis=0) for slot in slots[1:]]
    else:
        past = after(past, before) if before else past
        add = lambda a, b: (a.astype(F32) + b.astype(F32)).astype(BF16)
        sent = [
            jnp.concatenate([slots[1][0], add(slots[1][1], past[1])], axis=0),
            jnp.concatenate([add(slots[2][0], past[0]), slots[2][1]], axis=0),
        ]
    return [exchange(part, "dp", ndp, k + 1) for k, part in enumerate(sent)]


def both_cores(pieces):
    return [
        (k, c, start, exchange(piece, "core", 2, 1) if c else piece)
        for k, start, piece in pieces
        for c in range(2)
    ]


def stack_kernel(count, *refs):
    for i in range(count):
        refs[-1][i] = refs[i][...]


def stack_after(parts, before):
    dims = (len(parts),) + parts[0].shape
    return pl.pallas_call(
        functools.partial(stack_kernel, len(parts)),
        out_shape=shape(dims, parts[0].dtype),
        in_specs=[VMEM] * len(parts) + [HBM] * len(before),
        out_specs=VMEM,
        compiler_params=params(60),
        cost_estimate=cost(0, 4 * dims[0] * dims[1] * dims[2]),
        name="stack",
    )(*parts, *before)


def pack_kernel(index, *refs):
    width = refs[0].shape[2]
    for i in range(3):
        refs[-1][:, i * width : (i + 1) * width] = refs[i][index]


def pack(index, mats):
    _, rows, width = mats[0].shape
    return pl.pallas_call(
        functools.partial(pack_kernel, index),
        out_shape=shape((rows, 3 * width), BF16),
        in_specs=[VMEM] * 3,
        out_specs=VMEM,
        compiler_params=params(60),
        name="pack",
    )(*mats)


def finish_kernel(count, *refs):
    outs = refs[-3:]
    width = outs[0].shape[2]
    for j in range(count):
        for i in range(3):
            outs[i][j] = refs[j][:, i * width : (i + 1) * width].astype(F32)


def finish_after(sums, before):
    rows, width = sums[0].shape[0], sums[0].shape[1] // 3
    return pl.pallas_call(
        functools.partial(finish_kernel, len(sums)),
        out_shape=(shape((len(sums), rows, width), F32),) * 3,
        in_specs=[VMEM] * len(sums) + [HBM] * len(before),
        out_specs=(VMEM,) * 3,
        compiler_params=params(60),
        name="finish",
    )(*sums, *before)


def after_kernel(*refs):
    pass


def after(arrays, before):
    return pl.pallas_call(
        after_kernel,
        out_shape=tuple(shape(a.shape, a.dtype) for a in arrays),
        in_specs=[HBM] * (len(arrays) + len(before)),
        out_specs=(HBM,) * len(arrays),
        input_output_aliases={i: i for i in range(len(arrays))},
        name="after",
    )(*arrays, *before)


def block_rows(sizes):
    return MODEL_WIDTH // (2 * sizes["dp"] * sizes["z"])


def by_blocks(sizes):
    return block_rows(sizes) % 16 == 0


def gather_rows(block, along_dp, ids, sizes):
    ndp, nz = sizes["dp"], sizes["z"]
    pieces = both_cores(along_dp)
    if by_blocks(sizes):
        places = tuple((k, c, start, piece.shape[0]) for k, c, start, piece in pieces)
        return places, [piece for *_, piece in pieces]
    columns = block.shape[-1]
    whole = jnp.zeros((ndp, nz, 2, block_rows(sizes), columns), BF16)
    for k, c, start, piece in pieces:
        order = ids[1] ^ jnp.arange(start, start + piece.shape[0])
        whole = whole.at[ids[0] ^ k, order, ids[2] ^ c].set(piece)
    return None, [whole.reshape(MODEL_WIDTH, columns)]


def split_cores(columns, ids, sizes):
    ndp, nz = sizes["dp"], sizes["z"]
    rows = columns.shape[0]
    blocks = columns.reshape(rows, ndp, nz, 2, block_rows(sizes))
    blocks = jnp.take(jnp.take(blocks, ids[0] ^ jnp.arange(ndp), 1), ids[1] ^ jnp.arange(nz), 2)
    halves = [lax.dynamic_index_in_dim(blocks, ids[2] ^ c, 3, keepdims=False) for c in range(2)]
    return [half.reshape(rows, MODEL_WIDTH // 2) for half in halves]


def turn_kernel(ndp, nz, count, ids, *refs):
    block = MODEL_WIDTH // (2 * ndp * nz)
    turned = refs[-1]
    for i in range(count):
        turned[...] = jnp.transpose(refs[i][...])
        for k in range(ndp):
            for z in range(nz):
                for c in range(2):
                    at = ((ids[0] ^ k) * nz + (ids[1] ^ z)) * 2 + (ids[2] ^ c)
                    place = pl.ds(pl.multiple_of(at * block, block), block)
                    dest = refs[-1 - 2 * count + 2 * i + c]
                    dest[(k * nz + z) * block : (k * nz + z + 1) * block] = turned[place, :]


def turn(arrays, before, ids, sizes):
    if not by_blocks(sizes):
        return [[half.T for half in split_cores(array, ids, sizes)] for array in arrays]
    rows = arrays[0].shape[0]
    halves = pl.pallas_call(
        functools.partial(turn_kernel, sizes["dp"], sizes["z"], len(arrays)),
        out_shape=(shape((MODEL_WIDTH // 2, rows), BF16),) * (2 * len(arrays)),
        in_specs=[SMEM] + [VMEM] * len(arrays) + [HBM] * len(before),
        out_specs=(VMEM,) * (2 * len(arrays)),
        scratch_shapes=[pltpu.VMEM((MODEL_WIDTH, rows), BF16)],
        compiler_params=params(60),
        name="turn",
    )(ids, *arrays, *before)
    return [halves[2 * i : 2 * i + 2] for i in range(len(arrays))]


def sum_dp(own, slots, sizes, before=()):
    ndp, rows = sizes["dp"], block_rows(sizes)
    slots = [None, *slots]
    total = own
    for part in finish_sum(slots, start_sum(slots, ndp), ndp, before):
        total = total + part.astype(F32)
    return [total[z * rows : (z + 1) * rows] for z in range(sizes["z"])]


def leaving_z(blocks):
    sent = blocks[1::2] if len(blocks) == 4 else blocks[1:]
    return jnp.concatenate(sent, axis=0).astype(BF16)


def sum_z(blocks, payload, before=()):
    nz, rows = len(blocks), blocks[0].shape[0]
    if nz != 4:
        parts = [payload[z * rows : (z + 1) * rows] for z in range(nz - 1)]
        return [exchange(part, "z", nz, z + 1) for z, part in enumerate(parts)], payload
    near = exchange(payload, "z", nz, 1)
    (near,) = after([near], before) if before else [near]
    passed = (blocks[2] + near[rows:].astype(F32)).astype(BF16)
    return [near[:rows], exchange(passed, "z", nz, 2)], passed


def load_rows(ids, ndp, nz, places, parts, dest, sem):
    if places is None:
        loads = [pltpu.make_async_copy(parts[0], dest, sem.at[0])]
        loads[0].start()
        return loads
    rows = MODEL_WIDTH // (ndp * nz * 2)
    loads = []
    for (k, c, start, count), part in zip(places, parts):
        for z in range(count):
            block = ((ids[0] ^ k) * nz + (ids[1] ^ (start + z))) * 2 + (ids[2] ^ c)
            place = pl.ds(pl.multiple_of(block * rows, rows), rows)
            copy = pltpu.make_async_copy(part.at[z], dest.at[place, :], sem.at[len(loads)])
            loads.append(copy)
    for load in loads:
        load.start()
    return loads


def start_all(pairs, sem):
    copies = [pltpu.make_async_copy(a, b, sem.at[i]) for i, (a, b) in enumerate(pairs)]
    for copy in copies:
        copy.start()
    return copies


def wait_all(copies):
    for copy in copies:
        copy.wait()


def rms_scale(rows):
    return lax.rsqrt(jnp.mean(rows * rows, axis=-1, keepdims=True) + EPS)


def norm_back(normed, row_scale, grad):
    return row_scale * (grad - normed * jnp.mean(grad * normed, axis=-1, keepdims=True))


def swapped(vals):
    return pltpu.roll(vals, HEAD_SIZE // 2, 1)


def head(h):
    return slice(h * HEAD_SIZE, (h + 1) * HEAD_SIZE)


def seen(rows, length):
    q = lax.broadcasted_iota(jnp.int32, (rows, rows), 0)
    s = lax.broadcasted_iota(jnp.int32, (rows, rows), 1)
    return (s <= q) & (s < length)


def attention_probs(query, key, visible):
    scores = jnp.where(visible, nt(query, key) * SCALE, NEG_FILL)
    expon = jnp.exp(scores - jnp.max(scores, axis=-1, keepdims=True))
    return expon / jnp.sum(expon, axis=-1, keepdims=True)


def route_softmax(router_rows, hidden):
    logits = nt(router_rows, hidden)[:EXPERTS]
    expon = jnp.exp(logits - jnp.max(logits, axis=0, keepdims=True))
    return expon / jnp.sum(expon, axis=0, keepdims=True)


def attend_kernel(ndp, nz, places, count, ids, tokens, cosine, sine, *refs):
    parts = refs[:count]
    qkv, mixed, h_one, gains, router, w, sem = refs[-7:]
    rows = tokens.shape[0]
    loads = load_rows(ids, ndp, nz, places, parts, w, sem)
    tok = tokens[...].astype(F32)
    normed = tok * rms_scale(tok)
    for load in loads:
        load.wait()
    extra = jnp.transpose(w[:, QKV:].astype(F32))
    gains[...] = extra[:8]
    router[...] = extra[2 : 2 + ROUTER].astype(BF16)
    h_one[...] = (normed * extra[0:1]).astype(BF16)
    cos, sin = cosine[...], sine[...]
    for t in range(QKV // TILE):
        pre = nn(h_one[...], w[:, t * TILE : (t + 1) * TILE])
        for i in range(TILE // HEAD_SIZE):
            part = pre[:, head(i)]
            at = t * TILE + i * HEAD_SIZE
            if at < QW + KW:
                part = part * cos + swapped(part) * sin
            qkv[:, at : at + HEAD_SIZE] = part.astype(BF16)
    visible = seen(rows, ids[3])
    for h in range(QUERY_HEADS):
        g = h // GROUP
        probs = attention_probs(qkv[:, head(h)], qkv[:, head(QUERY_HEADS + g)], visible)
        values = qkv[:, head(QUERY_HEADS + KEY_VALUE_HEADS + g)]
        mixed[:, head(h)] = nn(probs.astype(BF16), values).astype(BF16)


def attend(ids, tokens, cosine, sine, weights, before, sizes):
    places, parts = weights
    ndp, nz = sizes["dp"], sizes["z"]
    rows = tokens.shape[0]
    return pl.pallas_call(
        functools.partial(attend_kernel, ndp, nz, places, len(parts)),
        out_shape=(
            shape((rows, QKV), BF16),
            shape((rows, QW), BF16),
            shape((rows, MODEL_WIDTH), BF16),
            shape((8, MODEL_WIDTH), F32),
            shape((ROUTER, MODEL_WIDTH), BF16),
        ),
        in_specs=[SMEM, VMEM, VMEM, VMEM] + [HBM] * (len(parts) + len(before)),
        out_specs=(VMEM,) * 5,
        scratch_shapes=[
            pltpu.VMEM((MODEL_WIDTH, FIRST), BF16),
            pltpu.SemaphoreType.DMA((2 * ndp * nz,)),
        ],
        compiler_params=params(60),
        cost_estimate=cost(2 * rows * MODEL_WIDTH * QKV, 10 * MIB, 12 * rows * rows),
        name="attend",
    )(ids, tokens, cosine, sine, *parts, *before)


def project_kernel(ndp, nz, places, ids, tokens, mixed, gains, *refs):
    *parts, residual, top, low, w, sem = refs
    loads = load_rows(ids, ndp, nz, places, parts, w, sem)
    for load in loads:
        load.wait()
    for t in range(MODEL_WIDTH // TILE):
        lane = slice(t * TILE, (t + 1) * TILE)
        residual[:, lane] = tokens[:, lane].astype(F32) + nn(mixed[...], w[:, lane])
    whole = residual[...]
    h_two = (whole * rms_scale(whole) * gains[1:2]).astype(BF16)
    half = top.shape[0]
    top[...], low[...] = h_two[:half], h_two[half:]


def project(ids, tokens, mixed, gains, weights, sizes):
    places, parts = weights
    ndp, nz = sizes["dp"], sizes["z"]
    rows = tokens.shape[0]
    return pl.pallas_call(
        functools.partial(project_kernel, ndp, nz, places),
        out_shape=(shape((rows, MODEL_WIDTH), F32),)
        + (shape((rows // 2, MODEL_WIDTH), BF16),) * 2,
        in_specs=[SMEM, VMEM, VMEM, VMEM] + [HBM] * len(parts),
        out_specs=(VMEM,) * 3,
        scratch_shapes=[
            pltpu.VMEM((QW, MODEL_WIDTH), BF16),
            pltpu.SemaphoreType.DMA((2 * ndp * nz,)),
        ],
        compiler_params=params(60),
        cost_estimate=cost(2 * rows * MODEL_WIDTH * QW, 8 * MIB),
        name="project",
    )(ids, tokens, mixed, gains, *parts)


def expert_kernel(ndp, rows, width, index, last, near, far, unread, *refs):
    it = iter(refs)
    take = lambda n: [next(it) for _ in range(n)]
    (expert_ref, router_ref) = take(2)
    prev_gates = take(index)
    hid_in, cot_in = take(len(near)), take(len(far))
    (w_in,) = take(1)
    prev_in = take(2) if index else []
    take(unread)
    out_hbm, back_hbm = take(2 * ndp - 1 if last else 1), take(2 * ndp if last else 1)
    gates_ref, terms_hbm = take(2)
    hid, cot, w, x, d, ge, inner, dg, du, pick, pick_t, slot_gate, slot_dot = take(13)
    (terms_buf,) = take(1)
    prev = take(2) if index else []
    in_sem, out_sem = take(2)
    depth = MODEL_WIDTH
    tiles = depth // TILE

    loads = {}

    def load(name, source, dest):
        copy = pltpu.make_async_copy(source, dest, in_sem.at[len(loads)])
        copy.start()
        loads[name] = copy

    for i, (k, start, count) in enumerate(near):
        load(("hid", i), hid_in[i], hid.at[k, pl.ds(start, count), :])
    for i, (k, start, count) in enumerate(far):
        load(("cot", i), cot_in[i], cot.at[k, pl.ds(start, count), :])
    load("w", w_in, w)
    for i in range(len(prev)):
        load(("prev", i), prev_in[i], prev[i])

    expert = expert_ref[0]
    which = lax.broadcasted_iota(jnp.int32, (EXPERTS, rows), 0) == expert
    earlier = (
        (
            lax.broadcasted_iota(jnp.int32, (rows, rows), 0)
            < lax.broadcasted_iota(jnp.int32, (rows, rows), 1)
        )
        .astype(F32)
        .astype(BF16)
    )
    slot = lax.broadcasted_iota(jnp.int32, (CAP, rows), 0).astype(F32)
    for s in range(ndp):
        for i, piece in enumerate(near):
            if piece[0] == s:
                loads["hid", i].wait()
        for i, piece in enumerate(far):
            if piece[0] == s:
                loads["cot", i].wait()
        hidden = hid[s]
        probs = route_softmax(router_ref[...], hidden)
        named = cot[s, rows : rows + NOTE, :rows]
        place = nn(named, earlier)[:EXPERTS]
        named = named[:EXPERTS].astype(F32)
        named_row = jnp.sum(jnp.where(which, named, 0.0), axis=0, keepdims=True)
        gate_row = jnp.sum(jnp.where(which, probs, 0.0), axis=0, keepdims=True)
        place_row = jnp.sum(jnp.where(which, place, 0.0), axis=0, keepdims=True)
        chosen = jnp.where((slot == place_row) & (named_row > 0.5), 1.0, 0.0)
        pick[s] = chosen.astype(BF16)
        pick_t[s] = jnp.transpose(chosen).astype(BF16)
        at = pl.ds(s * CAP, CAP)
        gate = jnp.sum(chosen * gate_row, axis=1, keepdims=True)
        slot_gate[at, :] = jnp.broadcast_to(gate, (CAP, 128))
        x[at, :] = nn(pick[s], hidden).astype(BF16)
        grads = nn(pick[s], cot[s, :rows])
        d[at, :] = grads.astype(BF16)
        ge[at, :] = (gate * grads).astype(BF16)
    loads["w"].wait()

    def hidden_units(t, carry):
        at = pl.multiple_of(t * TILE, TILE)
        gate_pre = nn(x[...], w[:, pl.ds(at, TILE)])
        up_pre = nn(x[...], w[:, pl.ds(width + at, TILE)])
        grad_inner = nn(ge[...], w[:, pl.ds(2 * width + at, TILE)])
        sig = 1.0 / (1.0 + jnp.exp(-gate_pre))
        act = gate_pre * sig
        inner[:, pl.ds(at, TILE)] = (act * up_pre).astype(BF16)
        dg[:, pl.ds(at, TILE)] = (
            grad_inner * up_pre * sig * (1.0 + gate_pre * (1.0 - sig))
        ).astype(BF16)
        du[:, pl.ds(at, TILE)] = (grad_inner * act).astype(BF16)
        return carry

    lax.fori_loop(0, width // TILE, hidden_units, 0)
    slot_dot[...] = jnp.zeros_like(slot_dot)
    for i in range(len(prev)):
        loads["prev", i].wait()

    noted = (rows + NOTE) // 2

    def stores(t):
        lane = pl.ds(pl.multiple_of(t * TILE, TILE), TILE)
        copies = [(terms_buf.at[lane, :], terms_hbm.at[lane, :])]
        if not last:
            body = pl.ds(0, rows)
            copies.append((hid.at[:, :, lane], out_hbm[0].at[:, :, lane]))
            copies.append((cot.at[:, body, lane], back_hbm[0].at[:, body, lane]))
        else:
            copies.append((hid.at[0, :, lane], out_hbm[0].at[:, lane]))
            for i in range(2, 2 * ndp):
                first = pl.ds(i % 2 * (rows // 2), rows // 2)
                copies.append((hid.at[i // 2, first, lane], out_hbm[i - 1].at[:, lane]))
            for i in range(2 * ndp):
                body = pl.ds(0, noted if i % 2 == 0 else rows - noted)
                taken = pl.ds(i % 2 * noted, noted if i % 2 == 0 else rows - noted)
                copies.append((cot.at[i // 2, taken, lane], back_hbm[i].at[body, lane]))
        return [
            pltpu.make_async_copy(source, dest, out_sem.at[i, t])
            for i, (source, dest) in enumerate(copies)
        ]

    def features(t, carry):
        lane = pl.ds(pl.multiple_of(t * TILE, TILE), TILE)
        result = nt(inner[...], w[lane, pl.ds(2 * width, width)]).astype(BF16).astype(F32)
        partial = jnp.sum(result * d[:, lane].astype(F32), axis=1, keepdims=True)
        slot_dot[...] += jnp.broadcast_to(partial, slot_dot.shape)
        gated = (slot_gate[:, :1] * result).astype(BF16)
        grad_in = (
            nt(dg[...], w[lane, pl.ds(0, width)]) + nt(du[...], w[lane, pl.ds(width, width)])
        ).astype(BF16)
        for s in range(ndp):
            part = slice(s * CAP, (s + 1) * CAP)
            sent = nn(pick_t[s], gated[part])
            back = nn(pick_t[s], grad_in[part])
            if prev:
                sent = sent + prev[0][s, :, lane].astype(F32)
                back = back + prev[1][s, :rows, lane].astype(F32)
            hid[s, :, lane] = sent.astype(BF16)
            cot[s, :rows, lane] = back.astype(BF16)
        x_t = jnp.transpose(x[:, lane])
        terms_buf[lane, pl.ds(0, width)] = nn(x_t, dg[...]).astype(BF16)
        terms_buf[lane, pl.ds(width, width)] = nn(x_t, du[...]).astype(BF16)
        ge_t = jnp.transpose(ge[:, lane])
        terms_buf[lane, pl.ds(2 * width, width)] = nn(ge_t, inner[...]).astype(BF16)
        for store in stores(t):
            store.start()
        return carry

    lax.fori_loop(0, tiles, features, 0)
    line = lax.broadcasted_iota(jnp.int32, (NOTE, 3 * rows), 0)
    notes = []
    for s in range(ndp):
        part = slice(s * CAP, (s + 1) * CAP)
        own = jnp.sum(pick[s].astype(F32) * slot_dot[part, :1], axis=0, keepdims=True)
        gates_ref[s] = own
        if not last:
            continue
        note = jnp.zeros((NOTE, 3 * rows), F32)
        for j, row in enumerate([p[s] for p in prev_gates] + [own]):
            high = row.astype(BF16).astype(F32)
            middle = (row - high).astype(BF16).astype(F32)
            low = row - high - middle
            at = expert - index + j
            note = jnp.where(line == at, jnp.concatenate([high, middle, low], axis=1), note)
        cot[s, rows : rows + NOTE, : 3 * rows] = note.astype(BF16)
        notes.append(
            pltpu.make_async_copy(
                cot.at[s, pl.ds(rows, NOTE), :],
                back_hbm[2 * s + 1].at[pl.ds(rows - noted, NOTE), :],
                out_sem.at[4 * ndp + 1, s],
            )
        )
        notes[-1].start()
    for t in range(tiles):
        for store in stores(t):
            store.wait()
    for note in notes:
        note.wait()


def run_expert(index, last, expert, router, hidden, grads, w_all, prev, prev_gates, ndp, before):
    rows = 2 * hidden[0][2].shape[0]
    near, far = (tuple((k, at, p.shape[0]) for k, at, p in group) for group in (hidden, grads))
    width = w_all.shape[1] // 3
    slots = ndp * CAP
    depth = MODEL_WIDTH
    tiles = depth // TILE
    scratch = [
        pltpu.VMEM((ndp, rows, depth), BF16),
        pltpu.VMEM((ndp, rows + NOTE, depth), BF16),
        pltpu.VMEM((depth, 3 * width), BF16),
        pltpu.VMEM((slots, depth), BF16),
        pltpu.VMEM((slots, depth), BF16),
        pltpu.VMEM((slots, depth), BF16),
        pltpu.VMEM((slots, width), BF16),
        pltpu.VMEM((slots, width), BF16),
        pltpu.VMEM((slots, width), BF16),
        pltpu.VMEM((ndp, CAP, rows), BF16),
        pltpu.VMEM((ndp, rows, CAP), BF16),
        pltpu.VMEM((slots, 128), F32),
        pltpu.VMEM((slots, 128), F32),
        pltpu.VMEM((depth, 3 * width), BF16),
    ]
    if index:
        scratch += [
            pltpu.VMEM((ndp, rows, depth), BF16),
            pltpu.VMEM((ndp, rows + NOTE, depth), BF16),
        ]
    scratch += [
        pltpu.SemaphoreType.DMA((len(near) + len(far) + 3,)),
        pltpu.SemaphoreType.DMA((4 * ndp + 2, max(tiles, ndp))),
    ]
    sent = [shape((ndp, rows, depth), BF16), shape((ndp, rows + NOTE, depth), BF16)]
    if last:
        sent = [shape((rows, depth), BF16)]
        sent += [shape((rows // 2, depth), BF16)] * (2 * ndp - 2)
        sent += [shape(((rows + NOTE) // 2, depth), BF16)] * (2 * ndp)
    flops = 2 * slots * depth * width * 9 + 8 * ndp * CAP * rows * depth
    return pl.pallas_call(
        functools.partial(
            expert_kernel, ndp, rows, width, index, last, near, far, len(before)
        ),
        out_shape=(
            *sent,
            shape((ndp, 1, rows), F32),
            shape((depth, 3 * width), BF16),
        ),
        in_specs=[SMEM, VMEM]
        + [VMEM] * len(prev_gates)
        + [HBM] * (len(near) + len(far) + 1 + len(prev) + len(before)),
        out_specs=(HBM,) * len(sent) + (VMEM, HBM),
        scratch_shapes=scratch,
        compiler_params=params(60),
        cost_estimate=cost(flops, 40 * MIB, slots * width),
        name="expert",
    )(
        expert,
        router,
        *prev_gates,
        *(piece for *_, piece in hidden),
        *(piece for *_, piece in grads),
        w_all,
        *prev,
        *before,
    )


def back_kernel(ndp, nz, places, count, given, unread, ids, gains, router, cosine, sine, *refs):
    refs = list(refs)
    take = lambda n: [refs.pop(0) for _ in range(n)]
    data, backs, parts = take(5), take(given), take(count)
    take(unread)
    out_resid, out_attn, out_pre, notes = take(4)
    residual, top, low, grads, qkv = held = take(5)
    got = take(given)
    w, grad_mixed, grad_resid, grad_attn, grad_pre, sem, data_sem, out_sem = refs
    rows = residual.shape[0]
    fetched = start_all(list(zip(backs + data[1:3] + data[:1] + data[3:], got + held[1:3] + held[:1] + held[3:])), data_sem)
    loads = load_rows(ids, ndp, nz, places, parts, w, sem)
    wait_all(fetched[:given])
    whole = jnp.concatenate([got[0][...], got[1][...]], axis=0).astype(F32)
    for part in got[2:]:
        whole = whole + part[...].astype(F32)
    grad_h = whole[:rows]
    note = whole[rows : rows + EXPERTS, : 3 * rows]
    grad_route = note[:, :rows] + note[:, rows : 2 * rows] + note[:, 2 * rows :]
    wait_all(fetched[given : given + 4])
    hidden = jnp.concatenate([top[...], low[...]], axis=0)
    probs = route_softmax(router[...], hidden)
    grad_logits = probs * (grad_route - jnp.sum(probs * grad_route, axis=0, keepdims=True))
    grad_logits = jnp.concatenate([grad_logits, jnp.zeros_like(grad_logits)], axis=0)
    grad_logits = grad_logits.astype(BF16)
    grad_h = grad_h + tn(grad_logits, router[...])
    res = residual[...]
    scale = rms_scale(res)
    normed = res * scale
    notes[0:8] = jnp.broadcast_to(
        jnp.sum(normed * grad_h, axis=0, keepdims=True), (8, MODEL_WIDTH)
    )
    notes[8:16] = nn(grad_logits, hidden)[:EXPERTS]
    live = lax.broadcasted_iota(jnp.int32, (rows, 1), 0) < ids[3]
    final = jnp.where(live, grads[...].astype(F32), 0.0)
    total = final + norm_back(normed, scale, grad_h * gains[1:2])
    grad_resid[...] = total
    grad_attn[...] = total.astype(BF16)
    stores = start_all([(grad_attn, out_attn), (grad_resid, out_resid)], out_sem)
    wait_all(loads)
    for t in range(QW // TILE):
        lane = slice(t * TILE, (t + 1) * TILE)
        grad_mixed[:, lane] = nt(grad_attn[...], w[lane, :]).astype(BF16)
    wait_all(fetched[given + 4 :])
    source = lax.broadcasted_iota(jnp.int32, (rows, rows), 0)
    visible = (source <= lax.broadcasted_iota(jnp.int32, (rows, rows), 1)) & (source < ids[3])
    cos, sin = cosine[...], sine[...]
    for g in range(KEY_VALUE_HEADS):
        key = qkv[:, head(QUERY_HEADS + g)]
        value = qkv[:, head(QUERY_HEADS + KEY_VALUE_HEADS + g)]
        grad_key = jnp.zeros((rows, HEAD_SIZE), F32)
        grad_value = jnp.zeros((rows, HEAD_SIZE), F32)
        for h in range(g * GROUP, (g + 1) * GROUP):
            query, grad = qkv[:, head(h)], grad_mixed[:, head(h)]
            scores = jnp.where(visible, nt(key, query) * SCALE, NEG_FILL)
            expon = jnp.exp(scores - jnp.max(scores, axis=0, keepdims=True))
            probs = expon / jnp.sum(expon, axis=0, keepdims=True)
            grad_probs = nt(value, grad)
            grad_value = grad_value + nn(probs.astype(BF16), grad)
            row_dot = jnp.sum(probs * grad_probs, axis=0, keepdims=True)
            grad_scores = (probs * (grad_probs - row_dot)).astype(BF16)
            grad_query = tn(grad_scores, key) * SCALE
            grad_key = grad_key + nn(grad_scores, query)
            grad_pre[:, head(h)] = (grad_query * cos - swapped(grad_query) * sin).astype(BF16)
        grad_key = grad_key * SCALE
        grad_pre[:, head(QUERY_HEADS + g)] = (
            grad_key * cos - swapped(grad_key) * sin
        ).astype(BF16)
        grad_pre[:, head(QUERY_HEADS + KEY_VALUE_HEADS + g)] = grad_value.astype(BF16)
    last = pltpu.make_async_copy(grad_pre, out_pre, out_sem.at[2])
    last.start()
    wait_all(stores + [last])


def back(
    ids, residual, h_two, grads, gains, router, cosine, sine, qkv, backs, weights, before, sizes
):
    ndp, nz = sizes["dp"], sizes["z"]
    places, parts = weights
    rows = residual.shape[0]
    data = [residual, *h_two, grads, qkv]
    made = [
        shape((rows, MODEL_WIDTH), F32),
        shape((rows, MODEL_WIDTH), BF16),
        shape((rows, QKV), BF16),
    ]
    room = lambda array: pltpu.VMEM(array.shape, array.dtype)
    return pl.pallas_call(
        functools.partial(
            back_kernel, ndp, nz, places, len(parts), len(backs), len(before)
        ),
        out_shape=(*made, shape((16, MODEL_WIDTH), F32)),
        in_specs=[SMEM]
        + [VMEM] * 4
        + [HBM] * (len(data) + len(backs) + len(parts) + len(before)),
        out_specs=(HBM, HBM, HBM, VMEM),
        scratch_shapes=[
            *(room(array) for array in data + backs),
            pltpu.VMEM((QW, MODEL_WIDTH), BF16),
            pltpu.VMEM((rows, QW), BF16),
            *(room(array) for array in made),
            pltpu.SemaphoreType.DMA((2 * ndp * nz,)),
            pltpu.SemaphoreType.DMA((len(data) + len(backs),)),
            pltpu.SemaphoreType.DMA((3,)),
        ],
        compiler_params=params(60),
        cost_estimate=cost(3 * rows * MODEL_WIDTH * QW, 16 * MIB, 12 * rows * rows),
        name="back",
    )(ids, gains, router, cosine, sine, *data, *backs, *parts, *before)


def tokens_back_kernel(ndp, nz, places, count, ids, tokens, gains, grad_pre, grad_resid, *refs):
    parts = refs[:count]
    grad_tokens, w, sem = refs[-3:]
    loads = load_rows(ids, ndp, nz, places, parts, w, sem)
    tok = tokens[...].astype(F32)
    scale = rms_scale(tok)
    normed = tok * scale
    for load in loads:
        load.wait()
    for t in range(MODEL_WIDTH // TILE):
        lane = slice(t * TILE, (t + 1) * TILE)
        grad_tokens[:, lane] = nt(grad_pre[...], w[lane, :QKV])
    grad_h = grad_tokens[...]
    grad_tokens[...] = grad_resid[...] + norm_back(normed, scale, grad_h * gains[0:1])


def tokens_back(ids, tokens, gains, grad_pre, grad_resid, weights, before, sizes):
    ndp, nz = sizes["dp"], sizes["z"]
    places, parts = weights
    rows = tokens.shape[0]
    return pl.pallas_call(
        functools.partial(tokens_back_kernel, ndp, nz, places, len(parts)),
        out_shape=shape((rows, MODEL_WIDTH), F32),
        in_specs=[SMEM] + [VMEM] * 4 + [HBM] * (len(parts) + len(before)),
        out_specs=VMEM,
        scratch_shapes=[
            pltpu.VMEM((MODEL_WIDTH, FIRST), BF16),
            pltpu.SemaphoreType.DMA((2 * ndp * nz,)),
        ],
        compiler_params=params(60),
        cost_estimate=cost(2 * rows * MODEL_WIDTH * QKV, 12 * MIB),
        name="tokens_back",
    )(ids, tokens, gains, grad_pre, grad_resid, *parts, *before)


def terms_kernel(ndp, nz, noted, unread, ids, *refs):
    refs = list(refs)
    take = lambda n: [refs.pop(0) for _ in range(n)]
    notes, given = take(2 if noted else 0), take(4)
    take(unread)
    count = 2 * ndp - 1
    outs, held, dests = take(count), take(4), take(count)
    note_rows, in_sem, out_sem = refs
    wait_all(start_all(list(zip(given, held)), in_sem))
    left = jnp.concatenate([held[0][...], held[1][...]], axis=1)
    right = jnp.concatenate([held[2][...], held[3][...]], axis=0)
    slot = MODEL_WIDTH // (2 * ndp)
    stores = []

    def put(lane, value):
        dests[0][:, lane] = value[:slot]
        for i in range(1, count):
            at = slot + (i - 1) * (slot // 2)
            dests[i][:, lane] = value[at : at + slot // 2].astype(BF16)
        pairs = [(dests[i].at[:, lane], outs[i].at[:, lane]) for i in range(count)]
        stores.extend(start_all(pairs, out_sem.at[len(stores) // count]))

    if noted:
        note = notes[0][...] + notes[1][...]
        block = jnp.concatenate([note, jnp.zeros((PAD - 16, note.shape[1]), F32)], axis=0)
        block = jnp.transpose(block)
    if noted == 1:
        note_rows[...] = block
        rows = MODEL_WIDTH // (2 * ndp * nz)
        taken = []
        for k in range(ndp):
            for z in range(nz):
                at = ((ids[0] ^ k) * nz + (ids[1] ^ z)) * 2 + ids[2]
                taken.append(note_rows[pl.ds(pl.multiple_of(at * rows, rows), rows), :])
        block = jnp.concatenate(taken, axis=0)
    if noted:
        put(slice(right.shape[1], right.shape[1] + PAD), block)
    for t in range(right.shape[1] // TILE):
        lane = slice(t * TILE, (t + 1) * TILE)
        put(lane, nn(left, right[:, lane]))
    wait_all(stores)


def weight_terms(ids, left, right, notes, before, sizes):
    ndp, nz = sizes["dp"], sizes["z"]
    slot = MODEL_WIDTH // (2 * ndp)
    columns = right[0].shape[1] + (PAD if notes else 0)
    noted = 0 if not notes else 1 if notes[0].shape[1] == MODEL_WIDTH else 2
    made = [shape((slot, columns), F32)] + [shape((slot // 2, columns), BF16)] * (2 * ndp - 2)
    room = lambda array: pltpu.VMEM(array.shape, array.dtype)
    arrays = [*left, *right]
    found = pl.pallas_call(
        functools.partial(terms_kernel, ndp, nz, noted, len(before)),
        out_shape=tuple(made),
        in_specs=[SMEM] + [VMEM] * len(notes) + [HBM] * (4 + len(before)),
        out_specs=(HBM,) * len(made),
        scratch_shapes=[
            *(room(array) for array in arrays + made),
            pltpu.VMEM((MODEL_WIDTH, PAD), F32),
            pltpu.SemaphoreType.DMA((4,)),
            pltpu.SemaphoreType.DMA((columns // TILE + 1, len(made))),
        ],
        compiler_params=params(60),
        cost_estimate=cost(2 * MODEL_WIDTH * left[0].shape[1] * columns, 5 * MIB),
        name="weight_terms",
    )(ids, *notes, *arrays, *before)
    return found[0], [tuple(found[i : i + 2]) for i in range(1, len(found), 2)]


def settle_kernel(count, *refs):
    own, got = refs[0], refs[1 : 1 + count]
    mats = refs[1 + count : 4 + count]
    gain = refs[4 + count]
    outs, gains, router = refs[-5:-2], refs[-2], refs[-1]
    total = own[...]
    for part in got:
        total = total + part[...].astype(F32)
    dot, at = jnp.zeros((total.shape[0], 1), F32), 0
    for mat, out in zip(mats, outs):
        width = mat.shape[1]
        part = total[:, at : at + width]
        out[...] = part
        dot = dot + jnp.sum(part * mat[...].astype(F32), axis=1, keepdims=True)
        at += width
    small = total[:, at:]
    router[...] = small[:, 8 : 8 + EXPERTS]
    lane = lax.broadcasted_iota(jnp.int32, small.shape, 1)
    turned = jnp.transpose(jnp.where(lane == 1, dot, small))
    gains[0:1] = turned[1:2] / gain[...]
    gains[1:2] = turned[0:1]


def settle(own, got, mats, gain, before):
    rows = own.shape[0]
    return pl.pallas_call(
        functools.partial(settle_kernel, len(got)),
        out_shape=tuple(shape(mat.shape, F32) for mat in mats)
        + (shape((2, rows), F32), shape((rows, EXPERTS), F32)),
        in_specs=[VMEM] * (1 + len(got) + 4) + [HBM] * len(before),
        out_specs=(VMEM,) * 5,
        compiler_params=params(60),
        name="settle",
    )(own, *got, *mats, gain, *before)


def rope_tables(rows):
    half = HEAD_SIZE // 2
    position = jnp.arange(rows).astype(F32)
    inverse = ROPE_BASE ** (-jnp.arange(half).astype(F32) / half)
    angles = position[:, None] * inverse[None, :]
    cosine, sine = jnp.cos(angles), jnp.sin(angles)
    return jnp.concatenate([cosine, cosine], axis=1), jnp.concatenate([-sine, sine], axis=1)


def per_device(
    sizes,
    tokens,
    lengths,
    routes,
    cotangent,
    gain_one,
    w_query,
    key_matrix,
    value_matrix,
    w_out,
    gain_two,
    w_router,
    w_gate,
    w_up,
    w_down,
):
    ndp = sizes["dp"]
    rows = tokens.shape[0]
    local, _, width = w_gate.shape
    me_dp = lax.axis_index("dp")
    length = lengths[0]
    ids = jnp.stack([me_dp, lax.axis_index("z"), lax.axis_index("core"), length]).astype(jnp.int32)
    live = (jnp.arange(rows) < length)[:, None]
    expert_ids = jnp.arange(EXPERTS, dtype=jnp.int32)

    extra = jnp.concatenate([gain_one[:, None], gain_two[:, None], w_router], axis=1)
    extra = jnp.pad(extra, ((0, 0), (0, PAD - extra.shape[1])))
    first = jnp.concatenate([w_query, key_matrix, value_matrix, extra], axis=1)
    named = jnp.any(routes[None, :, :] == expert_ids[:, None, None], axis=2).astype(BF16)
    named = jnp.pad(named, ((0, NOTE - EXPERTS), (0, MODEL_WIDTH - rows)))
    grad_low = jnp.where(live, cotangent, jnp.zeros_like(cotangent))
    grad_low = jnp.concatenate([grad_low, named], axis=0)
    grad_near = start_dp(grad_low, ndp)

    nz = sizes["z"]
    first_z = [first] + [exchange(first, "z", nz, k) for k in range(1, nz)]
    second_z = [w_out] + [exchange(w_out, "z", nz, k) for k in range(1, nz)]
    first_block = stack_after(first_z, grad_near)
    first_near = start_dp(first_block, ndp)
    first_dp = pass_on(first_block, first_near, ndp, second_z[1:])
    packed = after([pack(j, (w_gate, w_up, w_down)) for j in range(local)], first_z[1:] + grad_near)
    expert_mats = [lax.all_gather(p, ("z", "core"), axis=0, tiled=True) for p in packed]
    second_block = stack_after(second_z, [piece for *_, piece in first_dp[1:3]])
    second_dp = gather_direct(second_block, ndp)

    cosine, sine = rope_tables(rows)
    weights_in = gather_rows(first, first_dp, ids, sizes)
    qkv, mixed, h_one, gains, router = attend(ids, tokens, cosine, sine, weights_in, [], sizes)
    second_far = after([piece for *_, piece in second_dp[1:]], [mixed])
    second_dp = [(k, 0, piece) for k, piece in enumerate([second_block, *second_far])]
    grad_far = pass_on(grad_low, grad_near, ndp, second_far)
    weights_out = gather_rows(w_out, second_dp, ids, sizes)
    residual, *h_two = project(ids, tokens, mixed, gains, weights_out, sizes)
    hidden = gather_halves(h_two, ndp)
    turned = turn([mixed, h_one], [hidden[2][2]], ids, sizes)
    mixed, h_one = ([mine, exchange(other, "core", 2, 1)] for mine, other in turned)

    prev, gate_grads, sums = (), [], []
    for j in range(local):
        expert = (me_dp * local + j).astype(jnp.int32).reshape(1)
        *prev, grad_gate, terms = run_expert(
            j,
            j == local - 1,
            expert,
            router,
            hidden,
            grad_far,
            expert_mats[j],
            prev,
            gate_grads,
            ndp,
            [*mixed, *h_one],
        )
        gate_grads.append(grad_gate)
        sums.append(lax.psum_scatter(terms, ("z", "core"), scatter_dimension=0, tiled=True))
    count = 2 * ndp - 1
    outs, backs = prev[:count], prev[count:]
    pairs = [tuple(backs[2 * k : 2 * k + 2]) for k in range(ndp)]
    backs = [*pairs[0], *finish_sum(pairs, start_sum(pairs, ndp), ndp)]
    out_slots = [None] + [tuple(outs[i : i + 2]) for i in range(1, count, 2)]
    out_past = start_sum(out_slots, ndp)

    grad_resid, grad_attn, grad_pre, notes = back(
        ids,
        residual,
        h_two,
        cotangent,
        gains,
        router,
        cosine,
        sine,
        qkv,
        backs,
        weights_out,
        [],
        sizes,
    )
    if not by_blocks(sizes):
        notes = split_cores(notes, ids, sizes)
        notes = notes[0], exchange(notes[1], "core", 2, 1)
    else:
        notes = notes, exchange(notes, "core", 2, 1)
    grad_attn = grad_attn, exchange(grad_attn, "core", 2, 1)
    grad_pre = grad_pre, exchange(grad_pre, "core", 2, 1)
    out_terms = weight_terms(ids, mixed, grad_attn, (), grad_pre[1:], sizes)
    in_terms = weight_terms(
        ids, h_one, grad_pre, notes, sums[:-1] + [out_terms[0]] + out_past, sizes
    )
    out_blocks = sum_dp(*out_terms, sizes, in_terms[:1])
    in_blocks = sum_dp(*in_terms, sizes)
    out_payload, in_payload = leaving_z(out_blocks), leaving_z(in_blocks)
    late, _ = sum_z(out_blocks, out_payload, [in_payload])
    got, leaving = sum_z(in_blocks, in_payload)
    grad_tokens = tokens_back(
        ids, tokens, gains, grad_pre[0], grad_resid, weights_in, [in_payload], sizes
    )
    block = residual + outs[0].astype(F32)
    for part in finish_sum(out_slots, out_past, ndp, [in_payload]):
        block = block + part.astype(F32)
    block_out = block.astype(BF16)
    gain = gain_one.astype(F32)[None]
    *grad_in, grad_gains, grad_router = settle(
        in_blocks[0], got, (w_query, key_matrix, value_matrix), gain, [block_out]
    )
    expert_sums = finish_after(sums, [leaving])
    grad_out = out_blocks[0] + sum(part.astype(F32) for part in late)
    return (
        block_out,
        grad_tokens,
        grad_gains[0],
        *grad_in,
        grad_out,
        grad_gains[1],
        grad_router,
        *expert_sums,
    )


def solution(mesh):
    ndp, nf = mesh.shape["dp"], mesh.shape["fsdp"]
    sizes = {"dp": ndp, "z": nf // 2, "core": 2}
    split = Mesh(mesh.devices.reshape(ndp, nf // 2, 2), ("dp", "z", "core"))
    every = ("dp", "z", "core")
    rows = P(every, None)
    vector = P(every)
    expert = P("dp", ("z", "core"), None)

    def run(*args):
        return per_device(sizes, *args)

    return jax.shard_map(
        run,
        mesh=split,
        in_specs=(rows, vector, rows, rows, vector, rows, rows, rows, rows, vector, rows)
        + (expert,) * 3,
        out_specs=(rows, rows, vector, rows, rows, rows, rows, vector, rows) + (expert,) * 3,
        check_vma=False,
    )
```

```python
import functools

import jax
import jax.numpy as jnp
from jax import lax
from jax.experimental import pallas as pl
from jax.experimental.pallas import tpu as pltpu
from jax.sharding import Mesh
from jax.sharding import PartitionSpec as P

MODEL_WIDTH = 1536
QUERY_HEADS = 12
KEY_VALUE_HEADS = 2
HEAD_SIZE = 128
EXPERTS = 8
CAP = 160
GROUP = QUERY_HEADS // KEY_VALUE_HEADS
QW = QUERY_HEADS * HEAD_SIZE
KW = KEY_VALUE_HEADS * HEAD_SIZE
QKV = QW + 2 * KW
PAD = 128
FIRST = QKV + PAD
NOTE = 32
ROUTER = 16
EPS = 1e-06
ROPE_BASE = 1500000.0
NEG_FILL = -1e30
SCALE = HEAD_SIZE ** (-0.5)
F32 = jnp.float32
BF16 = jnp.bfloat16
TILE = 256
MIB = 1024 * 1024
HBM = pl.BlockSpec(memory_space=pltpu.HBM)
VMEM = pl.BlockSpec(memory_space=pltpu.VMEM)
SMEM = pl.BlockSpec(memory_space=pltpu.SMEM)


def nn(a, b):
    return lax.dot_general(a, b, (((1,), (0,)), ((), ())), preferred_element_type=F32)


def nt(a, b):
    return lax.dot_general(a, b, (((1,), (1,)), ((), ())), preferred_element_type=F32)


def tn(a, b):
    return lax.dot_general(a, b, (((0,), (0,)), ((), ())), preferred_element_type=F32)


def shape(dims, dtype):
    return jax.ShapeDtypeStruct(dims, dtype)


def params(mib):
    return pltpu.CompilerParams(vmem_limit_bytes=mib * MIB)


def cost(flops, data, special=0):
    return pl.CostEstimate(flops=flops, bytes_accessed=data, transcendentals=special)


def exchange(block, axis, size, step):
    return lax.ppermute(block, axis, [(i, i ^ step) for i in range(size)])


def start_dp(block, ndp):
    return [exchange(block, "dp", ndp, k) for k in ((1, 2) if ndp == 4 else range(1, ndp))]


def pass_on(block, near, ndp, before=()):
    if ndp != 4:
        return [(k, 0, piece) for k, piece in enumerate([block] + near)]
    side, up = after(near, before) if before else near
    half = block.shape[0] // 2
    return [
        (0, 0, block),
        (1, 0, side),
        (2, 0, up),
        (3, 0, exchange(side[:half], "dp", ndp, 2)),
        (3, half, exchange(up[half:], "dp", ndp, 1)),
    ]


def gather_direct(block, ndp):
    return [(k, 0, exchange(block, "dp", ndp, k) if k else block) for k in range(ndp)]


def gather_halves(halves, ndp):
    top, low = halves
    at = top.shape[0]
    if ndp != 4:
        return [
            (k, i * at, exchange(half, "dp", ndp, k) if k else half)
            for k in range(ndp)
            for i, half in enumerate(halves)
        ]
    side_top, up_low = exchange(top, "dp", ndp, 1), exchange(low, "dp", ndp, 2)
    side_low, up_top = exchange(low, "dp", ndp, 1), exchange(top, "dp", ndp, 2)
    return [
        (0, 0, top),
        (0, at, low),
        (1, 0, side_top),
        (2, at, up_low),
        (1, at, side_low),
        (2, 0, up_top),
        (3, 0, exchange(side_top, "dp", ndp, 2)),
        (3, at, exchange(up_low, "dp", ndp, 1)),
    ]


def start_sum(slots, ndp):
    if ndp != 4:
        return []
    return [exchange(slots[3][0], "dp", ndp, 1), exchange(slots[3][1], "dp", ndp, 2)]


def finish_sum(slots, past, ndp, before=()):
    if ndp != 4:
        sent = [jnp.concatenate(slot, axis=0) for slot in slots[1:]]
    else:
        past = after(past, before) if before else past
        add = lambda a, b: (a.astype(F32) + b.astype(F32)).astype(BF16)
        sent = [
            jnp.concatenate([slots[1][0], add(slots[1][1], past[1])], axis=0),
            jnp.concatenate([add(slots[2][0], past[0]), slots[2][1]], axis=0),
        ]
    return [exchange(part, "dp", ndp, k + 1) for k, part in enumerate(sent)]


def both_cores(pieces):
    return [
        (k, c, start, exchange(piece, "core", 2, 1) if c else piece)
        for k, start, piece in pieces
        for c in range(2)
    ]


def stack_kernel(count, *refs):
    for i in range(count):
        refs[-1][i] = refs[i][...]


def stack_after(parts, before):
    dims = (len(parts),) + parts[0].shape
    return pl.pallas_call(
        functools.partial(stack_kernel, len(parts)),
        out_shape=shape(dims, parts[0].dtype),
        in_specs=[VMEM] * len(parts) + [HBM] * len(before),
        out_specs=VMEM,
        compiler_params=params(60),
        cost_estimate=cost(0, 4 * dims[0] * dims[1] * dims[2]),
        name="stack",
    )(*parts, *before)


def pack_kernel(index, *refs):
    width = refs[0].shape[2]
    for i in range(3):
        refs[-1][:, i * width : (i + 1) * width] = refs[i][index]


def pack(index, mats):
    _, rows, width = mats[0].shape
    return pl.pallas_call(
        functools.partial(pack_kernel, index),
        out_shape=shape((rows, 3 * width), BF16),
        in_specs=[VMEM] * 3,
        out_specs=VMEM,
        compiler_params=params(60),
        name="pack",
    )(*mats)


def finish_kernel(count, *refs):
    outs = refs[-3:]
    width = outs[0].shape[2]
    for j in range(count):
        for i in range(3):
            outs[i][j] = refs[j][:, i * width : (i + 1) * width].astype(F32)


def finish_after(sums, before):
    rows, width = sums[0].shape[0], sums[0].shape[1] // 3
    return pl.pallas_call(
        functools.partial(finish_kernel, len(sums)),
        out_shape=(shape((len(sums), rows, width), F32),) * 3,
        in_specs=[VMEM] * len(sums) + [HBM] * len(before),
        out_specs=(VMEM,) * 3,
        compiler_params=params(60),
        name="finish",
    )(*sums, *before)


def after_kernel(*refs):
    pass


def after(arrays, before):
    return pl.pallas_call(
        after_kernel,
        out_shape=tuple(shape(a.shape, a.dtype) for a in arrays),
        in_specs=[HBM] * (len(arrays) + len(before)),
        out_specs=(HBM,) * len(arrays),
        input_output_aliases={i: i for i in range(len(arrays))},
        name="after",
    )(*arrays, *before)


def block_rows(sizes):
    return MODEL_WIDTH // (2 * sizes["dp"] * sizes["z"])


def by_blocks(sizes):
    return block_rows(sizes) % 16 == 0


def gather_rows(block, along_dp, ids, sizes):
    ndp, nz = sizes["dp"], sizes["z"]
    pieces = both_cores(along_dp)
    if by_blocks(sizes):
        places = tuple((k, c, start, piece.shape[0]) for k, c, start, piece in pieces)
        return places, [piece for *_, piece in pieces]
    columns = block.shape[-1]
    whole = jnp.zeros((ndp, nz, 2, block_rows(sizes), columns), BF16)
    for k, c, start, piece in pieces:
        order = ids[1] ^ jnp.arange(start, start + piece.shape[0])
        whole = whole.at[ids[0] ^ k, order, ids[2] ^ c].set(piece)
    return None, [whole.reshape(MODEL_WIDTH, columns)]


def split_cores(columns, ids, sizes):
    ndp, nz = sizes["dp"], sizes["z"]
    rows = columns.shape[0]
    blocks = columns.reshape(rows, ndp, nz, 2, block_rows(sizes))
    blocks = jnp.take(jnp.take(blocks, ids[0] ^ jnp.arange(ndp), 1), ids[1] ^ jnp.arange(nz), 2)
    halves = [lax.dynamic_index_in_dim(blocks, ids[2] ^ c, 3, keepdims=False) for c in range(2)]
    return [half.reshape(rows, MODEL_WIDTH // 2) for half in halves]


def turn_kernel(ndp, nz, count, ids, *refs):
    block = MODEL_WIDTH // (2 * ndp * nz)
    turned = refs[-1]
    for i in range(count):
        turned[...] = jnp.transpose(refs[i][...])
        for k in range(ndp):
            for z in range(nz):
                for c in range(2):
                    at = ((ids[0] ^ k) * nz + (ids[1] ^ z)) * 2 + (ids[2] ^ c)
                    place = pl.ds(pl.multiple_of(at * block, block), block)
                    dest = refs[-1 - 2 * count + 2 * i + c]
                    dest[(k * nz + z) * block : (k * nz + z + 1) * block] = turned[place, :]


def turn(arrays, before, ids, sizes):
    if not by_blocks(sizes):
        return [[half.T for half in split_cores(array, ids, sizes)] for array in arrays]
    rows = arrays[0].shape[0]
    halves = pl.pallas_call(
        functools.partial(turn_kernel, sizes["dp"], sizes["z"], len(arrays)),
        out_shape=(shape((MODEL_WIDTH // 2, rows), BF16),) * (2 * len(arrays)),
        in_specs=[SMEM] + [VMEM] * len(arrays) + [HBM] * len(before),
        out_specs=(VMEM,) * (2 * len(arrays)),
        scratch_shapes=[pltpu.VMEM((MODEL_WIDTH, rows), BF16)],
        compiler_params=params(60),
        name="turn",
    )(ids, *arrays, *before)
    return [halves[2 * i : 2 * i + 2] for i in range(len(arrays))]


def sum_dp(own, slots, sizes, before=()):
    ndp, rows = sizes["dp"], block_rows(sizes)
    slots = [None, *slots]
    total = own
    for part in finish_sum(slots, start_sum(slots, ndp), ndp, before):
        total = total + part.astype(F32)
    return [total[z * rows : (z + 1) * rows] for z in range(sizes["z"])]


def leaving_z(blocks):
    sent = blocks[1::2] if len(blocks) == 4 else blocks[1:]
    return jnp.concatenate(sent, axis=0).astype(BF16)


def sum_z(blocks, payload, before=()):
    nz, rows = len(blocks), blocks[0].shape[0]
    if nz != 4:
        parts = [payload[z * rows : (z + 1) * rows] for z in range(nz - 1)]
        return [exchange(part, "z", nz, z + 1) for z, part in enumerate(parts)], payload
    near = exchange(payload, "z", nz, 1)
    (near,) = after([near], before) if before else [near]
    passed = (blocks[2] + near[rows:].astype(F32)).astype(BF16)
    return [near[:rows], exchange(passed, "z", nz, 2)], passed


def load_rows(ids, ndp, nz, places, parts, dest, sem):
    if places is None:
        loads = [pltpu.make_async_copy(parts[0], dest, sem.at[0])]
        loads[0].start()
        return loads
    rows = MODEL_WIDTH // (ndp * nz * 2)
    loads = []
    for (k, c, start, count), part in zip(places, parts):
        for z in range(count):
            block = ((ids[0] ^ k) * nz + (ids[1] ^ (start + z))) * 2 + (ids[2] ^ c)
            place = pl.ds(pl.multiple_of(block * rows, rows), rows)
            copy = pltpu.make_async_copy(part.at[z], dest.at[place, :], sem.at[len(loads)])
            loads.append(copy)
    for load in loads:
        load.start()
    return loads


def start_all(pairs, sem):
    copies = [pltpu.make_async_copy(a, b, sem.at[i]) for i, (a, b) in enumerate(pairs)]
    for copy in copies:
        copy.start()
    return copies


def wait_all(copies):
    for copy in copies:
        copy.wait()


def rms_scale(rows):
    return lax.rsqrt(jnp.mean(rows * rows, axis=-1, keepdims=True) + EPS)


def norm_back(normed, row_scale, grad):
    return row_scale * (grad - normed * jnp.mean(grad * normed, axis=-1, keepdims=True))


def swapped(vals):
    return pltpu.roll(vals, HEAD_SIZE // 2, 1)


def head(h):
    return slice(h * HEAD_SIZE, (h + 1) * HEAD_SIZE)


def seen(rows, length):
    q = lax.broadcasted_iota(jnp.int32, (rows, rows), 0)
    s = lax.broadcasted_iota(jnp.int32, (rows, rows), 1)
    return (s <= q) & (s < length)


def attention_probs(query, key, visible):
    scores = jnp.where(visible, nt(query, key) * SCALE, NEG_FILL)
    expon = jnp.exp(scores - jnp.max(scores, axis=-1, keepdims=True))
    return expon / jnp.sum(expon, axis=-1, keepdims=True)


def route_softmax(router_rows, hidden):
    logits = nt(router_rows, hidden)[:EXPERTS]
    expon = jnp.exp(logits - jnp.max(logits, axis=0, keepdims=True))
    return expon / jnp.sum(expon, axis=0, keepdims=True)


def attend_kernel(ndp, nz, places, count, ids, tokens, cosine, sine, *refs):
    parts = refs[:count]
    qkv, mixed, h_one, gains, router, w, sem = refs[-7:]
    rows = tokens.shape[0]
    loads = load_rows(ids, ndp, nz, places, parts, w, sem)
    tok = tokens[...].astype(F32)
    normed = tok * rms_scale(tok)
    for load in loads:
        load.wait()
    extra = jnp.transpose(w[:, QKV:].astype(F32))
    gains[...] = extra[:8]
    router[...] = extra[2 : 2 + ROUTER].astype(BF16)
    h_one[...] = (normed * extra[0:1]).astype(BF16)
    cos, sin = cosine[...], sine[...]
    for t in range(QKV // TILE):
        pre = nn(h_one[...], w[:, t * TILE : (t + 1) * TILE])
        for i in range(TILE // HEAD_SIZE):
            part = pre[:, head(i)]
            at = t * TILE + i * HEAD_SIZE
            if at < QW + KW:
                part = part * cos + swapped(part) * sin
            qkv[:, at : at + HEAD_SIZE] = part.astype(BF16)
    visible = seen(rows, ids[3])
    for h in range(QUERY_HEADS):
        g = h // GROUP
        probs = attention_probs(qkv[:, head(h)], qkv[:, head(QUERY_HEADS + g)], visible)
        values = qkv[:, head(QUERY_HEADS + KEY_VALUE_HEADS + g)]
        mixed[:, head(h)] = nn(probs.astype(BF16), values).astype(BF16)


def attend(ids, tokens, cosine, sine, weights, before, sizes):
    places, parts = weights
    ndp, nz = sizes["dp"], sizes["z"]
    rows = tokens.shape[0]
    return pl.pallas_call(
        functools.partial(attend_kernel, ndp, nz, places, len(parts)),
        out_shape=(
            shape((rows, QKV), BF16),
            shape((rows, QW), BF16),
            shape((rows, MODEL_WIDTH), BF16),
            shape((8, MODEL_WIDTH), F32),
            shape((ROUTER, MODEL_WIDTH), BF16),
        ),
        in_specs=[SMEM, VMEM, VMEM, VMEM] + [HBM] * (len(parts) + len(before)),
        out_specs=(VMEM,) * 5,
        scratch_shapes=[
            pltpu.VMEM((MODEL_WIDTH, FIRST), BF16),
            pltpu.SemaphoreType.DMA((2 * ndp * nz,)),
        ],
        compiler_params=params(60),
        cost_estimate=cost(2 * rows * MODEL_WIDTH * QKV, 10 * MIB, 12 * rows * rows),
        name="attend",
    )(ids, tokens, cosine, sine, *parts, *before)


def project_kernel(ndp, nz, places, ids, tokens, mixed, gains, *refs):
    *parts, residual, top, low, w, sem = refs
    loads = load_rows(ids, ndp, nz, places, parts, w, sem)
    for load in loads:
        load.wait()
    for t in range(MODEL_WIDTH // TILE):
        lane = slice(t * TILE, (t + 1) * TILE)
        residual[:, lane] = tokens[:, lane].astype(F32) + nn(mixed[...], w[:, lane])
    whole = residual[...]
    h_two = (whole * rms_scale(whole) * gains[1:2]).astype(BF16)
    half = top.shape[0]
    top[...], low[...] = h_two[:half], h_two[half:]


def project(ids, tokens, mixed, gains, weights, sizes):
    places, parts = weights
    ndp, nz = sizes["dp"], sizes["z"]
    rows = tokens.shape[0]
    return pl.pallas_call(
        functools.partial(project_kernel, ndp, nz, places),
        out_shape=(shape((rows, MODEL_WIDTH), F32),)
        + (shape((rows // 2, MODEL_WIDTH), BF16),) * 2,
        in_specs=[SMEM, VMEM, VMEM, VMEM] + [HBM] * len(parts),
        out_specs=(VMEM,) * 3,
        scratch_shapes=[
            pltpu.VMEM((QW, MODEL_WIDTH), BF16),
            pltpu.SemaphoreType.DMA((2 * ndp * nz,)),
        ],
        compiler_params=params(60),
        cost_estimate=cost(2 * rows * MODEL_WIDTH * QW, 8 * MIB),
        name="project",
    )(ids, tokens, mixed, gains, *parts)


def expert_kernel(ndp, rows, width, index, last, near, far, unread, *refs):
    it = iter(refs)
    take = lambda n: [next(it) for _ in range(n)]
    (expert_ref, router_ref) = take(2)
    prev_gates = take(index)
    hid_in, cot_in = take(len(near)), take(len(far))
    (w_in,) = take(1)
    prev_in = take(2) if index else []
    take(unread)
    out_hbm, back_hbm = take(2 * ndp - 1 if last else 1), take(2 * ndp if last else 1)
    gates_ref, terms_hbm = take(2)
    hid, cot, w, x, d, ge, inner, dg, du, pick, pick_t, slot_gate, slot_dot = take(13)
    (terms_buf,) = take(1)
    prev = take(2) if index else []
    in_sem, out_sem = take(2)
    depth = MODEL_WIDTH
    tiles = depth // TILE

    loads = {}

    def load(name, source, dest):
        copy = pltpu.make_async_copy(source, dest, in_sem.at[len(loads)])
        copy.start()
        loads[name] = copy

    for i, (k, start, count) in enumerate(near):
        load(("hid", i), hid_in[i], hid.at[k, pl.ds(start, count), :])
    for i, (k, start, count) in enumerate(far):
        load(("cot", i), cot_in[i], cot.at[k, pl.ds(start, count), :])
    load("w", w_in, w)
    for i in range(len(prev)):
        load(("prev", i), prev_in[i], prev[i])

    expert = expert_ref[0]
    which = lax.broadcasted_iota(jnp.int32, (EXPERTS, rows), 0) == expert
    earlier = (
        (
            lax.broadcasted_iota(jnp.int32, (rows, rows), 0)
            < lax.broadcasted_iota(jnp.int32, (rows, rows), 1)
        )
        .astype(F32)
        .astype(BF16)
    )
    slot = lax.broadcasted_iota(jnp.int32, (CAP, rows), 0).astype(F32)
    for s in range(ndp):
        for i, piece in enumerate(near):
            if piece[0] == s:
                loads["hid", i].wait()
        for i, piece in enumerate(far):
            if piece[0] == s:
                loads["cot", i].wait()
        hidden = hid[s]
        probs = route_softmax(router_ref[...], hidden)
        named = cot[s, rows : rows + NOTE, :rows]
        place = nn(named, earlier)[:EXPERTS]
        named = named[:EXPERTS].astype(F32)
        named_row = jnp.sum(jnp.where(which, named, 0.0), axis=0, keepdims=True)
        gate_row = jnp.sum(jnp.where(which, probs, 0.0), axis=0, keepdims=True)
        place_row = jnp.sum(jnp.where(which, place, 0.0), axis=0, keepdims=True)
        chosen = jnp.where((slot == place_row) & (named_row > 0.5), 1.0, 0.0)
        pick[s] = chosen.astype(BF16)
        pick_t[s] = jnp.transpose(chosen).astype(BF16)
        at = pl.ds(s * CAP, CAP)
        gate = jnp.sum(chosen * gate_row, axis=1, keepdims=True)
        slot_gate[at, :] = jnp.broadcast_to(gate, (CAP, 128))
        x[at, :] = nn(pick[s], hidden).astype(BF16)
        grads = nn(pick[s], cot[s, :rows])
        d[at, :] = grads.astype(BF16)
        ge[at, :] = (gate * grads).astype(BF16)
    loads["w"].wait()

    def hidden_units(t, carry):
        at = pl.multiple_of(t * TILE, TILE)
        gate_pre = nn(x[...], w[:, pl.ds(at, TILE)])
        up_pre = nn(x[...], w[:, pl.ds(width + at, TILE)])
        grad_inner = nn(ge[...], w[:, pl.ds(2 * width + at, TILE)])
        sig = 1.0 / (1.0 + jnp.exp(-gate_pre))
        act = gate_pre * sig
        inner[:, pl.ds(at, TILE)] = (act * up_pre).astype(BF16)
        dg[:, pl.ds(at, TILE)] = (
            grad_inner * up_pre * sig * (1.0 + gate_pre * (1.0 - sig))
        ).astype(BF16)
        du[:, pl.ds(at, TILE)] = (grad_inner * act).astype(BF16)
        return carry

    lax.fori_loop(0, width // TILE, hidden_units, 0)
    slot_dot[...] = jnp.zeros_like(slot_dot)
    for i in range(len(prev)):
        loads["prev", i].wait()

    noted = (rows + NOTE) // 2

    def stores(t):
        lane = pl.ds(pl.multiple_of(t * TILE, TILE), TILE)
        copies = [(terms_buf.at[lane, :], terms_hbm.at[lane, :])]
        if not last:
            body = pl.ds(0, rows)
            copies.append((hid.at[:, :, lane], out_hbm[0].at[:, :, lane]))
            copies.append((cot.at[:, body, lane], back_hbm[0].at[:, body, lane]))
        else:
            copies.append((hid.at[0, :, lane], out_hbm[0].at[:, lane]))
            for i in range(2, 2 * ndp):
                first = pl.ds(i % 2 * (rows // 2), rows // 2)
                copies.append((hid.at[i // 2, first, lane], out_hbm[i - 1].at[:, lane]))
            for i in range(2 * ndp):
                body = pl.ds(0, noted if i % 2 == 0 else rows - noted)
                taken = pl.ds(i % 2 * noted, noted if i % 2 == 0 else rows - noted)
                copies.append((cot.at[i // 2, taken, lane], back_hbm[i].at[body, lane]))
        return [
            pltpu.make_async_copy(source, dest, out_sem.at[i, t])
            for i, (source, dest) in enumerate(copies)
        ]

    def features(t, carry):
        lane = pl.ds(pl.multiple_of(t * TILE, TILE), TILE)
        result = nt(inner[...], w[lane, pl.ds(2 * width, width)]).astype(BF16).astype(F32)
        partial = jnp.sum(result * d[:, lane].astype(F32), axis=1, keepdims=True)
        slot_dot[...] += jnp.broadcast_to(partial, slot_dot.shape)
        gated = (slot_gate[:, :1] * result).astype(BF16)
        grad_in = (
            nt(dg[...], w[lane, pl.ds(0, width)]) + nt(du[...], w[lane, pl.ds(width, width)])
        ).astype(BF16)
        for s in range(ndp):
            part = slice(s * CAP, (s + 1) * CAP)
            sent = nn(pick_t[s], gated[part])
            back = nn(pick_t[s], grad_in[part])
            if prev:
                sent = sent + prev[0][s, :, lane].astype(F32)
                back = back + prev[1][s, :rows, lane].astype(F32)
            hid[s, :, lane] = sent.astype(BF16)
            cot[s, :rows, lane] = back.astype(BF16)
        x_t = jnp.transpose(x[:, lane])
        terms_buf[lane, pl.ds(0, width)] = nn(x_t, dg[...]).astype(BF16)
        terms_buf[lane, pl.ds(width, width)] = nn(x_t, du[...]).astype(BF16)
        ge_t = jnp.transpose(ge[:, lane])
        terms_buf[lane, pl.ds(2 * width, width)] = nn(ge_t, inner[...]).astype(BF16)
        for store in stores(t):
            store.start()
        return carry

    lax.fori_loop(0, tiles, features, 0)
    line = lax.broadcasted_iota(jnp.int32, (NOTE, 3 * rows), 0)
    notes = []
    for s in range(ndp):
        part = slice(s * CAP, (s + 1) * CAP)
        own = jnp.sum(pick[s].astype(F32) * slot_dot[part, :1], axis=0, keepdims=True)
        gates_ref[s] = own
        if not last:
            continue
        note = jnp.zeros((NOTE, 3 * rows), F32)
        for j, row in enumerate([p[s] for p in prev_gates] + [own]):
            high = row.astype(BF16).astype(F32)
            middle = (row - high).astype(BF16).astype(F32)
            low = row - high - middle
            at = expert - index + j
            note = jnp.where(line == at, jnp.concatenate([high, middle, low], axis=1), note)
        cot[s, rows : rows + NOTE, : 3 * rows] = note.astype(BF16)
        notes.append(
            pltpu.make_async_copy(
                cot.at[s, pl.ds(rows, NOTE), :],
                back_hbm[2 * s + 1].at[pl.ds(rows - noted, NOTE), :],
                out_sem.at[4 * ndp + 1, s],
            )
        )
        notes[-1].start()
    for t in range(tiles):
        for store in stores(t):
            store.wait()
    for note in notes:
        note.wait()


def run_expert(index, last, expert, router, hidden, grads, w_all, prev, prev_gates, ndp, before):
    rows = 2 * hidden[0][2].shape[0]
    near, far = (tuple((k, at, p.shape[0]) for k, at, p in group) for group in (hidden, grads))
    width = w_all.shape[1] // 3
    slots = ndp * CAP
    depth = MODEL_WIDTH
    tiles = depth // TILE
    scratch = [
        pltpu.VMEM((ndp, rows, depth), BF16),
        pltpu.VMEM((ndp, rows + NOTE, depth), BF16),
        pltpu.VMEM((depth, 3 * width), BF16),
        pltpu.VMEM((slots, depth), BF16),
        pltpu.VMEM((slots, depth), BF16),
        pltpu.VMEM((slots, depth), BF16),
        pltpu.VMEM((slots, width), BF16),
        pltpu.VMEM((slots, width), BF16),
        pltpu.VMEM((slots, width), BF16),
        pltpu.VMEM((ndp, CAP, rows), BF16),
        pltpu.VMEM((ndp, rows, CAP), BF16),
        pltpu.VMEM((slots, 128), F32),
        pltpu.VMEM((slots, 128), F32),
        pltpu.VMEM((depth, 3 * width), BF16),
    ]
    if index:
        scratch += [
            pltpu.VMEM((ndp, rows, depth), BF16),
            pltpu.VMEM((ndp, rows + NOTE, depth), BF16),
        ]
    scratch += [
        pltpu.SemaphoreType.DMA((len(near) + len(far) + 3,)),
        pltpu.SemaphoreType.DMA((4 * ndp + 2, max(tiles, ndp))),
    ]
    sent = [shape((ndp, rows, depth), BF16), shape((ndp, rows + NOTE, depth), BF16)]
    if last:
        sent = [shape((rows, depth), BF16)]
        sent += [shape((rows // 2, depth), BF16)] * (2 * ndp - 2)
        sent += [shape(((rows + NOTE) // 2, depth), BF16)] * (2 * ndp)
    flops = 2 * slots * depth * width * 9 + 8 * ndp * CAP * rows * depth
    return pl.pallas_call(
        functools.partial(
            expert_kernel, ndp, rows, width, index, last, near, far, len(before)
        ),
        out_shape=(
            *sent,
            shape((ndp, 1, rows), F32),
            shape((depth, 3 * width), BF16),
        ),
        in_specs=[SMEM, VMEM]
        + [VMEM] * len(prev_gates)
        + [HBM] * (len(near) + len(far) + 1 + len(prev) + len(before)),
        out_specs=(HBM,) * len(sent) + (VMEM, HBM),
        scratch_shapes=scratch,
        compiler_params=params(60),
        cost_estimate=cost(flops, 40 * MIB, slots * width),
        name="expert",
    )(
        expert,
        router,
        *prev_gates,
        *(piece for *_, piece in hidden),
        *(piece for *_, piece in grads),
        w_all,
        *prev,
        *before,
    )


def back_kernel(ndp, nz, places, count, given, unread, ids, gains, router, cosine, sine, *refs):
    refs = list(refs)
    take = lambda n: [refs.pop(0) for _ in range(n)]
    data, backs, parts = take(5), take(given), take(count)
    take(unread)
    out_resid, out_attn, out_pre, notes = take(4)
    residual, top, low, grads, qkv = held = take(5)
    got = take(given)
    w, grad_mixed, grad_resid, grad_attn, grad_pre, sem, data_sem, out_sem = refs
    rows = residual.shape[0]
    fetched = start_all(list(zip(backs + data[1:3] + data[:1] + data[3:], got + held[1:3] + held[:1] + held[3:])), data_sem)
    loads = load_rows(ids, ndp, nz, places, parts, w, sem)
    wait_all(fetched[:given])
    whole = jnp.concatenate([got[0][...], got[1][...]], axis=0).astype(F32)
    for part in got[2:]:
        whole = whole + part[...].astype(F32)
    grad_h = whole[:rows]
    note = whole[rows : rows + EXPERTS, : 3 * rows]
    grad_route = note[:, :rows] + note[:, rows : 2 * rows] + note[:, 2 * rows :]
    wait_all(fetched[given : given + 4])
    hidden = jnp.concatenate([top[...], low[...]], axis=0)
    probs = route_softmax(router[...], hidden)
    grad_logits = probs * (grad_route - jnp.sum(probs * grad_route, axis=0, keepdims=True))
    grad_logits = jnp.concatenate([grad_logits, jnp.zeros_like(grad_logits)], axis=0)
    grad_logits = grad_logits.astype(BF16)
    grad_h = grad_h + tn(grad_logits, router[...])
    res = residual[...]
    scale = rms_scale(res)
    normed = res * scale
    notes[0:8] = jnp.broadcast_to(
        jnp.sum(normed * grad_h, axis=0, keepdims=True), (8, MODEL_WIDTH)
    )
    notes[8:16] = nn(grad_logits, hidden)[:EXPERTS]
    live = lax.broadcasted_iota(jnp.int32, (rows, 1), 0) < ids[3]
    final = jnp.where(live, grads[...].astype(F32), 0.0)
    total = final + norm_back(normed, scale, grad_h * gains[1:2])
    grad_resid[...] = total
    grad_attn[...] = total.astype(BF16)
    stores = start_all([(grad_attn, out_attn), (grad_resid, out_resid)], out_sem)
    wait_all(loads)
    for t in range(QW // TILE):
        lane = slice(t * TILE, (t + 1) * TILE)
        grad_mixed[:, lane] = nt(grad_attn[...], w[lane, :]).astype(BF16)
    wait_all(fetched[given + 4 :])
    source = lax.broadcasted_iota(jnp.int32, (rows, rows), 0)
    visible = (source <= lax.broadcasted_iota(jnp.int32, (rows, rows), 1)) & (source < ids[3])
    cos, sin = cosine[...], sine[...]
    for g in range(KEY_VALUE_HEADS):
        key = qkv[:, head(QUERY_HEADS + g)]
        value = qkv[:, head(QUERY_HEADS + KEY_VALUE_HEADS + g)]
        grad_key = jnp.zeros((rows, HEAD_SIZE), F32)
        grad_value = jnp.zeros((rows, HEAD_SIZE), F32)
        for h in range(g * GROUP, (g + 1) * GROUP):
            query, grad = qkv[:, head(h)], grad_mixed[:, head(h)]
            scores = jnp.where(visible, nt(key, query) * SCALE, NEG_FILL)
            expon = jnp.exp(scores - jnp.max(scores, axis=0, keepdims=True))
            probs = expon / jnp.sum(expon, axis=0, keepdims=True)
            grad_probs = nt(value, grad)
            grad_value = grad_value + nn(probs.astype(BF16), grad)
            row_dot = jnp.sum(probs * grad_probs, axis=0, keepdims=True)
            grad_scores = (probs * (grad_probs - row_dot)).astype(BF16)
            grad_query = tn(grad_scores, key) * SCALE
            grad_key = grad_key + nn(grad_scores, query)
            grad_pre[:, head(h)] = (grad_query * cos - swapped(grad_query) * sin).astype(BF16)
        grad_key = grad_key * SCALE
        grad_pre[:, head(QUERY_HEADS + g)] = (
            grad_key * cos - swapped(grad_key) * sin
        ).astype(BF16)
        grad_pre[:, head(QUERY_HEADS + KEY_VALUE_HEADS + g)] = grad_value.astype(BF16)
    last = pltpu.make_async_copy(grad_pre, out_pre, out_sem.at[2])
    last.start()
    wait_all(stores + [last])


def back(
    ids, residual, h_two, grads, gains, router, cosine, sine, qkv, backs, weights, before, sizes
):
    ndp, nz = sizes["dp"], sizes["z"]
    places, parts = weights
    rows = residual.shape[0]
    data = [residual, *h_two, grads, qkv]
    made = [
        shape((rows, MODEL_WIDTH), F32),
        shape((rows, MODEL_WIDTH), BF16),
        shape((rows, QKV), BF16),
    ]
    room = lambda array: pltpu.VMEM(array.shape, array.dtype)
    return pl.pallas_call(
        functools.partial(
            back_kernel, ndp, nz, places, len(parts), len(backs), len(before)
        ),
        out_shape=(*made, shape((16, MODEL_WIDTH), F32)),
        in_specs=[SMEM]
        + [VMEM] * 4
        + [HBM] * (len(data) + len(backs) + len(parts) + len(before)),
        out_specs=(HBM, HBM, HBM, VMEM),
        scratch_shapes=[
            *(room(array) for array in data + backs),
            pltpu.VMEM((QW, MODEL_WIDTH), BF16),
            pltpu.VMEM((rows, QW), BF16),
            *(room(array) for array in made),
            pltpu.SemaphoreType.DMA((2 * ndp * nz,)),
            pltpu.SemaphoreType.DMA((len(data) + len(backs),)),
            pltpu.SemaphoreType.DMA((3,)),
        ],
        compiler_params=params(60),
        cost_estimate=cost(3 * rows * MODEL_WIDTH * QW, 16 * MIB, 12 * rows * rows),
        name="back",
    )(ids, gains, router, cosine, sine, *data, *backs, *parts, *before)


def tokens_back_kernel(ndp, nz, places, count, ids, tokens, gains, grad_pre, grad_resid, *refs):
    parts = refs[:count]
    grad_tokens, w, sem = refs[-3:]
    loads = load_rows(ids, ndp, nz, places, parts, w, sem)
    tok = tokens[...].astype(F32)
    scale = rms_scale(tok)
    normed = tok * scale
    for load in loads:
        load.wait()
    for t in range(MODEL_WIDTH // TILE):
        lane = slice(t * TILE, (t + 1) * TILE)
        grad_tokens[:, lane] = nt(grad_pre[...], w[lane, :QKV])
    grad_h = grad_tokens[...]
    grad_tokens[...] = grad_resid[...] + norm_back(normed, scale, grad_h * gains[0:1])


def tokens_back(ids, tokens, gains, grad_pre, grad_resid, weights, before, sizes):
    ndp, nz = sizes["dp"], sizes["z"]
    places, parts = weights
    rows = tokens.shape[0]
    return pl.pallas_call(
        functools.partial(tokens_back_kernel, ndp, nz, places, len(parts)),
        out_shape=shape((rows, MODEL_WIDTH), F32),
        in_specs=[SMEM] + [VMEM] * 4 + [HBM] * (len(parts) + len(before)),
        out_specs=VMEM,
        scratch_shapes=[
            pltpu.VMEM((MODEL_WIDTH, FIRST), BF16),
            pltpu.SemaphoreType.DMA((2 * ndp * nz,)),
        ],
        compiler_params=params(60),
        cost_estimate=cost(2 * rows * MODEL_WIDTH * QKV, 12 * MIB),
        name="tokens_back",
    )(ids, tokens, gains, grad_pre, grad_resid, *parts, *before)


def terms_kernel(ndp, nz, noted, unread, ids, *refs):
    refs = list(refs)
    take = lambda n: [refs.pop(0) for _ in range(n)]
    notes, given = take(2 if noted else 0), take(4)
    take(unread)
    count = 2 * ndp - 1
    outs, held, dests = take(count), take(4), take(count)
    note_rows, in_sem, out_sem = refs
    wait_all(start_all(list(zip(given, held)), in_sem))
    left = jnp.concatenate([held[0][...], held[1][...]], axis=1)
    right = jnp.concatenate([held[2][...], held[3][...]], axis=0)
    slot = MODEL_WIDTH // (2 * ndp)
    stores = []

    def put(lane, value):
        dests[0][:, lane] = value[:slot]
        for i in range(1, count):
            at = slot + (i - 1) * (slot // 2)
            dests[i][:, lane] = value[at : at + slot // 2].astype(BF16)
        pairs = [(dests[i].at[:, lane], outs[i].at[:, lane]) for i in range(count)]
        stores.extend(start_all(pairs, out_sem.at[len(stores) // count]))

    if noted:
        note = notes[0][...] + notes[1][...]
        block = jnp.concatenate([note, jnp.zeros((PAD - 16, note.shape[1]), F32)], axis=0)
        block = jnp.transpose(block)
    if noted == 1:
        note_rows[...] = block
        rows = MODEL_WIDTH // (2 * ndp * nz)
        taken = []
        for k in range(ndp):
            for z in range(nz):
                at = ((ids[0] ^ k) * nz + (ids[1] ^ z)) * 2 + ids[2]
                taken.append(note_rows[pl.ds(pl.multiple_of(at * rows, rows), rows), :])
        block = jnp.concatenate(taken, axis=0)
    if noted:
        put(slice(right.shape[1], right.shape[1] + PAD), block)
    for t in range(right.shape[1] // TILE):
        lane = slice(t * TILE, (t + 1) * TILE)
        put(lane, nn(left, right[:, lane]))
    wait_all(stores)


def weight_terms(ids, left, right, notes, before, sizes):
    ndp, nz = sizes["dp"], sizes["z"]
    slot = MODEL_WIDTH // (2 * ndp)
    columns = right[0].shape[1] + (PAD if notes else 0)
    noted = 0 if not notes else 1 if notes[0].shape[1] == MODEL_WIDTH else 2
    made = [shape((slot, columns), F32)] + [shape((slot // 2, columns), BF16)] * (2 * ndp - 2)
    room = lambda array: pltpu.VMEM(array.shape, array.dtype)
    arrays = [*left, *right]
    found = pl.pallas_call(
        functools.partial(terms_kernel, ndp, nz, noted, len(before)),
        out_shape=tuple(made),
        in_specs=[SMEM] + [VMEM] * len(notes) + [HBM] * (4 + len(before)),
        out_specs=(HBM,) * len(made),
        scratch_shapes=[
            *(room(array) for array in arrays + made),
            pltpu.VMEM((MODEL_WIDTH, PAD), F32),
            pltpu.SemaphoreType.DMA((4,)),
            pltpu.SemaphoreType.DMA((columns // TILE + 1, len(made))),
        ],
        compiler_params=params(60),
        cost_estimate=cost(2 * MODEL_WIDTH * left[0].shape[1] * columns, 5 * MIB),
        name="weight_terms",
    )(ids, *notes, *arrays, *before)
    return found[0], [tuple(found[i : i + 2]) for i in range(1, len(found), 2)]


def settle_kernel(count, *refs):
    own, got = refs[0], refs[1 : 1 + count]
    mats = refs[1 + count : 4 + count]
    gain = refs[4 + count]
    outs, gains, router = refs[-5:-2], refs[-2], refs[-1]
    total = own[...]
    for part in got:
        total = total + part[...].astype(F32)
    dot, at = jnp.zeros((total.shape[0], 1), F32), 0
    for mat, out in zip(mats, outs):
        width = mat.shape[1]
        part = total[:, at : at + width]
        out[...] = part
        dot = dot + jnp.sum(part * mat[...].astype(F32), axis=1, keepdims=True)
        at += width
    small = total[:, at:]
    router[...] = small[:, 8 : 8 + EXPERTS]
    lane = lax.broadcasted_iota(jnp.int32, small.shape, 1)
    turned = jnp.transpose(jnp.where(lane == 1, dot, small))
    gains[0:1] = turned[1:2] / gain[...]
    gains[1:2] = turned[0:1]


def settle(own, got, mats, gain, before):
    rows = own.shape[0]
    return pl.pallas_call(
        functools.partial(settle_kernel, len(got)),
        out_shape=tuple(shape(mat.shape, F32) for mat in mats)
        + (shape((2, rows), F32), shape((rows, EXPERTS), F32)),
        in_specs=[VMEM] * (1 + len(got) + 4) + [HBM] * len(before),
        out_specs=(VMEM,) * 5,
        compiler_params=params(60),
        name="settle",
    )(own, *got, *mats, gain, *before)


def rope_tables(rows):
    half = HEAD_SIZE // 2
    position = jnp.arange(rows).astype(F32)
    inverse = ROPE_BASE ** (-jnp.arange(half).astype(F32) / half)
    angles = position[:, None] * inverse[None, :]
    cosine, sine = jnp.cos(angles), jnp.sin(angles)
    return jnp.concatenate([cosine, cosine], axis=1), jnp.concatenate([-sine, sine], axis=1)


def per_device(
    sizes,
    tokens,
    lengths,
    routes,
    cotangent,
    gain_one,
    w_query,
    key_matrix,
    value_matrix,
    w_out,
    gain_two,
    w_router,
    w_gate,
    w_up,
    w_down,
):
    ndp = sizes["dp"]
    rows = tokens.shape[0]
    local, _, width = w_gate.shape
    me_dp = lax.axis_index("dp")
    length = lengths[0]
    ids = jnp.stack([me_dp, lax.axis_index("z"), lax.axis_index("core"), length]).astype(jnp.int32)
    live = (jnp.arange(rows) < length)[:, None]
    expert_ids = jnp.arange(EXPERTS, dtype=jnp.int32)

    extra = jnp.concatenate([gain_one[:, None], gain_two[:, None], w_router], axis=1)
    extra = jnp.pad(extra, ((0, 0), (0, PAD - extra.shape[1])))
    first = jnp.concatenate([w_query, key_matrix, value_matrix, extra], axis=1)
    named = jnp.any(routes[None, :, :] == expert_ids[:, None, None], axis=2).astype(BF16)
    named = jnp.pad(named, ((0, NOTE - EXPERTS), (0, MODEL_WIDTH - rows)))
    grad_low = jnp.where(live, cotangent, jnp.zeros_like(cotangent))
    grad_low = jnp.concatenate([grad_low, named], axis=0)
    grad_near = start_dp(grad_low, ndp)

    nz = sizes["z"]
    first_z = [first] + [exchange(first, "z", nz, k) for k in range(1, nz)]
    second_z = [w_out] + [exchange(w_out, "z", nz, k) for k in range(1, nz)]
    first_block = stack_after(first_z, grad_near)
    first_near = start_dp(first_block, ndp)
    first_dp = pass_on(first_block, first_near, ndp, second_z[1:])
    packed = after([pack(j, (w_gate, w_up, w_down)) for j in range(local)], first_z[1:] + grad_near)
    expert_mats = [lax.all_gather(p, ("z", "core"), axis=0, tiled=True) for p in packed]
    second_block = stack_after(second_z, [piece for *_, piece in first_dp[1:3]])
    second_dp = gather_direct(second_block, ndp)

    cosine, sine = rope_tables(rows)
    weights_in = gather_rows(first, first_dp, ids, sizes)
    qkv, mixed, h_one, gains, router = attend(ids, tokens, cosine, sine, weights_in, [], sizes)
    second_far = after([piece for *_, piece in second_dp[1:]], [mixed])
    second_dp = [(k, 0, piece) for k, piece in enumerate([second_block, *second_far])]
    grad_far = pass_on(grad_low, grad_near, ndp, second_far)
    weights_out = gather_rows(w_out, second_dp, ids, sizes)
    residual, *h_two = project(ids, tokens, mixed, gains, weights_out, sizes)
    hidden = gather_halves(h_two, ndp)
    turned = turn([mixed, h_one], [hidden[2][2]], ids, sizes)
    mixed, h_one = ([mine, exchange(other, "core", 2, 1)] for mine, other in turned)

    prev, gate_grads, sums = (), [], []
    for j in range(local):
        expert = (me_dp * local + j).astype(jnp.int32).reshape(1)
        *prev, grad_gate, terms = run_expert(
            j,
            j == local - 1,
            expert,
            router,
            hidden,
            grad_far,
            expert_mats[j],
            prev,
            gate_grads,
            ndp,
            [*mixed, *h_one],
        )
        gate_grads.append(grad_gate)
        sums.append(lax.psum_scatter(terms, ("z", "core"), scatter_dimension=0, tiled=True))
    count = 2 * ndp - 1
    outs, backs = prev[:count], prev[count:]
    pairs = [tuple(backs[2 * k : 2 * k + 2]) for k in range(ndp)]
    backs = [*pairs[0], *finish_sum(pairs, start_sum(pairs, ndp), ndp)]
    out_slots = [None] + [tuple(outs[i : i + 2]) for i in range(1, count, 2)]
    out_past = start_sum(out_slots, ndp)

    grad_resid, grad_attn, grad_pre, notes = back(
        ids,
        residual,
        h_two,
        cotangent,
        gains,
        router,
        cosine,
        sine,
        qkv,
        backs,
        weights_out,
        [],
        sizes,
    )
    if not by_blocks(sizes):
        notes = split_cores(notes, ids, sizes)
        notes = notes[0], exchange(notes[1], "core", 2, 1)
    else:
        notes = notes, exchange(notes, "core", 2, 1)
    grad_attn = grad_attn, exchange(grad_attn, "core", 2, 1)
    grad_pre = grad_pre, exchange(grad_pre, "core", 2, 1)
    out_terms = weight_terms(ids, mixed, grad_attn, (), grad_pre[1:], sizes)
    in_terms = weight_terms(
        ids, h_one, grad_pre, notes, sums[:-1] + [out_terms[0]] + out_past, sizes
    )
    out_blocks = sum_dp(*out_terms, sizes, in_terms[:1])
    in_blocks = sum_dp(*in_terms, sizes)
    out_payload, in_payload = leaving_z(out_blocks), leaving_z(in_blocks)
    late, _ = sum_z(out_blocks, out_payload, [in_payload])
    got, leaving = sum_z(in_blocks, in_payload)
    grad_tokens = tokens_back(
        ids, tokens, gains, grad_pre[0], grad_resid, weights_in, [in_payload], sizes
    )
    block = residual + outs[0].astype(F32)
    for part in finish_sum(out_slots, out_past, ndp, [in_payload]):
        block = block + part.astype(F32)
    block_out = block.astype(BF16)
    gain = gain_one.astype(F32)[None]
    *grad_in, grad_gains, grad_router = settle(
        in_blocks[0], got, (w_query, key_matrix, value_matrix), gain, [block_out]
    )
    expert_sums = finish_after(sums, [leaving])
    late = [late[0], *after(late[1:], [leaving])]
    grad_out = out_blocks[0] + sum(part.astype(F32) for part in late)
    return (
        block_out,
        grad_tokens,
        grad_gains[0],
        *grad_in,
        grad_out,
        grad_gains[1],
        grad_router,
        *expert_sums,
    )


def solution(mesh):
    ndp, nf = mesh.shape["dp"], mesh.shape["fsdp"]
    sizes = {"dp": ndp, "z": nf // 2, "core": 2}
    split = Mesh(mesh.devices.reshape(ndp, nf // 2, 2), ("dp", "z", "core"))
    every = ("dp", "z", "core")
    rows = P(every, None)
    vector = P(every)
    expert = P("dp", ("z", "core"), None)

    def run(*args):
        return per_device(sizes, *args)

    return jax.shard_map(
        run,
        mesh=split,
        in_specs=(rows, vector, rows, rows, vector, rows, rows, rows, rows, vector, rows)
        + (expert,) * 3,
        out_specs=(rows, rows, vector, rows, rows, rows, rows, vector, rows) + (expert,) * 3,
        check_vma=False,
    )
```
